32 devices in a mesh: items: 2 (over x), rows: 16 (over z, y, core).
Axes of the slice: x: 2, y: 2, z: 4, core: 2. Of those that a mesh axis runs over, the one named last changes fastest.
Arguments:
- latents: float32 [2, 2048, 1536], P('items', 'rows'), may hold values from -6 to 6
- conditions: bfloat16 [2, 2, 1024], P('items'), may hold values from -6 to 6
- captions: bfloat16 [2, 2, 256, 4096], P('items'), may hold values from -6 to 6
- row_counts: int32 [2, 16, 2], P('items', 'rows'), may hold values from 16 to 112, as said below
- text_lengths: int32 [2, 2], P('items'), may hold values from 64 to 256, as said below
- qkv_weight: bfloat16 [1536, 4608], P(('items', 'rows')), may hold values from -0.15625 to 0.15625
- text_weight: bfloat16 [4096, 3072], P(('items', 'rows')), may hold values from -0.09375 to 0.09375
- out_weight: bfloat16 [1536, 1536], P(('items', 'rows')), may hold values from -0.15625 to 0.15625
- gate_up_weight: bfloat16 [1536, 8192], P(('items', 'rows')), may hold values from -0.15625 to 0.15625
- down_weight: bfloat16 [4096, 1536], P(('items', 'rows')), may hold values from -0.09375 to 0.09375
- ada_weight: bfloat16 [1024, 6144], P(('items', 'rows')), may hold values from -0.1875 to 0.1875
- ada_bias: bfloat16 [6144], P(('items', 'rows')), may hold values from -3 to 3
- norm_gains: bfloat16 [7, 1536], P(None, ('items', 'rows')), may hold values from 0.5 to 1.5
- head_gates: bfloat16 [24], replicated, may hold values from -3 to 3
- cotangent: float32 [2, 2048, 1536], P('items', 'rows'), may hold values from -6 to 6
Outputs:
- block_out: float32 [2, 2048, 1536], P('items', 'rows')
- latent_grad: float32 [2, 2048, 1536], P('items', 'rows')
- qkv_grad: float32 [1536, 4608], P(('items', 'rows'))
- text_grad: float32 [4096, 3072], P(('items', 'rows'))
- out_grad: float32 [1536, 1536], P(('items', 'rows'))
- gate_up_grad: float32 [1536, 8192], P(('items', 'rows'))
- down_grad: float32 [4096, 1536], P(('items', 'rows'))
- ada_grad: float32 [1024, 6144], P(('items', 'rows'))
- bias_grad: float32 [6144], P(('items', 'rows'))
- gains_grad: float32 [7, 1536], P(None, ('items', 'rows'))
- head_gates_grad: float32 [24], replicated
The draws below stay inside these ranges and needn't reach their ends.
Inputs may be any that keep to these rules, and one draw needn't show every extreme that they name: `row_counts`: for each group and each device of rows, how many of that device's 128 rows belong to the group's clip (first) and to its image (second); the clip's rows come first; the two sum to 128. `text_lengths`: live caption tokens are the first ones of each caption.
All inputs are finite; a program needn't handle non-finite values.
Results may differ from the reference program's by a relative error of at most 0.013.
Values may be sent and summed in bfloat16 or wider, within the bound.
A program may use at most 768 MiB of HBM per device.

```python
import jax
import jax.numpy as jnp
from jax import lax

D = 1536
HEADS = 24
HEAD = 64
FF = 4096
TEXT_DIM = 4096
COND = 1024
TEXT = 256
FRAMES = 2
TOK_DEV = 128
GROUPS = 2
SHARDS = 16
TOKENS_G = 2048
N_ROWS = 16


def draw_row_counts(key, part):
    key = jax.random.fold_in(key, 11)
    drawn = jax.random.randint(key, (GROUPS, SHARDS), TOK_DEV // 2, 7 * TOK_DEV // 8 + 1)
    first_device = jnp.arange(SHARDS, dtype=jnp.int32)[None, :] == 0
    clip_rows = jnp.where(first_device, 7 * TOK_DEV // 8, drawn)
    return jnp.stack([clip_rows, TOK_DEV - clip_rows], axis=-1).astype(jnp.int32)


def draw_text_lengths(key, part):
    key = jax.random.fold_in(key, 5)
    drawn = jax.random.randint(key, (GROUPS, FRAMES), TEXT // 4, TEXT + 1)
    group_line = jnp.arange(GROUPS, dtype=jnp.int32)[:, None]
    frame_line = jnp.arange(FRAMES, dtype=jnp.int32)[None, :]
    longest = (group_line == 0) & (frame_line == 0)
    shortest = (group_line == GROUPS - 1) & (frame_line == FRAMES - 1)
    return jnp.where(longest, TEXT, jnp.where(shortest, TEXT // 4, drawn)).astype(jnp.int32)


def shard_levels(rng, extent, cuts, low, top_value):
    loudness = 1.0
    for axis_at, shards_of in cuts:
        heights = jax.random.uniform(jax.random.fold_in(jax.random.fold_in(rng, 6), axis_at), (shards_of,), jnp.float32, low / len(cuts), top_value / len(cuts))
        loudness = loudness * jnp.repeat(jnp.exp(heights), extent[axis_at] // shards_of).reshape((-1,) + (1,) * (len(extent) - 1 - axis_at))
    return loudness


def gaussian(own_key, shape, scale, reach, split=(), kind=jnp.bfloat16):
    entries = scale * jax.random.normal(own_key, shape, jnp.float32)
    if split:
        entries = entries * shard_levels(own_key, shape, split, -0.22, 0.18)
    return jnp.clip(entries, -reach, reach).astype(kind)


def setup_inputs(seed: int = 0) -> dict:
    streams_of = jax.random.split(jax.random.key(seed), 16)
    return {
        "latents": gaussian(streams_of[0], (GROUPS, TOKENS_G, D), 1.0, 6.0, ((0, 2), (1, 16)), jnp.float32),
        "conditions": gaussian(streams_of[1], (GROUPS, FRAMES, COND), 1.0, 6.0, ((0, 2),)),
        "captions": gaussian(streams_of[2], (GROUPS, FRAMES, TEXT, TEXT_DIM), 1.0, 6.0, ((0, 2),)),
        "row_counts": draw_row_counts(jax.random.fold_in(streams_of[15], 71), 0),
        "text_lengths": draw_text_lengths(jax.random.fold_in(streams_of[15], 71), 0),
        "qkv_weight": gaussian(streams_of[5], (D, 3 * D), D ** -0.5, 0.15625, ((0, 32),)),
        "text_weight": gaussian(streams_of[6], (TEXT_DIM, 2 * D), TEXT_DIM ** -0.5, 0.09375, ((0, 32),)),
        "out_weight": gaussian(streams_of[7], (D, D), D ** -0.5, 0.15625, ((0, 32),)),
        "gate_up_weight": gaussian(streams_of[8], (D, 2 * FF), D ** -0.5, 0.15625, ((0, 32),)),
        "down_weight": gaussian(streams_of[9], (FF, D), FF ** -0.5, 0.09375, ((0, 32),)),
        "ada_weight": gaussian(streams_of[10], (COND, 4 * D), COND ** -0.5, 0.1875, ((0, 32),)),
        "ada_bias": gaussian(streams_of[11], (4 * D,), 0.5, 3.0, ((0, 32),)),
        "norm_gains": jnp.clip(1.0 + 0.1 * jax.random.normal(streams_of[12], (7, D), jnp.float32), 0.5, 1.5).astype(jnp.bfloat16),
        "head_gates": gaussian(streams_of[13], (HEADS,), 1.0, 3.0),
        "cotangent": gaussian(streams_of[14], (GROUPS, TOKENS_G, D), 1.0, 6.0, ((0, 2), (1, 16)), jnp.float32),
    }


epsilon = 1e-05
theta_base = 10000.0
score_scale = 0.125
masked_value = -1e+30
highest = lax.Precision.HIGHEST

@jax.custom_vjp
def low(v):
    return lax.optimization_barrier(v.astype(jnp.bfloat16)).astype(jnp.float32)

@jax.custom_vjp
def low_back(v):
    return v

def low_keep(v):
    return (low(v), None)

def low_pass(kept, grad):
    return (grad,)

def back_keep(v):
    return (v, None)

def back_low(kept, grad):
    return (low(grad),)
low.defvjp(low_keep, low_pass)
low_back.defvjp(back_keep, back_low)

def matmul(left, right):
    return jnp.dot(left, right, precision=highest, preferred_element_type=jnp.float32)

def normed(value, gain_row):
    return value * lax.rsqrt(lax.optimization_barrier(jnp.mean(value * value, axis=-1, keepdims=True)) + epsilon) * gain_row

def rotate(value, position, head_size):
    width = value.shape[-1]
    pair_index = jnp.arange(width, dtype=jnp.int32) % head_size // 2
    frequency = theta_base ** (-2.0 * pair_index.astype(jnp.float32) / head_size)
    angle = position[:, None] * frequency[None, :]
    paired = value.reshape(value.shape[0], width // 2, 2)
    turned = jnp.stack([-paired[:, :, 1], paired[:, :, 0]], axis=-1).reshape(value.shape)
    return value * jnp.cos(angle) + turned * jnp.sin(angle)

def group_forward(latent, conditioning, caption_set, row_table, text_limit, qkv_weight, text_weight, out_weight, gate_up_weight, down_weight, ada_weight, ada_bias, norm_gains, head_gates):
    group_rows = TOK_DEV * N_ROWS
    row_line = jnp.arange(group_rows, dtype=jnp.int32)
    shard_of = row_line // TOK_DEV
    within = row_line % TOK_DEV
    bounds = jnp.cumsum(row_table, axis=1)
    before = jnp.cumsum(row_table, axis=0) - row_table
    row_bounds = bounds[shard_of]
    frame_rows = lax.optimization_barrier(jnp.sum((within[:, None] >= row_bounds[:, :-1]).astype(jnp.int32), axis=1))
    frame_onehot = frame_rows[:, None] == jnp.arange(FRAMES, dtype=jnp.int32)[None, :]
    offsets = lax.optimization_barrier(jnp.sum(jnp.where(frame_onehot, before[shard_of] - row_bounds + row_table[shard_of], 0), axis=1))
    positions = (offsets + within).astype(jnp.float32)
    onehot_float = frame_onehot.astype(jnp.float32)
    modulation = matmul(low(jax.nn.silu(conditioning)), ada_weight) + ada_bias
    mod_rows = matmul(onehot_float, modulation)
    text_raw = low_back(matmul(caption_set.reshape(FRAMES * TEXT, TEXT_DIM), text_weight))
    text_keys = low(normed(text_raw[:, :D], norm_gains[6])).reshape(FRAMES * TEXT, HEADS, HEAD)
    text_values = low(text_raw[:, D:]).reshape(FRAMES * TEXT, HEADS, HEAD)
    attn_in = low(normed(latent, norm_gains[0]) * (1.0 + mod_rows[:, :D]))
    qkv_raw = low_back(matmul(attn_in, qkv_weight))
    queries = low(rotate(normed(qkv_raw[:, :D], norm_gains[4]), positions, HEAD)).reshape(group_rows, HEADS, HEAD)
    key_heads = low(rotate(normed(qkv_raw[:, D:2 * D], norm_gains[5]), positions, HEAD)).reshape(group_rows, HEADS, HEAD)
    value_heads = low(qkv_raw[:, 2 * D:]).reshape(group_rows, HEADS, HEAD)
    text_line = jnp.arange(FRAMES * TEXT, dtype=jnp.int32)
    text_frame = text_line // TEXT
    text_live = text_line % TEXT < jnp.repeat(text_limit, TEXT)
    gate_heads = jnp.tanh(head_gates)
    block_rows = 512 if group_rows % 512 == 0 else group_rows

    def attend(block_pair):
        query_block, frame_block = block_pair
        scores = jnp.einsum('qhe,khe->hqk', query_block, key_heads, precision=highest) * score_scale
        scores = jnp.where((frame_block[:, None] == frame_rows[None, :])[None], scores, masked_value)
        own_out = jnp.einsum('hqk,khe->qhe', jax.nn.softmax(scores, axis=-1), value_heads, precision=highest)
        cross_scores = jnp.einsum('qhe,khe->hqk', query_block, text_keys, precision=highest) * score_scale
        allowed = (frame_block[:, None] == text_frame[None, :]) & text_live[None, :]
        cross_scores = jnp.where(allowed[None], cross_scores, masked_value)
        cross_out = jnp.einsum('hqk,khe->qhe', jax.nn.softmax(cross_scores, axis=-1), text_values, precision=highest)
        return own_out + gate_heads[None, :, None] * cross_out
    mixed_heads = lax.map(jax.checkpoint(attend), (queries.reshape(group_rows // block_rows, block_rows, HEADS, HEAD), frame_rows.reshape(group_rows // block_rows, block_rows)))
    mixed_rows = low(low_back(mixed_heads.reshape(group_rows, D)))
    attn_proj = low_back(matmul(mixed_rows, out_weight))
    state_rows = latent + jnp.tanh(mod_rows[:, D:2 * D]) * normed(attn_proj, norm_gains[1])
    ffn_in = low(normed(state_rows, norm_gains[2]) * (1.0 + mod_rows[:, 2 * D:3 * D]))
    gate_up = low_back(matmul(ffn_in, gate_up_weight))
    activated = low(jax.nn.silu(gate_up[:, :FF]) * gate_up[:, FF:])
    down_out = low_back(matmul(activated, down_weight))
    return state_rows + jnp.tanh(mod_rows[:, 3 * D:]) * normed(down_out, norm_gains[3])

def reference(latents, conditions, captions, row_counts, text_lengths, qkv_weight, text_weight, out_weight, gate_up_weight, down_weight, ada_weight, ada_bias, norm_gains, head_gates, cotangent):
    weight_set = tuple((weight_arg.astype(jnp.float32) for weight_arg in (qkv_weight, text_weight, out_weight, gate_up_weight, down_weight, ada_weight, ada_bias, norm_gains, head_gates)))

    def forward_all(latent_all, weights_in):
        outputs = []
        for group_index in range(GROUPS):
            outputs.append(group_forward(latent_all[group_index], conditions[group_index].astype(jnp.float32), captions[group_index].astype(jnp.float32), row_counts[group_index], text_lengths[group_index], weights_in[0], weights_in[1], weights_in[2], weights_in[3], weights_in[4], weights_in[5], weights_in[6], weights_in[7], weights_in[8]))
        return jnp.stack(outputs)
    block_out, back_function = jax.vjp(forward_all, latents, weight_set)
    latent_grad, weight_grads = back_function(cotangent)
    return (block_out, latent_grad, weight_grads[0], weight_grads[1], weight_grads[2], weight_grads[3], weight_grads[4], weight_grads[5], weight_grads[6], weight_grads[7], weight_grads[8])
```

```python
import jax
import jax.numpy as jnp
import numpy as np
from jax import lax
from jax.experimental import pallas as pl
from jax.experimental.pallas import tpu as pltpu
from jax.sharding import Mesh
from jax.sharding import PartitionSpec as P

D = 1536
HEADS = 24
HEAD = 64
FF = 4096
TEXT_DIM = 4096
COND = 1024
TEXT = 256
FRAMES = 2
TOK = 128
GROUPS = 2
M = 8
LOCAL = HEADS // M * HEAD
ROWS = M * TOK
WIDE = 256
APART = 8192.0

epsilon = 1e-05
theta_base = 10000.0
highest = lax.Precision.HIGHEST
MESH = pl.DeviceIdType.MESH
f32 = jnp.float32
bf16 = jnp.bfloat16
ANY = pl.BlockSpec(memory_space=pl.ANY)
VMEM = pl.BlockSpec(memory_space=pltpu.VMEM)


def flip(where, mask):
    return tuple(a if b == 0 else a ^ b for a, b in zip(where, mask))


class Job:
    def __init__(self, x, shape, masks, src, dst, pass_on=(), by=None, source=None):
        self.x, self.shape, self.masks, self.src, self.dst = x, shape, masks, src, dst
        self.pass_on, self.by, self.source = tuple(pass_on), by, source
        if source is not None:
            self.x = None
        self.dtype = x.dtype

    def count(self):
        return len(self.masks) + len(self.pass_on)

    def block(self):
        return self.shape[len(self.dst((0, 0, 0))) :]

    def peers(self):
        return set(self.masks) | ({self.by} if self.pass_on else set())


class Transfers:
    def __init__(self, jobs):
        self.jobs = jobs
        self.sent = [j for j in jobs if j.source is None]
        self.total = sum(j.count() for j in jobs)

    def operands(self):
        return [j.x for j in self.sent]

    def out_shapes(self):
        return [jax.ShapeDtypeStruct(j.shape, j.dtype) for j in self.jobs]

    def scratch(self):
        if not self.jobs:
            return []
        return [
            pltpu.SemaphoreType.DMA((self.total,)),
            pltpu.SemaphoreType.DMA((self.total,)),
            pltpu.SemaphoreType.DMA((2, len(self.jobs))),
        ] + [pltpu.VMEM(j.block(), j.dtype) for j in self.jobs]

    def peers(self):
        found = set()
        for j in self.jobs:
            found |= j.peers()
        return found

    def bind(self, me, ins, outs, sems):
        self.me, self.outs, self.sems = me, outs, sems
        left = list(ins)
        self.ins = []
        for j in self.jobs:
            self.ins.append(left.pop(0) if j.source is None else outs[self.jobs.index(j.source)])
        self.base, at = [], 0
        for j in self.jobs:
            self.base.append(at)
            at += j.count()
        self.arrived, self.kept, self.settled, self.chained, self.forwarded = set(), set(), set(), set(), set()

    def remote(self, src, dst, slot, dest):
        return pltpu.make_async_remote_copy(
            src_ref=src,
            dst_ref=dst,
            send_sem=self.sems[0].at[slot],
            recv_sem=self.sems[1].at[slot],
            device_id=dest,
            device_id_type=MESH,
        )

    def send(self, k, i):
        j = self.jobs[k]
        if i < len(j.masks):
            dest = flip(self.me, j.masks[i])
            at = j.src(dest)
            src = self.ins[k] if at is None else self.ins[k].at[at]
            return self.remote(src, self.outs[k].at[j.dst(self.me)], self.base[k] + i, dest)
        mask = j.pass_on[i - len(j.masks)]
        block = self.outs[k].at[j.dst(flip(self.me, mask))]
        return self.remote(block, block, self.base[k] + i, flip(self.me, j.by))

    def own(self, k, leg):
        j = self.jobs[k]
        room = self.sems[3 + k]
        if leg == 0:
            at = j.src(self.me)
            src = self.ins[k] if at is None else self.ins[k].at[at]
            return pltpu.make_async_copy(src, room, self.sems[2].at[0, k])
        return pltpu.make_async_copy(room, self.outs[k].at[j.dst(self.me)], self.sems[2].at[1, k])

    def start_job(self, k):
        j = self.jobs[k]
        for i in range(len(j.masks)):
            self.send(k, i).start()
        self.own(k, 0).start()

    def start(self):
        for k, j in enumerate(self.jobs):
            if j.source is None:
                self.start_job(k)

    def receive(self, k, i):
        if (k, i) not in self.arrived:
            self.arrived.add((k, i))
            self.send(k, i).wait_recv()

    def take(self, k):
        self.keep(k)
        for i in range(self.jobs[k].count()):
            self.receive(k, i)
        if k not in self.settled:
            self.settled.add(k)
            self.own(k, 1).wait()

    def keep(self, k):
        if k not in self.kept:
            self.kept.add(k)
            self.own(k, 0).wait()
            self.own(k, 1).start()

    def chain(self):
        for k, j in enumerate(self.jobs):
            if j.source is not None and k not in self.chained:
                self.chained.add(k)
                self.take(self.jobs.index(j.source))
                self.start_job(k)

    def forward(self):
        self.chain()
        for k in range(len(self.jobs)):
            self.keep(k)
        for k, j in enumerate(self.jobs):
            if k not in self.forwarded:
                self.forwarded.add(k)
                for n, mask in enumerate(j.pass_on):
                    self.receive(k, j.masks.index(mask))
                    self.send(k, len(j.masks) + n).start()

    def finish(self):
        self.forward()
        for k, j in enumerate(self.jobs):
            self.take(k)
            for i in range(j.count()):
                self.send(k, i).wait_send()


class Plan:
    def __init__(self, times):
        self.times = times
        self.sets = GROUPS * times
        self.rows = times * M
        self.next_id = 0
        ones = [(i, t, m) for i in range(GROUPS) for t in range(times) for m in range(M)]
        self.all = ones[1:]
        self.ring = [(0, 0, m) for m in range(1, M)]
        self.chips = [(0, 0, m) for m in range(2, M, 2)]
        self.mate = (0, 0, 1)
        self.time = [(0, t, 0) for t in range(1, times)]
        self.item = (1, 0, 0)
        self.span = [(i, t, 0) for i in range(GROUPS) for t in range(times)][1:]
        self.group = [(0, t, m) for t in range(times) for m in range(M)][1:]

    def identity(self):
        self.next_id += 1
        return self.next_id

    def set_of(self, where):
        return where[0] * self.times + where[1]

    def gather_ring(self, x):
        return Job(
            x,
            (M,) + x.shape,
            [self.mate] + self.chips,
            lambda dest: None,
            lambda sender: (sender[2],),
            self.chips,
            self.mate,
        )

    def direct_ring(self, x):
        return Job(x, (M,) + x.shape, self.ring, lambda dest: None, lambda sender: (sender[2],))

    def scatter_ring(self, x):
        return Job(x, x.shape, self.ring, lambda dest: (dest[2],), lambda sender: (sender[2],))

    def gather_span(self, x, shape=None, source=None):
        return Job(
            x,
            (self.sets,) + (x.shape if shape is None else shape),
            [self.item] + self.time,
            lambda dest: None,
            lambda sender: (self.set_of(sender),),
            self.time,
            self.item,
            source,
        )

    def scatter_span(self, x):
        return Job(x, x.shape, self.span, lambda dest: (self.set_of(dest),), lambda sender: (self.set_of(sender),))

    def gather_time(self, x):
        return Job(x, (self.times,) + x.shape, self.time, lambda dest: None, lambda sender: (sender[1],))

    def gather_time_part(self, x, start, count):
        return Job(
            x,
            (self.times, count) + x.shape[1:],
            self.time,
            lambda dest: (pl.ds(start, count),),
            lambda sender: (sender[1],),
        )

    def swap_item_part(self, x, start, count):
        return Job(
            x,
            (GROUPS, count) + x.shape[1:],
            [self.item],
            lambda dest: (pl.ds(start, count),),
            lambda sender: (sender[0],),
        )

    def scatter_time(self, x):
        return Job(x, x.shape, self.time, lambda dest: (dest[1],), lambda sender: (sender[1],))

    def scatter_item(self, x):
        return Job(x, x.shape, [self.item], lambda dest: (dest[0],), lambda sender: (sender[0],))

    def gather_all(self, x):
        return Job(
            x,
            (self.sets, M) + x.shape,
            self.all,
            lambda dest: None,
            lambda sender: (self.set_of(sender), sender[2]),
        )

    def scatter_all(self, x):
        return Job(
            x,
            x.shape,
            self.all,
            lambda dest: (self.set_of(dest), dest[2]),
            lambda sender: (self.set_of(sender), sender[2]),
        )

    def swap_item(self, x):
        return Job(x, (GROUPS,) + x.shape, [self.item], lambda dest: None, lambda sender: (sender[0],))

    def gather_group(self, x):
        return Job(
            x,
            (self.times, M) + x.shape,
            self.group,
            lambda dest: None,
            lambda sender: (sender[1], sender[2]),
        )

    def scatter_group(self, x):
        return Job(
            x,
            x.shape,
            self.group,
            lambda dest: (dest[1], dest[2]),
            lambda sender: (sender[1], sender[2]),
        )


def here():
    return (lax.axis_index("items"), lax.axis_index("times"), lax.axis_index("ring"))


def greet(me, peers):
    barrier = pltpu.get_barrier_semaphore()
    for mask in sorted(peers):
        pl.semaphore_signal(barrier, inc=1, device_id=flip(me, mask), device_id_type=MESH)
    pl.semaphore_wait(barrier, len(peers))


def exchange(plan, name, jobs):
    moves = Transfers(jobs)
    n_in, n_out = len(moves.sent), len(jobs)

    def kernel(*refs):
        me = here()
        greet(me, moves.peers())
        moves.bind(me, refs[:n_in], refs[n_in : n_in + n_out], refs[n_in + n_out :])
        moves.start()
        moves.finish()

    return pl.pallas_call(
        kernel,
        out_shape=moves.out_shapes(),
        in_specs=[ANY] * n_in,
        out_specs=[ANY] * n_out,
        scratch_shapes=moves.scratch(),
        name=name,
        compiler_params=pltpu.CompilerParams(
            collective_id=plan.identity(), has_side_effects=True, vmem_limit_bytes=32 * 2**20
        ),
    )(*moves.operands())


def product_scatter(plan, name, factors, turned, jobs=()):
    moves = Transfers(list(jobs))
    n_factors = len(factors)
    n_in, n_out = len(moves.sent), len(moves.jobs)
    contract = (((1,), (1,)), ((), ())) if turned else (((1,), (0,)), ((), ()))

    def kernel(*refs):
        factor_refs, refs = refs[: 2 * n_factors], refs[2 * n_factors :]
        ins = refs[:n_in]
        out_ref = refs[n_in]
        outs = refs[1 + n_in : 1 + n_in + n_out]
        to_mate, from_mate, part, to_chip, from_chip, send_sem, recv_sem = refs[1 + n_in + n_out : 8 + n_in + n_out]
        me = here()
        ring = me[2]
        core, chip = ring % 2, ring // 2
        greet(me, moves.peers() | {plan.mate} | set(plan.chips))
        if moves.jobs:
            moves.bind(me, ins, outs, refs[8 + n_in + n_out :])
            moves.start()

        def mate_copy(d):
            return pltpu.make_async_remote_copy(
                src_ref=to_mate.at[d],
                dst_ref=from_mate.at[d],
                send_sem=send_sem.at[d],
                recv_sem=recv_sem.at[d],
                device_id=flip(me, plan.mate),
                device_id_type=MESH,
            )

        def chip_copy(d):
            return pltpu.make_async_remote_copy(
                src_ref=to_chip.at[d - 1],
                dst_ref=from_chip.at[d - 1],
                send_sem=send_sem.at[3 + d],
                recv_sem=recv_sem.at[3 + d],
                device_id=flip(me, (0, 0, 2 * d)),
                device_id_type=MESH,
            )

        def block(d, which):
            start = pl.multiple_of((chip ^ d) * (2 * TOK) + which * TOK, TOK)
            products = [
                lax.dot_general(
                    factor_refs[2 * i][pl.ds(start, TOK), :],
                    factor_refs[2 * i + 1][...],
                    contract,
                    preferred_element_type=f32,
                )
                for i in range(n_factors)
            ]
            return sum(products[1:], products[0])

        for d in (3, 2, 1, 0):
            to_mate[d] = block(d, 1 - core).astype(bf16)
            mate_copy(d).start()
        for d in (3, 2, 1):
            part[...] = block(d, core)
            mate_copy(d).wait_recv()
            to_chip[d - 1] = (part[...] + from_mate[d].astype(f32)).astype(bf16)
            chip_copy(d).start()
        part[...] = block(0, core)
        mate_copy(0).wait_recv()
        part[...] = part[...] + from_mate[0].astype(f32)
        for d in (3, 2, 1):
            chip_copy(d).wait_recv()
        out_ref[...] = part[...] + (
            from_chip[0].astype(f32) + from_chip[1].astype(f32) + from_chip[2].astype(f32)
        )
        for d in range(4):
            mate_copy(d).wait_send()
        for d in (1, 2, 3):
            chip_copy(d).wait_send()
        if moves.jobs:
            moves.finish()

    result = pl.pallas_call(
        kernel,
        out_shape=[jax.ShapeDtypeStruct((TOK, D), f32)] + moves.out_shapes(),
        in_specs=[VMEM] * (2 * n_factors) + [ANY] * n_in,
        out_specs=[VMEM] + [ANY] * n_out,
        scratch_shapes=[
            pltpu.VMEM((4, TOK, D), bf16),
            pltpu.VMEM((4, TOK, D), bf16),
            pltpu.VMEM((TOK, D), f32),
            pltpu.VMEM((3, TOK, D), bf16),
            pltpu.VMEM((3, TOK, D), bf16),
            pltpu.SemaphoreType.DMA((7,)),
            pltpu.SemaphoreType.DMA((7,)),
        ]
        + moves.scratch(),
        name=name,
        compiler_params=pltpu.CompilerParams(
            collective_id=plan.identity(), has_side_effects=True, vmem_limit_bytes=48 * 2**20
        ),
    )(*[x for pair in factors for x in pair], *moves.operands())
    return result[0], result[1:]


def normed(value, gain_row):
    return value * lax.rsqrt(jnp.mean(value * value, axis=-1, keepdims=True) + epsilon) * gain_row


def attn_head(input_rows, scale_rows, gain_row):
    return normed(input_rows, gain_row) * (1.0 + scale_rows)


def attn_tail(input_rows, proj_rows, gate_rows, gain_row):
    return input_rows + jnp.tanh(gate_rows) * normed(proj_rows, gain_row)


def dot(a, b, dims=(1, 0)):
    return lax.dot_general(a, b, (((dims[0],), (dims[1],)), ((), ())), preferred_element_type=f32)


def halves_order():
    col = np.arange(LOCAL)
    head, pair, odd = col // HEAD, col % HEAD // 2, col % 2
    place = odd * (LOCAL // 2) + head * (HEAD // 2) + pair
    order = np.zeros(LOCAL, np.int64)
    order[place] = col
    full = np.concatenate([order, LOCAL + order, 2 * LOCAL + col])
    return order, full


def shuffle(order):
    n = order.shape[0]
    line = jnp.arange(n, dtype=jnp.int32)
    return (line[:, None] == jnp.asarray(order, jnp.int32)[None, :]).astype(bf16)


def turn(rows, cos, sin):
    half = LOCAL // 2
    first, second = rows[:, :half], rows[:, half:]
    return jnp.concatenate([first * cos - second * sin, second * cos + first * sin], axis=1)


def lane_masks():
    lane = np.arange(WIDE)
    query, value = np.zeros((8, WIDE), np.float32), np.zeros((8, WIDE), np.float32)
    back = np.zeros((8, WIDE), np.float32)
    half = HEAD // 2
    for h in range(LOCAL // HEAD):
        query[h] = ((lane < LOCAL) & (lane % (LOCAL // 2) // half == h)) | (lane == LOCAL) | (lane == LOCAL + 1)
        query[h] += (lane >= LOCAL + 2 + 3 * h) & (lane < LOCAL + 5 + 3 * h)
        value[h] = ((lane >= HEAD) & (lane // HEAD - 1 == h)) | (lane // 16 == h)
        back[h] = ((lane >= HEAD) & (lane // HEAD - 1 == h)) | (lane == 2 * h) | (lane == 2 * h + 1)
    return query, value, back


def widen(packed_ref, feature, key_ref, value_ref, rows):
    lane = lax.broadcasted_iota(jnp.int32, (rows, 128), 1)
    middle = packed_ref[:, 128:256].astype(f32)
    key_ref[:rows, :128] = packed_ref[:, :128]
    key_ref[:rows, 128:] = jnp.where(lane < HEAD, middle, feature.astype(f32)).astype(bf16)
    value_ref[:rows, :128] = jnp.where(lane < HEAD, 1.0, middle).astype(bf16)
    value_ref[:rows, 128:] = packed_ref[:, 256:]


def flash_forward(plan, query, packed, features, text_packed, text_features, gates, jobs):
    heads = LOCAL // HEAD
    text_rows = text_packed.shape[0]
    keys_job = plan.gather_time(packed)
    moves = Transfers([keys_job] + list(jobs))
    n_in, n_out = len(moves.sent) - 1, len(moves.jobs)
    block = 256

    def kernel(*refs):
        query_ref, packed_ref, feature_ref, text_ref, text_feature_ref, gate_ref, qmask_ref, vmask_ref = refs[:8]
        ins = refs[8 : 9 + n_in]
        mixed_ref, self_ref, cross_ref = refs[9 + n_in : 12 + n_in]
        outs = refs[12 + n_in : 12 + n_in + n_out]
        key_ref, value_ref, far_ref, max_ref, sem = refs[12 + n_in + n_out : 17 + n_in + n_out]
        me = here()
        greet(me, moves.peers())
        moves.bind(me, ins, outs, refs[17 + n_in + n_out :])
        moves.start()

        def segment(rows, first, out_ref):
            def body(at, carry):
                where = pl.ds(pl.multiple_of(at * block, block), block)
                query_rows = query_ref[where, :]
                total = jnp.zeros((block, WIDE), f32)
                tops = jnp.zeros((block, WIDE), f32)
                for h in range(heads):
                    own_query = query_rows * qmask_ref[h : h + 1, :]
                    scores = lax.dot_general(
                        own_query, key_ref[:rows, :], (((1,), (1,)), ((), ())), preferred_element_type=f32
                    )
                    top = jnp.max(scores, axis=1, keepdims=True)
                    weights = jnp.exp(scores - top).astype(bf16)
                    product = jnp.dot(weights, value_ref[:rows, :], preferred_element_type=f32)
                    total += product * vmask_ref[h : h + 1, :]
                    tops += top * vmask_ref[h : h + 1, :]
                if first:
                    out_ref[where, :] = total
                    max_ref[where, :] = tops
                else:
                    before = max_ref[where, :]
                    after = jnp.maximum(before, tops)
                    out_ref[where, :] = out_ref[where, :] * jnp.exp(before - after) + total * jnp.exp(tops - after)
                    max_ref[where, :] = after
                return carry

            lax.fori_loop(0, ROWS // block, body, 0)

        def close(out_ref):
            def body(at, carry):
                where = pl.ds(pl.multiple_of(at * block, block), block)
                lane = lax.broadcasted_iota(jnp.int32, (block, WIDE), 1)
                values = out_ref[where, :]
                share = jnp.ones((block, WIDE), f32)
                for h in range(heads):
                    share = jnp.where(
                        (lane >= HEAD * (h + 1)) & (lane < HEAD * (h + 2)), values[:, 16 * h : 16 * h + 1], share
                    )
                logs = max_ref[where, :] + jnp.log(jnp.maximum(values, 1e-30))
                out_ref[where, :] = jnp.where(
                    lane < HEAD, jnp.where(lane < 16 * heads, logs, 0.0), values / share
                )
                return carry

            lax.fori_loop(0, ROWS // block, body, 0)

        widen(text_ref, text_feature_ref[...], key_ref, value_ref, text_rows)
        segment(text_rows, True, cross_ref)
        close(cross_ref)
        moves.chain()
        own_rows = pl.ds(pl.multiple_of(me[1] * ROWS, ROWS), ROWS)
        widen(packed_ref, feature_ref[own_rows, :], key_ref, value_ref, ROWS)
        segment(ROWS, True, self_ref)
        for i, mask in enumerate(plan.time):
            moves.receive(0, i)
            far = me[1] ^ mask[1]
            bring = pltpu.make_async_copy(outs[0].at[far], far_ref, sem)
            bring.start()
            bring.wait()
            far_rows = pl.ds(pl.multiple_of(far * ROWS, ROWS), ROWS)
            widen(far_ref, feature_ref[far_rows, :], key_ref, value_ref, ROWS)
            segment(ROWS, False, self_ref)
        moves.forward()
        close(self_ref)
        lane = lax.broadcasted_iota(jnp.int32, (ROWS, WIDE), 1)
        both = self_ref[...] + gate_ref[...] * cross_ref[...]
        mixed_ref[...] = jnp.where(lane < HEAD, 0.0, both).astype(bf16)
        moves.finish()

    qmask, vmask, _ = lane_masks()
    result = pl.pallas_call(
        kernel,
        out_shape=[
            jax.ShapeDtypeStruct((ROWS, WIDE), bf16),
            jax.ShapeDtypeStruct((ROWS, WIDE), f32),
            jax.ShapeDtypeStruct((ROWS, WIDE), f32),
        ]
        + moves.out_shapes(),
        in_specs=[VMEM] * 8 + [ANY] * (n_in + 1),
        out_specs=[VMEM] * 3 + [ANY] * n_out,
        scratch_shapes=[
            pltpu.VMEM((ROWS, WIDE), bf16),
            pltpu.VMEM((ROWS, WIDE), bf16),
            pltpu.VMEM((ROWS, 2 * LOCAL), bf16),
            pltpu.VMEM((ROWS, WIDE), f32),
            pltpu.SemaphoreType.DMA(()),
        ]
        + moves.scratch(),
        name="flash_forward",
        compiler_params=pltpu.CompilerParams(
            collective_id=plan.identity(), has_side_effects=True, vmem_limit_bytes=56 * 2**20
        ),
    )(
        query,
        packed,
        features,
        text_packed,
        text_features,
        gates,
        jnp.asarray(qmask, bf16),
        jnp.asarray(vmask, f32),
        *moves.operands(),
    )
    return result[0], result[1], result[2], result[3], result[4:]


def flash_backward(
    plan, query, packed_all, features, text_packed, text_features, self_out, cross_out, d_mixed, gates_q, gates_v, jobs
):
    heads = LOCAL // HEAD
    text_rows = text_packed.shape[0]
    moves = Transfers(list(jobs))
    n_in, n_out = len(moves.sent), len(moves.jobs)
    block = 256
    others = len(plan.time)
    turned = (((1,), (1,)), ((), ()))
    sunk = (((0,), (0,)), ((), ()))

    def kernel(*refs):
        (query_ref, packed_ref, feature_ref, text_ref, text_feature_ref, self_ref, cross_ref, d_ref) = refs[:8]
        gateq_ref, gatev_ref, qmask_ref, bmask_ref = refs[8:12]
        ins = refs[12 : 12 + n_in]
        dq_ref, dk_ref, dv_ref, tdk_ref, tdv_ref, sums_ref = refs[12 + n_in : 18 + n_in]
        outs = refs[18 + n_in : 18 + n_in + n_out]
        (key_ref, value_ref, near_ref, qs_ref, ds_ref, to_ref, from_ref, tto_ref, tfrom_ref, sem, send_sem, recv_sem) = refs[
            18 + n_in + n_out : 30 + n_in + n_out
        ]
        me = here()
        greet(me, moves.peers() | set(plan.time))
        if moves.jobs:
            moves.bind(me, ins, outs, refs[30 + n_in + n_out :])
            moves.start()

        def prepare(out_ref):
            def body(at, carry):
                where = pl.ds(pl.multiple_of(at * block, block), block)
                lane = lax.broadcasted_iota(jnp.int32, (block, 128), 1)
                tail = query_ref[where, 128:].astype(f32)
                out_rows = out_ref[where, :]
                d_rows = d_ref[where, :].astype(f32)
                product = d_rows * out_rows
                head_tile = jnp.where(lane < HEAD, 0.0, d_rows[:, :128])
                for h in range(heads):
                    log = -out_rows[:, 16 * h : 16 * h + 1]
                    for j in range(3):
                        piece = log.astype(bf16).astype(f32)
                        log = log - piece
                        tail = jnp.where(lane == HEAD + 2 + 3 * h + j, piece, tail)
                    delta = -jnp.sum(product * bmask_ref[h : h + 1, :].astype(f32), axis=1, keepdims=True)
                    for j in range(2):
                        piece = delta.astype(bf16).astype(f32)
                        delta = delta - piece
                        head_tile = jnp.where(lane == 2 * h + j, piece, head_tile)
                qs_ref[where, :128] = query_ref[where, :128]
                qs_ref[where, 128:] = tail.astype(bf16)
                ds_ref[where, :128] = head_tile.astype(bf16)
                ds_ref[where, 128:] = d_ref[where, 128:]
                return carry

            lax.fori_loop(0, ROWS // block, body, 0)

        def segment(rows, first, k_ref, v_ref, scale):
            k_ref[...] = jnp.zeros_like(k_ref)
            v_ref[...] = jnp.zeros_like(v_ref)

            def body(at, carry):
                where = pl.ds(pl.multiple_of(at * block, block), block)
                query_rows, d_rows = qs_ref[where, :], ds_ref[where, :]
                total = jnp.zeros((block, WIDE), f32)
                for h in range(heads):
                    own_query = query_rows * qmask_ref[h : h + 1, :]
                    own_d = d_rows * bmask_ref[h : h + 1, :]
                    keys = key_ref[:rows, :]
                    weights = jnp.exp(lax.dot_general(keys, own_query, turned, preferred_element_type=f32))
                    d_weights = lax.dot_general(value_ref[:rows, :], own_d, turned, preferred_element_type=f32)
                    d_scores = (weights * d_weights).astype(bf16)
                    v_ref[...] += jnp.dot(weights.astype(bf16), own_d, preferred_element_type=f32)
                    k_ref[...] += jnp.dot(d_scores, own_query, preferred_element_type=f32)
                    d_query = lax.dot_general(d_scores, keys, sunk, preferred_element_type=f32)
                    total += d_query * qmask_ref[h : h + 1, :].astype(f32)
                total = total * scale
                if first:
                    dq_ref[where, :] = total
                else:
                    dq_ref[where, :] += total
                return carry

            lax.fori_loop(0, ROWS // block, body, 0)

        def pack(k_ref, v_ref, rows):
            lane = lax.broadcasted_iota(jnp.int32, (rows, 128), 1)
            middle = jnp.where(lane < HEAD, k_ref[:, 128:], v_ref[:, :128])
            return k_ref[:, :128].astype(bf16), middle.astype(bf16), v_ref[:, 128:].astype(bf16)

        def bring(which):
            copy = pltpu.make_async_copy(packed_ref.at[which], near_ref, sem)
            copy.start()
            copy.wait()
            rows = pl.ds(pl.multiple_of(which * ROWS, ROWS), ROWS)
            widen(near_ref, feature_ref[rows, :], key_ref, value_ref, ROWS)

        def send(src, dst, slot, mask):
            return pltpu.make_async_remote_copy(
                src_ref=src,
                dst_ref=dst,
                send_sem=send_sem.at[slot],
                recv_sem=recv_sem.at[slot],
                device_id=flip(me, mask),
                device_id_type=MESH,
            )

        far_copies = [send(to_ref.at[i], from_ref.at[i], i, mask) for i, mask in enumerate(plan.time)]
        text_copies = [send(tto_ref, tfrom_ref.at[i], others + i, mask) for i, mask in enumerate(plan.time)]

        prepare(self_ref)
        for i, mask in enumerate(plan.time):
            bring(me[1] ^ mask[1])
            segment(ROWS, i == 0, dk_ref, dv_ref, 0.125)
            to_ref[i, :, :128], to_ref[i, :, 128:256], to_ref[i, :, 256:] = pack(dk_ref, dv_ref, ROWS)
            far_copies[i].start()
        bring(me[1])
        segment(ROWS, others == 0, dk_ref, dv_ref, 0.125)
        prepare(cross_ref)
        widen(text_ref, text_feature_ref[...], key_ref, value_ref, text_rows)
        segment(text_rows, False, tdk_ref, tdv_ref, 0.125 * gateq_ref[...])
        tdk_ref[...] = tdk_ref[...] * gateq_ref[...]
        tdv_ref[...] = tdv_ref[...] * gatev_ref[...]
        if others:
            tto_ref[:, :128], tto_ref[:, 128:256], tto_ref[:, 256:] = pack(tdk_ref, tdv_ref, text_rows)
            for copy in text_copies:
                copy.start()
        sums_ref[...] = jnp.sum(d_ref[...].astype(f32) * cross_ref[...], axis=0, keepdims=True)
        if moves.jobs:
            moves.forward()
        lane = lax.broadcasted_iota(jnp.int32, (ROWS, 128), 1)
        for i in range(others):
            far_copies[i].wait_recv()
            middle = from_ref[i, :, 128:256].astype(f32)
            dk_ref[:, :128] += from_ref[i, :, :128].astype(f32)
            dk_ref[:, 128:] += middle
            dv_ref[:, :128] += middle
            dv_ref[:, 128:] += from_ref[i, :, 256:].astype(f32)
        for i in range(others):
            text_copies[i].wait_recv()
            middle = tfrom_ref[i, :, 128:256].astype(f32)
            tdk_ref[:, :128] += tfrom_ref[i, :, :128].astype(f32)
            tdk_ref[:, 128:] += middle
            tdv_ref[:, :128] += middle
            tdv_ref[:, 128:] += tfrom_ref[i, :, 256:].astype(f32)
        for copy in far_copies + text_copies:
            copy.wait_send()
        if moves.jobs:
            moves.finish()

    qmask, _, bmask = lane_masks()
    result = pl.pallas_call(
        kernel,
        out_shape=[
            jax.ShapeDtypeStruct((ROWS, WIDE), f32),
            jax.ShapeDtypeStruct((ROWS, WIDE), f32),
            jax.ShapeDtypeStruct((ROWS, WIDE), f32),
            jax.ShapeDtypeStruct((text_rows, WIDE), f32),
            jax.ShapeDtypeStruct((text_rows, WIDE), f32),
            jax.ShapeDtypeStruct((1, WIDE), f32),
        ]
        + moves.out_shapes(),
        in_specs=[VMEM, ANY] + [VMEM] * 10 + [ANY] * n_in,
        out_specs=[VMEM] * 6 + [ANY] * n_out,
        scratch_shapes=[
            pltpu.VMEM((ROWS, WIDE), bf16),
            pltpu.VMEM((ROWS, WIDE), bf16),
            pltpu.VMEM((ROWS, 2 * LOCAL), bf16),
            pltpu.VMEM((ROWS, WIDE), bf16),
            pltpu.VMEM((ROWS, WIDE), bf16),
            pltpu.VMEM((max(others, 1), ROWS, 2 * LOCAL), bf16),
            pltpu.VMEM((max(others, 1), ROWS, 2 * LOCAL), bf16),
            pltpu.VMEM((text_rows, 2 * LOCAL), bf16),
            pltpu.VMEM((max(others, 1), text_rows, 2 * LOCAL), bf16),
            pltpu.SemaphoreType.DMA(()),
            pltpu.SemaphoreType.DMA((max(2 * others, 1),)),
            pltpu.SemaphoreType.DMA((max(2 * others, 1),)),
        ]
        + moves.scratch(),
        name="flash_backward",
        compiler_params=pltpu.CompilerParams(
            collective_id=plan.identity(), has_side_effects=True, vmem_limit_bytes=56 * 2**20
        ),
    )(
        query,
        packed_all,
        features,
        text_packed,
        text_features,
        self_out,
        cross_out,
        d_mixed,
        gates_q,
        gates_v,
        jnp.asarray(qmask, bf16),
        jnp.asarray(bmask, bf16),
        *moves.operands(),
    )
    return result[:6], result[6:]


def shards(
    latents,
    conditions,
    captions,
    row_counts,
    text_lengths,
    qkv_weight,
    text_weight,
    out_weight,
    gate_up_weight,
    down_weight,
    ada_weight,
    ada_bias,
    norm_gains,
    head_gates,
    cotangent,
):
    times = lax.axis_size("times")
    plan = Plan(times)
    sets, rows_axis = plan.sets, plan.rows
    devices = sets * M
    item, time, ring = here()
    place = (item * times + time) * M + ring
    group_place = time * M + ring
    heads = LOCAL // HEAD

    k_rows = qkv_weight.shape[0]
    t_rows = text_weight.shape[0]
    o_rows = out_weight.shape[0]
    d_rows = down_weight.shape[0]
    a_rows = ada_weight.shape[0]
    bias_n = ada_bias.shape[0]
    gain_n = norm_gains.shape[1]
    part_n = 4 * D // rows_axis

    package = jnp.concatenate(
        [norm_gains.astype(f32).reshape(-1), ada_bias.astype(f32), row_counts[0, 0].astype(f32)]
    )
    package_n = package.shape[0]
    lines = -(-package_n // 1024) * 8
    package = jnp.pad(package, (0, lines * 128 - package_n)).reshape(lines, 128)
    silu_own = jax.nn.silu(conditions[0].astype(f32)).astype(bf16)
    order, order_full = halves_order()
    mix = shuffle(order_full)
    qkv_send = qkv_weight.reshape(k_rows, 3, M, LOCAL).transpose(2, 0, 1, 3).reshape(M, k_rows, 3 * LOCAL)
    text_send = text_weight.reshape(t_rows, 2, M, LOCAL).transpose(2, 0, 1, 3).reshape(M, t_rows, 2 * LOCAL)
    gate_up_send = gate_up_weight.reshape(k_rows, 2, sets, M, d_rows).transpose(1, 3, 0, 2, 4)
    gate_up_send = gate_up_send.reshape(2, M, k_rows, sets * d_rows)
    out_forth = [(o, (o % sets) * M + o // sets) for o in range(devices)]
    out_back = [(b, a) for a, b in out_forth]
    axes = ("items", "times", "ring")
    out_shard = lax.ppermute(out_weight, axes, out_forth)
    half = M // 2

    packages, silu_both, qkv_shard, text_shard, down_time = exchange(
        plan,
        "gather_small",
        [
            plan.gather_all(package),
            plan.swap_item(silu_own),
            plan.scatter_ring(qkv_send),
            plan.scatter_ring(text_send),
            plan.gather_time(down_weight),
        ],
    )
    packages = packages.reshape(devices, lines * 128)
    gains = packages[:, : 7 * gain_n].reshape(devices, 7, gain_n).transpose(1, 0, 2).reshape(7, D)
    bias = packages[:, 7 * gain_n : 7 * gain_n + bias_n].reshape(4 * D)
    counts_all = packages[:, 7 * gain_n + bias_n : package_n].astype(jnp.int32).reshape(GROUPS, rows_axis, FRAMES)
    counts = lax.dynamic_index_in_dim(counts_all, item, 0, keepdims=False)
    silu_slice = lax.dynamic_slice_in_dim(silu_both.reshape(GROUPS * FRAMES, COND), place * a_rows, a_rows, 1)

    partial = dot(silu_slice, ada_weight).reshape(GROUPS, FRAMES, rows_axis, part_n)
    partial = partial.transpose(0, 2, 1, 3).reshape(sets, M, FRAMES, part_n)
    parts, qkv_time_a, text_a, gate_shard, out_time = exchange(
        plan,
        "scatter_modulation",
        [
            plan.scatter_all(partial),
            plan.gather_time_part(qkv_shard, 0, half),
            plan.swap_item_part(text_shard, 0, half),
            plan.scatter_ring(gate_up_send[0]),
            plan.gather_time(out_shard),
        ],
    )
    own_part = jnp.sum(parts, axis=(0, 1))
    modulation, qkv_time_b, text_b, up_shard = exchange(
        plan,
        "gather_modulation",
        [
            plan.gather_group(own_part),
            plan.gather_time_part(qkv_shard, half, half),
            plan.swap_item_part(text_shard, half, half),
            plan.scatter_ring(gate_up_send[1]),
        ],
    )
    modulation = modulation.reshape(rows_axis, FRAMES, part_n).transpose(1, 0, 2).reshape(FRAMES, 4 * D) + bias

    line = jnp.arange(TOK, dtype=jnp.int32)[None, :]
    clip = counts[:, :1]
    before = jnp.cumsum(counts, axis=0) - counts
    frame_all = (line >= clip).astype(jnp.int32)
    position_all = jnp.where(frame_all == 0, before[:, :1] + line, before[:, 1:] + line - clip)
    frame_k = frame_all.reshape(-1)
    frame_q = lax.dynamic_slice_in_dim(frame_k, time * ROWS, ROWS)
    position_q = lax.dynamic_slice_in_dim(position_all.reshape(-1), time * ROWS, ROWS).astype(f32)
    frame_own = lax.dynamic_index_in_dim(frame_all, group_place, 0, keepdims=False)
    mod_rows = jnp.where(frame_own[:, None] == 0, modulation[0][None], modulation[1][None])
    scale_attn, gate_attn = mod_rows[:, :D], mod_rows[:, D : 2 * D]
    scale_ffn, gate_ffn = mod_rows[:, 2 * D : 3 * D], mod_rows[:, 3 * D :]
    onehot = (frame_own[:, None] == jnp.arange(FRAMES, dtype=jnp.int32)[None, :]).astype(f32)
    text_line = jnp.arange(FRAMES * TEXT, dtype=jnp.int32)
    text_frame = text_line // TEXT
    text_live = text_line % TEXT < jnp.repeat(text_lengths[0], TEXT)

    inputs = latents[0]
    attn_in_float, attn_head_back = jax.vjp(attn_head, inputs, scale_attn, gains[0])
    attn_in = attn_in_float.astype(bf16)

    caption_rows = captions[0].reshape(FRAMES * TEXT, TEXT_DIM)
    width = half * t_rows
    own_captions = jnp.concatenate(
        [
            lax.dynamic_slice_in_dim(caption_rows, ((i * times + time) * 2 + h) * width, width, 1)
            for h in range(2)
            for i in range(GROUPS)
        ],
        axis=1,
    )
    text_full = jnp.concatenate(
        [text_a.reshape(GROUPS * width, 2 * LOCAL), text_b.reshape(GROUPS * width, 2 * LOCAL)], axis=0
    )
    text_partial = dot(own_captions, text_full).astype(bf16)
    attn_in_all, qkv_a, qkv_b, out_full, text_parts = exchange(
        plan,
        "gather_attn_in",
        [
            plan.gather_ring(attn_in),
            plan.swap_item(qkv_time_a),
            plan.swap_item(qkv_time_b),
            plan.swap_item(out_time),
            plan.gather_time(text_partial),
        ],
    )
    attn_in_all = attn_in_all.reshape(ROWS, D)
    qkv_full = jnp.concatenate([qkv_a, qkv_b], axis=2).reshape(D, 3 * LOCAL)
    qkv_full = dot(qkv_full, mix).astype(bf16)
    qkv_raw = dot(attn_in_all, qkv_full)
    text_raw = jnp.sum(text_parts.astype(f32), axis=0)
    q_raw, k_raw, v_raw = qkv_raw[:, :LOCAL], qkv_raw[:, LOCAL : 2 * LOCAL], qkv_raw[:, 2 * LOCAL :]
    tk_raw, tv_raw = text_raw[:, :LOCAL], text_raw[:, LOCAL:]

    squares = jnp.concatenate(
        [jnp.sum(q_raw * q_raw, axis=1), jnp.sum(k_raw * k_raw, axis=1), jnp.sum(tk_raw * tk_raw, axis=1)]
    ).reshape(-1, 128)
    (squares_all,) = exchange(plan, "gather_squares", [plan.direct_ring(squares)])
    out_full = jnp.pad(out_full.reshape(LOCAL, D), ((HEAD, 0), (0, 0)))
    inverse = lax.rsqrt(jnp.sum(squares_all, axis=0).reshape(-1) / D + epsilon)
    q_inv, k_inv, t_inv = inverse[:ROWS, None], inverse[ROWS : 2 * ROWS, None], inverse[2 * ROWS :, None]

    def own_gain(row):
        return lax.dynamic_slice_in_dim(gains[row], ring * LOCAL, LOCAL)

    def halves(vector):
        return vector.reshape(heads, HEAD // 2, 2).transpose(2, 0, 1).reshape(LOCAL)

    gain_q, gain_k, gain_t = own_gain(4), own_gain(5), own_gain(6)
    gain_q, gain_k = halves(gain_q), halves(gain_k)
    pair = jnp.arange(LOCAL // 2, dtype=jnp.int32) % (HEAD // 2)
    frequency = theta_base ** (-2.0 * pair.astype(f32) / HEAD)
    angle = position_q[:, None] * frequency[None, :]
    cos, sin = jnp.cos(angle), jnp.sin(angle)
    query = turn(q_raw * q_inv * gain_q, cos, sin).astype(bf16) * jnp.asarray(0.125, bf16)
    key = turn(k_raw * k_inv * gain_k, cos, sin).astype(bf16)
    text_key = ((tk_raw * t_inv) * gain_t).astype(bf16)
    text_key = dot(text_key, shuffle(order)).astype(bf16)
    text_value = tv_raw.astype(bf16)

    feature = jnp.arange(128, dtype=jnp.int32)[None, :]

    def key_features(apart_first, apart_second):
        ones = (feature >= HEAD + 2) & (feature < HEAD + 2 + 3 * heads)
        pick = jnp.where(feature == HEAD, apart_first[:, None], (feature == HEAD + 1) & apart_second[:, None])
        return jnp.where(pick | ones, 1.0, 0.0).astype(bf16)

    features = key_features(frame_k == 1, frame_k == 0)
    text_features = key_features(~((text_frame == 0) & text_live), ~((text_frame == 1) & text_live))
    lanes = jnp.arange(WIDE - LOCAL, dtype=jnp.int32)[None, :]
    query = jnp.concatenate(
        [query, jnp.where(lanes == frame_q[:, None], -APART, 0.0).astype(bf16)], axis=1
    )
    packed = jnp.concatenate([key, v_raw.astype(bf16)], axis=1)
    text_packed = jnp.concatenate([text_key, text_value], axis=1)
    own_gates = jnp.tanh(lax.dynamic_slice_in_dim(head_gates.astype(f32), ring * heads, heads))
    gates_v = jnp.concatenate([jnp.zeros((HEAD,), f32), jnp.repeat(own_gates, HEAD)]).reshape(1, WIDE)
    gates_q = jnp.concatenate(
        [jnp.tile(jnp.repeat(own_gates, HEAD // 2), 2), jnp.zeros((WIDE - LOCAL,), f32)]
    ).reshape(1, WIDE)

    mixed, self_out, cross_out, kv_all, (gate_time, down_full) = flash_forward(
        plan,
        query,
        packed,
        features,
        text_packed,
        text_features,
        gates_v,
        [plan.gather_time(gate_shard), plan.swap_item(down_time)],
    )
    down_full = down_full.reshape(sets * d_rows, D)
    attn_proj, (up_time, gate_full) = product_scatter(
        plan, "out_proj", [(mixed, out_full)], False, [plan.gather_time(up_shard), plan.swap_item(gate_time)]
    )
    gate_full = gate_full.reshape(D, sets * d_rows)

    state_rows, attn_tail_back = jax.vjp(attn_tail, inputs, attn_proj, gate_attn, gains[1])
    ffn_in_float, ffn_head_back = jax.vjp(attn_head, state_rows, scale_ffn, gains[2])
    ffn_in_all, up_full = exchange(
        plan, "gather_ffn_in", [plan.gather_ring(ffn_in_float.astype(bf16)), plan.swap_item(up_time)]
    )
    ffn_in_all = ffn_in_all.reshape(ROWS, D)
    up_full = up_full.reshape(D, sets * d_rows)
    gate, up = dot(ffn_in_all, gate_full), dot(ffn_in_all, up_full)

    def swiglu(gate_rows, up_rows):
        return jax.nn.silu(gate_rows) * up_rows

    activated, swiglu_back = jax.vjp(swiglu, gate, up)
    activated = activated.astype(bf16)
    down_out, _ = product_scatter(plan, "down", [(activated, down_full)], False)
    result_rows, ffn_tail_back = jax.vjp(attn_tail, state_rows, down_out, gate_ffn, gains[3])

    d_state_tail, d_down, d_gate_ffn, d_gain_four = ffn_tail_back(cotangent[0])
    (d_down_all,) = exchange(plan, "gather_d_down", [plan.gather_ring(d_down.astype(bf16))])
    d_down_all = d_down_all.reshape(ROWS, D)
    grad_down = dot(activated, d_down_all, (0, 0)).astype(bf16)
    d_activated = dot(d_down_all, down_full, (1, 1))
    d_gate, d_up = swiglu_back(d_activated)
    d_gate, d_up = d_gate.astype(bf16), d_up.astype(bf16)
    span_block = (GROUPS, times, M * k_rows, sets * d_rows)

    def add(parts):
        return jnp.sum(parts.astype(f32), axis=0)

    d_ffn_in, (down_parts,) = product_scatter(
        plan,
        "d_ffn_in",
        [(d_gate, gate_full), (d_up, up_full)],
        True,
        [plan.scatter_item(grad_down.reshape(GROUPS, times, d_rows, D))],
    )
    down_sum = add(down_parts).astype(bf16)
    grad_gate = dot(ffn_in_all, d_gate, (0, 0)).astype(bf16).reshape(span_block)
    grad_up = dot(ffn_in_all, d_up, (0, 0)).astype(bf16).reshape(span_block)
    d_state_head, d_scale_ffn, d_gain_three = ffn_head_back(d_ffn_in)
    d_state = d_state_tail + d_state_head
    d_inputs_tail, d_proj, d_gate_attn, d_gain_two = attn_tail_back(d_state)
    d_proj_all, gate_parts, down_parts = exchange(
        plan,
        "gather_d_proj",
        [plan.gather_ring(d_proj.astype(bf16)), plan.scatter_item(grad_gate), plan.scatter_time(down_sum)],
    )
    d_proj_all = d_proj_all.reshape(ROWS, D)
    down_grad = add(down_parts)
    gate_sum = add(gate_parts).astype(bf16)
    grad_out = dot(mixed, d_proj_all, (0, 0))[HEAD:].astype(bf16)
    d_mixed = dot(d_proj_all, out_full, (1, 1)).astype(bf16)
    (dq, dk, dv, tdk, tdv, gate_sums), (gate_parts, up_parts, out_parts) = flash_backward(
        plan,
        query,
        kv_all,
        features,
        text_packed,
        text_features,
        self_out,
        cross_out,
        d_mixed,
        gates_q,
        gates_v,
        [
            plan.scatter_time(gate_sum),
            plan.scatter_item(grad_up),
            plan.scatter_item(grad_out.reshape(GROUPS, times, o_rows, D)),
        ],
    )
    gate_sum = add(gate_parts).astype(bf16).reshape(M, k_rows, sets * d_rows)
    up_sum = add(up_parts).astype(bf16)
    out_sum = add(out_parts).astype(bf16)
    gate_sums = jnp.sum(gate_sums[0, HEAD:].reshape(heads, HEAD), axis=1)
    dq, dk, dv, tdk, tdv = dq[:, :LOCAL], dk[:, :LOCAL], dv[:, HEAD:], tdk[:, :LOCAL], tdv[:, HEAD:]

    d_query = turn(dq, cos, -sin)
    d_key = turn(dk, cos, -sin)
    d_tk = dot(tdk.astype(bf16), shuffle(order), (1, 1))
    qn, kn, tn = q_raw * q_inv, k_raw * k_inv, tk_raw * t_inv
    d_gain_q, d_gain_k, d_gain_t = jnp.sum(d_query * qn, axis=0), jnp.sum(d_key * kn, axis=0), jnp.sum(d_tk * tn, axis=0)
    d_qn, d_kn, d_tn = d_query * gain_q, d_key * gain_k, d_tk * gain_t
    sums = jnp.concatenate(
        [jnp.sum(d_qn * qn, axis=1), jnp.sum(d_kn * kn, axis=1), jnp.sum(d_tn * tn, axis=1)]
    ).reshape(-1, 128)
    sums_all, out_parts = exchange(plan, "gather_sums", [plan.direct_ring(sums), plan.scatter_time(out_sum)])
    out_grad = lax.ppermute(add(out_parts), axes, out_back)
    means = jnp.sum(sums_all, axis=0).reshape(-1) / D
    q_mean, k_mean, t_mean = means[:ROWS, None], means[ROWS : 2 * ROWS, None], means[2 * ROWS :, None]
    d_qkv = jnp.concatenate(
        [(d_qn - qn * q_mean) * q_inv, (d_kn - kn * k_mean) * k_inv, dv], axis=1
    ).astype(bf16)
    d_text = jnp.concatenate([(d_tn - tn * t_mean) * t_inv, tdv], axis=1).astype(bf16)
    grad_qkv = dot(dot(attn_in_all, d_qkv, (0, 0)).astype(bf16), mix, (1, 1)).astype(bf16)
    grad_text = dot(own_captions, d_text, (0, 0)).astype(bf16)
    grad_text = grad_text.reshape(2, GROUPS, width, 2 * LOCAL).transpose(1, 0, 2, 3)
    grad_qkv = grad_qkv.reshape(GROUPS, times, 2, half * k_rows, 3 * LOCAL)
    d_attn_in, (qkv_parts_a, qkv_parts_b, text_parts, up_parts) = product_scatter(
        plan,
        "d_attn_in",
        [(d_qkv, qkv_full)],
        True,
        [
            plan.scatter_item(grad_qkv[:, :, 0]),
            plan.scatter_time(grad_qkv[:, :, 1].transpose(1, 0, 2, 3)),
            plan.scatter_item(grad_text),
            plan.scatter_time(up_sum),
        ],
    )
    qkv_sum_a = add(qkv_parts_a).astype(bf16)
    qkv_sum_b = add(qkv_parts_b).astype(bf16)
    text_sum = add(text_parts).astype(bf16).reshape(M, t_rows, 2 * LOCAL)
    up_sum = add(up_parts).astype(bf16).reshape(M, k_rows, sets * d_rows)
    d_inputs_head, d_scale_attn, d_gain_one = attn_head_back(d_attn_in)
    grad_latent = d_inputs_tail + d_inputs_head

    d_mod_rows = jnp.concatenate([d_scale_attn, d_gate_attn, d_scale_ffn, d_gate_ffn], axis=1)
    d_mod = jnp.einsum("tf,td->fd", onehot, d_mod_rows, precision=highest)
    d_mod = d_mod.reshape(FRAMES, rows_axis, part_n).transpose(1, 0, 2).reshape(times, M, FRAMES, part_n)

    def spread(vector):
        return lax.dynamic_update_slice_in_dim(jnp.zeros((D,), f32), vector, ring * LOCAL, 0)

    def unhalve(vector):
        return vector.reshape(2, heads, HEAD // 2).transpose(1, 2, 0).reshape(LOCAL)

    first = (time == 0).astype(f32)
    d_gains = jnp.stack(
        [
            d_gain_one,
            d_gain_two,
            d_gain_three,
            d_gain_four,
            spread(unhalve(d_gain_q)),
            spread(unhalve(d_gain_k)),
            spread(d_gain_t * first),
            jnp.zeros((D,), f32),
        ]
    )
    d_gains = d_gains.reshape(8, devices, gain_n).transpose(1, 0, 2).reshape(sets, M, 8, gain_n)
    gate_row = lax.dynamic_update_slice_in_dim(
        jnp.zeros((HEADS,), f32), gate_sums * (1.0 - own_gates * own_gates), ring * heads, 0
    )
    gate_row = jnp.pad(gate_row, (0, 128 - HEADS)).reshape(1, 128)
    d_mod_parts, d_gain_parts, gate_rows, qkv_parts_a, qkv_parts_b, text_pieces, gate_pieces, up_pieces = exchange(
        plan,
        "scatter_grads",
        [
            plan.scatter_group(d_mod),
            plan.scatter_all(d_gains),
            plan.gather_all(gate_row),
            plan.scatter_time(qkv_sum_a),
            plan.scatter_item(qkv_sum_b),
            plan.scatter_ring(text_sum),
            plan.scatter_ring(gate_sum),
            plan.scatter_ring(up_sum),
        ],
    )
    gains_grad = jnp.sum(d_gain_parts, axis=(0, 1))[:7]
    gates_grad = jnp.sum(gate_rows, axis=(0, 1, 2))[:HEADS]
    text_grad = text_pieces.reshape(M, t_rows, 2, LOCAL).transpose(1, 2, 0, 3).reshape(t_rows, 2 * D).astype(f32)
    gate_up_grad = jnp.stack([gate_pieces, up_pieces]).reshape(2, M, k_rows, sets, d_rows)
    gate_up_grad = gate_up_grad.transpose(2, 0, 3, 1, 4).reshape(k_rows, 2 * FF).astype(f32)
    qkv_sum = jnp.concatenate([add(qkv_parts_a), add(qkv_parts_b)], axis=0).astype(bf16)
    d_mod_all, qkv_pieces = exchange(
        plan,
        "gather_d_mod",
        [
            plan.gather_all(jnp.sum(d_mod_parts, axis=(0, 1))),
            plan.scatter_ring(qkv_sum.reshape(M, k_rows, 3 * LOCAL)),
        ],
    )
    qkv_grad = qkv_pieces.reshape(M, k_rows, 3, LOCAL).transpose(1, 2, 0, 3).reshape(k_rows, 3 * D).astype(f32)
    d_mod_all = (
        d_mod_all.reshape(GROUPS, rows_axis, FRAMES, part_n).transpose(0, 2, 1, 3).reshape(GROUPS * FRAMES, 4 * D)
    )
    ada_grad = jnp.einsum("fc,fd->cd", silu_slice.astype(f32), d_mod_all, precision=highest)
    bias_grad = lax.dynamic_slice_in_dim(jnp.sum(d_mod_all, axis=0), place * bias_n, bias_n)
    return (
        result_rows[None],
        grad_latent[None],
        qkv_grad,
        text_grad,
        out_grad,
        gate_up_grad,
        down_grad,
        ada_grad,
        bias_grad,
        gains_grad,
        gates_grad,
    )


def solution(mesh):
    items, rows = mesh.shape["items"], mesh.shape["rows"]
    fine = Mesh(mesh.devices.reshape(items, rows // M, M), ("items", "times", "ring"))
    whole = ("items", "times", "ring")
    rows_of = ("times", "ring")
    return jax.shard_map(
        shards,
        mesh=fine,
        in_specs=(
            P("items", rows_of, None),
            P("items", None, None),
            P("items", None, None, None),
            P("items", rows_of, None),
            P("items", None),
            P(whole, None),
            P(whole, None),
            P(whole, None),
            P(whole, None),
            P(whole, None),
            P(whole, None),
            P(whole),
            P(None, whole),
            P(),
            P("items", rows_of, None),
        ),
        out_specs=(
            P("items", rows_of, None),
            P("items", rows_of, None),
            P(whole, None),
            P(whole, None),
            P(whole, None),
            P(whole, None),
            P(whole, None),
            P(whole, None),
            P(whole),
            P(None, whole),
            P(),
        ),
        check_vma=False,
    )
```

```python
import jax
import jax.numpy as jnp
import numpy as np
from jax import lax
from jax.experimental import pallas as pl
from jax.experimental.pallas import tpu as pltpu
from jax.sharding import Mesh
from jax.sharding import PartitionSpec as P

D = 1536
HEADS = 24
HEAD = 64
FF = 4096
TEXT_DIM = 4096
COND = 1024
TEXT = 256
FRAMES = 2
TOK = 128
GROUPS = 2
M = 8
LOCAL = HEADS // M * HEAD
ROWS = M * TOK
WIDE = 256
APART = 8192.0

epsilon = 1e-05
theta_base = 10000.0
highest = lax.Precision.HIGHEST
MESH = pl.DeviceIdType.MESH
f32 = jnp.float32
bf16 = jnp.bfloat16
ANY = pl.BlockSpec(memory_space=pl.ANY)
VMEM = pl.BlockSpec(memory_space=pltpu.VMEM)


def flip(where, mask):
    return tuple(a if b == 0 else a ^ b for a, b in zip(where, mask))


class Job:
    def __init__(self, x, shape, masks, src, dst, pass_on=(), by=None, source=None, piece=None):
        self.x, self.shape, self.masks, self.src, self.dst = x, shape, masks, src, dst
        self.piece = piece
        self.pass_on, self.by, self.source = tuple(pass_on), by, source
        if source is not None:
            self.x = None
        self.dtype = x.dtype

    def count(self):
        return len(self.masks) + len(self.pass_on)

    def block(self):
        return self.piece or self.shape[len(self.dst((0, 0, 0))) :]

    def peers(self):
        return set(self.masks) | ({self.by} if self.pass_on else set())


class Transfers:
    def __init__(self, jobs):
        self.jobs = jobs
        self.sent = [j for j in jobs if j.source is None]
        self.total = sum(j.count() for j in jobs)

    def operands(self):
        return [j.x for j in self.sent]

    def out_shapes(self):
        return [jax.ShapeDtypeStruct(j.shape, j.dtype) for j in self.jobs]

    def scratch(self):
        if not self.jobs:
            return []
        return [
            pltpu.SemaphoreType.DMA((self.total,)),
            pltpu.SemaphoreType.DMA((self.total,)),
            pltpu.SemaphoreType.DMA((2, len(self.jobs))),
        ] + [pltpu.VMEM(j.block(), j.dtype) for j in self.jobs]

    def peers(self):
        found = set()
        for j in self.jobs:
            found |= j.peers()
        return found

    def bind(self, me, ins, outs, sems):
        self.me, self.outs, self.sems = me, outs, sems
        left = list(ins)
        self.ins = []
        for j in self.jobs:
            self.ins.append(left.pop(0) if j.source is None else outs[self.jobs.index(j.source)])
        self.base, at = [], 0
        for j in self.jobs:
            self.base.append(at)
            at += j.count()
        self.arrived, self.kept, self.settled, self.chained, self.forwarded = set(), set(), set(), set(), set()

    def remote(self, src, dst, slot, dest):
        return pltpu.make_async_remote_copy(
            src_ref=src,
            dst_ref=dst,
            send_sem=self.sems[0].at[slot],
            recv_sem=self.sems[1].at[slot],
            device_id=dest,
            device_id_type=MESH,
        )

    def send(self, k, i):
        j = self.jobs[k]
        if i < len(j.masks):
            dest = flip(self.me, j.masks[i])
            at = j.src(dest)
            src = self.ins[k] if at is None else self.ins[k].at[at]
            return self.remote(src, self.outs[k].at[j.dst(self.me)], self.base[k] + i, dest)
        mask = j.pass_on[i - len(j.masks)]
        block = self.outs[k].at[j.dst(flip(self.me, mask))]
        return self.remote(block, block, self.base[k] + i, flip(self.me, j.by))

    def own(self, k, leg):
        j = self.jobs[k]
        room = self.sems[3 + k]
        if leg == 0:
            at = j.src(self.me)
            src = self.ins[k] if at is None else self.ins[k].at[at]
            return pltpu.make_async_copy(src, room, self.sems[2].at[0, k])
        return pltpu.make_async_copy(room, self.outs[k].at[j.dst(self.me)], self.sems[2].at[1, k])

    def start_job(self, k):
        j = self.jobs[k]
        for i in range(len(j.masks)):
            self.send(k, i).start()
        self.own(k, 0).start()

    def start(self):
        for k, j in enumerate(self.jobs):
            if j.source is None:
                self.start_job(k)

    def receive(self, k, i):
        if (k, i) not in self.arrived:
            self.arrived.add((k, i))
            self.send(k, i).wait_recv()

    def take(self, k):
        self.keep(k)
        for i in range(self.jobs[k].count()):
            self.receive(k, i)
        if k not in self.settled:
            self.settled.add(k)
            self.own(k, 1).wait()

    def keep(self, k):
        if k not in self.kept:
            self.kept.add(k)
            self.own(k, 0).wait()
            self.own(k, 1).start()

    def chain(self):
        for k, j in enumerate(self.jobs):
            if j.source is not None and k not in self.chained:
                self.chained.add(k)
                self.take(self.jobs.index(j.source))
                self.start_job(k)

    def forward(self):
        self.chain()
        for k in range(len(self.jobs)):
            self.keep(k)
        for k, j in enumerate(self.jobs):
            if k not in self.forwarded:
                self.forwarded.add(k)
                for n, mask in enumerate(j.pass_on):
                    self.receive(k, j.masks.index(mask))
                    self.send(k, len(j.masks) + n).start()

    def finish(self):
        self.forward()
        for k, j in enumerate(self.jobs):
            self.take(k)
            for i in range(j.count()):
                self.send(k, i).wait_send()


class Plan:
    def __init__(self, times):
        self.times = times
        self.sets = GROUPS * times
        self.rows = times * M
        self.next_id = 0
        ones = [(i, t, m) for i in range(GROUPS) for t in range(times) for m in range(M)]
        self.all = ones[1:]
        self.ring = [(0, 0, m) for m in range(1, M)]
        self.chips = [(0, 0, m) for m in range(2, M, 2)]
        self.mate = (0, 0, 1)
        self.time = [(0, t, 0) for t in range(1, times)]
        self.item = (1, 0, 0)
        self.span = [(i, t, 0) for i in range(GROUPS) for t in range(times)][1:]
        self.group = [(0, t, m) for t in range(times) for m in range(M)][1:]

    def identity(self):
        self.next_id += 1
        return self.next_id

    def set_of(self, where):
        return where[0] * self.times + where[1]

    def gather_ring(self, x):
        return Job(
            x,
            (M,) + x.shape,
            [self.mate] + self.chips,
            lambda dest: None,
            lambda sender: (sender[2],),
            self.chips,
            self.mate,
        )

    def direct_ring(self, x):
        return Job(x, (M,) + x.shape, self.ring, lambda dest: None, lambda sender: (sender[2],))

    def scatter_ring(self, x):
        return Job(x, x.shape, self.ring, lambda dest: (dest[2],), lambda sender: (sender[2],))

    def gather_span(self, x, shape=None, source=None):
        return Job(
            x,
            (self.sets,) + (x.shape if shape is None else shape),
            [self.item] + self.time,
            lambda dest: None,
            lambda sender: (self.set_of(sender),),
            self.time,
            self.item,
            source,
        )

    def scatter_span(self, x):
        return Job(x, x.shape, self.span, lambda dest: (self.set_of(dest),), lambda sender: (self.set_of(sender),))

    def gather_time(self, x):
        return Job(x, (self.times,) + x.shape, self.time, lambda dest: None, lambda sender: (sender[1],))

    def stack_time(self, x):
        n = x.shape[0]
        return Job(
            x,
            (self.times * n,) + x.shape[1:],
            self.time,
            lambda dest: None,
            lambda sender: (pl.ds(pl.multiple_of(sender[1] * n, n), n),),
            piece=x.shape,
        )

    def stack_item(self, x, source=None):
        shape = x.shape if source is None else source.shape
        n = shape[0]
        return Job(
            x,
            (GROUPS * n,) + shape[1:],
            [self.item],
            lambda dest: None,
            lambda sender: (pl.ds(pl.multiple_of(sender[0] * n, n), n),),
            source=source,
            piece=shape,
        )

    def split_time(self, x):
        n = x.shape[0] // self.times
        return Job(
            x,
            (self.times, n) + x.shape[1:],
            self.time,
            lambda dest: (pl.ds(pl.multiple_of(dest[1] * n, n), n),),
            lambda sender: (sender[1],),
        )

    def gather_time_part(self, x, start, count):
        return Job(
            x,
            (self.times, count) + x.shape[1:],
            self.time,
            lambda dest: (pl.ds(start, count),),
            lambda sender: (sender[1],),
        )

    def swap_item_part(self, x, start, count):
        return Job(
            x,
            (GROUPS, count) + x.shape[1:],
            [self.item],
            lambda dest: (pl.ds(start, count),),
            lambda sender: (sender[0],),
        )

    def scatter_time(self, x):
        return Job(x, x.shape, self.time, lambda dest: (dest[1],), lambda sender: (sender[1],))

    def scatter_item(self, x):
        return Job(x, x.shape, [self.item], lambda dest: (dest[0],), lambda sender: (sender[0],))

    def gather_all(self, x):
        return Job(
            x,
            (self.sets, M) + x.shape,
            self.all,
            lambda dest: None,
            lambda sender: (self.set_of(sender), sender[2]),
        )

    def scatter_all(self, x):
        return Job(
            x,
            x.shape,
            self.all,
            lambda dest: (self.set_of(dest), dest[2]),
            lambda sender: (self.set_of(sender), sender[2]),
        )

    def swap_item(self, x):
        return Job(x, (GROUPS,) + x.shape, [self.item], lambda dest: None, lambda sender: (sender[0],))

    def gather_group(self, x):
        return Job(
            x,
            (self.times, M) + x.shape,
            self.group,
            lambda dest: None,
            lambda sender: (sender[1], sender[2]),
        )

    def scatter_group(self, x):
        return Job(
            x,
            x.shape,
            self.group,
            lambda dest: (dest[1], dest[2]),
            lambda sender: (sender[1], sender[2]),
        )


def here():
    return (lax.axis_index("items"), lax.axis_index("times"), lax.axis_index("ring"))


def greet(me, peers):
    barrier = pltpu.get_barrier_semaphore()
    for mask in sorted(peers):
        pl.semaphore_signal(barrier, inc=1, device_id=flip(me, mask), device_id_type=MESH)
    pl.semaphore_wait(barrier, len(peers))


def exchange(plan, name, jobs):
    moves = Transfers(jobs)
    n_in, n_out = len(moves.sent), len(jobs)

    def kernel(*refs):
        me = here()
        greet(me, moves.peers())
        moves.bind(me, refs[:n_in], refs[n_in : n_in + n_out], refs[n_in + n_out :])
        moves.start()
        moves.finish()

    return pl.pallas_call(
        kernel,
        out_shape=moves.out_shapes(),
        in_specs=[ANY] * n_in,
        out_specs=[ANY] * n_out,
        scratch_shapes=moves.scratch(),
        name=name,
        compiler_params=pltpu.CompilerParams(
            collective_id=plan.identity(), has_side_effects=True, vmem_limit_bytes=32 * 2**20
        ),
    )(*moves.operands())


def product_scatter(plan, name, factors, turned, jobs=()):
    moves = Transfers(list(jobs))
    n_factors = len(factors)
    n_in, n_out = len(moves.sent), len(moves.jobs)
    contract = (((1,), (1,)), ((), ())) if turned else (((1,), (0,)), ((), ()))

    def kernel(*refs):
        factor_refs, refs = refs[: 2 * n_factors], refs[2 * n_factors :]
        ins = refs[:n_in]
        out_ref = refs[n_in]
        outs = refs[1 + n_in : 1 + n_in + n_out]
        to_mate, from_mate, part, to_chip, from_chip, send_sem, recv_sem = refs[1 + n_in + n_out : 8 + n_in + n_out]
        me = here()
        ring = me[2]
        core, chip = ring % 2, ring // 2
        greet(me, moves.peers() | {plan.mate} | set(plan.chips))
        if moves.jobs:
            moves.bind(me, ins, outs, refs[8 + n_in + n_out :])
            moves.start()

        def mate_copy(d):
            return pltpu.make_async_remote_copy(
                src_ref=to_mate.at[d],
                dst_ref=from_mate.at[d],
                send_sem=send_sem.at[d],
                recv_sem=recv_sem.at[d],
                device_id=flip(me, plan.mate),
                device_id_type=MESH,
            )

        def chip_copy(d):
            return pltpu.make_async_remote_copy(
                src_ref=to_chip.at[d - 1],
                dst_ref=from_chip.at[d - 1],
                send_sem=send_sem.at[3 + d],
                recv_sem=recv_sem.at[3 + d],
                device_id=flip(me, (0, 0, 2 * d)),
                device_id_type=MESH,
            )

        def block(d, which):
            start = pl.multiple_of((chip ^ d) * (2 * TOK) + which * TOK, TOK)
            products = [
                lax.dot_general(
                    factor_refs[2 * i][pl.ds(start, TOK), :],
                    factor_refs[2 * i + 1][...],
                    contract,
                    preferred_element_type=f32,
                )
                for i in range(n_factors)
            ]
            return sum(products[1:], products[0])

        for d in (3, 2, 1, 0):
            to_mate[d] = block(d, 1 - core).astype(bf16)
            mate_copy(d).start()
        for d in (3, 2, 1):
            part[...] = block(d, core)
            mate_copy(d).wait_recv()
            to_chip[d - 1] = (part[...] + from_mate[d].astype(f32)).astype(bf16)
            chip_copy(d).start()
        part[...] = block(0, core)
        mate_copy(0).wait_recv()
        part[...] = part[...] + from_mate[0].astype(f32)
        for d in (3, 2, 1):
            chip_copy(d).wait_recv()
        out_ref[...] = part[...] + (
            from_chip[0].astype(f32) + from_chip[1].astype(f32) + from_chip[2].astype(f32)
        )
        for d in range(4):
            mate_copy(d).wait_send()
        for d in (1, 2, 3):
            chip_copy(d).wait_send()
        if moves.jobs:
            moves.finish()

    result = pl.pallas_call(
        kernel,
        out_shape=[jax.ShapeDtypeStruct((TOK, D), f32)] + moves.out_shapes(),
        in_specs=[VMEM] * (2 * n_factors) + [ANY] * n_in,
        out_specs=[VMEM] + [ANY] * n_out,
        scratch_shapes=[
            pltpu.VMEM((4, TOK, D), bf16),
            pltpu.VMEM((4, TOK, D), bf16),
            pltpu.VMEM((TOK, D), f32),
            pltpu.VMEM((3, TOK, D), bf16),
            pltpu.VMEM((3, TOK, D), bf16),
            pltpu.SemaphoreType.DMA((7,)),
            pltpu.SemaphoreType.DMA((7,)),
        ]
        + moves.scratch(),
        name=name,
        compiler_params=pltpu.CompilerParams(
            collective_id=plan.identity(), has_side_effects=True, vmem_limit_bytes=48 * 2**20
        ),
    )(*[x for pair in factors for x in pair], *moves.operands())
    return result[0], result[1:]


def feed_forward(
    plan, mixed, out_full, latents, cotangent, modulation, gains, first_rows, gate_time, up_shard, down_full, d_rows
):
    width = down_full.shape[0]
    deep = out_full.shape[0]
    up_job = plan.stack_time(up_shard)
    moves = Transfers([plan.stack_item(gate_time), up_job, plan.stack_item(up_shard, up_job)])
    n_in, n_out = len(moves.sent), len(moves.jobs)
    turned = (((1,), (1,)), ((), ()))
    sunk = (((0,), (0,)), ((), ()))
    plain = (((1,), (0,)), ((), ()))
    chip_rows = 2 * TOK
    part_rows = D // GROUPS
    others = len(plan.time)
    slab = plan.times * d_rows

    def kernel(*refs):
        (mixed_ref, out_w, latent_ref, cot_ref, mod_ref, gain_ref, first_ref, down_w) = refs[:8]
        ins = refs[8 : 8 + n_in]
        refs = refs[8 + n_in :]
        (result_ref, d_state_ref, d_mixed_ref, grad_out_ref, gate_sum_ref, up_sum_ref, down_grad_ref, sums_ref) = refs[:8]
        outs = refs[8 : 8 + n_out]
        refs = refs[8 + n_out :]
        (gate_w, up_w, ffn_all, down_all, proj_all, gate_ref, up_ref, act_ref, d_gate_ref, d_up_ref) = refs[:10]
        (grad_gate, grad_up, grad_down, from_gate, from_up, from_down, down_sum, from_time) = refs[10:18]
        (to_mate, from_mate, to_chip, from_chip, part, proj_ref, state_ref, own_ref, send_sem, recv_sem, local_sem) = refs[
            18:29
        ]
        me = here()
        item, time, ring = me
        core, chip = ring % 2, ring // 2
        greet(me, moves.peers() | {plan.mate, plan.item} | set(plan.chips) | set(plan.time))
        moves.bind(me, ins, outs, refs[29:])
        moves.start()
        used = [0]

        def link(src, dst, mask):
            slot = used[0]
            used[0] += 1
            return pltpu.make_async_remote_copy(
                src_ref=src,
                dst_ref=dst,
                send_sem=send_sem.at[slot],
                recv_sem=recv_sem.at[slot],
                device_id=flip(me, mask),
                device_id_type=MESH,
            )

        def rows_at(index, count):
            return pl.ds(pl.multiple_of(index * count, count), count)

        def scatter(product, meanwhile=lambda: None):
            mates = [link(to_mate.at[d], from_mate.at[d], plan.mate) for d in range(4)]
            chips = [link(to_chip.at[d - 1], from_chip.at[d - 1], (0, 0, 2 * d)) for d in (1, 2, 3)]
            for d in (3, 2, 1, 0):
                to_mate[d] = product((chip ^ d) * 2 + 1 - core).astype(bf16)
                mates[d].start()
            for d in (3, 2, 1):
                part[...] = product((chip ^ d) * 2 + core)
                mates[d].wait_recv()
                to_chip[d - 1] = (part[...] + from_mate[d].astype(f32)).astype(bf16)
                chips[d - 1].start()
            part[...] = product(chip * 2 + core)
            mates[0].wait_recv()
            part[...] = part[...] + from_mate[0].astype(f32)
            meanwhile()
            for copy in chips:
                copy.wait_recv()
            part[...] = part[...] + (
                from_chip[0].astype(f32) + from_chip[1].astype(f32) + from_chip[2].astype(f32)
            )
            for copy in mates + chips:
                copy.wait_send()

        def gather(all_ref, each, meanwhile=lambda: None):
            own = all_ref.at[rows_at(ring, TOK)]
            first = [link(own, own, plan.mate)] + [link(own, own, (0, 0, 2 * d)) for d in (1, 2, 3)]
            for copy in first[1:] + first[:1]:
                copy.start()
            meanwhile()
            first[0].wait_recv()
            each(chip)
            later = []
            for d in (1, 2, 3):
                first[d].wait_recv()
                block = all_ref.at[rows_at(ring ^ (2 * d), TOK)]
                copy = link(block, block, plan.mate)
                copy.start()
                later.append(copy)
            for d in (1, 2, 3):
                later[d - 1].wait_recv()
                each(chip ^ d)
            for copy in first + later:
                copy.wait_send()

        is_first = first_ref[...] > 0.5

        def modulated(index):
            cols = pl.ds(index * D, D)
            return jnp.where(is_first, mod_ref[0:1, cols], mod_ref[1:2, cols])

        def column_sums(at, values):
            total = jnp.sum(values, axis=0, keepdims=True)
            start = jnp.sum(jnp.where(is_first, values, 0.0), axis=0, keepdims=True)
            sums_ref[at : at + 1, :] = start
            sums_ref[at + 1 : at + 2, :] = total - start

        def scale_of(values):
            return lax.rsqrt(jnp.mean(values * values, axis=1, keepdims=True) + epsilon)

        def norm_back(d_hat, hat, inverse):
            return inverse * (d_hat - hat * jnp.mean(d_hat * hat, axis=1, keepdims=True))

        def load(job, target):
            moves.take(job)
            copy = pltpu.make_async_copy(outs[job], target, local_sem.at[0])
            copy.start()
            copy.wait()

        def out_product(block):
            return jnp.dot(mixed_ref[rows_at(block, TOK), :], out_w[...], preferred_element_type=f32)

        scatter(out_product)
        moves.chain()
        proj_ref[...] = part[...]
        proj = proj_ref[...]
        gate_attn = jnp.tanh(modulated(1))
        state_ref[...] = latent_ref[...] + gate_attn * (proj * scale_of(proj) * gain_ref[1:2, :])
        state = state_ref[...]
        ffn_in = state * scale_of(state) * gain_ref[2:3, :] * (1.0 + modulated(2))
        ffn_all[rows_at(ring, TOK), :] = ffn_in.astype(bf16)

        def forward_chip(which):
            rows = rows_at(which, chip_rows)
            block = ffn_all[rows, :]
            gate = jnp.dot(block, gate_w[...], preferred_element_type=f32)
            up = jnp.dot(block, up_w[...], preferred_element_type=f32)
            gate_ref[rows, :] = gate
            up_ref[rows, :] = up
            act_ref[rows, :] = (gate * (1.0 / (1.0 + jnp.exp(-gate))) * up).astype(bf16)

        def weights_here():
            load(0, gate_w)
            load(2, up_w)

        gather(ffn_all, forward_chip, weights_here)

        def down_product(block):
            return jnp.dot(act_ref[rows_at(block, TOK), :], down_w[...], preferred_element_type=f32)

        scatter(down_product)

        down = part[...]
        inverse = scale_of(down)
        hat = down * inverse
        gate_ffn = jnp.tanh(modulated(3))
        gain = gain_ref[3:4, :]
        cot = cot_ref[...]
        result_ref[...] = state_ref[...] + gate_ffn * (hat * gain)
        column_sums(7, cot * (hat * gain) * (1.0 - gate_ffn * gate_ffn))
        d_norm = cot * gate_ffn
        sums_ref[2:3, :] = jnp.sum(d_norm * hat, axis=0, keepdims=True)
        down_all[rows_at(ring, TOK), :] = norm_back(d_norm * gain, hat, inverse).astype(bf16)

        def backward_chip(which):
            rows = rows_at(which, chip_rows)
            d_act = lax.dot_general(down_all[rows, :], down_w[...], turned, preferred_element_type=f32)
            gate, up = gate_ref[rows, :], up_ref[rows, :]
            sigmoid = 1.0 / (1.0 + jnp.exp(-gate))
            d_up_ref[rows, :] = (d_act * (gate * sigmoid)).astype(bf16)
            d_gate_ref[rows, :] = (d_act * up * (sigmoid * (1.0 + gate * (1.0 - sigmoid)))).astype(bf16)

        gather(down_all, backward_chip)

        away = 1 - item
        down_link = link(grad_down.at[rows_at(away, slab)], from_down, plan.item)
        gate_link = link(grad_gate.at[rows_at(away, part_rows)], from_gate, plan.item)
        up_link = link(grad_up.at[rows_at(away, part_rows)], from_up, plan.item)
        time_links = [link(down_sum.at[rows_at(time ^ mask[1], d_rows)], from_time.at[i], mask) for i, mask in enumerate(plan.time)]

        def down_gradient():
            grad_down[...] = lax.dot_general(act_ref[...], down_all[...], sunk, preferred_element_type=f32).astype(bf16)
            down_link.start()

        def gate_gradients():
            down_gradient()
            grad_gate[...] = lax.dot_general(ffn_all[...], d_gate_ref[...], sunk, preferred_element_type=f32).astype(bf16)
            gate_link.start()
            grad_up[...] = lax.dot_general(ffn_all[...], d_up_ref[...], sunk, preferred_element_type=f32).astype(bf16)
            up_link.start()

        def back_product(block):
            rows = rows_at(block, TOK)
            return lax.dot_general(d_gate_ref[rows, :], gate_w[...], turned, preferred_element_type=f32) + lax.dot_general(
                d_up_ref[rows, :], up_w[...], turned, preferred_element_type=f32
            )

        scatter(back_product, gate_gradients)

        d_ffn = part[...]
        state = state_ref[...]
        inverse = scale_of(state)
        hat = state * inverse
        gain = gain_ref[2:3, :]
        column_sums(5, d_ffn * (hat * gain))
        d_norm = d_ffn * (1.0 + modulated(2))
        sums_ref[1:2, :] = jnp.sum(d_norm * hat, axis=0, keepdims=True)
        d_state_ref[...] = cot_ref[...] + norm_back(d_norm * gain, hat, inverse)
        d_state = d_state_ref[...]
        proj = proj_ref[...]
        inverse = scale_of(proj)
        hat = proj * inverse
        gate_attn = jnp.tanh(modulated(1))
        gain = gain_ref[1:2, :]
        column_sums(3, d_state * (hat * gain) * (1.0 - gate_attn * gate_attn))
        d_norm = d_state * gate_attn
        sums_ref[0:1, :] = jnp.sum(d_norm * hat, axis=0, keepdims=True)
        proj_all[rows_at(ring, TOK), :] = norm_back(d_norm * gain, hat, inverse).astype(bf16)

        def down_time():
            down_link.wait_recv()
            mine = grad_down[rows_at(item, slab), :].astype(f32) + from_down[...].astype(f32)
            down_sum[...] = mine.astype(bf16)
            for copy in time_links:
                copy.start()

        def mixed_chip(which):
            rows = rows_at(which, chip_rows)
            d_mixed_ref[rows, :] = lax.dot_general(
                proj_all[rows, :], out_w[...], turned, preferred_element_type=f32
            ).astype(bf16)

        gather(proj_all, mixed_chip, down_time)
        grad_out_ref[...] = lax.dot_general(mixed_ref[...], proj_all[...], sunk, preferred_element_type=f32).astype(bf16)
        gate_link.wait_recv()
        gate_sum_ref[...] = (
            grad_gate[rows_at(item, part_rows), :].astype(f32) + from_gate[...].astype(f32)
        ).astype(bf16)
        own_ref[...] = down_sum[rows_at(time, d_rows), :].astype(f32)
        for i, copy in enumerate(time_links):
            copy.wait_recv()
            own_ref[...] += from_time[i].astype(f32)
        down_grad_ref[...] = own_ref[...]
        up_link.wait_recv()
        up_sum_ref[...] = (grad_up[rows_at(item, part_rows), :].astype(f32) + from_up[...].astype(f32)).astype(bf16)
        for copy in [down_link, gate_link, up_link] + time_links:
            copy.wait_send()
        moves.finish()

    links = 7 * 3 + 7 * 3 + 3 + others
    result = pl.pallas_call(
        kernel,
        out_shape=[
            jax.ShapeDtypeStruct((TOK, D), f32),
            jax.ShapeDtypeStruct((TOK, D), f32),
            jax.ShapeDtypeStruct((ROWS, deep), bf16),
            jax.ShapeDtypeStruct((deep, D), bf16),
            jax.ShapeDtypeStruct((part_rows, width), bf16),
            jax.ShapeDtypeStruct((part_rows, width), bf16),
            jax.ShapeDtypeStruct((d_rows, D), f32),
            jax.ShapeDtypeStruct((16, D), f32),
        ]
        + moves.out_shapes(),
        in_specs=[VMEM] * 8 + [ANY] * n_in,
        out_specs=[VMEM] * 8 + [ANY] * n_out,
        scratch_shapes=[
            pltpu.VMEM((D, width), bf16),
            pltpu.VMEM((D, width), bf16),
            pltpu.VMEM((ROWS, D), bf16),
            pltpu.VMEM((ROWS, D), bf16),
            pltpu.VMEM((ROWS, D), bf16),
            pltpu.VMEM((ROWS, width), f32),
            pltpu.VMEM((ROWS, width), f32),
            pltpu.VMEM((ROWS, width), bf16),
            pltpu.VMEM((ROWS, width), bf16),
            pltpu.VMEM((ROWS, width), bf16),
            pltpu.VMEM((D, width), bf16),
            pltpu.VMEM((D, width), bf16),
            pltpu.VMEM((width, D), bf16),
            pltpu.VMEM((part_rows, width), bf16),
            pltpu.VMEM((part_rows, width), bf16),
            pltpu.VMEM((slab, D), bf16),
            pltpu.VMEM((slab, D), bf16),
            pltpu.VMEM((max(others, 1), d_rows, D), bf16),
            pltpu.VMEM((4, TOK, D), bf16),
            pltpu.VMEM((4, TOK, D), bf16),
            pltpu.VMEM((3, TOK, D), bf16),
            pltpu.VMEM((3, TOK, D), bf16),
            pltpu.VMEM((TOK, D), f32),
            pltpu.VMEM((TOK, D), f32),
            pltpu.VMEM((TOK, D), f32),
            pltpu.VMEM((d_rows, D), f32),
            pltpu.SemaphoreType.DMA((links,)),
            pltpu.SemaphoreType.DMA((links,)),
            pltpu.SemaphoreType.DMA((1,)),
        ]
        + moves.scratch(),
        name="feed_forward",
        compiler_params=pltpu.CompilerParams(
            collective_id=plan.identity(), has_side_effects=True, vmem_limit_bytes=60 * 2**20
        ),
    )(mixed, out_full, latents, cotangent, modulation, gains, first_rows, down_full, *moves.operands())
    return result[:8]


def normed(value, gain_row):
    return value * lax.rsqrt(jnp.mean(value * value, axis=-1, keepdims=True) + epsilon) * gain_row


def attn_head(input_rows, scale_rows, gain_row):
    return normed(input_rows, gain_row) * (1.0 + scale_rows)


def dot(a, b, dims=(1, 0)):
    return lax.dot_general(a, b, (((dims[0],), (dims[1],)), ((), ())), preferred_element_type=f32)


def halves_order():
    col = np.arange(LOCAL)
    head, pair, odd = col // HEAD, col % HEAD // 2, col % 2
    place = odd * (LOCAL // 2) + head * (HEAD // 2) + pair
    order = np.zeros(LOCAL, np.int64)
    order[place] = col
    full = np.concatenate([order, LOCAL + order, 2 * LOCAL + col])
    return order, full


def shuffle(order):
    n = order.shape[0]
    line = jnp.arange(n, dtype=jnp.int32)
    return (line[:, None] == jnp.asarray(order, jnp.int32)[None, :]).astype(bf16)


def turn(rows, cos, sin):
    half = LOCAL // 2
    first, second = rows[:, :half], rows[:, half:]
    return jnp.concatenate([first * cos - second * sin, second * cos + first * sin], axis=1)


def lane_masks():
    lane = np.arange(WIDE)
    query, value = np.zeros((8, WIDE), np.float32), np.zeros((8, WIDE), np.float32)
    back = np.zeros((8, WIDE), np.float32)
    half = HEAD // 2
    for h in range(LOCAL // HEAD):
        query[h] = ((lane < LOCAL) & (lane % (LOCAL // 2) // half == h)) | (lane == LOCAL) | (lane == LOCAL + 1)
        query[h] += (lane >= LOCAL + 2 + 3 * h) & (lane < LOCAL + 5 + 3 * h)
        value[h] = ((lane >= HEAD) & (lane // HEAD - 1 == h)) | (lane // 16 == h)
        back[h] = ((lane >= HEAD) & (lane // HEAD - 1 == h)) | (lane == 2 * h) | (lane == 2 * h + 1)
    return query, value, back


def widen(packed_ref, feature, key_ref, value_ref, rows):
    lane = lax.broadcasted_iota(jnp.int32, (rows, 128), 1)
    middle = packed_ref[:, 128:256].astype(f32)
    key_ref[:rows, :128] = packed_ref[:, :128]
    key_ref[:rows, 128:] = jnp.where(lane < HEAD, middle, feature.astype(f32)).astype(bf16)
    value_ref[:rows, :128] = jnp.where(lane < HEAD, 1.0, middle).astype(bf16)
    value_ref[:rows, 128:] = packed_ref[:, 256:]


def flash_forward(plan, query, packed, features, text_packed, text_features, gates, jobs):
    heads = LOCAL // HEAD
    text_rows = text_packed.shape[0]
    keys_job = plan.gather_time(packed)
    moves = Transfers([keys_job] + list(jobs))
    n_in, n_out = len(moves.sent) - 1, len(moves.jobs)
    block = 256

    def kernel(*refs):
        query_ref, packed_ref, feature_ref, text_ref, text_feature_ref, gate_ref, qmask_ref, vmask_ref = refs[:8]
        ins = refs[8 : 9 + n_in]
        mixed_ref, self_ref, cross_ref = refs[9 + n_in : 12 + n_in]
        outs = refs[12 + n_in : 12 + n_in + n_out]
        key_ref, value_ref, far_ref, max_ref, sem = refs[12 + n_in + n_out : 17 + n_in + n_out]
        me = here()
        greet(me, moves.peers())
        moves.bind(me, ins, outs, refs[17 + n_in + n_out :])
        moves.start()

        def segment(rows, first, out_ref):
            def body(at, carry):
                where = pl.ds(pl.multiple_of(at * block, block), block)
                query_rows = query_ref[where, :]
                total = jnp.zeros((block, WIDE), f32)
                tops = jnp.zeros((block, WIDE), f32)
                for h in range(heads):
                    own_query = query_rows * qmask_ref[h : h + 1, :]
                    scores = lax.dot_general(
                        own_query, key_ref[:rows, :], (((1,), (1,)), ((), ())), preferred_element_type=f32
                    )
                    top = jnp.max(scores, axis=1, keepdims=True)
                    weights = jnp.exp(scores - top).astype(bf16)
                    product = jnp.dot(weights, value_ref[:rows, :], preferred_element_type=f32)
                    total += product * vmask_ref[h : h + 1, :]
                    tops += top * vmask_ref[h : h + 1, :]
                if first:
                    out_ref[where, :] = total
                    max_ref[where, :] = tops
                else:
                    before = max_ref[where, :]
                    after = jnp.maximum(before, tops)
                    out_ref[where, :] = out_ref[where, :] * jnp.exp(before - after) + total * jnp.exp(tops - after)
                    max_ref[where, :] = after
                return carry

            lax.fori_loop(0, ROWS // block, body, 0)

        def close(out_ref):
            def body(at, carry):
                where = pl.ds(pl.multiple_of(at * block, block), block)
                lane = lax.broadcasted_iota(jnp.int32, (block, WIDE), 1)
                values = out_ref[where, :]
                share = jnp.ones((block, WIDE), f32)
                for h in range(heads):
                    share = jnp.where(
                        (lane >= HEAD * (h + 1)) & (lane < HEAD * (h + 2)), values[:, 16 * h : 16 * h + 1], share
                    )
                logs = max_ref[where, :] + jnp.log(jnp.maximum(values, 1e-30))
                out_ref[where, :] = jnp.where(
                    lane < HEAD, jnp.where(lane < 16 * heads, logs, 0.0), values / share
                )
                return carry

            lax.fori_loop(0, ROWS // block, body, 0)

        widen(text_ref, text_feature_ref[...], key_ref, value_ref, text_rows)
        segment(text_rows, True, cross_ref)
        close(cross_ref)
        moves.chain()
        own_rows = pl.ds(pl.multiple_of(me[1] * ROWS, ROWS), ROWS)
        widen(packed_ref, feature_ref[own_rows, :], key_ref, value_ref, ROWS)
        segment(ROWS, True, self_ref)
        for i, mask in enumerate(plan.time):
            moves.receive(0, i)
            far = me[1] ^ mask[1]
            bring = pltpu.make_async_copy(outs[0].at[far], far_ref, sem)
            bring.start()
            bring.wait()
            far_rows = pl.ds(pl.multiple_of(far * ROWS, ROWS), ROWS)
            widen(far_ref, feature_ref[far_rows, :], key_ref, value_ref, ROWS)
            segment(ROWS, False, self_ref)
        moves.forward()
        close(self_ref)
        lane = lax.broadcasted_iota(jnp.int32, (ROWS, WIDE), 1)
        both = self_ref[...] + gate_ref[...] * cross_ref[...]
        mixed_ref[...] = jnp.where(lane < HEAD, 0.0, both).astype(bf16)
        moves.finish()

    qmask, vmask, _ = lane_masks()
    result = pl.pallas_call(
        kernel,
        out_shape=[
            jax.ShapeDtypeStruct((ROWS, WIDE), bf16),
            jax.ShapeDtypeStruct((ROWS, WIDE), f32),
            jax.ShapeDtypeStruct((ROWS, WIDE), f32),
        ]
        + moves.out_shapes(),
        in_specs=[VMEM] * 8 + [ANY] * (n_in + 1),
        out_specs=[VMEM] * 3 + [ANY] * n_out,
        scratch_shapes=[
            pltpu.VMEM((ROWS, WIDE), bf16),
            pltpu.VMEM((ROWS, WIDE), bf16),
            pltpu.VMEM((ROWS, 2 * LOCAL), bf16),
            pltpu.VMEM((ROWS, WIDE), f32),
            pltpu.SemaphoreType.DMA(()),
        ]
        + moves.scratch(),
        name="flash_forward",
        compiler_params=pltpu.CompilerParams(
            collective_id=plan.identity(), has_side_effects=True, vmem_limit_bytes=56 * 2**20
        ),
    )(
        query,
        packed,
        features,
        text_packed,
        text_features,
        gates,
        jnp.asarray(qmask, bf16),
        jnp.asarray(vmask, f32),
        *moves.operands(),
    )
    return result[0], result[1], result[2], result[3], result[4:]


def flash_backward(
    plan, query, packed_all, features, text_packed, text_features, self_out, cross_out, d_mixed, gates_q, gates_v, jobs
):
    heads = LOCAL // HEAD
    text_rows = text_packed.shape[0]
    moves = Transfers(list(jobs))
    n_in, n_out = len(moves.sent), len(moves.jobs)
    block = 256
    others = len(plan.time)
    turned = (((1,), (1,)), ((), ()))
    sunk = (((0,), (0,)), ((), ()))

    def kernel(*refs):
        (query_ref, packed_ref, feature_ref, text_ref, text_feature_ref, self_ref, cross_ref, d_ref) = refs[:8]
        gateq_ref, gatev_ref, qmask_ref, bmask_ref = refs[8:12]
        ins = refs[12 : 12 + n_in]
        dq_ref, dk_ref, dv_ref, tdk_ref, tdv_ref, sums_ref = refs[12 + n_in : 18 + n_in]
        outs = refs[18 + n_in : 18 + n_in + n_out]
        (key_ref, value_ref, near_ref, qs_ref, ds_ref, to_ref, from_ref, tto_ref, tfrom_ref, sem, send_sem, recv_sem) = refs[
            18 + n_in + n_out : 30 + n_in + n_out
        ]
        me = here()
        greet(me, moves.peers() | set(plan.time))
        if moves.jobs:
            moves.bind(me, ins, outs, refs[30 + n_in + n_out :])
            moves.start()

        def prepare(out_ref):
            def body(at, carry):
                where = pl.ds(pl.multiple_of(at * block, block), block)
                lane = lax.broadcasted_iota(jnp.int32, (block, 128), 1)
                tail = query_ref[where, 128:].astype(f32)
                out_rows = out_ref[where, :]
                d_rows = d_ref[where, :].astype(f32)
                product = d_rows * out_rows
                head_tile = jnp.where(lane < HEAD, 0.0, d_rows[:, :128])
                for h in range(heads):
                    log = -out_rows[:, 16 * h : 16 * h + 1]
                    for j in range(3):
                        piece = log.astype(bf16).astype(f32)
                        log = log - piece
                        tail = jnp.where(lane == HEAD + 2 + 3 * h + j, piece, tail)
                    delta = -jnp.sum(product * bmask_ref[h : h + 1, :].astype(f32), axis=1, keepdims=True)
                    for j in range(2):
                        piece = delta.astype(bf16).astype(f32)
                        delta = delta - piece
                        head_tile = jnp.where(lane == 2 * h + j, piece, head_tile)
                qs_ref[where, :128] = query_ref[where, :128]
                qs_ref[where, 128:] = tail.astype(bf16)
                ds_ref[where, :128] = head_tile.astype(bf16)
                ds_ref[where, 128:] = d_ref[where, 128:]
                return carry

            lax.fori_loop(0, ROWS // block, body, 0)

        def segment(rows, first, k_ref, v_ref, scale):
            k_ref[...] = jnp.zeros_like(k_ref)
            v_ref[...] = jnp.zeros_like(v_ref)

            def body(at, carry):
                where = pl.ds(pl.multiple_of(at * block, block), block)
                query_rows, d_rows = qs_ref[where, :], ds_ref[where, :]
                total = jnp.zeros((block, WIDE), f32)
                for h in range(heads):
                    own_query = query_rows * qmask_ref[h : h + 1, :]
                    own_d = d_rows * bmask_ref[h : h + 1, :]
                    keys = key_ref[:rows, :]
                    weights = jnp.exp(lax.dot_general(keys, own_query, turned, preferred_element_type=f32))
                    d_weights = lax.dot_general(value_ref[:rows, :], own_d, turned, preferred_element_type=f32)
                    d_scores = (weights * d_weights).astype(bf16)
                    v_ref[...] += jnp.dot(weights.astype(bf16), own_d, preferred_element_type=f32)
                    k_ref[...] += jnp.dot(d_scores, own_query, preferred_element_type=f32)
                    d_query = lax.dot_general(d_scores, keys, sunk, preferred_element_type=f32)
                    total += d_query * qmask_ref[h : h + 1, :].astype(f32)
                total = total * scale
                if first:
                    dq_ref[where, :] = total
                else:
                    dq_ref[where, :] += total
                return carry

            lax.fori_loop(0, ROWS // block, body, 0)

        def pack(k_ref, v_ref, rows):
            lane = lax.broadcasted_iota(jnp.int32, (rows, 128), 1)
            middle = jnp.where(lane < HEAD, k_ref[:, 128:], v_ref[:, :128])
            return k_ref[:, :128].astype(bf16), middle.astype(bf16), v_ref[:, 128:].astype(bf16)

        def bring(which):
            copy = pltpu.make_async_copy(packed_ref.at[which], near_ref, sem)
            copy.start()
            copy.wait()
            rows = pl.ds(pl.multiple_of(which * ROWS, ROWS), ROWS)
            widen(near_ref, feature_ref[rows, :], key_ref, value_ref, ROWS)

        def send(src, dst, slot, mask):
            return pltpu.make_async_remote_copy(
                src_ref=src,
                dst_ref=dst,
                send_sem=send_sem.at[slot],
                recv_sem=recv_sem.at[slot],
                device_id=flip(me, mask),
                device_id_type=MESH,
            )

        far_copies = [send(to_ref.at[i], from_ref.at[i], i, mask) for i, mask in enumerate(plan.time)]
        text_copies = [send(tto_ref, tfrom_ref.at[i], others + i, mask) for i, mask in enumerate(plan.time)]

        prepare(self_ref)
        for i, mask in enumerate(plan.time):
            bring(me[1] ^ mask[1])
            segment(ROWS, i == 0, dk_ref, dv_ref, 0.125)
            to_ref[i, :, :128], to_ref[i, :, 128:256], to_ref[i, :, 256:] = pack(dk_ref, dv_ref, ROWS)
            far_copies[i].start()
        bring(me[1])
        segment(ROWS, others == 0, dk_ref, dv_ref, 0.125)
        prepare(cross_ref)
        widen(text_ref, text_feature_ref[...], key_ref, value_ref, text_rows)
        segment(text_rows, False, tdk_ref, tdv_ref, 0.125 * gateq_ref[...])
        tdk_ref[...] = tdk_ref[...] * gateq_ref[...]
        tdv_ref[...] = tdv_ref[...] * gatev_ref[...]
        if others:
            tto_ref[:, :128], tto_ref[:, 128:256], tto_ref[:, 256:] = pack(tdk_ref, tdv_ref, text_rows)
            for copy in text_copies:
                copy.start()
        sums_ref[...] = jnp.sum(d_ref[...].astype(f32) * cross_ref[...], axis=0, keepdims=True)
        if moves.jobs:
            moves.forward()
        lane = lax.broadcasted_iota(jnp.int32, (ROWS, 128), 1)
        for i in range(others):
            far_copies[i].wait_recv()
            middle = from_ref[i, :, 128:256].astype(f32)
            dk_ref[:, :128] += from_ref[i, :, :128].astype(f32)
            dk_ref[:, 128:] += middle
            dv_ref[:, :128] += middle
            dv_ref[:, 128:] += from_ref[i, :, 256:].astype(f32)
        for i in range(others):
            text_copies[i].wait_recv()
            middle = tfrom_ref[i, :, 128:256].astype(f32)
            tdk_ref[:, :128] += tfrom_ref[i, :, :128].astype(f32)
            tdk_ref[:, 128:] += middle
            tdv_ref[:, :128] += middle
            tdv_ref[:, 128:] += tfrom_ref[i, :, 256:].astype(f32)
        for copy in far_copies + text_copies:
            copy.wait_send()
        if moves.jobs:
            moves.finish()

    qmask, _, bmask = lane_masks()
    result = pl.pallas_call(
        kernel,
        out_shape=[
            jax.ShapeDtypeStruct((ROWS, WIDE), f32),
            jax.ShapeDtypeStruct((ROWS, WIDE), f32),
            jax.ShapeDtypeStruct((ROWS, WIDE), f32),
            jax.ShapeDtypeStruct((text_rows, WIDE), f32),
            jax.ShapeDtypeStruct((text_rows, WIDE), f32),
            jax.ShapeDtypeStruct((1, WIDE), f32),
        ]
        + moves.out_shapes(),
        in_specs=[VMEM, ANY] + [VMEM] * 10 + [ANY] * n_in,
        out_specs=[VMEM] * 6 + [ANY] * n_out,
        scratch_shapes=[
            pltpu.VMEM((ROWS, WIDE), bf16),
            pltpu.VMEM((ROWS, WIDE), bf16),
            pltpu.VMEM((ROWS, 2 * LOCAL), bf16),
            pltpu.VMEM((ROWS, WIDE), bf16),
            pltpu.VMEM((ROWS, WIDE), bf16),
            pltpu.VMEM((max(others, 1), ROWS, 2 * LOCAL), bf16),
            pltpu.VMEM((max(others, 1), ROWS, 2 * LOCAL), bf16),
            pltpu.VMEM((text_rows, 2 * LOCAL), bf16),
            pltpu.VMEM((max(others, 1), text_rows, 2 * LOCAL), bf16),
            pltpu.SemaphoreType.DMA(()),
            pltpu.SemaphoreType.DMA((max(2 * others, 1),)),
            pltpu.SemaphoreType.DMA((max(2 * others, 1),)),
        ]
        + moves.scratch(),
        name="flash_backward",
        compiler_params=pltpu.CompilerParams(
            collective_id=plan.identity(), has_side_effects=True, vmem_limit_bytes=56 * 2**20
        ),
    )(
        query,
        packed_all,
        features,
        text_packed,
        text_features,
        self_out,
        cross_out,
        d_mixed,
        gates_q,
        gates_v,
        jnp.asarray(qmask, bf16),
        jnp.asarray(bmask, bf16),
        *moves.operands(),
    )
    return result[:6], result[6:]


def shards(
    latents,
    conditions,
    captions,
    row_counts,
    text_lengths,
    qkv_weight,
    text_weight,
    out_weight,
    gate_up_weight,
    down_weight,
    ada_weight,
    ada_bias,
    norm_gains,
    head_gates,
    cotangent,
):
    times = lax.axis_size("times")
    plan = Plan(times)
    sets, rows_axis = plan.sets, plan.rows
    devices = sets * M
    item, time, ring = here()
    place = (item * times + time) * M + ring
    group_place = time * M + ring
    heads = LOCAL // HEAD

    k_rows = qkv_weight.shape[0]
    t_rows = text_weight.shape[0]
    o_rows = out_weight.shape[0]
    d_rows = down_weight.shape[0]
    a_rows = ada_weight.shape[0]
    bias_n = ada_bias.shape[0]
    gain_n = norm_gains.shape[1]
    part_n = 4 * D // rows_axis

    package = jnp.concatenate(
        [norm_gains.astype(f32).reshape(-1), ada_bias.astype(f32), row_counts[0, 0].astype(f32)]
    )
    package_n = package.shape[0]
    lines = -(-package_n // 1024) * 8
    package = jnp.pad(package, (0, lines * 128 - package_n)).reshape(lines, 128)
    silu_own = jax.nn.silu(conditions[0].astype(f32)).astype(bf16)
    order, order_full = halves_order()
    mix = shuffle(order_full)
    qkv_send = qkv_weight.reshape(k_rows, 3, M, LOCAL).transpose(2, 0, 1, 3).reshape(M, k_rows, 3 * LOCAL)
    text_send = text_weight.reshape(t_rows, 2, M, LOCAL).transpose(2, 0, 1, 3).reshape(M, t_rows, 2 * LOCAL)
    gate_up_send = gate_up_weight.reshape(k_rows, 2, sets, M, d_rows).transpose(1, 3, 0, 2, 4)
    gate_up_send = gate_up_send.reshape(2, M, k_rows, sets * d_rows)
    out_forth = [(o, (o % sets) * M + o // sets) for o in range(devices)]
    out_back = [(b, a) for a, b in out_forth]
    axes = ("items", "times", "ring")
    out_shard = lax.ppermute(out_weight, axes, out_forth)
    half = M // 2

    packages, silu_both, qkv_shard, text_shard, down_time = exchange(
        plan,
        "gather_small",
        [
            plan.gather_all(package),
            plan.swap_item(silu_own),
            plan.scatter_ring(qkv_send),
            plan.scatter_ring(text_send),
            plan.gather_time(down_weight),
        ],
    )
    packages = packages.reshape(devices, lines * 128)
    gains = packages[:, : 7 * gain_n].reshape(devices, 7, gain_n).transpose(1, 0, 2).reshape(7, D)
    bias = packages[:, 7 * gain_n : 7 * gain_n + bias_n].reshape(4 * D)
    counts_all = packages[:, 7 * gain_n + bias_n : package_n].astype(jnp.int32).reshape(GROUPS, rows_axis, FRAMES)
    counts = lax.dynamic_index_in_dim(counts_all, item, 0, keepdims=False)
    silu_slice = lax.dynamic_slice_in_dim(silu_both.reshape(GROUPS * FRAMES, COND), place * a_rows, a_rows, 1)

    partial = dot(silu_slice, ada_weight).reshape(GROUPS, FRAMES, rows_axis, part_n)
    partial = partial.transpose(0, 2, 1, 3).reshape(sets, M, FRAMES, part_n)
    parts, qkv_time_a, text_a, gate_shard, out_time = exchange(
        plan,
        "scatter_modulation",
        [
            plan.scatter_all(partial),
            plan.gather_time_part(qkv_shard, 0, half),
            plan.swap_item_part(text_shard, 0, half),
            plan.scatter_ring(gate_up_send[0]),
            plan.gather_time(out_shard),
        ],
    )
    own_part = jnp.sum(parts, axis=(0, 1))
    modulation, qkv_time_b, text_b, up_shard = exchange(
        plan,
        "gather_modulation",
        [
            plan.gather_group(own_part),
            plan.gather_time_part(qkv_shard, half, half),
            plan.swap_item_part(text_shard, half, half),
            plan.scatter_ring(gate_up_send[1]),
        ],
    )
    modulation = modulation.reshape(rows_axis, FRAMES, part_n).transpose(1, 0, 2).reshape(FRAMES, 4 * D) + bias

    line = jnp.arange(TOK, dtype=jnp.int32)[None, :]
    clip = counts[:, :1]
    before = jnp.cumsum(counts, axis=0) - counts
    frame_all = (line >= clip).astype(jnp.int32)
    position_all = jnp.where(frame_all == 0, before[:, :1] + line, before[:, 1:] + line - clip)
    frame_k = frame_all.reshape(-1)
    frame_q = lax.dynamic_slice_in_dim(frame_k, time * ROWS, ROWS)
    position_q = lax.dynamic_slice_in_dim(position_all.reshape(-1), time * ROWS, ROWS).astype(f32)
    frame_own = lax.dynamic_index_in_dim(frame_all, group_place, 0, keepdims=False)
    mod_rows = jnp.where(frame_own[:, None] == 0, modulation[0, :D][None], modulation[1, :D][None])
    scale_attn = mod_rows
    onehot = (frame_own[:, None] == jnp.arange(FRAMES, dtype=jnp.int32)[None, :]).astype(f32)
    text_line = jnp.arange(FRAMES * TEXT, dtype=jnp.int32)
    text_frame = text_line // TEXT
    text_live = text_line % TEXT < jnp.repeat(text_lengths[0], TEXT)

    inputs = latents[0]
    attn_in_float, attn_head_back = jax.vjp(attn_head, inputs, scale_attn, gains[0])
    attn_in = attn_in_float.astype(bf16)

    caption_rows = captions[0].reshape(FRAMES * TEXT, TEXT_DIM)
    width = half * t_rows
    own_captions = jnp.concatenate(
        [
            lax.dynamic_slice_in_dim(caption_rows, ((i * times + time) * 2 + h) * width, width, 1)
            for h in range(2)
            for i in range(GROUPS)
        ],
        axis=1,
    )
    text_full = jnp.concatenate(
        [text_a.reshape(GROUPS * width, 2 * LOCAL), text_b.reshape(GROUPS * width, 2 * LOCAL)], axis=0
    )
    text_partial = dot(own_captions, text_full).astype(bf16)
    attn_in_all, qkv_a, qkv_b, out_full, text_parts = exchange(
        plan,
        "gather_attn_in",
        [
            plan.gather_ring(attn_in),
            plan.swap_item(qkv_time_a),
            plan.swap_item(qkv_time_b),
            plan.swap_item(out_time),
            plan.gather_time(text_partial),
        ],
    )
    attn_in_all = attn_in_all.reshape(ROWS, D)
    qkv_full = jnp.concatenate([qkv_a, qkv_b], axis=2).reshape(D, 3 * LOCAL)
    qkv_full = dot(qkv_full, mix).astype(bf16)
    qkv_raw = dot(attn_in_all, qkv_full)
    text_raw = jnp.sum(text_parts.astype(f32), axis=0)
    q_raw, k_raw, v_raw = qkv_raw[:, :LOCAL], qkv_raw[:, LOCAL : 2 * LOCAL], qkv_raw[:, 2 * LOCAL :]
    tk_raw, tv_raw = text_raw[:, :LOCAL], text_raw[:, LOCAL:]

    squares = jnp.concatenate(
        [jnp.sum(q_raw * q_raw, axis=1), jnp.sum(k_raw * k_raw, axis=1), jnp.sum(tk_raw * tk_raw, axis=1)]
    ).reshape(-1, 128)
    (squares_all,) = exchange(plan, "gather_squares", [plan.direct_ring(squares)])
    out_full = jnp.pad(out_full.reshape(LOCAL, D), ((HEAD, 0), (0, 0)))
    inverse = lax.rsqrt(jnp.sum(squares_all, axis=0).reshape(-1) / D + epsilon)
    q_inv, k_inv, t_inv = inverse[:ROWS, None], inverse[ROWS : 2 * ROWS, None], inverse[2 * ROWS :, None]

    def own_gain(row):
        return lax.dynamic_slice_in_dim(gains[row], ring * LOCAL, LOCAL)

    def halves(vector):
        return vector.reshape(heads, HEAD // 2, 2).transpose(2, 0, 1).reshape(LOCAL)

    gain_q, gain_k, gain_t = own_gain(4), own_gain(5), own_gain(6)
    gain_q, gain_k = halves(gain_q), halves(gain_k)
    pair = jnp.arange(LOCAL // 2, dtype=jnp.int32) % (HEAD // 2)
    frequency = theta_base ** (-2.0 * pair.astype(f32) / HEAD)
    angle = position_q[:, None] * frequency[None, :]
    cos, sin = jnp.cos(angle), jnp.sin(angle)
    query = turn(q_raw * q_inv * gain_q, cos, sin).astype(bf16) * jnp.asarray(0.125, bf16)
    key = turn(k_raw * k_inv * gain_k, cos, sin).astype(bf16)
    text_key = ((tk_raw * t_inv) * gain_t).astype(bf16)
    text_key = dot(text_key, shuffle(order)).astype(bf16)
    text_value = tv_raw.astype(bf16)

    feature = jnp.arange(128, dtype=jnp.int32)[None, :]

    def key_features(apart_first, apart_second):
        ones = (feature >= HEAD + 2) & (feature < HEAD + 2 + 3 * heads)
        pick = jnp.where(feature == HEAD, apart_first[:, None], (feature == HEAD + 1) & apart_second[:, None])
        return jnp.where(pick | ones, 1.0, 0.0).astype(bf16)

    features = key_features(frame_k == 1, frame_k == 0)
    text_features = key_features(~((text_frame == 0) & text_live), ~((text_frame == 1) & text_live))
    lanes = jnp.arange(WIDE - LOCAL, dtype=jnp.int32)[None, :]
    query = jnp.concatenate(
        [query, jnp.where(lanes == frame_q[:, None], -APART, 0.0).astype(bf16)], axis=1
    )
    packed = jnp.concatenate([key, v_raw.astype(bf16)], axis=1)
    text_packed = jnp.concatenate([text_key, text_value], axis=1)
    own_gates = jnp.tanh(lax.dynamic_slice_in_dim(head_gates.astype(f32), ring * heads, heads))
    gates_v = jnp.concatenate([jnp.zeros((HEAD,), f32), jnp.repeat(own_gates, HEAD)]).reshape(1, WIDE)
    gates_q = jnp.concatenate(
        [jnp.tile(jnp.repeat(own_gates, HEAD // 2), 2), jnp.zeros((WIDE - LOCAL,), f32)]
    ).reshape(1, WIDE)

    mixed, self_out, cross_out, kv_all, (gate_time, down_full) = flash_forward(
        plan,
        query,
        packed,
        features,
        text_packed,
        text_features,
        gates_v,
        [plan.stack_time(gate_shard.reshape(M * k_rows, sets * d_rows)), plan.swap_item(down_time)],
    )
    down_full = down_full.reshape(sets * d_rows, D)
    first_rows = (frame_own == 0).astype(f32)[:, None]
    (result_rows, d_state, d_mixed, grad_out, gate_sum, up_sum, down_grad, ffn_sums) = feed_forward(
        plan,
        mixed,
        out_full,
        inputs,
        cotangent[0],
        modulation,
        gains,
        first_rows,
        gate_time,
        up_shard.reshape(M * k_rows, sets * d_rows),
        down_full,
        d_rows,
    )
    grad_out = grad_out[HEAD:]

    def add(parts):
        return jnp.sum(parts.astype(f32), axis=0)

    (dq, dk, dv, tdk, tdv, gate_sums), (gate_parts, out_parts) = flash_backward(
        plan,
        query,
        kv_all,
        features,
        text_packed,
        text_features,
        self_out,
        cross_out,
        d_mixed,
        gates_q,
        gates_v,
        [
            plan.split_time(gate_sum),
            plan.scatter_item(grad_out.reshape(GROUPS, times, o_rows, D)),
        ],
    )
    gate_sum = add(gate_parts).astype(bf16).reshape(M, k_rows, sets * d_rows)
    out_sum = add(out_parts).astype(bf16)
    gate_sums = jnp.sum(gate_sums[0, HEAD:].reshape(heads, HEAD), axis=1)
    dq, dk, dv, tdk, tdv = dq[:, :LOCAL], dk[:, :LOCAL], dv[:, HEAD:], tdk[:, :LOCAL], tdv[:, HEAD:]

    d_query = turn(dq, cos, -sin)
    d_key = turn(dk, cos, -sin)
    d_tk = dot(tdk.astype(bf16), shuffle(order), (1, 1))
    qn, kn, tn = q_raw * q_inv, k_raw * k_inv, tk_raw * t_inv
    d_gain_q, d_gain_k, d_gain_t = jnp.sum(d_query * qn, axis=0), jnp.sum(d_key * kn, axis=0), jnp.sum(d_tk * tn, axis=0)
    d_qn, d_kn, d_tn = d_query * gain_q, d_key * gain_k, d_tk * gain_t
    sums = jnp.concatenate(
        [jnp.sum(d_qn * qn, axis=1), jnp.sum(d_kn * kn, axis=1), jnp.sum(d_tn * tn, axis=1)]
    ).reshape(-1, 128)
    sums_all, out_parts = exchange(plan, "gather_sums", [plan.direct_ring(sums), plan.scatter_time(out_sum)])
    out_grad = lax.ppermute(add(out_parts), axes, out_back)
    means = jnp.sum(sums_all, axis=0).reshape(-1) / D
    q_mean, k_mean, t_mean = means[:ROWS, None], means[ROWS : 2 * ROWS, None], means[2 * ROWS :, None]
    d_qkv = jnp.concatenate(
        [(d_qn - qn * q_mean) * q_inv, (d_kn - kn * k_mean) * k_inv, dv], axis=1
    ).astype(bf16)
    d_text = jnp.concatenate([(d_tn - tn * t_mean) * t_inv, tdv], axis=1).astype(bf16)
    grad_qkv = dot(dot(attn_in_all, d_qkv, (0, 0)).astype(bf16), mix, (1, 1)).astype(bf16)
    grad_text = dot(own_captions, d_text, (0, 0)).astype(bf16)
    grad_text = grad_text.reshape(2, GROUPS, width, 2 * LOCAL).transpose(1, 0, 2, 3)
    grad_qkv = grad_qkv.reshape(GROUPS, times, 2, half * k_rows, 3 * LOCAL)
    d_attn_in, (qkv_parts_a, qkv_parts_b, text_parts, up_parts) = product_scatter(
        plan,
        "d_attn_in",
        [(d_qkv, qkv_full)],
        True,
        [
            plan.scatter_item(grad_qkv[:, :, 0]),
            plan.scatter_time(grad_qkv[:, :, 1].transpose(1, 0, 2, 3)),
            plan.scatter_item(grad_text),
            plan.split_time(up_sum),
        ],
    )
    qkv_sum_a = add(qkv_parts_a).astype(bf16)
    qkv_sum_b = add(qkv_parts_b).astype(bf16)
    text_sum = add(text_parts).astype(bf16).reshape(M, t_rows, 2 * LOCAL)
    up_sum = add(up_parts).astype(bf16).reshape(M, k_rows, sets * d_rows)
    d_inputs_head, d_scale_attn, d_gain_one = attn_head_back(d_attn_in)
    grad_latent = d_state + d_inputs_head

    d_mod = jnp.concatenate(
        [jnp.einsum("tf,td->fd", onehot, d_scale_attn, precision=highest), ffn_sums[3:5], ffn_sums[5:7], ffn_sums[7:9]], axis=1
    )
    d_mod = d_mod.reshape(FRAMES, rows_axis, part_n).transpose(1, 0, 2).reshape(times, M, FRAMES, part_n)

    def spread(vector):
        return lax.dynamic_update_slice_in_dim(jnp.zeros((D,), f32), vector, ring * LOCAL, 0)

    def unhalve(vector):
        return vector.reshape(2, heads, HEAD // 2).transpose(1, 2, 0).reshape(LOCAL)

    first = (time == 0).astype(f32)
    d_gains = jnp.stack(
        [
            d_gain_one,
            ffn_sums[0],
            ffn_sums[1],
            ffn_sums[2],
            spread(unhalve(d_gain_q)),
            spread(unhalve(d_gain_k)),
            spread(d_gain_t * first),
            jnp.zeros((D,), f32),
        ]
    )
    d_gains = d_gains.reshape(8, devices, gain_n).transpose(1, 0, 2).reshape(sets, M, 8, gain_n)
    gate_row = lax.dynamic_update_slice_in_dim(
        jnp.zeros((HEADS,), f32), gate_sums * (1.0 - own_gates * own_gates), ring * heads, 0
    )
    gate_row = jnp.pad(gate_row, (0, 128 - HEADS)).reshape(1, 128)
    d_mod_parts, d_gain_parts, gate_rows, qkv_parts_a, qkv_parts_b, text_pieces, gate_pieces, up_pieces = exchange(
        plan,
        "scatter_grads",
        [
            plan.scatter_group(d_mod),
            plan.scatter_all(d_gains),
            plan.gather_all(gate_row),
            plan.scatter_time(qkv_sum_a),
            plan.scatter_item(qkv_sum_b),
            plan.scatter_ring(text_sum),
            plan.scatter_ring(gate_sum),
            plan.scatter_ring(up_sum),
        ],
    )
    gains_grad = jnp.sum(d_gain_parts, axis=(0, 1))[:7]
    gates_grad = jnp.sum(gate_rows, axis=(0, 1, 2))[:HEADS]
    text_grad = text_pieces.reshape(M, t_rows, 2, LOCAL).transpose(1, 2, 0, 3).reshape(t_rows, 2 * D).astype(f32)
    gate_up_grad = jnp.stack([gate_pieces, up_pieces]).reshape(2, M, k_rows, sets, d_rows)
    gate_up_grad = gate_up_grad.transpose(2, 0, 3, 1, 4).reshape(k_rows, 2 * FF).astype(f32)
    qkv_sum = jnp.concatenate([add(qkv_parts_a), add(qkv_parts_b)], axis=0).astype(bf16)
    d_mod_all, qkv_pieces = exchange(
        plan,
        "gather_d_mod",
        [
            plan.gather_all(jnp.sum(d_mod_parts, axis=(0, 1))),
            plan.scatter_ring(qkv_sum.reshape(M, k_rows, 3 * LOCAL)),
        ],
    )
    qkv_grad = qkv_pieces.reshape(M, k_rows, 3, LOCAL).transpose(1, 2, 0, 3).reshape(k_rows, 3 * D).astype(f32)
    d_mod_all = (
        d_mod_all.reshape(GROUPS, rows_axis, FRAMES, part_n).transpose(0, 2, 1, 3).reshape(GROUPS * FRAMES, 4 * D)
    )
    ada_grad = jnp.einsum("fc,fd->cd", silu_slice.astype(f32), d_mod_all, precision=highest)
    bias_grad = lax.dynamic_slice_in_dim(jnp.sum(d_mod_all, axis=0), place * bias_n, bias_n)
    return (
        result_rows[None],
        grad_latent[None],
        qkv_grad,
        text_grad,
        out_grad,
        gate_up_grad,
        down_grad,
        ada_grad,
        bias_grad,
        gains_grad,
        gates_grad,
    )


def solution(mesh):
    items, rows = mesh.shape["items"], mesh.shape["rows"]
    fine = Mesh(mesh.devices.reshape(items, rows // M, M), ("items", "times", "ring"))
    whole = ("items", "times", "ring")
    rows_of = ("times", "ring")
    return jax.shard_map(
        shards,
        mesh=fine,
        in_specs=(
            P("items", rows_of, None),
            P("items", None, None),
            P("items", None, None, None),
            P("items", rows_of, None),
            P("items", None),
            P(whole, None),
            P(whole, None),
            P(whole, None),
            P(whole, None),
            P(whole, None),
            P(whole, None),
            P(whole),
            P(None, whole),
            P(),
            P("items", rows_of, None),
        ),
        out_specs=(
            P("items", rows_of, None),
            P("items", rows_of, None),
            P(whole, None),
            P(whole, None),
            P(whole, None),
            P(whole, None),
            P(whole, None),
            P(whole, None),
            P(whole),
            P(None, whole),
            P(),
        ),
        check_vma=False,
    )
```

```python
import jax
import jax.numpy as jnp
import numpy as np
from jax import lax
from jax.experimental import pallas as pl
from jax.experimental.pallas import tpu as pltpu
from jax.sharding import Mesh
from jax.sharding import PartitionSpec as P

D = 1536
HEADS = 24
HEAD = 64
FF = 4096
TEXT_DIM = 4096
COND = 1024
TEXT = 256
FRAMES = 2
TOK = 128
GROUPS = 2
M = 8
LOCAL = HEADS // M * HEAD
ROWS = M * TOK
WIDE = 256
SPARE = 96
APART = 8192.0

epsilon = 1e-05
theta_base = 10000.0
highest = lax.Precision.HIGHEST
MESH = pl.DeviceIdType.MESH
f32 = jnp.float32
bf16 = jnp.bfloat16
ANY = pl.BlockSpec(memory_space=pl.ANY)
VMEM = pl.BlockSpec(memory_space=pltpu.VMEM)


def flip(where, mask):
    return tuple(a if b == 0 else a ^ b for a, b in zip(where, mask))


class Job:
    def __init__(self, x, shape, masks, src, dst, pass_on=(), by=None, source=None, piece=None):
        self.x, self.shape, self.masks, self.src, self.dst = x, shape, masks, src, dst
        self.piece = piece
        self.pass_on, self.by, self.source = tuple(pass_on), by, source
        if source is not None:
            self.x = None
        self.dtype = x.dtype

    def count(self):
        return len(self.masks) + len(self.pass_on)

    def block(self):
        return self.piece or self.shape[len(self.dst((0, 0, 0))) :]

    def peers(self):
        return set(self.masks) | ({self.by} if self.pass_on else set())


class Transfers:
    def __init__(self, jobs):
        self.jobs = jobs
        self.sent = [j for j in jobs if j.source is None]
        self.total = sum(j.count() for j in jobs)

    def operands(self):
        return [j.x for j in self.sent]

    def out_shapes(self):
        return [jax.ShapeDtypeStruct(j.shape, j.dtype) for j in self.jobs]

    def scratch(self):
        if not self.jobs:
            return []
        return [
            pltpu.SemaphoreType.DMA((self.total,)),
            pltpu.SemaphoreType.DMA((self.total,)),
            pltpu.SemaphoreType.DMA((2, len(self.jobs))),
        ] + [pltpu.VMEM(j.block(), j.dtype) for j in self.jobs]

    def peers(self):
        found = set()
        for j in self.jobs:
            found |= j.peers()
        return found

    def bind(self, me, ins, outs, sems):
        self.me, self.outs, self.sems = me, outs, sems
        left = list(ins)
        self.ins = []
        for j in self.jobs:
            self.ins.append(left.pop(0) if j.source is None else outs[self.jobs.index(j.source)])
        self.base, at = [], 0
        for j in self.jobs:
            self.base.append(at)
            at += j.count()
        self.arrived, self.kept, self.settled, self.chained, self.forwarded = set(), set(), set(), set(), set()

    def remote(self, src, dst, slot, dest):
        return pltpu.make_async_remote_copy(
            src_ref=src,
            dst_ref=dst,
            send_sem=self.sems[0].at[slot],
            recv_sem=self.sems[1].at[slot],
            device_id=dest,
            device_id_type=MESH,
        )

    def send(self, k, i):
        j = self.jobs[k]
        if i < len(j.masks):
            dest = flip(self.me, j.masks[i])
            at = j.src(dest)
            src = self.ins[k] if at is None else self.ins[k].at[at]
            return self.remote(src, self.outs[k].at[j.dst(self.me)], self.base[k] + i, dest)
        mask = j.pass_on[i - len(j.masks)]
        block = self.outs[k].at[j.dst(flip(self.me, mask))]
        return self.remote(block, block, self.base[k] + i, flip(self.me, j.by))

    def own(self, k, leg):
        j = self.jobs[k]
        room = self.sems[3 + k]
        if leg == 0:
            at = j.src(self.me)
            src = self.ins[k] if at is None else self.ins[k].at[at]
            return pltpu.make_async_copy(src, room, self.sems[2].at[0, k])
        return pltpu.make_async_copy(room, self.outs[k].at[j.dst(self.me)], self.sems[2].at[1, k])

    def start_job(self, k):
        j = self.jobs[k]
        for i in range(len(j.masks)):
            self.send(k, i).start()
        self.own(k, 0).start()

    def start(self, late=()):
        for k, j in enumerate(self.jobs):
            if j.source is None and k not in late:
                self.start_job(k)

    def receive(self, k, i):
        if (k, i) not in self.arrived:
            self.arrived.add((k, i))
            self.send(k, i).wait_recv()

    def take(self, k):
        self.keep(k)
        for i in range(self.jobs[k].count()):
            self.receive(k, i)
        if k not in self.settled:
            self.settled.add(k)
            self.own(k, 1).wait()

    def keep(self, k):
        if k not in self.kept:
            self.kept.add(k)
            self.own(k, 0).wait()
            self.own(k, 1).start()

    def chain(self, late=()):
        for k, j in enumerate(self.jobs):
            if j.source is not None and k not in self.chained and k not in late:
                self.chained.add(k)
                self.take(self.jobs.index(j.source))
                self.start_job(k)

    def forward(self):
        self.chain()
        for k in range(len(self.jobs)):
            self.keep(k)
        for k, j in enumerate(self.jobs):
            if k not in self.forwarded:
                self.forwarded.add(k)
                for n, mask in enumerate(j.pass_on):
                    self.receive(k, j.masks.index(mask))
                    self.send(k, len(j.masks) + n).start()

    def finish(self):
        self.forward()
        for k, j in enumerate(self.jobs):
            self.take(k)
            for i in range(j.count()):
                self.send(k, i).wait_send()


class Plan:
    def __init__(self, times):
        self.times = times
        self.sets = GROUPS * times
        self.rows = times * M
        self.next_id = 0
        ones = [(i, t, m) for i in range(GROUPS) for t in range(times) for m in range(M)]
        self.all = ones[1:]
        self.ring = [(0, 0, m) for m in range(1, M)]
        self.chips = [(0, 0, m) for m in range(2, M, 2)]
        self.mate = (0, 0, 1)
        self.time = [(0, t, 0) for t in range(1, times)]
        self.item = (1, 0, 0)
        self.span = [(i, t, 0) for i in range(GROUPS) for t in range(times)][1:]
        self.group = [(0, t, m) for t in range(times) for m in range(M)][1:]

    def identity(self):
        self.next_id += 1
        return self.next_id

    def set_of(self, where):
        return where[0] * self.times + where[1]

    def gather_ring(self, x):
        return Job(
            x,
            (M,) + x.shape,
            [self.mate] + self.chips,
            lambda dest: None,
            lambda sender: (sender[2],),
            self.chips,
            self.mate,
        )

    def direct_ring(self, x):
        return Job(x, (M,) + x.shape, self.ring, lambda dest: None, lambda sender: (sender[2],))

    def scatter_ring(self, x):
        return Job(x, x.shape, self.ring, lambda dest: (dest[2],), lambda sender: (sender[2],))

    def gather_span(self, x, shape=None, source=None):
        return Job(
            x,
            (self.sets,) + (x.shape if shape is None else shape),
            [self.item] + self.time,
            lambda dest: None,
            lambda sender: (self.set_of(sender),),
            self.time,
            self.item,
            source,
        )

    def scatter_span(self, x):
        return Job(x, x.shape, self.span, lambda dest: (self.set_of(dest),), lambda sender: (self.set_of(sender),))

    def gather_time(self, x):
        return Job(x, (self.times,) + x.shape, self.time, lambda dest: None, lambda sender: (sender[1],))

    def stack_time(self, x):
        n = x.shape[0]
        return Job(
            x,
            (self.times * n,) + x.shape[1:],
            self.time,
            lambda dest: None,
            lambda sender: (pl.ds(pl.multiple_of(sender[1] * n, n), n),),
            piece=x.shape,
        )

    def stack_item(self, x, source=None):
        shape = x.shape if source is None else source.shape
        n = shape[0]
        return Job(
            x,
            (GROUPS * n,) + shape[1:],
            [self.item],
            lambda dest: None,
            lambda sender: (pl.ds(pl.multiple_of(sender[0] * n, n), n),),
            source=source,
            piece=shape,
        )

    def split_time(self, x):
        n = x.shape[0] // self.times
        return Job(
            x,
            (self.times, n) + x.shape[1:],
            self.time,
            lambda dest: (pl.ds(pl.multiple_of(dest[1] * n, n), n),),
            lambda sender: (sender[1],),
        )

    def scatter_group_ring(self, x):
        return Job(
            x,
            (self.times,) + x.shape,
            self.group,
            lambda dest: (dest[2],),
            lambda sender: (sender[1], sender[2]),
        )

    def swap_source(self, source):
        return Job(
            source.x if source.x is not None else source,
            (GROUPS,) + source.shape,
            [self.item],
            lambda dest: None,
            lambda sender: (sender[0],),
            source=source,
        )

    def gather_time_source(self, source):
        return Job(
            source,
            (self.times,) + source.shape,
            self.time,
            lambda dest: None,
            lambda sender: (sender[1],),
            source=source,
        )

    def ring_of_times(self, x, source=None):
        shape = x.shape if source is None else source.shape
        return Job(
            x if source is None else source,
            (M, shape[0]) + tuple(shape[2:]),
            self.ring,
            lambda dest: (slice(None), dest[2]),
            lambda sender: (sender[2],),
            source=source,
        )

    def times_of_ring(self, source):
        shape = source.shape
        return Job(
            source,
            (shape[1], shape[0]) + tuple(shape[2:]),
            self.time,
            lambda dest: (slice(None), dest[1]),
            lambda sender: (sender[1],),
            source=source,
        )

    def scatter_time(self, x):
        return Job(x, x.shape, self.time, lambda dest: (dest[1],), lambda sender: (sender[1],))

    def scatter_item(self, x):
        return Job(x, x.shape, [self.item], lambda dest: (dest[0],), lambda sender: (sender[0],))

    def gather_all(self, x):
        return Job(
            x,
            (self.sets, M) + x.shape,
            self.all,
            lambda dest: None,
            lambda sender: (self.set_of(sender), sender[2]),
        )

    def scatter_all(self, x):
        return Job(
            x,
            x.shape,
            self.all,
            lambda dest: (self.set_of(dest), dest[2]),
            lambda sender: (self.set_of(sender), sender[2]),
        )

    def swap_item(self, x):
        return Job(x, (GROUPS,) + x.shape, [self.item], lambda dest: None, lambda sender: (sender[0],))

    def gather_group(self, x):
        return Job(
            x,
            (self.times, M) + x.shape,
            self.group,
            lambda dest: None,
            lambda sender: (sender[1], sender[2]),
        )

    def scatter_group(self, x):
        return Job(
            x,
            x.shape,
            self.group,
            lambda dest: (dest[1], dest[2]),
            lambda sender: (sender[1], sender[2]),
        )


def here():
    return (lax.axis_index("items"), lax.axis_index("times"), lax.axis_index("ring"))


def greet(me, peers):
    barrier = pltpu.get_barrier_semaphore()
    for mask in sorted(peers):
        pl.semaphore_signal(barrier, inc=1, device_id=flip(me, mask), device_id_type=MESH)
    pl.semaphore_wait(barrier, len(peers))


def exchange(plan, name, jobs):
    moves = Transfers(jobs)
    n_in, n_out = len(moves.sent), len(jobs)

    def kernel(*refs):
        me = here()
        greet(me, moves.peers())
        moves.bind(me, refs[:n_in], refs[n_in : n_in + n_out], refs[n_in + n_out :])
        moves.start()
        moves.finish()

    return pl.pallas_call(
        kernel,
        out_shape=moves.out_shapes(),
        in_specs=[ANY] * n_in,
        out_specs=[ANY] * n_out,
        scratch_shapes=moves.scratch(),
        name=name,
        compiler_params=pltpu.CompilerParams(
            collective_id=plan.identity(), has_side_effects=True, vmem_limit_bytes=32 * 2**20
        ),
    )(*moves.operands())


def lane_masks():
    lane = np.arange(WIDE)
    query, value = np.zeros((8, WIDE), np.float32), np.zeros((8, WIDE), np.float32)
    back = np.zeros((8, WIDE), np.float32)
    inner = lane % 128
    for h in range(LOCAL // HEAD):
        query[h] = ((inner < SPARE) & (inner // (HEAD // 2) == h)) | (lane == 128 + SPARE) | (lane == 129 + SPARE)
        query[h] += (lane >= 130 + SPARE + 3 * h) & (lane < 133 + SPARE + 3 * h)
        value[h] = ((lane >= HEAD) & (lane // HEAD - 1 == h)) | (lane // 16 == h)
        back[h] = ((lane >= HEAD) & (lane // HEAD - 1 == h)) | (lane == 2 * h) | (lane == 2 * h + 1)
    return query, value, back


def wide_order():
    col = np.arange(LOCAL)
    head, pair, odd = col // HEAD, col % HEAD // 2, col % 2
    return odd * 128 + head * (HEAD // 2) + pair, HEAD + col


def placing(places, width):
    return (jnp.asarray(places, jnp.int32)[:, None] == jnp.arange(width, dtype=jnp.int32)[None, :]).astype(bf16)


def widen(packed_ref, feature, key_ref, value_ref, rows):
    lane = lax.broadcasted_iota(jnp.int32, (rows, 128), 1)
    first, second = packed_ref[:, :128].astype(f32), packed_ref[:, 128:256].astype(f32)
    key_ref[:rows, :128] = jnp.where(lane < SPARE, first, 0.0).astype(bf16)
    key_ref[:rows, 128:] = jnp.where(lane < SPARE, second, feature.astype(f32)).astype(bf16)
    moved = jnp.where(lane < SPARE, pltpu.roll(first, 96, 1), second)
    value_ref[:rows, :128] = jnp.where(lane < HEAD, 1.0, moved).astype(bf16)
    value_ref[:rows, 128:] = packed_ref[:, 256:]


def pack(key_first, key_second, value_first, value_second, packed_ref, rows):
    lane = lax.broadcasted_iota(jnp.int32, (rows, 128), 1)
    packed_ref[:, :128] = jnp.where(lane < SPARE, key_first, pltpu.roll(value_first, 32, 1)).astype(bf16)
    packed_ref[:, 128:256] = jnp.where(lane < SPARE, key_second, value_first).astype(bf16)
    packed_ref[:, 256:] = value_second.astype(bf16)


def unpack(packed, rows):
    lane = lax.broadcasted_iota(jnp.int32, (rows, 128), 1)
    first, second = packed[:, :128].astype(f32), packed[:, 128:256].astype(f32)
    moved = jnp.where(lane < SPARE, pltpu.roll(first, 96, 1), second)
    return (
        jnp.where(lane < SPARE, first, 0.0),
        jnp.where(lane < SPARE, second, 0.0),
        jnp.where(lane < HEAD, 0.0, moved),
        packed[:, 256:].astype(f32),
    )


def fold_rows(values):
    ones = jnp.ones((8, WIDE), f32)
    sums = lax.dot_general(ones, values, (((1,), (1,)), ((), ())), precision=highest, preferred_element_type=f32)
    return jnp.concatenate([sums[0:1, 128 * i : 128 * (i + 1)] for i in range(values.shape[0] // 128)], axis=0)


def spread_rows(folded, out_ref):
    n = folded.shape[0]
    row = lax.broadcasted_iota(jnp.int32, (n, 128), 0)
    ones = jnp.ones((n, 128), f32)
    for i in range(n):
        out_ref[128 * i : 128 * (i + 1), :] = lax.dot_general(
            jnp.where(row == i, folded, 0.0),
            ones,
            (((0,), (0,)), ((), ())),
            precision=highest,
            preferred_element_type=f32,
        )


class Links:
    def __init__(self, me, send_sem, recv_sem):
        self.me, self.send_sem, self.recv_sem, self.used = me, send_sem, recv_sem, 0

    def __call__(self, src, dst, mask):
        slot = self.used
        self.used += 1
        return pltpu.make_async_remote_copy(
            src_ref=src,
            dst_ref=dst,
            send_sem=self.send_sem.at[slot],
            recv_sem=self.recv_sem.at[slot],
            device_id=flip(self.me, mask),
            device_id_type=MESH,
        )


def rows_at(index, count):
    return pl.ds(pl.multiple_of(index * count, count), count)


def ring_sum(plan, link, me, buffers, product, meanwhile=lambda: None):
    to_mate, from_mate, to_chip, from_chip, part = buffers
    core, chip = me[2] % 2, me[2] // 2
    mates = [link(to_mate.at[d], from_mate.at[d], plan.mate) for d in range(4)]
    chips = [link(to_chip.at[d - 1], from_chip.at[d - 1], (0, 0, 2 * d)) for d in (1, 2, 3)]
    for d in (3, 2, 1, 0):
        to_mate[d] = product((chip ^ d) * 2 + 1 - core).astype(bf16)
        mates[d].start()
    for d in (3, 2, 1):
        part[...] = product((chip ^ d) * 2 + core)
        mates[d].wait_recv()
        to_chip[d - 1] = (part[...] + from_mate[d].astype(f32)).astype(bf16)
        chips[d - 1].start()
    part[...] = product(chip * 2 + core)
    mates[0].wait_recv()
    part[...] = part[...] + from_mate[0].astype(f32)
    meanwhile()
    for copy in chips:
        copy.wait_recv()
    part[...] = part[...] + (from_chip[0].astype(f32) + from_chip[1].astype(f32) + from_chip[2].astype(f32))
    for copy in mates + chips:
        copy.wait_send()


def ring_gather(plan, link, me, all_ref, each, meanwhile=lambda: None):
    ring = me[2]
    chip = ring // 2
    own = all_ref.at[rows_at(ring, TOK)]
    first = [link(own, own, plan.mate)] + [link(own, own, (0, 0, 2 * d)) for d in (1, 2, 3)]
    for copy in first[1:] + first[:1]:
        copy.start()
    meanwhile()
    first[0].wait_recv()
    each(chip)
    later = []
    for d in (1, 2, 3):
        first[d].wait_recv()
        block = all_ref.at[rows_at(ring ^ (2 * d), TOK)]
        copy = link(block, block, plan.mate)
        copy.start()
        later.append(copy)
    for d in (1, 2, 3):
        later[d - 1].wait_recv()
        each(chip ^ d)
    for copy in first + later:
        copy.wait_send()


def ring_share(plan, link, all_ref):
    copies = [link(all_ref.at[0], all_ref.at[i + 1], mask) for i, mask in enumerate(plan.ring)]
    for copy in copies:
        copy.start()
    return copies


def scale_of(values):
    return lax.rsqrt(jnp.mean(values * values, axis=1, keepdims=True) + epsilon)


def norm_back(d_hat, hat, inverse):
    return inverse * (d_hat - hat * jnp.mean(d_hat * hat, axis=1, keepdims=True))


RING_BUFFERS = [
    pltpu.VMEM((4, TOK, D), bf16),
    pltpu.VMEM((4, TOK, D), bf16),
    pltpu.VMEM((3, TOK, D), bf16),
    pltpu.VMEM((3, TOK, D), bf16),
    pltpu.VMEM((TOK, D), f32),
]


def params(plan, megabytes):
    return pltpu.CompilerParams(
        collective_id=plan.identity(), has_side_effects=True, vmem_limit_bytes=megabytes * 2**20
    )


def prologue(plan, tiles, package, cond, ada_weight, jobs):
    moves = Transfers([plan.gather_all(package)] + list(jobs))
    n_in, n_out = len(moves.sent), len(moves.jobs)
    total_tiles = 4 * D // 128
    peers, group = plan.all, plan.group

    def kernel(*refs):
        cond_ref, ada_ref = refs[:2]
        ins = refs[2 : 2 + n_in]
        mod_ref, cond_out = refs[2 + n_in : 4 + n_in]
        outs = refs[4 + n_in : 4 + n_in + n_out]
        refs = refs[4 + n_in + n_out :]
        cond_in, part_ref, send_ref, recv_ref, sum_ref, mod_in, send_sem, recv_sem = refs[:8]
        me = here()
        greet(me, moves.peers() | set(peers))
        link = Links(me, send_sem, recv_sem)
        swap = link(cond_ref.at[1], cond_in, plan.item)
        swap.start()
        moves.bind(me, ins, outs, refs[8:])
        moves.start()
        deep = ada_ref.shape[0]
        part_ref[0] = jnp.dot(cond_ref[0][:, :deep].astype(bf16), ada_ref[...], preferred_element_type=f32)
        swap.wait_recv()
        cond_out[...] = cond_in[...]
        part_ref[1] = jnp.dot(cond_in[:, :deep].astype(bf16), ada_ref[...], preferred_element_type=f32)
        for g in range(GROUPS):
            for r in range(plan.rows):
                for f in range(FRAMES):
                    for j in range(tiles):
                        tile = r * tiles + j
                        at = f * tiles + j
                        if tile < total_tiles:
                            send_ref[g, r, at : at + 1, :] = part_ref[g, f : f + 1, 128 * tile : 128 * (tile + 1)]
        copies = []
        for i, mask in enumerate(peers):
            dest = flip(me, mask)
            copies.append(link(send_ref.at[mask[0], dest[1] * M + dest[2]], recv_ref.at[i], mask))
            copies[-1].start()
        place = me[1] * M + me[2]
        total = send_ref[0, place]
        for i, copy in enumerate(copies):
            copy.wait_recv()
            total = total + recv_ref[i]
        sum_ref[...] = total
        mod_in[place] = total
        shares = [link(sum_ref, mod_in.at[place], mask) for mask in group]
        for copy in shares:
            copy.start()
        moves.forward()
        for copy in shares:
            copy.wait_recv()
        mod_ref[...] = mod_in[...]
        for copy in [swap] + copies + shares:
            copy.wait_send()
        moves.finish()

    links = 1 + len(peers) + len(group)
    result = pl.pallas_call(
        kernel,
        out_shape=[jax.ShapeDtypeStruct((plan.rows, 8, 128), f32), jax.ShapeDtypeStruct((8, 128), f32)]
        + moves.out_shapes(),
        in_specs=[VMEM] * 2 + [ANY] * n_in,
        out_specs=[VMEM] * 2 + [ANY] * n_out,
        scratch_shapes=[
            pltpu.VMEM((8, 128), f32),
            pltpu.VMEM((GROUPS, 8, 4 * D), f32),
            pltpu.VMEM((GROUPS, plan.rows, 8, 128), f32),
            pltpu.VMEM((len(peers), 8, 128), f32),
            pltpu.VMEM((8, 128), f32),
            pltpu.VMEM((plan.rows, 8, 128), f32),
            pltpu.SemaphoreType.DMA((links,)),
            pltpu.SemaphoreType.DMA((links,)),
        ]
        + moves.scratch(),
        name="prologue",
        compiler_params=params(plan, 40),
    )(cond, ada_weight, *moves.operands())
    return result[0], result[1], result[2:]


def attention_forward(
    plan,
    latents,
    modulation,
    gains,
    first_rows,
    captions,
    text_weight,
    mix,
    text_mix,
    gain_wide,
    cos,
    sin,
    query_features,
    features,
    text_features,
    gates,
    qkv_time,
    out_shard,
    gate_send,
    up_send,
):
    heads = LOCAL // HEAD
    text_rows = captions.shape[0]
    text_deep = text_weight.shape[0]
    others = len(plan.time)
    out_job = plan.gather_time(out_shard)
    gate_job = plan.scatter_ring(gate_send)
    jobs = [
        plan.stack_item(qkv_time),
        out_job,
        plan.swap_source(out_job),
        gate_job,
        plan.scatter_ring(up_send),
        plan.gather_time_source(gate_job),
    ]
    moves = Transfers(jobs)
    n_in, n_out = len(moves.sent), len(moves.jobs)
    block = 256
    chip_rows = 2 * TOK
    span = text_deep // GROUPS
    folded = 2 * ROWS // 128 + text_rows // 128
    folded_rows = -(-folded // 8) * 8

    def kernel(*refs):
        (latent_ref, mod_ref, gain_ref, first_ref, caption_ref, text_w, mix_ref, text_mix_ref) = refs[:8]
        (wide_ref, cos_ref, sin_ref, qfeature_ref, feature_ref, text_feature_ref, gate_ref, qmask_ref, vmask_ref) = refs[8:17]
        ins = refs[17 : 17 + n_in]
        refs = refs[17 + n_in :]
        (mixed_ref, self_ref, cross_ref, attn_all, query_ref, packed_out, text_packed) = refs[:7]
        (qn_ref, kn_ref, qinv_ref, kinv_ref, tn_ref, tinv_ref) = refs[7:13]
        outs = refs[13 : 13 + n_out]
        refs = refs[13 + n_out :]
        (key_ref, value_ref, packed_ref, far_ref, max_ref, raw_w, weight_ref, raw_ref, own_caps, text_part, text_far) = refs[:11]
        (text_raw, sums_ref, send_sem, recv_sem, local_sem) = refs[11:16]
        me = here()
        item, time, ring = me
        greet(me, moves.peers() | {plan.mate} | set(plan.chips) | set(plan.ring) | set(plan.time))
        link = Links(me, send_sem, recv_sem)
        moves.bind(me, ins, outs, refs[16:])
        loads = []
        for i in range(GROUPS):
            where = pl.ds(pl.multiple_of((i * plan.times + time) * span, span), span)
            loads.append(
                pltpu.make_async_copy(caption_ref.at[:, where], own_caps.at[:, i * span : (i + 1) * span], local_sem.at[i])
            )
            loads[-1].start()

        is_first = first_ref[...] > 0.5
        scale = jnp.where(is_first, mod_ref[0:1, :D], mod_ref[1:2, :D])
        rows = latent_ref[...]
        attn_in = rows * scale_of(rows) * gain_ref[0:1, :] * (1.0 + scale)
        attn_all[rows_at(ring, TOK), :] = attn_in.astype(bf16)

        text_copies = [link(text_part, text_far.at[i], mask) for i, mask in enumerate(plan.time)]

        def text_projection():
            moves.start(late=(3, 4))
            for copy in loads:
                copy.wait()
            text_wide = jnp.dot(text_w[...], text_mix_ref[...], preferred_element_type=f32).astype(bf16)
            text_part[...] = jnp.dot(own_caps[...], text_wide, preferred_element_type=f32).astype(bf16)
            for copy in text_copies:
                copy.start()
            moves.take(0)
            copy = pltpu.make_async_copy(outs[0], raw_w, local_sem.at[0])
            copy.start()
            copy.wait()
            weight_ref[...] = jnp.dot(raw_w[...], mix_ref[...], preferred_element_type=f32).astype(bf16)

        def project(which):
            where = rows_at(which, chip_rows)
            raw_ref[where, :] = jnp.dot(attn_all[where, :], weight_ref[...], preferred_element_type=f32)

        ring_gather(plan, link, me, attn_all, project, text_projection)
        moves.start_job(3)
        moves.start_job(4)
        moves.chain(late=(5,))

        total = text_part[...].astype(f32)
        for i, copy in enumerate(text_copies):
            copy.wait_recv()
            total = total + text_far[i].astype(f32)
        text_raw[...] = total
        q_raw, k_raw, t_raw = raw_ref[:, :WIDE], raw_ref[:, WIDE : 2 * WIDE], total[:, :WIDE]
        squares = [fold_rows(q_raw * q_raw), fold_rows(k_raw * k_raw), fold_rows(t_raw * t_raw)]
        if folded_rows > folded:
            squares.append(jnp.zeros((folded_rows - folded, 128), f32))
        sums_ref[0] = jnp.concatenate(squares, axis=0)
        shares = ring_share(plan, link, sums_ref)
        for copy in shares:
            copy.wait_recv()
        total = sums_ref[0]
        for i in range(1, M):
            total = total + sums_ref[i]
        inverse = lax.rsqrt(total / D + epsilon)
        n = ROWS // 128
        spread_rows(inverse[:n], qinv_ref)
        spread_rows(inverse[n : 2 * n], kinv_ref)
        spread_rows(inverse[2 * n : folded], tinv_ref)

        def turn(where, at, inv_ref, n_ref, gain_row):
            first = raw_ref[where, at : at + 128] * inv_ref[where, :]
            second = raw_ref[where, at + 128 : at + 256] * inv_ref[where, :]
            n_ref[where, :128], n_ref[where, 128:] = first, second
            first = first * wide_ref[gain_row : gain_row + 1, :128]
            second = second * wide_ref[gain_row : gain_row + 1, 128:]
            cosine, sine = cos_ref[where, :], sin_ref[where, :]
            return first * cosine - second * sine, second * cosine + first * sine

        def shape(at, carry):
            where = rows_at(at, block)
            first, second = turn(where, 0, qinv_ref, qn_ref, 0)
            query_ref[where, :128] = (first.astype(bf16).astype(f32) * 0.125).astype(bf16)
            lane = lax.broadcasted_iota(jnp.int32, (block, 128), 1)
            second = jnp.where(lane < SPARE, second.astype(bf16).astype(f32) * 0.125, qfeature_ref[where, :].astype(f32))
            query_ref[where, 128:] = second.astype(bf16)
            first, second = turn(where, WIDE, kinv_ref, kn_ref, 1)
            values = raw_ref[where, 2 * WIDE :]
            pack(first, second, values[:, :128], values[:, 128:], packed_ref.at[where, :], block)
            return carry

        lax.fori_loop(0, ROWS // block, shape, 0)
        key_copies = [link(packed_ref, far_ref.at[i], mask) for i, mask in enumerate(plan.time)]
        for copy in key_copies:
            copy.start()
        first = text_raw[:, :128] * tinv_ref[...]
        second = text_raw[:, 128:256] * tinv_ref[...]
        tn_ref[:, :128], tn_ref[:, 128:] = first, second
        pack(
            first * wide_ref[2:3, :128],
            second * wide_ref[2:3, 128:],
            text_raw[:, 256:384],
            text_raw[:, 384:],
            text_packed,
            text_rows,
        )

        def segment(rows, first, out_ref):
            def body(at, carry):
                where = rows_at(at, block)
                query_rows = query_ref[where, :]
                total = jnp.zeros((block, WIDE), f32)
                tops = jnp.zeros((block, WIDE), f32)
                for h in range(heads):
                    own_query = query_rows * qmask_ref[h : h + 1, :]
                    scores = lax.dot_general(
                        own_query, key_ref[:rows, :], (((1,), (1,)), ((), ())), preferred_element_type=f32
                    )
                    top = jnp.max(scores, axis=1, keepdims=True)
                    weights = jnp.exp(scores - top).astype(bf16)
                    product = jnp.dot(weights, value_ref[:rows, :], preferred_element_type=f32)
                    total += product * vmask_ref[h : h + 1, :]
                    tops += top * vmask_ref[h : h + 1, :]
                if first:
                    out_ref[where, :] = total
                    max_ref[where, :] = tops
                else:
                    before = max_ref[where, :]
                    after = jnp.maximum(before, tops)
                    out_ref[where, :] = out_ref[where, :] * jnp.exp(before - after) + total * jnp.exp(tops - after)
                    max_ref[where, :] = after
                return carry

            lax.fori_loop(0, ROWS // block, body, 0)

        def close(out_ref):
            def body(at, carry):
                where = rows_at(at, block)
                lane = lax.broadcasted_iota(jnp.int32, (block, WIDE), 1)
                values = out_ref[where, :]
                share = jnp.ones((block, WIDE), f32)
                for h in range(heads):
                    share = jnp.where(
                        (lane >= HEAD * (h + 1)) & (lane < HEAD * (h + 2)), values[:, 16 * h : 16 * h + 1], share
                    )
                logs = max_ref[where, :] + jnp.log(jnp.maximum(values, 1e-30))
                out_ref[where, :] = jnp.where(
                    lane < HEAD, jnp.where(lane < 16 * heads, logs, 0.0), values / share
                )
                return carry

            lax.fori_loop(0, ROWS // block, body, 0)

        widen(text_packed, text_feature_ref[...], key_ref, value_ref, text_rows)
        segment(text_rows, True, cross_ref)
        close(cross_ref)
        widen(packed_ref, feature_ref[rows_at(time, ROWS), :], key_ref, value_ref, ROWS)
        packed_out[time] = packed_ref[...]
        segment(ROWS, True, self_ref)
        for i, mask in enumerate(plan.time):
            key_copies[i].wait_recv()
            if i == others - 1:
                moves.chain()
            far = time ^ mask[1]
            packed_out[far] = far_ref[i]
            widen(far_ref.at[i], feature_ref[rows_at(far, ROWS), :], key_ref, value_ref, ROWS)
            segment(ROWS, False, self_ref)
        close(self_ref)
        lane = lax.broadcasted_iota(jnp.int32, (ROWS, WIDE), 1)
        both = self_ref[...] + gate_ref[...] * cross_ref[...]
        mixed_ref[...] = jnp.where(lane < HEAD, 0.0, both).astype(bf16)
        for copy in text_copies + shares + key_copies:
            copy.wait_send()
        moves.finish()

    qmask, vmask, _ = lane_masks()
    links = 7 + (M - 1) + 2 * others
    result = pl.pallas_call(
        kernel,
        out_shape=[
            jax.ShapeDtypeStruct((ROWS, WIDE), bf16),
            jax.ShapeDtypeStruct((ROWS, WIDE), f32),
            jax.ShapeDtypeStruct((ROWS, WIDE), f32),
            jax.ShapeDtypeStruct((ROWS, D), bf16),
            jax.ShapeDtypeStruct((ROWS, WIDE), bf16),
            jax.ShapeDtypeStruct((plan.times, ROWS, 2 * LOCAL), bf16),
            jax.ShapeDtypeStruct((text_rows, 2 * LOCAL), bf16),
            jax.ShapeDtypeStruct((ROWS, WIDE), f32),
            jax.ShapeDtypeStruct((ROWS, WIDE), f32),
            jax.ShapeDtypeStruct((ROWS, 128), f32),
            jax.ShapeDtypeStruct((ROWS, 128), f32),
            jax.ShapeDtypeStruct((text_rows, WIDE), f32),
            jax.ShapeDtypeStruct((text_rows, 128), f32),
        ]
        + moves.out_shapes(),
        in_specs=[VMEM] * 4 + [ANY] + [VMEM] * 12 + [ANY] * n_in,
        out_specs=[VMEM] * 13 + [ANY] * n_out,
        scratch_shapes=[
            pltpu.VMEM((ROWS, WIDE), bf16),
            pltpu.VMEM((ROWS, WIDE), bf16),
            pltpu.VMEM((ROWS, 2 * LOCAL), bf16),
            pltpu.VMEM((max(others, 1), ROWS, 2 * LOCAL), bf16),
            pltpu.VMEM((ROWS, WIDE), f32),
            pltpu.VMEM((D, 3 * LOCAL), bf16),
            pltpu.VMEM((D, 3 * WIDE), bf16),
            pltpu.VMEM((ROWS, 3 * WIDE), f32),
            pltpu.VMEM((text_rows, text_deep), bf16),
            pltpu.VMEM((text_rows, 2 * WIDE), bf16),
            pltpu.VMEM((max(others, 1), text_rows, 2 * WIDE), bf16),
            pltpu.VMEM((text_rows, 2 * WIDE), f32),
            pltpu.VMEM((M, folded_rows, 128), f32),
            pltpu.SemaphoreType.DMA((links,)),
            pltpu.SemaphoreType.DMA((links,)),
            pltpu.SemaphoreType.DMA((GROUPS,)),
        ]
        + moves.scratch(),
        name="attention_forward",
        compiler_params=params(plan, 60),
    )(
        latents,
        modulation,
        gains,
        first_rows,
        captions,
        text_weight,
        mix,
        text_mix,
        gain_wide,
        cos,
        sin,
        query_features,
        features,
        text_features,
        gates,
        jnp.asarray(qmask, bf16),
        jnp.asarray(vmask, f32),
        *moves.operands(),
    )
    return result[:13], result[13:]


def attention_backward(
    plan,
    query,
    packed_all,
    features,
    text_packed,
    text_features,
    self_out,
    cross_out,
    d_mixed,
    gates_q,
    gates_v,
    hats,
    inverses,
    text_hat,
    text_inverse,
    cos,
    sin,
    gain_wide,
    captions,
    attn_all,
    qkv_full,
    mix,
    text_mix,
    latents,
    d_state,
    modulation,
    gains,
    first_rows,
    gate_sum,
    up_sum,
    grad_out,
):
    heads = LOCAL // HEAD
    text_rows = text_packed.shape[0]
    gate_job = plan.scatter_time(gate_sum)
    up_job = plan.ring_of_times(up_sum)
    jobs = [gate_job, plan.ring_of_times(None, gate_job), up_job, plan.times_of_ring(up_job), plan.scatter_span(grad_out)]
    moves = Transfers(jobs)
    n_in, n_out = len(moves.sent), len(moves.jobs)
    block = 256
    others = len(plan.time)
    room = max(others, 1)
    turned = (((1,), (1,)), ((), ()))
    sunk = (((0,), (0,)), ((), ()))
    local3 = qkv_full.shape[1]
    text_deep = captions.shape[1] // plan.times
    span = text_deep // GROUPS
    set_rows = D // plan.sets
    half = set_rows // 2
    folded = 2 * ROWS // 128
    text_folded = max(8, text_rows // 128)

    def kernel(*refs):
        (query_ref, packed_in, feature_ref, text_ref, text_feature_ref, self_ref, cross_ref, d_ref) = refs[:8]
        (gateq_ref, gatev_ref, qmask_ref, bmask_ref, qn_ref, kn_ref, qinv_ref, kinv_ref, tn_ref, tinv_ref) = refs[8:18]
        (cos_ref, sin_ref, wide_ref, caption_ref, attn_ref, qkv_w, mix_ref, text_mix_ref) = refs[18:26]
        (latent_ref, d_state_ref, mod_ref, gain_ref, first_ref) = refs[26:31]
        ins = refs[31 : 31 + n_in]
        refs = refs[31 + n_in :]
        latent_grad, sums_out, wide_out, qkv_out, text_out = refs[:5]
        outs = refs[5 : 5 + n_out]
        refs = refs[5 + n_out :]
        (key_ref, value_ref, near_ref, qs_ref, ds_ref, dq_ref, dk_ref, dv_ref, tdk_ref, tdv_ref) = refs[:10]
        (to_ref, from_ref, tto_ref, tfrom_ref, du_ref, d_text, own_caps, grad_qkv, grad_text) = refs[10:19]
        (a_item, a_sum, a_time, b_time, b_sum, b_item, text_item, share_ref, tshare_ref, mean_ref) = refs[19:29]
        buffers = refs[29:34]
        send_sem, recv_sem, local_sem = refs[34:37]
        me = here()
        item, time, ring = me
        greet(me, moves.peers() | set(plan.time) | set(plan.ring) | {plan.item})
        link = Links(me, send_sem, recv_sem)
        moves.bind(me, ins, outs, refs[37:])
        moves.start()
        loads = []
        for i in range(GROUPS):
            where = pl.ds(pl.multiple_of((i * plan.times + time) * span, span), span)
            loads.append(
                pltpu.make_async_copy(
                    caption_ref.at[:, where], own_caps.at[:, i * span : (i + 1) * span], local_sem.at[1 + i]
                )
            )
            loads[-1].start()

        def prepare(out_ref):
            def body(at, carry):
                where = rows_at(at, block)
                lane = lax.broadcasted_iota(jnp.int32, (block, 128), 1)
                tail = query_ref[where, 128:].astype(f32)
                out_rows = out_ref[where, :]
                d_rows = d_ref[where, :].astype(f32)
                product = d_rows * out_rows
                head_tile = jnp.where(lane < HEAD, 0.0, d_rows[:, :128])
                for h in range(heads):
                    log = -out_rows[:, 16 * h : 16 * h + 1]
                    for j in range(3):
                        piece = log.astype(bf16).astype(f32)
                        log = log - piece
                        tail = jnp.where(lane == SPARE + 2 + 3 * h + j, piece, tail)
                    delta = -jnp.sum(product * bmask_ref[h : h + 1, :].astype(f32), axis=1, keepdims=True)
                    for j in range(2):
                        piece = delta.astype(bf16).astype(f32)
                        delta = delta - piece
                        head_tile = jnp.where(lane == 2 * h + j, piece, head_tile)
                qs_ref[where, :128] = query_ref[where, :128]
                qs_ref[where, 128:] = tail.astype(bf16)
                ds_ref[where, :128] = head_tile.astype(bf16)
                ds_ref[where, 128:] = d_ref[where, 128:]
                return carry

            lax.fori_loop(0, ROWS // block, body, 0)

        def segment(rows, first, k_ref, v_ref, scale):
            k_ref[...] = jnp.zeros_like(k_ref)
            v_ref[...] = jnp.zeros_like(v_ref)

            def body(at, carry):
                where = rows_at(at, block)
                query_rows, d_rows = qs_ref[where, :], ds_ref[where, :]
                total = jnp.zeros((block, WIDE), f32)
                for h in range(heads):
                    own_query = query_rows * qmask_ref[h : h + 1, :]
                    own_d = d_rows * bmask_ref[h : h + 1, :]
                    keys = key_ref[:rows, :]
                    weights = jnp.exp(lax.dot_general(keys, own_query, turned, preferred_element_type=f32))
                    d_weights = lax.dot_general(value_ref[:rows, :], own_d, turned, preferred_element_type=f32)
                    d_scores = (weights * d_weights).astype(bf16)
                    v_ref[...] += jnp.dot(weights.astype(bf16), own_d, preferred_element_type=f32)
                    k_ref[...] += jnp.dot(d_scores, own_query, preferred_element_type=f32)
                    d_query = lax.dot_general(d_scores, keys, sunk, preferred_element_type=f32)
                    total += d_query * qmask_ref[h : h + 1, :].astype(f32)
                total = total * scale
                if first:
                    dq_ref[where, :] = total
                else:
                    dq_ref[where, :] += total
                return carry

            lax.fori_loop(0, ROWS // block, body, 0)

        def bring(which):
            copy = pltpu.make_async_copy(packed_in.at[which], near_ref, local_sem.at[0])
            copy.start()
            copy.wait()
            widen(near_ref, feature_ref[rows_at(which, ROWS), :], key_ref, value_ref, ROWS)

        far_copies = [link(to_ref.at[i], from_ref.at[i], mask) for i, mask in enumerate(plan.time)]
        text_copies = [link(tto_ref, tfrom_ref.at[i], mask) for i, mask in enumerate(plan.time)]

        prepare(self_ref)
        for i, mask in enumerate(plan.time):
            bring(time ^ mask[1])
            segment(ROWS, i == 0, dk_ref, dv_ref, 0.125)
            pack(dk_ref[:, :128], dk_ref[:, 128:], dv_ref[:, :128], dv_ref[:, 128:], to_ref.at[i], ROWS)
            far_copies[i].start()
        moves.chain(late=(3,))
        bring(time)
        segment(ROWS, others == 0, dk_ref, dv_ref, 0.125)
        prepare(cross_ref)
        widen(text_ref, text_feature_ref[...], key_ref, value_ref, text_rows)
        segment(text_rows, False, tdk_ref, tdv_ref, 0.125 * gateq_ref[...])
        tdk_ref[...] = tdk_ref[...] * gateq_ref[...]
        tdv_ref[...] = tdv_ref[...] * gatev_ref[...]
        pack(tdk_ref[:, :128], tdk_ref[:, 128:], tdv_ref[:, :128], tdv_ref[:, 128:], tto_ref, text_rows)
        for copy in text_copies:
            copy.start()
        wide_out[...] = jnp.zeros_like(wide_out)
        wide_out[3:4, :] = jnp.sum(d_ref[...].astype(f32) * cross_ref[...], axis=0, keepdims=True)
        for i in range(others):
            far_copies[i].wait_recv()
            k_first, k_second, v_first, v_second = unpack(from_ref.at[i], ROWS)
            dk_ref[:, :128] += k_first
            dk_ref[:, 128:] += k_second
            dv_ref[:, :128] += v_first
            dv_ref[:, 128:] += v_second

        def unturn(d_all, hat_ref, gain_row):
            pieces = []
            for at in range(ROWS // block):
                where = slice(at * block, (at + 1) * block)
                first, second = d_all[where, :128], d_all[where, 128:]
                cosine, sine = cos_ref[where, :], sin_ref[where, :]
                lane = lax.broadcasted_iota(jnp.int32, (block, 128), 1)
                first, second = jnp.where(lane < SPARE, first, 0.0), jnp.where(lane < SPARE, second, 0.0)
                both = jnp.concatenate([first * cosine + second * sine, second * cosine - first * sine], axis=1)
                hat = hat_ref[where, :]
                wide_out[gain_row : gain_row + 1, :] += jnp.sum(both * hat, axis=0, keepdims=True)
                both = both * wide_ref[gain_row : gain_row + 1, :]
                d_all[where, :] = both
                pieces.append(fold_rows(both * hat))
            return pieces

        pieces = unturn(dq_ref, qn_ref, 0) + unturn(dk_ref, kn_ref, 1)
        share_ref[0] = jnp.concatenate(pieces, axis=0)
        shares = ring_share(plan, link, share_ref)
        for copy in shares:
            copy.wait_recv()
        total = share_ref[0]
        for i in range(1, M):
            total = total + share_ref[i]
        total = total / D
        n = ROWS // 128

        def settle(d_all, hat_ref, inv_ref, means):
            spread_rows(means, mean_ref)
            for c in (0, 128):
                lanes = slice(c, c + 128)
                d_all[:, lanes] = (d_all[:, lanes] - hat_ref[:, lanes] * mean_ref[...]) * inv_ref[...]

        settle(dq_ref, qn_ref, qinv_ref, total[:n])
        settle(dk_ref, kn_ref, kinv_ref, total[n:])
        for at in range(ROWS // block):
            where = slice(at * block, (at + 1) * block)
            lane = lax.broadcasted_iota(jnp.int32, (block, 128), 1)
            values = jnp.concatenate([jnp.where(lane < HEAD, 0.0, dv_ref[where, :128]), dv_ref[where, 128:]], axis=1)
            wide = jnp.concatenate([dq_ref[where, :], dk_ref[where, :], values], axis=1).astype(bf16)
            du_ref[where, :] = lax.dot_general(wide, mix_ref[...], turned, preferred_element_type=f32).astype(bf16)

        grad_qkv[...] = lax.dot_general(attn_ref[...], du_ref[...], sunk, preferred_element_type=f32).astype(bf16)
        away = 1 - item

        def part(i, t, which):
            return pl.ds(pl.multiple_of((i * plan.times + t) * set_rows + which * half, half), half)

        a_items = [link(grad_qkv.at[part(away, t, 0)], a_item.at[t], plan.item) for t in range(plan.times)]
        b_times = [
            link(grad_qkv.at[part(i, time ^ mask[1], 1)], b_time.at[k, i], mask)
            for k, mask in enumerate(plan.time)
            for i in range(GROUPS)
        ]
        a_times = [link(a_sum.at[time ^ mask[1]], a_time.at[k], mask) for k, mask in enumerate(plan.time)]
        b_items = [link(b_sum.at[away], b_item, plan.item)]
        text_items = [link(grad_text.at[rows_at(away, span)], text_item, plan.item)]
        for copy in a_items + b_times:
            copy.start()
        moves.chain()

        def meanwhile():
            for i, copy in enumerate(text_copies):
                copy.wait_recv()
                k_first, k_second, v_first, v_second = unpack(tfrom_ref.at[i], text_rows)
                tdk_ref[:, :128] += k_first
                tdk_ref[:, 128:] += k_second
                tdv_ref[:, :128] += v_first
                tdv_ref[:, 128:] += v_second
            lane = lax.broadcasted_iota(jnp.int32, (text_rows, WIDE), 1) % 128
            d_keys = jnp.where(lane < SPARE, tdk_ref[...], 0.0)
            hat = tn_ref[...]
            wide_out[2:3, :] = jnp.sum(d_keys * hat, axis=0, keepdims=True)
            d_keys = d_keys * wide_ref[2:3, :]
            tdk_ref[...] = d_keys
            sums = fold_rows(d_keys * hat)
            if text_folded > text_rows // 128:
                sums = jnp.concatenate([sums, jnp.zeros((text_folded - text_rows // 128, 128), f32)], axis=0)
            tshare_ref[0] = sums
            text_shares = ring_share(plan, link, tshare_ref)
            for t, copy in enumerate(a_items):
                copy.wait_recv()
                a_sum[t] = (grad_qkv[part(item, t, 0), :].astype(f32) + a_item[t].astype(f32)).astype(bf16)
            for copy in a_times:
                copy.start()
            for copy in text_shares:
                copy.wait_recv()
            total = tshare_ref[0]
            for i in range(1, M):
                total = total + tshare_ref[i]
            total = total / D
            spread_rows(total[: text_rows // 128], mean_ref.at[:text_rows])
            for c in (0, 128):
                lanes = slice(c, c + 128)
                tdk_ref[:, lanes] = (tdk_ref[:, lanes] - tn_ref[:, lanes] * mean_ref[:text_rows, :]) * tinv_ref[...]
            lane = lax.broadcasted_iota(jnp.int32, (text_rows, WIDE), 1)
            values = jnp.where(lane < HEAD, 0.0, tdv_ref[...])
            wide = jnp.concatenate([tdk_ref[...], values], axis=1).astype(bf16)
            d_text[...] = lax.dot_general(wide, text_mix_ref[...], turned, preferred_element_type=f32).astype(bf16)
            for copy in loads:
                copy.wait()
            grad_text[...] = lax.dot_general(own_caps[...], d_text[...], sunk, preferred_element_type=f32).astype(bf16)
            text_items[0].start()
            for copy in text_shares:
                copy.wait_send()
            for copy in b_times:
                copy.wait_recv()
            for i in range(GROUPS):
                total = grad_qkv[part(i, time, 1), :].astype(f32)
                for k in range(others):
                    total = total + b_time[k, i].astype(f32)
                b_sum[i] = total.astype(bf16)
            b_items[0].start()

        def back_product(which):
            return lax.dot_general(du_ref[rows_at(which, TOK), :], qkv_w[...], turned, preferred_element_type=f32)

        ring_sum(plan, link, me, buffers, back_product, meanwhile)

        d_in = buffers[4][...]
        rows = latent_ref[...]
        inverse = scale_of(rows)
        hat = rows * inverse
        gain = gain_ref[0:1, :]
        is_first = first_ref[...] > 0.5
        scale = jnp.where(is_first, mod_ref[0:1, :D], mod_ref[1:2, :D])
        sums_out[...] = jnp.zeros_like(sums_out)
        values = d_in * (hat * gain)
        total = jnp.sum(values, axis=0, keepdims=True)
        start = jnp.sum(jnp.where(is_first, values, 0.0), axis=0, keepdims=True)
        sums_out[1:2, :] = start
        sums_out[2:3, :] = total - start
        d_norm = d_in * (1.0 + scale)
        sums_out[0:1, :] = jnp.sum(d_norm * hat, axis=0, keepdims=True)
        latent_grad[...] = d_state_ref[...] + norm_back(d_norm * gain, hat, inverse)

        total = a_sum[time].astype(f32)
        for k, copy in enumerate(a_times):
            copy.wait_recv()
            total = total + a_time[k].astype(f32)
        qkv_out[:half, :] = total.astype(bf16)
        b_items[0].wait_recv()
        qkv_out[half:, :] = (b_sum[item].astype(f32) + b_item[...].astype(f32)).astype(bf16)
        text_items[0].wait_recv()
        text_out[...] = (grad_text[rows_at(item, span), :].astype(f32) + text_item[...].astype(f32)).astype(bf16)
        for copy in far_copies + text_copies + shares + a_items + b_times + a_times + b_items + text_items:
            copy.wait_send()
        moves.finish()

    qmask, _, bmask = lane_masks()
    links = 2 * others + 2 * (M - 1) + plan.times + GROUPS * others + others + 2 + 7
    result = pl.pallas_call(
        kernel,
        out_shape=[
            jax.ShapeDtypeStruct((TOK, D), f32),
            jax.ShapeDtypeStruct((8, D), f32),
            jax.ShapeDtypeStruct((8, WIDE), f32),
            jax.ShapeDtypeStruct((set_rows, local3), bf16),
            jax.ShapeDtypeStruct((span, 2 * LOCAL), bf16),
        ]
        + moves.out_shapes(),
        in_specs=[VMEM, ANY] + [VMEM] * 19 + [ANY] + [VMEM] * 9 + [ANY] * n_in,
        out_specs=[VMEM] * 5 + [ANY] * n_out,
        scratch_shapes=[
            pltpu.VMEM((ROWS, WIDE), bf16),
            pltpu.VMEM((ROWS, WIDE), bf16),
            pltpu.VMEM((ROWS, 2 * LOCAL), bf16),
            pltpu.VMEM((ROWS, WIDE), bf16),
            pltpu.VMEM((ROWS, WIDE), bf16),
            pltpu.VMEM((ROWS, WIDE), f32),
            pltpu.VMEM((ROWS, WIDE), f32),
            pltpu.VMEM((ROWS, WIDE), f32),
            pltpu.VMEM((text_rows, WIDE), f32),
            pltpu.VMEM((text_rows, WIDE), f32),
            pltpu.VMEM((room, ROWS, 2 * LOCAL), bf16),
            pltpu.VMEM((room, ROWS, 2 * LOCAL), bf16),
            pltpu.VMEM((text_rows, 2 * LOCAL), bf16),
            pltpu.VMEM((room, text_rows, 2 * LOCAL), bf16),
            pltpu.VMEM((ROWS, local3), bf16),
            pltpu.VMEM((text_rows, 2 * LOCAL), bf16),
            pltpu.VMEM((text_rows, text_deep), bf16),
            pltpu.VMEM((D, local3), bf16),
            pltpu.VMEM((text_deep, 2 * LOCAL), bf16),
            pltpu.VMEM((plan.times, half, local3), bf16),
            pltpu.VMEM((plan.times, half, local3), bf16),
            pltpu.VMEM((room, half, local3), bf16),
            pltpu.VMEM((room, GROUPS, half, local3), bf16),
            pltpu.VMEM((GROUPS, half, local3), bf16),
            pltpu.VMEM((half, local3), bf16),
            pltpu.VMEM((span, 2 * LOCAL), bf16),
            pltpu.VMEM((M, folded, 128), f32),
            pltpu.VMEM((M, text_folded, 128), f32),
            pltpu.VMEM((ROWS, 128), f32),
        ]
        + RING_BUFFERS
        + [
            pltpu.SemaphoreType.DMA((links,)),
            pltpu.SemaphoreType.DMA((links,)),
            pltpu.SemaphoreType.DMA((1 + GROUPS,)),
        ]
        + moves.scratch(),
        name="attention_backward",
        compiler_params=params(plan, 63),
    )(
        query,
        packed_all,
        features,
        text_packed,
        text_features,
        self_out,
        cross_out,
        d_mixed,
        gates_q,
        gates_v,
        jnp.asarray(qmask, bf16),
        jnp.asarray(bmask, bf16),
        *hats,
        *inverses,
        text_hat,
        text_inverse,
        cos,
        sin,
        gain_wide,
        captions,
        attn_all,
        qkv_full,
        mix,
        text_mix,
        latents,
        d_state,
        modulation,
        gains,
        first_rows,
        *moves.operands(),
    )
    return result[:5], result[5:]


def finish(plan, small, jobs):
    moves = Transfers(list(jobs))
    n_in, n_out = len(moves.sent), len(moves.jobs)
    peers = plan.all

    def kernel(*refs):
        small_ref = refs[0]
        ins = refs[1 : 1 + n_in]
        all_ref = refs[1 + n_in]
        outs = refs[2 + n_in : 2 + n_in + n_out]
        recv_ref, sum_ref, all_in, send_sem, recv_sem = refs[2 + n_in + n_out : 7 + n_in + n_out]
        me = here()
        greet(me, moves.peers() | set(peers))
        link = Links(me, send_sem, recv_sem)
        moves.bind(me, ins, outs, refs[7 + n_in + n_out :])
        copies = []
        for i, mask in enumerate(peers):
            dest = flip(me, mask)
            copies.append(link(small_ref.at[plan.set_of(dest), dest[2]], recv_ref.at[i], mask))
            copies[-1].start()
        moves.start()
        own = small_ref[plan.set_of(me), me[2]]
        group, everyone = own[:8], own[8:]
        for i, mask in enumerate(peers):
            copies[i].wait_recv()
            if mask[0] == 0:
                group = group + recv_ref[i, :8, :]
            everyone = everyone + recv_ref[i, 8:, :]
        sum_ref[:8, :] = group
        sum_ref[8:, :] = everyone
        place = plan.set_of(me) * M + me[2]
        shares = [link(sum_ref, all_in.at[place], mask) for mask in peers]
        for copy in shares:
            copy.start()
        all_in[place] = sum_ref[...]
        for copy in shares:
            copy.wait_recv()
        all_ref[...] = all_in[...]
        for copy in copies + shares:
            copy.wait_send()
        moves.finish()

    devices = plan.sets * M
    result = pl.pallas_call(
        kernel,
        out_shape=[jax.ShapeDtypeStruct((devices, 16, 128), f32)] + moves.out_shapes(),
        in_specs=[VMEM] + [ANY] * n_in,
        out_specs=[VMEM] + [ANY] * n_out,
        scratch_shapes=[
            pltpu.VMEM((len(peers), 16, 128), f32),
            pltpu.VMEM((16, 128), f32),
            pltpu.VMEM((devices, 16, 128), f32),
            pltpu.SemaphoreType.DMA((2 * len(peers),)),
            pltpu.SemaphoreType.DMA((2 * len(peers),)),
        ]
        + moves.scratch(),
        name="finish",
        compiler_params=params(plan, 40),
    )(small, *moves.operands())
    return result[0], result[1:]


def feed_forward(
    plan, mixed, out_full, latents, cotangent, modulation, gains, first_rows, gate_time, up_shard, down_weight
):
    d_rows = down_weight.shape[0]
    width = plan.sets * d_rows
    deep = out_full.shape[0]
    up_job = plan.stack_time(up_shard)
    down_job = plan.stack_time(down_weight)
    moves = Transfers(
        [plan.stack_item(gate_time), up_job, plan.stack_item(up_shard, up_job), down_job, plan.stack_item(down_weight, down_job)]
    )
    n_in, n_out = len(moves.sent), len(moves.jobs)
    turned = (((1,), (1,)), ((), ()))
    sunk = (((0,), (0,)), ((), ()))
    plain = (((1,), (0,)), ((), ()))
    chip_rows = 2 * TOK
    part_rows = D // GROUPS
    others = len(plan.time)
    slab = plan.times * d_rows

    def kernel(*refs):
        (mixed_ref, out_w, latent_ref, cot_ref, mod_ref, gain_ref, first_ref) = refs[:7]
        ins = refs[7 : 7 + n_in]
        refs = refs[7 + n_in :]
        (result_ref, d_state_ref, d_mixed_ref, grad_out_ref, gate_sum_ref, up_sum_ref, down_grad_ref, sums_ref) = refs[:8]
        outs = refs[8 : 8 + n_out]
        refs = refs[8 + n_out :]
        (gate_w, up_w, down_w, ffn_all, down_all, proj_all, gate_ref, up_ref, act_ref, d_gate_ref, d_up_ref) = refs[:11]
        (grad_gate, grad_up, grad_down, from_gate, from_up, from_down, down_sum, from_time) = refs[11:19]
        (to_mate, from_mate, to_chip, from_chip, part, proj_ref, state_ref, own_ref, send_sem, recv_sem, local_sem) = refs[
            19:30
        ]
        me = here()
        item, time, ring = me
        core, chip = ring % 2, ring // 2
        greet(me, moves.peers() | {plan.mate, plan.item} | set(plan.chips) | set(plan.time))
        moves.bind(me, ins, outs, refs[30:])
        moves.start()
        used = [0]

        def link(src, dst, mask):
            slot = used[0]
            used[0] += 1
            return pltpu.make_async_remote_copy(
                src_ref=src,
                dst_ref=dst,
                send_sem=send_sem.at[slot],
                recv_sem=recv_sem.at[slot],
                device_id=flip(me, mask),
                device_id_type=MESH,
            )

        def rows_at(index, count):
            return pl.ds(pl.multiple_of(index * count, count), count)

        def scatter(product, meanwhile=lambda: None):
            mates = [link(to_mate.at[d], from_mate.at[d], plan.mate) for d in range(4)]
            chips = [link(to_chip.at[d - 1], from_chip.at[d - 1], (0, 0, 2 * d)) for d in (1, 2, 3)]
            for d in (3, 2, 1, 0):
                to_mate[d] = product((chip ^ d) * 2 + 1 - core).astype(bf16)
                mates[d].start()
            for d in (3, 2, 1):
                part[...] = product((chip ^ d) * 2 + core)
                mates[d].wait_recv()
                to_chip[d - 1] = (part[...] + from_mate[d].astype(f32)).astype(bf16)
                chips[d - 1].start()
            part[...] = product(chip * 2 + core)
            mates[0].wait_recv()
            part[...] = part[...] + from_mate[0].astype(f32)
            meanwhile()
            for copy in chips:
                copy.wait_recv()
            part[...] = part[...] + (
                from_chip[0].astype(f32) + from_chip[1].astype(f32) + from_chip[2].astype(f32)
            )
            for copy in mates + chips:
                copy.wait_send()

        def gather(all_ref, each, meanwhile=lambda: None):
            own = all_ref.at[rows_at(ring, TOK)]
            first = [link(own, own, plan.mate)] + [link(own, own, (0, 0, 2 * d)) for d in (1, 2, 3)]
            for copy in first[1:] + first[:1]:
                copy.start()
            meanwhile()
            first[0].wait_recv()
            each(chip)
            later = []
            for d in (1, 2, 3):
                first[d].wait_recv()
                block = all_ref.at[rows_at(ring ^ (2 * d), TOK)]
                copy = link(block, block, plan.mate)
                copy.start()
                later.append(copy)
            for d in (1, 2, 3):
                later[d - 1].wait_recv()
                each(chip ^ d)
            for copy in first + later:
                copy.wait_send()

        is_first = first_ref[...] > 0.5

        def modulated(index):
            cols = pl.ds(index * D, D)
            return jnp.where(is_first, mod_ref[0:1, cols], mod_ref[1:2, cols])

        def column_sums(at, values):
            total = jnp.sum(values, axis=0, keepdims=True)
            start = jnp.sum(jnp.where(is_first, values, 0.0), axis=0, keepdims=True)
            sums_ref[at : at + 1, :] = start
            sums_ref[at + 1 : at + 2, :] = total - start

        def scale_of(values):
            return lax.rsqrt(jnp.mean(values * values, axis=1, keepdims=True) + epsilon)

        def norm_back(d_hat, hat, inverse):
            return inverse * (d_hat - hat * jnp.mean(d_hat * hat, axis=1, keepdims=True))

        def load(job, target):
            moves.take(job)
            copy = pltpu.make_async_copy(outs[job], target, local_sem.at[0])
            copy.start()
            copy.wait()

        def out_product(block):
            return jnp.dot(mixed_ref[rows_at(block, TOK), :], out_w[...], preferred_element_type=f32)

        scatter(out_product)
        moves.chain(late=(4,))
        proj_ref[...] = part[...]
        proj = proj_ref[...]
        gate_attn = jnp.tanh(modulated(1))
        state_ref[...] = latent_ref[...] + gate_attn * (proj * scale_of(proj) * gain_ref[1:2, :])
        state = state_ref[...]
        ffn_in = state * scale_of(state) * gain_ref[2:3, :] * (1.0 + modulated(2))
        ffn_all[rows_at(ring, TOK), :] = ffn_in.astype(bf16)

        def forward_chip(which):
            rows = rows_at(which, chip_rows)
            block = ffn_all[rows, :]
            gate = jnp.dot(block, gate_w[...], preferred_element_type=f32)
            up = jnp.dot(block, up_w[...], preferred_element_type=f32)
            gate_ref[rows, :] = gate
            up_ref[rows, :] = up
            act_ref[rows, :] = (gate * (1.0 / (1.0 + jnp.exp(-gate))) * up).astype(bf16)

        def weights_here():
            load(0, gate_w)
            load(2, up_w)
            moves.chain()

        gather(ffn_all, forward_chip, weights_here)

        load(4, down_w)

        def down_product(block):
            return jnp.dot(act_ref[rows_at(block, TOK), :], down_w[...], preferred_element_type=f32)

        scatter(down_product)

        down = part[...]
        inverse = scale_of(down)
        hat = down * inverse
        gate_ffn = jnp.tanh(modulated(3))
        gain = gain_ref[3:4, :]
        cot = cot_ref[...]
        result_ref[...] = state_ref[...] + gate_ffn * (hat * gain)
        column_sums(7, cot * (hat * gain) * (1.0 - gate_ffn * gate_ffn))
        d_norm = cot * gate_ffn
        sums_ref[2:3, :] = jnp.sum(d_norm * hat, axis=0, keepdims=True)
        down_all[rows_at(ring, TOK), :] = norm_back(d_norm * gain, hat, inverse).astype(bf16)

        def backward_chip(which):
            rows = rows_at(which, chip_rows)
            d_act = lax.dot_general(down_all[rows, :], down_w[...], turned, preferred_element_type=f32)
            gate, up = gate_ref[rows, :], up_ref[rows, :]
            sigmoid = 1.0 / (1.0 + jnp.exp(-gate))
            d_up_ref[rows, :] = (d_act * (gate * sigmoid)).astype(bf16)
            d_gate_ref[rows, :] = (d_act * up * (sigmoid * (1.0 + gate * (1.0 - sigmoid)))).astype(bf16)

        gather(down_all, backward_chip)

        away = 1 - item
        down_link = link(grad_down.at[rows_at(away, slab)], from_down, plan.item)
        gate_link = link(grad_gate.at[rows_at(away, part_rows)], from_gate, plan.item)
        up_link = link(grad_up.at[rows_at(away, part_rows)], from_up, plan.item)
        time_links = [link(down_sum.at[rows_at(time ^ mask[1], d_rows)], from_time.at[i], mask) for i, mask in enumerate(plan.time)]

        def down_gradient():
            grad_down[...] = lax.dot_general(act_ref[...], down_all[...], sunk, preferred_element_type=f32).astype(bf16)
            down_link.start()

        def gate_gradients():
            down_gradient()
            grad_gate[...] = lax.dot_general(ffn_all[...], d_gate_ref[...], sunk, preferred_element_type=f32).astype(bf16)
            gate_link.start()
            grad_up[...] = lax.dot_general(ffn_all[...], d_up_ref[...], sunk, preferred_element_type=f32).astype(bf16)
            up_link.start()

        def back_product(block):
            rows = rows_at(block, TOK)
            return lax.dot_general(d_gate_ref[rows, :], gate_w[...], turned, preferred_element_type=f32) + lax.dot_general(
                d_up_ref[rows, :], up_w[...], turned, preferred_element_type=f32
            )

        scatter(back_product, gate_gradients)

        d_ffn = part[...]
        state = state_ref[...]
        inverse = scale_of(state)
        hat = state * inverse
        gain = gain_ref[2:3, :]
        column_sums(5, d_ffn * (hat * gain))
        d_norm = d_ffn * (1.0 + modulated(2))
        sums_ref[1:2, :] = jnp.sum(d_norm * hat, axis=0, keepdims=True)
        d_state_ref[...] = cot_ref[...] + norm_back(d_norm * gain, hat, inverse)
        d_state = d_state_ref[...]
        proj = proj_ref[...]
        inverse = scale_of(proj)
        hat = proj * inverse
        gate_attn = jnp.tanh(modulated(1))
        gain = gain_ref[1:2, :]
        column_sums(3, d_state * (hat * gain) * (1.0 - gate_attn * gate_attn))
        d_norm = d_state * gate_attn
        sums_ref[0:1, :] = jnp.sum(d_norm * hat, axis=0, keepdims=True)
        proj_all[rows_at(ring, TOK), :] = norm_back(d_norm * gain, hat, inverse).astype(bf16)

        def down_time():
            down_link.wait_recv()
            mine = grad_down[rows_at(item, slab), :].astype(f32) + from_down[...].astype(f32)
            down_sum[...] = mine.astype(bf16)
            for copy in time_links:
                copy.start()

        def mixed_chip(which):
            rows = rows_at(which, chip_rows)
            d_mixed_ref[rows, :] = lax.dot_general(
                proj_all[rows, :], out_w[...], turned, preferred_element_type=f32
            ).astype(bf16)

        gather(proj_all, mixed_chip, down_time)
        grad_out_ref[...] = lax.dot_general(mixed_ref[...], proj_all[...], sunk, preferred_element_type=f32).astype(bf16)
        gate_link.wait_recv()
        gate_sum_ref[...] = (
            grad_gate[rows_at(item, part_rows), :].astype(f32) + from_gate[...].astype(f32)
        ).astype(bf16)
        own_ref[...] = down_sum[rows_at(time, d_rows), :].astype(f32)
        for i, copy in enumerate(time_links):
            copy.wait_recv()
            own_ref[...] += from_time[i].astype(f32)
        down_grad_ref[...] = own_ref[...]
        up_link.wait_recv()
        up_sum_ref[...] = (grad_up[rows_at(item, part_rows), :].astype(f32) + from_up[...].astype(f32)).astype(bf16)
        for copy in [down_link, gate_link, up_link] + time_links:
            copy.wait_send()
        moves.finish()

    links = 7 * 3 + 7 * 3 + 3 + others
    result = pl.pallas_call(
        kernel,
        out_shape=[
            jax.ShapeDtypeStruct((TOK, D), f32),
            jax.ShapeDtypeStruct((TOK, D), f32),
            jax.ShapeDtypeStruct((ROWS, deep), bf16),
            jax.ShapeDtypeStruct((deep, D), bf16),
            jax.ShapeDtypeStruct((part_rows, width), bf16),
            jax.ShapeDtypeStruct((part_rows, width), bf16),
            jax.ShapeDtypeStruct((d_rows, D), f32),
            jax.ShapeDtypeStruct((16, D), f32),
        ]
        + moves.out_shapes(),
        in_specs=[VMEM] * 7 + [ANY] * n_in,
        out_specs=[VMEM] * 8 + [ANY] * n_out,
        scratch_shapes=[
            pltpu.VMEM((D, width), bf16),
            pltpu.VMEM((D, width), bf16),
            pltpu.VMEM((width, D), bf16),
            pltpu.VMEM((ROWS, D), bf16),
            pltpu.VMEM((ROWS, D), bf16),
            pltpu.VMEM((ROWS, D), bf16),
            pltpu.VMEM((ROWS, width), f32),
            pltpu.VMEM((ROWS, width), f32),
            pltpu.VMEM((ROWS, width), bf16),
            pltpu.VMEM((ROWS, width), bf16),
            pltpu.VMEM((ROWS, width), bf16),
            pltpu.VMEM((D, width), bf16),
            pltpu.VMEM((D, width), bf16),
            pltpu.VMEM((width, D), bf16),
            pltpu.VMEM((part_rows, width), bf16),
            pltpu.VMEM((part_rows, width), bf16),
            pltpu.VMEM((slab, D), bf16),
            pltpu.VMEM((slab, D), bf16),
            pltpu.VMEM((max(others, 1), d_rows, D), bf16),
            pltpu.VMEM((4, TOK, D), bf16),
            pltpu.VMEM((4, TOK, D), bf16),
            pltpu.VMEM((3, TOK, D), bf16),
            pltpu.VMEM((3, TOK, D), bf16),
            pltpu.VMEM((TOK, D), f32),
            pltpu.VMEM((TOK, D), f32),
            pltpu.VMEM((TOK, D), f32),
            pltpu.VMEM((d_rows, D), f32),
            pltpu.SemaphoreType.DMA((links,)),
            pltpu.SemaphoreType.DMA((links,)),
            pltpu.SemaphoreType.DMA((1,)),
        ]
        + moves.scratch(),
        name="feed_forward",
        compiler_params=params(plan, 60),
    )(mixed, out_full, latents, cotangent, modulation, gains, first_rows, *moves.operands())
    return result[:8]


def shards(
    latents,
    conditions,
    captions,
    row_counts,
    text_lengths,
    qkv_weight,
    text_weight,
    out_weight,
    gate_up_weight,
    down_weight,
    ada_weight,
    ada_bias,
    norm_gains,
    head_gates,
    cotangent,
):
    times = lax.axis_size("times")
    plan = Plan(times)
    sets, rows_axis = plan.sets, plan.rows
    devices = sets * M
    item, time, ring = here()
    place = (item * times + time) * M + ring
    group_place = time * M + ring
    heads = LOCAL // HEAD

    k_rows = qkv_weight.shape[0]
    t_rows = text_weight.shape[0]
    o_rows = out_weight.shape[0]
    d_rows = down_weight.shape[0]
    a_rows = ada_weight.shape[0]
    bias_n = ada_bias.shape[0]
    gain_n = norm_gains.shape[1]
    tiles = -(-(4 * D // 128) // rows_axis)

    package = jnp.concatenate(
        [norm_gains.astype(f32).reshape(-1), ada_bias.astype(f32), row_counts[0, 0].astype(f32)]
    )
    package_n = package.shape[0]
    lines = -(-package_n // 1024) * 8
    package = jnp.pad(package, (0, lines * 128 - package_n)).reshape(lines, 128)

    silu = jax.nn.silu(conditions[0].astype(f32)).astype(bf16).astype(f32)
    other_place = ((1 - item) * times + time) * M + ring
    cond = jnp.stack(
        [lax.dynamic_slice_in_dim(silu, p * a_rows, a_rows, 1) for p in (place, other_place)]
    )
    cond = jnp.pad(cond, ((0, 0), (0, 8 - FRAMES), (0, 128 - a_rows)))

    key_places, value_places = wide_order()
    mix = placing(np.concatenate([key_places, WIDE + key_places, 2 * WIDE + value_places]), 3 * WIDE)
    text_mix = placing(np.concatenate([key_places, WIDE + value_places]), 2 * WIDE)
    qkv_send = qkv_weight.reshape(k_rows, 3, M, LOCAL).transpose(2, 0, 1, 3).reshape(M, k_rows, 3 * LOCAL)
    text_send = text_weight.reshape(t_rows, 2, M, LOCAL).transpose(2, 0, 1, 3).reshape(M, t_rows, 2 * LOCAL)
    gate_up_send = gate_up_weight.reshape(k_rows, 2, sets, M, d_rows).transpose(1, 3, 0, 2, 4)
    gate_up_send = gate_up_send.reshape(2, M, k_rows, sets * d_rows)
    out_forth = [(o, (o % sets) * M + o // sets) for o in range(devices)]
    out_back = [(b, a) for a, b in out_forth]
    axes = ("items", "times", "ring")
    out_shard = lax.ppermute(out_weight, axes, out_forth)

    text_job = plan.scatter_ring(text_send)
    mod_tiles, cond_other, (packages, qkv_time, _, text_full) = prologue(
        plan,
        tiles,
        package,
        cond,
        ada_weight,
        [plan.scatter_group_ring(qkv_send), text_job, plan.swap_source(text_job)],
    )
    packages = packages.reshape(devices, lines * 128)
    gains = packages[:, : 7 * gain_n].reshape(devices, 7, gain_n).transpose(1, 0, 2).reshape(7, D)
    gains = jnp.pad(gains, ((0, 1), (0, 0)))
    bias = packages[:, 7 * gain_n : 7 * gain_n + bias_n].reshape(4 * D)
    counts_all = packages[:, 7 * gain_n + bias_n : package_n].astype(jnp.int32).reshape(GROUPS, rows_axis, FRAMES)
    counts = lax.dynamic_index_in_dim(counts_all, item, 0, keepdims=False)

    def from_tiles(array):
        lead = array.shape[:-3]
        array = array[..., : FRAMES * tiles, :].reshape(lead + (rows_axis, FRAMES, tiles, 128))
        array = jnp.moveaxis(array, -3, -4).reshape(lead + (FRAMES, rows_axis * tiles * 128))
        return array[..., : 4 * D]

    modulation = from_tiles(mod_tiles) + bias

    line = jnp.arange(TOK, dtype=jnp.int32)[None, :]
    clip = counts[:, :1]
    before = jnp.cumsum(counts, axis=0) - counts
    frame_all = (line >= clip).astype(jnp.int32)
    position_all = jnp.where(frame_all == 0, before[:, :1] + line, before[:, 1:] + line - clip)
    frame_k = frame_all.reshape(-1)
    frame_q = lax.dynamic_slice_in_dim(frame_k, time * ROWS, ROWS)
    position_q = lax.dynamic_slice_in_dim(position_all.reshape(-1), time * ROWS, ROWS).astype(f32)
    frame_own = lax.dynamic_index_in_dim(frame_all, group_place, 0, keepdims=False)
    first_rows = (frame_own == 0).astype(f32)[:, None]
    text_line = jnp.arange(FRAMES * TEXT, dtype=jnp.int32)
    text_frame = text_line // TEXT
    text_live = text_line % TEXT < jnp.repeat(text_lengths[0], TEXT)

    feature = jnp.arange(128, dtype=jnp.int32)[None, :]

    def key_features(apart_first, apart_second):
        ones = (feature >= SPARE + 2) & (feature < SPARE + 2 + 3 * heads)
        pick = jnp.where(feature == SPARE, apart_first[:, None], (feature == SPARE + 1) & apart_second[:, None])
        return jnp.where(pick | ones, 1.0, 0.0).astype(bf16)

    features = key_features(frame_k == 1, frame_k == 0)
    text_features = key_features(~((text_frame == 0) & text_live), ~((text_frame == 1) & text_live))
    query_features = jnp.where(feature == SPARE + frame_q[:, None], -APART, 0.0).astype(bf16)
    pair = jnp.arange(128, dtype=jnp.int32)
    frequency = theta_base ** (-2.0 * (pair % (HEAD // 2)).astype(f32) / HEAD)
    angle = position_q[:, None] * frequency[None, :]
    live_lane = (pair < SPARE)[None, :]
    cos, sin = jnp.where(live_lane, jnp.cos(angle), 0.0), jnp.where(live_lane, jnp.sin(angle), 0.0)
    own_gates = jnp.tanh(lax.dynamic_slice_in_dim(head_gates.astype(f32), ring * heads, heads))
    gates_v = jnp.concatenate([jnp.zeros((HEAD,), f32), jnp.repeat(own_gates, HEAD)]).reshape(1, WIDE)
    half_gates = jnp.pad(jnp.repeat(own_gates, HEAD // 2), (0, 128 - SPARE))
    gates_q = jnp.concatenate([half_gates, half_gates]).reshape(1, WIDE)
    gain_wide = lax.dynamic_slice(gains, (4, ring * LOCAL), (3, LOCAL))
    gain_wide = gain_wide.reshape(3, heads, HEAD // 2, 2).transpose(0, 3, 1, 2).reshape(3, 2, SPARE)
    gain_wide = jnp.pad(gain_wide, ((0, 5), (0, 0), (0, 128 - SPARE))).reshape(8, WIDE)

    inputs = latents[0]
    caption_rows = captions[0].reshape(FRAMES * TEXT, TEXT_DIM)
    forward, (qkv_full, _, out_full, _, up_shard, gate_time) = attention_forward(
        plan,
        inputs,
        modulation,
        gains,
        first_rows,
        caption_rows,
        text_full.reshape(GROUPS * M * t_rows, 2 * LOCAL),
        mix,
        text_mix,
        gain_wide,
        cos,
        sin,
        query_features,
        features,
        text_features,
        gates_v,
        qkv_time.reshape(times * M * k_rows, 3 * LOCAL),
        out_shard,
        gate_up_send[0],
        gate_up_send[1],
    )
    (mixed, self_out, cross_out, attn_all, query, packed_all, text_packed, qn, kn, q_inv, k_inv, tn, t_inv) = forward
    out_full = jnp.pad(out_full.reshape(LOCAL, D), ((HEAD, 0), (0, 0)))

    (result_rows, d_state, d_mixed, grad_out, gate_sum, up_sum, down_grad, ffn_sums) = feed_forward(
        plan,
        mixed,
        out_full,
        inputs,
        cotangent[0],
        modulation,
        gains,
        first_rows,
        gate_time.reshape(times * M * k_rows, sets * d_rows),
        up_shard.reshape(M * k_rows, sets * d_rows),
        down_weight,
    )
    ring_shape = (times, M, k_rows, sets * d_rows)
    (grad_latent, attn_sums, wide_sums, qkv_sum, text_sum), (_, gate_parts, _, up_parts, out_parts) = attention_backward(
        plan,
        query,
        packed_all,
        features,
        text_packed,
        text_features,
        self_out,
        cross_out,
        d_mixed,
        gates_q,
        gates_v,
        (qn, kn),
        (q_inv, k_inv),
        tn,
        t_inv,
        cos,
        sin,
        gain_wide,
        caption_rows,
        attn_all,
        qkv_full,
        mix,
        text_mix,
        inputs,
        d_state,
        modulation,
        gains,
        first_rows,
        gate_sum.reshape(ring_shape),
        up_sum.reshape(ring_shape),
        grad_out[HEAD:].reshape(sets, o_rows, D),
    )

    def add(parts, axis=0):
        return jnp.sum(parts.astype(f32), axis=axis)

    d_mod = jnp.concatenate([attn_sums[1:3], ffn_sums[3:5], ffn_sums[5:7], ffn_sums[7:9]], axis=1)
    d_mod = jnp.pad(d_mod, ((0, 0), (0, rows_axis * tiles * 128 - 4 * D)))
    d_mod = d_mod.reshape(FRAMES, rows_axis, tiles, 128).transpose(1, 0, 2, 3).reshape(rows_axis, FRAMES * tiles, 128)
    d_mod = jnp.pad(d_mod, ((0, 0), (0, 8 - FRAMES * tiles), (0, 0)))
    d_mod = jnp.tile(d_mod, (GROUPS, 1, 1))
    wide_gains = wide_sums[:3].reshape(3, 2, 128)[:, :, :SPARE].reshape(3, 2, heads, HEAD // 2)
    wide_gains = wide_gains.transpose(0, 2, 3, 1).reshape(3, LOCAL)
    wide_gains = wide_gains * jnp.stack([jnp.ones(()), jnp.ones(()), (time == 0).astype(f32)])[:, None]
    wide_gains = lax.dynamic_update_slice(jnp.zeros((3, D), f32), wide_gains, (0, ring * LOCAL))
    gate_sums = jnp.sum(wide_sums[3, HEAD:].reshape(heads, HEAD), axis=1) * (1.0 - own_gates * own_gates)
    gate_row = lax.dynamic_update_slice_in_dim(jnp.zeros((1, D), f32), gate_sums[None], ring * heads, 1)
    d_gains = jnp.concatenate([attn_sums[:1], ffn_sums[:3], wide_gains, gate_row], axis=0)
    gain_tiles = D // 128
    d_gains = d_gains.reshape(8, gain_tiles, 128).transpose(1, 0, 2)
    d_gains = jnp.pad(d_gains, ((0, devices - gain_tiles), (0, 0), (0, 0)))
    small = jnp.concatenate([d_mod, d_gains], axis=1).reshape(sets, M, 16, 128)
    small_all, (qkv_pieces, text_pieces) = finish(
        plan,
        small,
        [
            plan.scatter_ring(qkv_sum.reshape(M, k_rows, 3 * LOCAL)),
            plan.scatter_ring(text_sum.reshape(M, t_rows, 2 * LOCAL)),
        ],
    )
    gains_all = small_all[:gain_tiles, 8:].transpose(1, 0, 2).reshape(8, D)
    gains_grad = lax.dynamic_slice_in_dim(gains_all[:7], place * gain_n, gain_n, 1)
    gates_grad = gains_all[7, :HEADS]
    d_mod_all = from_tiles(small_all[:, :8].reshape(GROUPS, rows_axis, 8, 128)).reshape(GROUPS * FRAMES, 4 * D)
    cond_own, cond_other = cond[0, :FRAMES], cond_other[:FRAMES]
    silu_both = jnp.where(
        item == 0, jnp.concatenate([cond_own, cond_other]), jnp.concatenate([cond_other, cond_own])
    )
    ada_grad = jnp.einsum("fc,fd->cd", silu_both[:, :a_rows], d_mod_all, precision=highest)
    bias_grad = lax.dynamic_slice_in_dim(jnp.sum(d_mod_all, axis=0), place * bias_n, bias_n)
    out_grad = lax.ppermute(add(out_parts), axes, out_back)
    qkv_grad = qkv_pieces.reshape(M, k_rows, 3, LOCAL).transpose(1, 2, 0, 3).reshape(k_rows, 3 * D).astype(f32)
    text_grad = text_pieces.reshape(M, t_rows, 2, LOCAL).transpose(1, 2, 0, 3).reshape(t_rows, 2 * D).astype(f32)
    gate_up_grad = jnp.stack([add(gate_parts, 1), add(up_parts, 0)]).reshape(2, M, k_rows, sets, d_rows)
    gate_up_grad = gate_up_grad.transpose(2, 0, 3, 1, 4).reshape(k_rows, 2 * FF)
    return (
        result_rows[None],
        grad_latent[None],
        qkv_grad,
        text_grad,
        out_grad,
        gate_up_grad,
        down_grad,
        ada_grad,
        bias_grad,
        gains_grad,
        gates_grad,
    )


def solution(mesh):
    items, rows = mesh.shape["items"], mesh.shape["rows"]
    fine = Mesh(mesh.devices.reshape(items, rows // M, M), ("items", "times", "ring"))
    whole = ("items", "times", "ring")
    rows_of = ("times", "ring")
    return jax.shard_map(
        shards,
        mesh=fine,
        in_specs=(
            P("items", rows_of, None),
            P("items", None, None),
            P("items", None, None, None),
            P("items", rows_of, None),
            P("items", None),
            P(whole, None),
            P(whole, None),
            P(whole, None),
            P(whole, None),
            P(whole, None),
            P(whole, None),
            P(whole),
            P(None, whole),
            P(),
            P("items", rows_of, None),
        ),
        out_specs=(
            P("items", rows_of, None),
            P("items", rows_of, None),
            P(whole, None),
            P(whole, None),
            P(whole, None),
            P(whole, None),
            P(whole, None),
            P(whole, None),
            P(whole),
            P(None, whole),
            P(),
        ),
        check_vma=False,
    )
```

```python
import jax
import jax.numpy as jnp
import numpy as np
from jax import lax
from jax.experimental import pallas as pl
from jax.experimental.pallas import tpu as pltpu
from jax.sharding import Mesh
from jax.sharding import PartitionSpec as P

D = 1536
HEADS = 24
HEAD = 64
FF = 4096
TEXT_DIM = 4096
COND = 1024
TEXT = 256
FRAMES = 2
TOK = 128
GROUPS = 2
M = 8
LOCAL = HEADS // M * HEAD
ROWS = M * TOK
WIDE = 256
SPARE = 96
APART = 8192.0

epsilon = 1e-05
theta_base = 10000.0
highest = lax.Precision.HIGHEST
MESH = pl.DeviceIdType.MESH
f32 = jnp.float32
bf16 = jnp.bfloat16
ANY = pl.BlockSpec(memory_space=pl.ANY)
VMEM = pl.BlockSpec(memory_space=pltpu.VMEM)


def flip(where, mask):
    return tuple(a if b == 0 else a ^ b for a, b in zip(where, mask))


class Job:
    def __init__(self, x, shape, masks, src, dst, pass_on=(), by=None, source=None, piece=None):
        self.x, self.shape, self.masks, self.src, self.dst = x, shape, masks, src, dst
        self.piece = piece
        self.pass_on, self.by, self.source = tuple(pass_on), by, source
        if source is not None:
            self.x = None
        self.dtype = x.dtype

    def count(self):
        return len(self.masks) + len(self.pass_on)

    def block(self):
        return self.piece or self.shape[len(self.dst((0, 0, 0))) :]

    def peers(self):
        return set(self.masks) | ({self.by} if self.pass_on else set())


class Transfers:
    def __init__(self, jobs):
        self.jobs = jobs
        self.sent = [j for j in jobs if j.source is None]
        self.total = sum(j.count() for j in jobs)

    def operands(self):
        return [j.x for j in self.sent]

    def out_shapes(self):
        return [jax.ShapeDtypeStruct(j.shape, j.dtype) for j in self.jobs]

    def scratch(self):
        if not self.jobs:
            return []
        return [
            pltpu.SemaphoreType.DMA((self.total,)),
            pltpu.SemaphoreType.DMA((self.total,)),
            pltpu.SemaphoreType.DMA((2, len(self.jobs))),
        ] + [pltpu.VMEM(j.block(), j.dtype) for j in self.jobs]

    def peers(self):
        found = set()
        for j in self.jobs:
            found |= j.peers()
        return found

    def bind(self, me, ins, outs, sems):
        self.me, self.outs, self.sems = me, outs, sems
        left = list(ins)
        self.ins = []
        for j in self.jobs:
            self.ins.append(left.pop(0) if j.source is None else outs[self.jobs.index(j.source)])
        self.base, at = [], 0
        for j in self.jobs:
            self.base.append(at)
            at += j.count()
        self.arrived, self.kept, self.settled, self.chained, self.forwarded = set(), set(), set(), set(), set()

    def remote(self, src, dst, slot, dest):
        return pltpu.make_async_remote_copy(
            src_ref=src,
            dst_ref=dst,
            send_sem=self.sems[0].at[slot],
            recv_sem=self.sems[1].at[slot],
            device_id=dest,
            device_id_type=MESH,
        )

    def send(self, k, i):
        j = self.jobs[k]
        if i < len(j.masks):
            dest = flip(self.me, j.masks[i])
            at = j.src(dest)
            src = self.ins[k] if at is None else self.ins[k].at[at]
            return self.remote(src, self.outs[k].at[j.dst(self.me)], self.base[k] + i, dest)
        mask = j.pass_on[i - len(j.masks)]
        block = self.outs[k].at[j.dst(flip(self.me, mask))]
        return self.remote(block, block, self.base[k] + i, flip(self.me, j.by))

    def own(self, k, leg):
        j = self.jobs[k]
        room = self.sems[3 + k]
        if leg == 0:
            at = j.src(self.me)
            src = self.ins[k] if at is None else self.ins[k].at[at]
            return pltpu.make_async_copy(src, room, self.sems[2].at[0, k])
        return pltpu.make_async_copy(room, self.outs[k].at[j.dst(self.me)], self.sems[2].at[1, k])

    def start_job(self, k):
        j = self.jobs[k]
        for i in range(len(j.masks)):
            self.send(k, i).start()
        self.own(k, 0).start()

    def start(self, late=()):
        for k, j in enumerate(self.jobs):
            if j.source is None and k not in late:
                self.start_job(k)

    def receive(self, k, i):
        if (k, i) not in self.arrived:
            self.arrived.add((k, i))
            self.send(k, i).wait_recv()

    def take(self, k):
        self.keep(k)
        for i in range(self.jobs[k].count()):
            self.receive(k, i)
        if k not in self.settled:
            self.settled.add(k)
            self.own(k, 1).wait()

    def keep(self, k):
        if k not in self.kept:
            self.kept.add(k)
            self.own(k, 0).wait()
            self.own(k, 1).start()

    def chain(self, late=()):
        for k, j in enumerate(self.jobs):
            if j.source is not None and k not in self.chained and k not in late:
                self.chained.add(k)
                self.take(self.jobs.index(j.source))
                self.start_job(k)

    def forward(self):
        self.chain()
        for k in range(len(self.jobs)):
            self.keep(k)
        for k, j in enumerate(self.jobs):
            if k not in self.forwarded:
                self.forwarded.add(k)
                for n, mask in enumerate(j.pass_on):
                    self.receive(k, j.masks.index(mask))
                    self.send(k, len(j.masks) + n).start()

    def finish(self):
        self.forward()
        for k, j in enumerate(self.jobs):
            self.take(k)
            for i in range(j.count()):
                self.send(k, i).wait_send()


class Plan:
    def __init__(self, times):
        self.times = times
        self.sets = GROUPS * times
        self.rows = times * M
        self.next_id = 0
        ones = [(i, t, m) for i in range(GROUPS) for t in range(times) for m in range(M)]
        self.all = ones[1:]
        self.ring = [(0, 0, m) for m in range(1, M)]
        self.chips = [(0, 0, m) for m in range(2, M, 2)]
        self.mate = (0, 0, 1)
        self.time = [(0, t, 0) for t in range(1, times)]
        self.item = (1, 0, 0)
        self.span = [(i, t, 0) for i in range(GROUPS) for t in range(times)][1:]
        self.group = [(0, t, m) for t in range(times) for m in range(M)][1:]

    def identity(self):
        self.next_id += 1
        return self.next_id

    def set_of(self, where):
        return where[0] * self.times + where[1]

    def gather_ring(self, x):
        return Job(
            x,
            (M,) + x.shape,
            [self.mate] + self.chips,
            lambda dest: None,
            lambda sender: (sender[2],),
            self.chips,
            self.mate,
        )

    def direct_ring(self, x):
        return Job(x, (M,) + x.shape, self.ring, lambda dest: None, lambda sender: (sender[2],))

    def scatter_ring(self, x):
        return Job(x, x.shape, self.ring, lambda dest: (dest[2],), lambda sender: (sender[2],))

    def gather_span(self, x, shape=None, source=None):
        return Job(
            x,
            (self.sets,) + (x.shape if shape is None else shape),
            [self.item] + self.time,
            lambda dest: None,
            lambda sender: (self.set_of(sender),),
            self.time,
            self.item,
            source,
        )

    def scatter_span(self, x):
        return Job(x, x.shape, self.span, lambda dest: (self.set_of(dest),), lambda sender: (self.set_of(sender),))

    def gather_time(self, x):
        return Job(x, (self.times,) + x.shape, self.time, lambda dest: None, lambda sender: (sender[1],))

    def stack_time(self, x):
        n = x.shape[0]
        return Job(
            x,
            (self.times * n,) + x.shape[1:],
            self.time,
            lambda dest: None,
            lambda sender: (pl.ds(pl.multiple_of(sender[1] * n, n), n),),
            piece=x.shape,
        )

    def stack_item(self, x, source=None):
        shape = x.shape if source is None else source.shape
        n = shape[0]
        return Job(
            x,
            (GROUPS * n,) + shape[1:],
            [self.item],
            lambda dest: None,
            lambda sender: (pl.ds(pl.multiple_of(sender[0] * n, n), n),),
            source=source,
            piece=shape,
        )

    def split_time(self, x):
        n = x.shape[0] // self.times
        return Job(
            x,
            (self.times, n) + x.shape[1:],
            self.time,
            lambda dest: (pl.ds(pl.multiple_of(dest[1] * n, n), n),),
            lambda sender: (sender[1],),
        )

    def scatter_group_ring(self, x):
        return Job(
            x,
            (self.times,) + x.shape,
            self.group,
            lambda dest: (dest[2],),
            lambda sender: (sender[1], sender[2]),
        )

    def swap_source(self, source):
        return Job(
            source.x if source.x is not None else source,
            (GROUPS,) + source.shape,
            [self.item],
            lambda dest: None,
            lambda sender: (sender[0],),
            source=source,
        )

    def gather_time_source(self, source):
        return Job(
            source,
            (self.times,) + source.shape,
            self.time,
            lambda dest: None,
            lambda sender: (sender[1],),
            source=source,
        )

    def ring_of_times(self, x, source=None):
        shape = x.shape if source is None else source.shape
        return Job(
            x if source is None else source,
            (M, shape[0]) + tuple(shape[2:]),
            self.ring,
            lambda dest: (slice(None), dest[2]),
            lambda sender: (sender[2],),
            source=source,
        )

    def times_of_ring(self, x):
        shape = x.shape
        return Job(
            x,
            (shape[1], shape[0]) + tuple(shape[2:]),
            self.time,
            lambda dest: (slice(None), dest[1]),
            lambda sender: (sender[1],),
        )

    def scatter_time(self, x):
        return Job(x, x.shape, self.time, lambda dest: (dest[1],), lambda sender: (sender[1],))

    def scatter_item(self, x):
        return Job(x, x.shape, [self.item], lambda dest: (dest[0],), lambda sender: (sender[0],))

    def gather_all(self, x):
        return Job(
            x,
            (self.sets, M) + x.shape,
            self.all,
            lambda dest: None,
            lambda sender: (self.set_of(sender), sender[2]),
        )

    def scatter_all(self, x):
        return Job(
            x,
            x.shape,
            self.all,
            lambda dest: (self.set_of(dest), dest[2]),
            lambda sender: (self.set_of(sender), sender[2]),
        )

    def swap_item(self, x):
        return Job(x, (GROUPS,) + x.shape, [self.item], lambda dest: None, lambda sender: (sender[0],))

    def gather_group(self, x):
        return Job(
            x,
            (self.times, M) + x.shape,
            self.group,
            lambda dest: None,
            lambda sender: (sender[1], sender[2]),
        )

    def scatter_group(self, x):
        return Job(
            x,
            x.shape,
            self.group,
            lambda dest: (dest[1], dest[2]),
            lambda sender: (sender[1], sender[2]),
        )


def here():
    return (lax.axis_index("items"), lax.axis_index("times"), lax.axis_index("ring"))


def greet(me, peers):
    barrier = pltpu.get_barrier_semaphore()
    for mask in sorted(peers):
        pl.semaphore_signal(barrier, inc=1, device_id=flip(me, mask), device_id_type=MESH)
    pl.semaphore_wait(barrier, len(peers))


def exchange(plan, name, jobs):
    moves = Transfers(jobs)
    n_in, n_out = len(moves.sent), len(jobs)

    def kernel(*refs):
        me = here()
        greet(me, moves.peers())
        moves.bind(me, refs[:n_in], refs[n_in : n_in + n_out], refs[n_in + n_out :])
        moves.start()
        moves.finish()

    return pl.pallas_call(
        kernel,
        out_shape=moves.out_shapes(),
        in_specs=[ANY] * n_in,
        out_specs=[ANY] * n_out,
        scratch_shapes=moves.scratch(),
        name=name,
        compiler_params=pltpu.CompilerParams(
            collective_id=plan.identity(), has_side_effects=True, vmem_limit_bytes=32 * 2**20
        ),
    )(*moves.operands())


def lane_masks():
    lane = np.arange(WIDE)
    query, value = np.zeros((8, WIDE), np.float32), np.zeros((8, WIDE), np.float32)
    back = np.zeros((8, WIDE), np.float32)
    inner = lane % 128
    for h in range(LOCAL // HEAD):
        query[h] = ((inner < SPARE) & (inner // (HEAD // 2) == h)) | (lane == 128 + SPARE) | (lane == 129 + SPARE)
        query[h] += (lane >= 130 + SPARE + 3 * h) & (lane < 133 + SPARE + 3 * h)
        value[h] = ((lane >= HEAD) & (lane // HEAD - 1 == h)) | (lane // 16 == h)
        back[h] = ((lane >= HEAD) & (lane // HEAD - 1 == h)) | (lane == 2 * h) | (lane == 2 * h + 1)
    return query, value, back


def wide_order():
    col = np.arange(LOCAL)
    head, pair, odd = col // HEAD, col % HEAD // 2, col % 2
    return odd * 128 + head * (HEAD // 2) + pair, HEAD + col


def placing(places, width):
    return (jnp.asarray(places, jnp.int32)[:, None] == jnp.arange(width, dtype=jnp.int32)[None, :]).astype(bf16)


def widen(packed_ref, feature, key_ref, value_ref, rows):
    lane = lax.broadcasted_iota(jnp.int32, (rows, 128), 1)
    first, second = packed_ref[:, :128].astype(f32), packed_ref[:, 128:256].astype(f32)
    key_ref[:rows, :128] = jnp.where(lane < SPARE, first, 0.0).astype(bf16)
    key_ref[:rows, 128:] = jnp.where(lane < SPARE, second, feature.astype(f32)).astype(bf16)
    moved = jnp.where(lane < SPARE, pltpu.roll(first, 96, 1), second)
    value_ref[:rows, :128] = jnp.where(lane < HEAD, 1.0, moved).astype(bf16)
    value_ref[:rows, 128:] = packed_ref[:, 256:]


def pack(key_first, key_second, value_first, value_second, packed_ref, rows):
    lane = lax.broadcasted_iota(jnp.int32, (rows, 128), 1)
    packed_ref[:, :128] = jnp.where(lane < SPARE, key_first, pltpu.roll(value_first, 32, 1)).astype(bf16)
    packed_ref[:, 128:256] = jnp.where(lane < SPARE, key_second, value_first).astype(bf16)
    packed_ref[:, 256:] = value_second.astype(bf16)


def unpack(packed, rows):
    lane = lax.broadcasted_iota(jnp.int32, (rows, 128), 1)
    first, second = packed[:, :128].astype(f32), packed[:, 128:256].astype(f32)
    moved = jnp.where(lane < SPARE, pltpu.roll(first, 96, 1), second)
    return (
        jnp.where(lane < SPARE, first, 0.0),
        jnp.where(lane < SPARE, second, 0.0),
        jnp.where(lane < HEAD, 0.0, moved),
        packed[:, 256:].astype(f32),
    )


def fold_rows(values):
    ones = jnp.ones((8, WIDE), f32)
    sums = lax.dot_general(ones, values, (((1,), (1,)), ((), ())), precision=highest, preferred_element_type=f32)
    return jnp.concatenate([sums[0:1, 128 * i : 128 * (i + 1)] for i in range(values.shape[0] // 128)], axis=0)


def spread_rows(folded, out_ref):
    n = folded.shape[0]
    row = lax.broadcasted_iota(jnp.int32, (n, 128), 0)
    ones = jnp.ones((n, 128), f32)
    for i in range(n):
        out_ref[128 * i : 128 * (i + 1), :] = lax.dot_general(
            jnp.where(row == i, folded, 0.0),
            ones,
            (((0,), (0,)), ((), ())),
            precision=highest,
            preferred_element_type=f32,
        )


class Links:
    def __init__(self, me, send_sem, recv_sem):
        self.me, self.send_sem, self.recv_sem, self.used = me, send_sem, recv_sem, 0

    def __call__(self, src, dst, mask):
        slot = self.used
        self.used += 1
        return pltpu.make_async_remote_copy(
            src_ref=src,
            dst_ref=dst,
            send_sem=self.send_sem.at[slot],
            recv_sem=self.recv_sem.at[slot],
            device_id=flip(self.me, mask),
            device_id_type=MESH,
        )


def rows_at(index, count):
    return pl.ds(pl.multiple_of(index * count, count), count)


ASIDE, ABOVE = (0, 0, 2), (0, 0, 4)


def ring_sum(plan, link, me, buffers, product, meanwhile=lambda: None):
    to_mate, from_mate, to_chip, from_chip, part = buffers
    core, chip = me[2] % 2, me[2] // 2
    mates = [link(to_mate.at[d], from_mate.at[d], plan.mate) for d in range(4)]
    across = link(to_chip.at[2], from_chip.at[2], ASIDE)
    aside = link(to_chip.at[0], from_chip.at[0], ASIDE)
    above = link(to_chip.at[1], from_chip.at[1], ABOVE)
    for d in (3, 1, 2, 0):
        to_mate[d] = product((chip ^ d) * 2 + 1 - core).astype(bf16)
        mates[d].start()

    def both_cores(d):
        total = product((chip ^ d) * 2 + core)
        mates[d].wait_recv()
        return total + from_mate[d].astype(f32)

    to_chip[2] = both_cores(3).astype(bf16)
    across.start()
    to_chip[0] = both_cores(1).astype(bf16)
    aside.start()
    part[...] = both_cores(2)
    across.wait_recv()
    to_chip[1] = (part[...] + from_chip[2].astype(f32)).astype(bf16)
    above.start()
    part[...] = both_cores(0)
    meanwhile()
    aside.wait_recv()
    above.wait_recv()
    part[...] = part[...] + (from_chip[0].astype(f32) + from_chip[1].astype(f32))
    for copy in mates + [across, aside, above]:
        copy.wait_send()


def ring_gather(plan, link, me, all_ref, each, meanwhile=lambda: None, ready=lambda: None):
    ring = me[2]
    chip = ring // 2

    def block(place):
        return all_ref.at[rows_at(place, TOK)]

    mate = link(block(ring), block(ring), plan.mate)
    aside = link(block(ring), block(ring), ASIDE)
    above = link(block(ring), block(ring), ABOVE)
    for copy in (above, aside, mate):
        copy.start()
    meanwhile()
    later = []

    def hand_over(place):
        later.append(link(block(place), block(place), plan.mate))
        later[-1].start()

    above.wait_recv()
    onward = link(block(ring ^ 4), block(ring ^ 4), ASIDE)
    onward.start()
    hand_over(ring ^ 4)
    aside.wait_recv()
    hand_over(ring ^ 2)
    ready()
    mate.wait_recv()
    each(chip)
    later[0].wait_recv()
    each(chip ^ 2)
    later[1].wait_recv()
    each(chip ^ 1)
    onward.wait_recv()
    hand_over(ring ^ 6)
    later[2].wait_recv()
    each(chip ^ 3)
    for copy in [mate, aside, above, onward] + later:
        copy.wait_send()


def ring_share(plan, link, all_ref):
    copies = [link(all_ref.at[0], all_ref.at[i + 1], mask) for i, mask in enumerate(plan.ring)]
    for copy in copies:
        copy.start()
    return copies


def scale_of(values):
    return lax.rsqrt(jnp.mean(values * values, axis=1, keepdims=True) + epsilon)


def norm_back(d_hat, hat, inverse):
    return inverse * (d_hat - hat * jnp.mean(d_hat * hat, axis=1, keepdims=True))


RING_BUFFERS = [
    pltpu.VMEM((4, TOK, D), bf16),
    pltpu.VMEM((4, TOK, D), bf16),
    pltpu.VMEM((3, TOK, D), bf16),
    pltpu.VMEM((3, TOK, D), bf16),
    pltpu.VMEM((TOK, D), f32),
]


def params(plan, megabytes):
    return pltpu.CompilerParams(
        collective_id=plan.identity(), has_side_effects=True, vmem_limit_bytes=megabytes * 2**20
    )


def prologue(plan, tiles, package, cond, ada_weight, jobs):
    moves = Transfers([plan.gather_all(package)] + list(jobs))
    n_in, n_out = len(moves.sent), len(moves.jobs)
    total_tiles = 4 * D // 128
    peers, group = plan.all, plan.group

    def kernel(*refs):
        cond_ref, ada_ref = refs[:2]
        ins = refs[2 : 2 + n_in]
        mod_ref, cond_out = refs[2 + n_in : 4 + n_in]
        outs = refs[4 + n_in : 4 + n_in + n_out]
        refs = refs[4 + n_in + n_out :]
        cond_in, part_ref, send_ref, recv_ref, sum_ref, mod_in, send_sem, recv_sem = refs[:8]
        me = here()
        greet(me, moves.peers() | set(peers))
        link = Links(me, send_sem, recv_sem)
        swap = link(cond_ref.at[1], cond_in, plan.item)
        swap.start()
        moves.bind(me, ins, outs, refs[8:])
        moves.start()
        deep = ada_ref.shape[0]
        part_ref[0] = jnp.dot(cond_ref[0][:, :deep].astype(bf16), ada_ref[...], preferred_element_type=f32)
        swap.wait_recv()
        cond_out[...] = cond_in[...]
        part_ref[1] = jnp.dot(cond_in[:, :deep].astype(bf16), ada_ref[...], preferred_element_type=f32)
        for g in range(GROUPS):
            for r in range(plan.rows):
                for f in range(FRAMES):
                    for j in range(tiles):
                        tile = r * tiles + j
                        at = f * tiles + j
                        if tile < total_tiles:
                            send_ref[g, r, at : at + 1, :] = part_ref[g, f : f + 1, 128 * tile : 128 * (tile + 1)]
        copies = []
        for i, mask in enumerate(peers):
            dest = flip(me, mask)
            copies.append(link(send_ref.at[mask[0], dest[1] * M + dest[2]], recv_ref.at[i], mask))
            copies[-1].start()
        moves.chain()
        place = me[1] * M + me[2]
        total = send_ref[0, place]
        for i, copy in enumerate(copies):
            copy.wait_recv()
            total = total + recv_ref[i]
        sum_ref[...] = total
        mod_in[place] = total
        shares = [link(sum_ref, mod_in.at[place], mask) for mask in group]
        for copy in shares:
            copy.start()
        moves.forward()
        for copy in shares:
            copy.wait_recv()
        mod_ref[...] = mod_in[...]
        for copy in [swap] + copies + shares:
            copy.wait_send()
        moves.finish()

    links = 1 + len(peers) + len(group)
    result = pl.pallas_call(
        kernel,
        out_shape=[jax.ShapeDtypeStruct((plan.rows, 8, 128), f32), jax.ShapeDtypeStruct((8, 128), f32)]
        + moves.out_shapes(),
        in_specs=[VMEM] * 2 + [ANY] * n_in,
        out_specs=[VMEM] * 2 + [ANY] * n_out,
        scratch_shapes=[
            pltpu.VMEM((8, 128), f32),
            pltpu.VMEM((GROUPS, 8, 4 * D), f32),
            pltpu.VMEM((GROUPS, plan.rows, 8, 128), f32),
            pltpu.VMEM((len(peers), 8, 128), f32),
            pltpu.VMEM((8, 128), f32),
            pltpu.VMEM((plan.rows, 8, 128), f32),
            pltpu.SemaphoreType.DMA((links,)),
            pltpu.SemaphoreType.DMA((links,)),
        ]
        + moves.scratch(),
        name="prologue",
        compiler_params=params(plan, 40),
    )(cond, ada_weight, *moves.operands())
    return result[0], result[1], result[2:]


def attention_forward(
    plan,
    latents,
    modulation,
    gains,
    first_rows,
    captions,
    text_weight,
    mix,
    text_mix,
    gain_wide,
    cos,
    sin,
    query_features,
    features,
    text_features,
    gates,
    qkv_time,
    out_shard,
    gate_send,
    up_send,
):
    heads = LOCAL // HEAD
    text_rows = captions.shape[0]
    text_deep = text_weight.shape[0]
    others = len(plan.time)
    out_job = plan.gather_time(out_shard)
    gate_job = plan.scatter_ring(gate_send)
    gate_time = plan.gather_time_source(gate_job)
    jobs = [
        plan.stack_item(qkv_time),
        out_job,
        plan.swap_source(out_job),
        gate_job,
        plan.scatter_ring(up_send),
        gate_time,
        plan.swap_source(gate_time),
    ]
    moves = Transfers(jobs)
    n_in, n_out = len(moves.sent), len(moves.jobs)
    block = 256
    chip_rows = 2 * TOK
    span = text_deep // GROUPS
    folded = 2 * ROWS // 128 + text_rows // 128
    folded_rows = -(-folded // 8) * 8

    def kernel(*refs):
        (latent_ref, mod_ref, gain_ref, first_ref, caption_ref, text_w, mix_ref, text_mix_ref) = refs[:8]
        (wide_ref, cos_ref, sin_ref, qfeature_ref, feature_ref, text_feature_ref, gate_ref, qmask_ref, vmask_ref) = refs[8:17]
        ins = refs[17 : 17 + n_in]
        refs = refs[17 + n_in :]
        (mixed_ref, self_ref, cross_ref, attn_all, query_ref, packed_out, text_packed) = refs[:7]
        (qn_ref, kn_ref, qinv_ref, kinv_ref, tn_ref, tinv_ref) = refs[7:13]
        outs = refs[13 : 13 + n_out]
        refs = refs[13 + n_out :]
        (key_ref, value_ref, packed_ref, far_ref, max_ref, raw_w, weight_ref, raw_ref, own_caps, text_part, text_far) = refs[:11]
        (text_raw, sums_ref, send_sem, recv_sem, local_sem) = refs[11:16]
        me = here()
        item, time, ring = me
        greet(me, moves.peers() | {plan.mate} | set(plan.chips) | set(plan.ring) | set(plan.time))
        link = Links(me, send_sem, recv_sem)
        moves.bind(me, ins, outs, refs[16:])
        loads = []
        for i in range(GROUPS):
            where = pl.ds(pl.multiple_of((i * plan.times + time) * span, span), span)
            loads.append(
                pltpu.make_async_copy(caption_ref.at[:, where], own_caps.at[:, i * span : (i + 1) * span], local_sem.at[i])
            )
            loads[-1].start()

        is_first = first_ref[...] > 0.5
        scale = jnp.where(is_first, mod_ref[0:1, :D], mod_ref[1:2, :D])
        rows = latent_ref[...]
        attn_in = rows * scale_of(rows) * gain_ref[0:1, :] * (1.0 + scale)
        attn_all[rows_at(ring, TOK), :] = attn_in.astype(bf16)

        text_copies = [link(text_part, text_far.at[i], mask) for i, mask in enumerate(plan.time)]

        def text_projection():
            moves.start(late=(4,))
            for copy in loads:
                copy.wait()
            text_part[...] = jnp.dot(own_caps[...], text_w[...], preferred_element_type=f32).astype(bf16)
            for copy in text_copies:
                copy.start()

        def weights_here():
            moves.take(0)
            copy = pltpu.make_async_copy(outs[0], raw_w, local_sem.at[0])
            copy.start()
            copy.wait()
            weight_ref[...] = jnp.dot(raw_w[...], mix_ref[...], preferred_element_type=f32).astype(bf16)

        def project(which):
            where = rows_at(which, chip_rows)
            raw_ref[where, :] = jnp.dot(attn_all[where, :], weight_ref[...], preferred_element_type=f32)

        ring_gather(plan, link, me, attn_all, project, text_projection, weights_here)
        moves.start_job(4)
        moves.chain(late=(6,))

        total = text_part[...].astype(f32)
        for i, copy in enumerate(text_copies):
            copy.wait_recv()
            total = total + text_far[i].astype(f32)
        text_raw[...] = jnp.dot(total, text_mix_ref[...].astype(f32), precision=highest, preferred_element_type=f32)
        q_raw, k_raw, t_raw = raw_ref[:, :WIDE], raw_ref[:, WIDE : 2 * WIDE], text_raw[:, :WIDE]
        squares = [fold_rows(q_raw * q_raw), fold_rows(k_raw * k_raw), fold_rows(t_raw * t_raw)]
        if folded_rows > folded:
            squares.append(jnp.zeros((folded_rows - folded, 128), f32))
        sums_ref[0] = jnp.concatenate(squares, axis=0)
        shares = ring_share(plan, link, sums_ref)
        for copy in shares:
            copy.wait_recv()
        total = sums_ref[0]
        for i in range(1, M):
            total = total + sums_ref[i]
        inverse = lax.rsqrt(total / D + epsilon)
        n = ROWS // 128
        spread_rows(inverse[:n], qinv_ref)
        spread_rows(inverse[n : 2 * n], kinv_ref)
        spread_rows(inverse[2 * n : folded], tinv_ref)

        def turn(where, at, inv_ref, n_ref, gain_row):
            first = raw_ref[where, at : at + 128] * inv_ref[where, :]
            second = raw_ref[where, at + 128 : at + 256] * inv_ref[where, :]
            n_ref[where, :128], n_ref[where, 128:] = first, second
            first = first * wide_ref[gain_row : gain_row + 1, :128]
            second = second * wide_ref[gain_row : gain_row + 1, 128:]
            cosine, sine = cos_ref[where, :], sin_ref[where, :]
            return first * cosine - second * sine, second * cosine + first * sine

        def shape(at, carry):
            where = rows_at(at, block)
            first, second = turn(where, 0, qinv_ref, qn_ref, 0)
            query_ref[where, :128] = (first.astype(bf16).astype(f32) * 0.125).astype(bf16)
            lane = lax.broadcasted_iota(jnp.int32, (block, 128), 1)
            second = jnp.where(lane < SPARE, second.astype(bf16).astype(f32) * 0.125, qfeature_ref[where, :].astype(f32))
            query_ref[where, 128:] = second.astype(bf16)
            first, second = turn(where, WIDE, kinv_ref, kn_ref, 1)
            values = raw_ref[where, 2 * WIDE :]
            pack(first, second, values[:, :128], values[:, 128:], packed_ref.at[where, :], block)
            return carry

        lax.fori_loop(0, ROWS // block, shape, 0)
        key_copies = [link(packed_ref, far_ref.at[i], mask) for i, mask in enumerate(plan.time)]
        for copy in key_copies:
            copy.start()
        moves.chain()
        first = text_raw[:, :128] * tinv_ref[...]
        second = text_raw[:, 128:256] * tinv_ref[...]
        tn_ref[:, :128], tn_ref[:, 128:] = first, second
        pack(
            first * wide_ref[2:3, :128],
            second * wide_ref[2:3, 128:],
            text_raw[:, 256:384],
            text_raw[:, 384:],
            text_packed,
            text_rows,
        )

        def segment(rows, first, out_ref):
            def body(at, carry):
                where = rows_at(at, block)
                query_rows = query_ref[where, :]
                total = jnp.zeros((block, WIDE), f32)
                tops = jnp.zeros((block, WIDE), f32)
                for h in range(heads):
                    own_query = query_rows * qmask_ref[h : h + 1, :]
                    scores = lax.dot_general(
                        own_query, key_ref[:rows, :], (((1,), (1,)), ((), ())), preferred_element_type=f32
                    )
                    top = jnp.max(scores, axis=1, keepdims=True)
                    weights = jnp.exp(scores - top).astype(bf16)
                    product = jnp.dot(weights, value_ref[:rows, :], preferred_element_type=f32)
                    total += product * vmask_ref[h : h + 1, :]
                    tops += top * vmask_ref[h : h + 1, :]
                if first:
                    out_ref[where, :] = total
                    max_ref[where, :] = tops
                else:
                    before = max_ref[where, :]
                    after = jnp.maximum(before, tops)
                    out_ref[where, :] = out_ref[where, :] * jnp.exp(before - after) + total * jnp.exp(tops - after)
                    max_ref[where, :] = after
                return carry

            lax.fori_loop(0, ROWS // block, body, 0)

        def close(out_ref):
            def body(at, carry):
                where = rows_at(at, block)
                lane = lax.broadcasted_iota(jnp.int32, (block, WIDE), 1)
                values = out_ref[where, :]
                share = jnp.ones((block, WIDE), f32)
                for h in range(heads):
                    share = jnp.where(
                        (lane >= HEAD * (h + 1)) & (lane < HEAD * (h + 2)), values[:, 16 * h : 16 * h + 1], share
                    )
                logs = max_ref[where, :] + jnp.log(jnp.maximum(values, 1e-30))
                out_ref[where, :] = jnp.where(
                    lane < HEAD, jnp.where(lane < 16 * heads, logs, 0.0), values / share
                )
                return carry

            lax.fori_loop(0, ROWS // block, body, 0)

        widen(text_packed, text_feature_ref[...], key_ref, value_ref, text_rows)
        segment(text_rows, True, cross_ref)
        close(cross_ref)
        widen(packed_ref, feature_ref[rows_at(time, ROWS), :], key_ref, value_ref, ROWS)
        packed_out[time] = packed_ref[...]
        segment(ROWS, True, self_ref)
        for i, mask in enumerate(plan.time):
            key_copies[i].wait_recv()
            far = time ^ mask[1]
            packed_out[far] = far_ref[i]
            widen(far_ref.at[i], feature_ref[rows_at(far, ROWS), :], key_ref, value_ref, ROWS)
            segment(ROWS, False, self_ref)
        close(self_ref)
        lane = lax.broadcasted_iota(jnp.int32, (ROWS, WIDE), 1)
        both = self_ref[...] + gate_ref[...] * cross_ref[...]
        mixed_ref[...] = jnp.where(lane < HEAD, 0.0, both).astype(bf16)
        for copy in text_copies + shares + key_copies:
            copy.wait_send()
        moves.finish()

    qmask, vmask, _ = lane_masks()
    links = 7 + (M - 1) + 2 * others
    result = pl.pallas_call(
        kernel,
        out_shape=[
            jax.ShapeDtypeStruct((ROWS, WIDE), bf16),
            jax.ShapeDtypeStruct((ROWS, WIDE), f32),
            jax.ShapeDtypeStruct((ROWS, WIDE), f32),
            jax.ShapeDtypeStruct((ROWS, D), bf16),
            jax.ShapeDtypeStruct((ROWS, WIDE), bf16),
            jax.ShapeDtypeStruct((plan.times, ROWS, 2 * LOCAL), bf16),
            jax.ShapeDtypeStruct((text_rows, 2 * LOCAL), bf16),
            jax.ShapeDtypeStruct((ROWS, WIDE), f32),
            jax.ShapeDtypeStruct((ROWS, WIDE), f32),
            jax.ShapeDtypeStruct((ROWS, 128), f32),
            jax.ShapeDtypeStruct((ROWS, 128), f32),
            jax.ShapeDtypeStruct((text_rows, WIDE), f32),
            jax.ShapeDtypeStruct((text_rows, 128), f32),
        ]
        + moves.out_shapes(),
        in_specs=[VMEM] * 4 + [ANY] + [VMEM] * 12 + [ANY] * n_in,
        out_specs=[VMEM] * 13 + [ANY] * n_out,
        scratch_shapes=[
            pltpu.VMEM((ROWS, WIDE), bf16),
            pltpu.VMEM((ROWS, WIDE), bf16),
            pltpu.VMEM((ROWS, 2 * LOCAL), bf16),
            pltpu.VMEM((max(others, 1), ROWS, 2 * LOCAL), bf16),
            pltpu.VMEM((ROWS, WIDE), f32),
            pltpu.VMEM((D, 3 * LOCAL), bf16),
            pltpu.VMEM((D, 3 * WIDE), bf16),
            pltpu.VMEM((ROWS, 3 * WIDE), f32),
            pltpu.VMEM((text_rows, text_deep), bf16),
            pltpu.VMEM((text_rows, 2 * LOCAL), bf16),
            pltpu.VMEM((max(others, 1), text_rows, 2 * LOCAL), bf16),
            pltpu.VMEM((text_rows, 2 * WIDE), f32),
            pltpu.VMEM((M, folded_rows, 128), f32),
            pltpu.SemaphoreType.DMA((links,)),
            pltpu.SemaphoreType.DMA((links,)),
            pltpu.SemaphoreType.DMA((GROUPS,)),
        ]
        + moves.scratch(),
        name="attention_forward",
        compiler_params=params(plan, 60),
    )(
        latents,
        modulation,
        gains,
        first_rows,
        captions,
        text_weight,
        mix,
        text_mix,
        gain_wide,
        cos,
        sin,
        query_features,
        features,
        text_features,
        gates,
        jnp.asarray(qmask, bf16),
        jnp.asarray(vmask, f32),
        *moves.operands(),
    )
    return result[:13], result[13:]


def attention_backward(
    plan,
    query,
    packed_all,
    features,
    text_packed,
    text_features,
    self_out,
    cross_out,
    d_mixed,
    gates_q,
    gates_v,
    hats,
    inverses,
    text_hat,
    text_inverse,
    cos,
    sin,
    gain_wide,
    captions,
    attn_all,
    qkv_full,
    mix,
    text_mix,
    latents,
    d_state,
    modulation,
    gains,
    first_rows,
    gate_sum,
    up_sum,
    grad_out,
):
    heads = LOCAL // HEAD
    text_rows = text_packed.shape[0]
    gate_job = plan.scatter_time(gate_sum)
    up_job = plan.ring_of_times(up_sum)
    jobs = [gate_job, plan.ring_of_times(None, gate_job), up_job, plan.scatter_span(grad_out)]
    moves = Transfers(jobs)
    n_in, n_out = len(moves.sent), len(moves.jobs)
    block = 256
    others = len(plan.time)
    room = max(others, 1)
    turned = (((1,), (1,)), ((), ()))
    sunk = (((0,), (0,)), ((), ()))
    local3 = qkv_full.shape[1]
    text_deep = captions.shape[1] // plan.times
    span = text_deep // GROUPS
    set_rows = D // plan.sets
    half = set_rows // 2
    folded = 2 * ROWS // 128
    text_folded = max(8, text_rows // 128)

    def kernel(*refs):
        (query_ref, packed_in, feature_ref, text_ref, text_feature_ref, self_ref, cross_ref, d_ref) = refs[:8]
        (gateq_ref, gatev_ref, qmask_ref, bmask_ref, qn_ref, kn_ref, qinv_ref, kinv_ref, tn_ref, tinv_ref) = refs[8:18]
        (cos_ref, sin_ref, wide_ref, caption_ref, attn_ref, qkv_w, mix_ref, text_mix_ref) = refs[18:26]
        (latent_ref, d_state_ref, mod_ref, gain_ref, first_ref) = refs[26:31]
        ins = refs[31 : 31 + n_in]
        refs = refs[31 + n_in :]
        latent_grad, sums_out, wide_out, qkv_out, text_out = refs[:5]
        outs = refs[5 : 5 + n_out]
        refs = refs[5 + n_out :]
        (key_ref, value_ref, near_ref, qs_ref, ds_ref, dq_ref, dk_ref, dv_ref, tdk_ref, tdv_ref) = refs[:10]
        (to_ref, from_ref, tto_ref, tfrom_ref, du_ref, d_text, own_caps, grad_qkv, grad_text) = refs[10:19]
        (a_item, a_sum, a_time, b_time, b_sum, b_item, text_item, share_ref, tshare_ref, mean_ref) = refs[19:29]
        buffers = refs[29:34]
        send_sem, recv_sem, local_sem = refs[34:37]
        me = here()
        item, time, ring = me
        greet(me, moves.peers() | set(plan.time) | set(plan.ring) | {plan.item})
        link = Links(me, send_sem, recv_sem)
        moves.bind(me, ins, outs, refs[37:])
        moves.start(late=(3,))
        loads = []
        for i in range(GROUPS):
            where = pl.ds(pl.multiple_of((i * plan.times + time) * span, span), span)
            loads.append(
                pltpu.make_async_copy(
                    caption_ref.at[:, where], own_caps.at[:, i * span : (i + 1) * span], local_sem.at[1 + i]
                )
            )
            loads[-1].start()

        def prepare(out_ref):
            def body(at, carry):
                where = rows_at(at, block)
                lane = lax.broadcasted_iota(jnp.int32, (block, 128), 1)
                tail = query_ref[where, 128:].astype(f32)
                out_rows = out_ref[where, :]
                d_rows = d_ref[where, :].astype(f32)
                product = d_rows * out_rows
                head_tile = jnp.where(lane < HEAD, 0.0, d_rows[:, :128])
                for h in range(heads):
                    log = -out_rows[:, 16 * h : 16 * h + 1]
                    for j in range(3):
                        piece = log.astype(bf16).astype(f32)
                        log = log - piece
                        tail = jnp.where(lane == SPARE + 2 + 3 * h + j, piece, tail)
                    delta = -jnp.sum(product * bmask_ref[h : h + 1, :].astype(f32), axis=1, keepdims=True)
                    for j in range(2):
                        piece = delta.astype(bf16).astype(f32)
                        delta = delta - piece
                        head_tile = jnp.where(lane == 2 * h + j, piece, head_tile)
                qs_ref[where, :128] = query_ref[where, :128]
                qs_ref[where, 128:] = tail.astype(bf16)
                ds_ref[where, :128] = head_tile.astype(bf16)
                ds_ref[where, 128:] = d_ref[where, 128:]
                return carry

            lax.fori_loop(0, ROWS // block, body, 0)

        def segment(rows, first, k_ref, v_ref, scale):
            k_ref[...] = jnp.zeros_like(k_ref)
            v_ref[...] = jnp.zeros_like(v_ref)

            def body(at, carry):
                where = rows_at(at, block)
                query_rows, d_rows = qs_ref[where, :], ds_ref[where, :]
                total = jnp.zeros((block, WIDE), f32)
                for h in range(heads):
                    own_query = query_rows * qmask_ref[h : h + 1, :]
                    own_d = d_rows * bmask_ref[h : h + 1, :]
                    keys = key_ref[:rows, :]
                    weights = jnp.exp(lax.dot_general(keys, own_query, turned, preferred_element_type=f32))
                    d_weights = lax.dot_general(value_ref[:rows, :], own_d, turned, preferred_element_type=f32)
                    d_scores = (weights * d_weights).astype(bf16)
                    v_ref[...] += jnp.dot(weights.astype(bf16), own_d, preferred_element_type=f32)
                    k_ref[...] += jnp.dot(d_scores, own_query, preferred_element_type=f32)
                    d_query = lax.dot_general(d_scores, keys, sunk, preferred_element_type=f32)
                    total += d_query * qmask_ref[h : h + 1, :].astype(f32)
                total = total * scale
                if first:
                    dq_ref[where, :] = total
                else:
                    dq_ref[where, :] += total
                return carry

            lax.fori_loop(0, ROWS // block, body, 0)

        def bring(which):
            copy = pltpu.make_async_copy(packed_in.at[which], near_ref, local_sem.at[0])
            copy.start()
            copy.wait()
            widen(near_ref, feature_ref[rows_at(which, ROWS), :], key_ref, value_ref, ROWS)

        far_copies = [link(to_ref.at[i], from_ref.at[i], mask) for i, mask in enumerate(plan.time)]
        text_copies = [link(tto_ref, tfrom_ref.at[i], mask) for i, mask in enumerate(plan.time)]

        prepare(self_ref)
        for i, mask in enumerate(plan.time):
            bring(time ^ mask[1])
            segment(ROWS, i == 0, dk_ref, dv_ref, 0.125)
            pack(dk_ref[:, :128], dk_ref[:, 128:], dv_ref[:, :128], dv_ref[:, 128:], to_ref.at[i], ROWS)
            far_copies[i].start()
        moves.chain()
        bring(time)
        segment(ROWS, others == 0, dk_ref, dv_ref, 0.125)
        prepare(cross_ref)
        widen(text_ref, text_feature_ref[...], key_ref, value_ref, text_rows)
        segment(text_rows, False, tdk_ref, tdv_ref, 0.125 * gateq_ref[...])
        tdk_ref[...] = tdk_ref[...] * gateq_ref[...]
        tdv_ref[...] = tdv_ref[...] * gatev_ref[...]
        pack(tdk_ref[:, :128], tdk_ref[:, 128:], tdv_ref[:, :128], tdv_ref[:, 128:], tto_ref, text_rows)
        for copy in text_copies:
            copy.start()
        wide_out[...] = jnp.zeros_like(wide_out)
        wide_out[3:4, :] = jnp.sum(d_ref[...].astype(f32) * cross_ref[...], axis=0, keepdims=True)
        for i in range(others):
            far_copies[i].wait_recv()
            k_first, k_second, v_first, v_second = unpack(from_ref.at[i], ROWS)
            dk_ref[:, :128] += k_first
            dk_ref[:, 128:] += k_second
            dv_ref[:, :128] += v_first
            dv_ref[:, 128:] += v_second

        moves.start_job(3)

        def unturn(d_all, hat_ref, gain_row):
            pieces = []
            for at in range(ROWS // block):
                where = slice(at * block, (at + 1) * block)
                first, second = d_all[where, :128], d_all[where, 128:]
                cosine, sine = cos_ref[where, :], sin_ref[where, :]
                lane = lax.broadcasted_iota(jnp.int32, (block, 128), 1)
                first, second = jnp.where(lane < SPARE, first, 0.0), jnp.where(lane < SPARE, second, 0.0)
                both = jnp.concatenate([first * cosine + second * sine, second * cosine - first * sine], axis=1)
                hat = hat_ref[where, :]
                wide_out[gain_row : gain_row + 1, :] += jnp.sum(both * hat, axis=0, keepdims=True)
                both = both * wide_ref[gain_row : gain_row + 1, :]
                d_all[where, :] = both
                pieces.append(fold_rows(both * hat))
            return pieces

        pieces = unturn(dq_ref, qn_ref, 0) + unturn(dk_ref, kn_ref, 1)
        share_ref[0] = jnp.concatenate(pieces, axis=0)
        shares = ring_share(plan, link, share_ref)
        for copy in shares:
            copy.wait_recv()
        total = share_ref[0]
        for i in range(1, M):
            total = total + share_ref[i]
        total = total / D
        n = ROWS // 128

        def settle(d_all, hat_ref, inv_ref, means):
            spread_rows(means, mean_ref)
            for c in (0, 128):
                lanes = slice(c, c + 128)
                d_all[:, lanes] = (d_all[:, lanes] - hat_ref[:, lanes] * mean_ref[...]) * inv_ref[...]

        settle(dq_ref, qn_ref, qinv_ref, total[:n])
        settle(dk_ref, kn_ref, kinv_ref, total[n:])
        for at in range(ROWS // block):
            where = slice(at * block, (at + 1) * block)
            lane = lax.broadcasted_iota(jnp.int32, (block, 128), 1)
            values = jnp.concatenate([jnp.where(lane < HEAD, 0.0, dv_ref[where, :128]), dv_ref[where, 128:]], axis=1)
            wide = jnp.concatenate([dq_ref[where, :], dk_ref[where, :], values], axis=1).astype(bf16)
            du_ref[where, :] = lax.dot_general(wide, mix_ref[...], turned, preferred_element_type=f32).astype(bf16)

        away = 1 - item

        def part(i, t, which):
            return pl.ds(pl.multiple_of((i * plan.times + t) * set_rows + which * half, half), half)

        a_items = [link(grad_qkv.at[part(away, t, 0)], a_item.at[t], plan.item) for t in range(plan.times)]
        b_times = [
            link(grad_qkv.at[part(i, time ^ mask[1], 1)], b_time.at[k, i], mask)
            for k, mask in enumerate(plan.time)
            for i in range(GROUPS)
        ]
        a_times = [link(a_sum.at[time ^ mask[1]], a_time.at[k], mask) for k, mask in enumerate(plan.time)]
        b_items = [link(b_sum.at[away], b_item, plan.item)]
        text_items = [link(grad_text.at[rows_at(away, span)], text_item, plan.item)]

        def meanwhile():
            grad_qkv[...] = lax.dot_general(attn_ref[...], du_ref[...], sunk, preferred_element_type=f32).astype(bf16)
            for copy in a_items + b_times:
                copy.start()
            for i, copy in enumerate(text_copies):
                copy.wait_recv()
                k_first, k_second, v_first, v_second = unpack(tfrom_ref.at[i], text_rows)
                tdk_ref[:, :128] += k_first
                tdk_ref[:, 128:] += k_second
                tdv_ref[:, :128] += v_first
                tdv_ref[:, 128:] += v_second
            lane = lax.broadcasted_iota(jnp.int32, (text_rows, WIDE), 1) % 128
            d_keys = jnp.where(lane < SPARE, tdk_ref[...], 0.0)
            hat = tn_ref[...]
            wide_out[2:3, :] = jnp.sum(d_keys * hat, axis=0, keepdims=True)
            d_keys = d_keys * wide_ref[2:3, :]
            tdk_ref[...] = d_keys
            sums = fold_rows(d_keys * hat)
            if text_folded > text_rows // 128:
                sums = jnp.concatenate([sums, jnp.zeros((text_folded - text_rows // 128, 128), f32)], axis=0)
            tshare_ref[0] = sums
            text_shares = ring_share(plan, link, tshare_ref)
            for t, copy in enumerate(a_items):
                copy.wait_recv()
                a_sum[t] = (grad_qkv[part(item, t, 0), :].astype(f32) + a_item[t].astype(f32)).astype(bf16)
            for copy in a_times:
                copy.start()
            for copy in text_shares:
                copy.wait_recv()
            total = tshare_ref[0]
            for i in range(1, M):
                total = total + tshare_ref[i]
            total = total / D
            spread_rows(total[: text_rows // 128], mean_ref.at[:text_rows])
            for c in (0, 128):
                lanes = slice(c, c + 128)
                tdk_ref[:, lanes] = (tdk_ref[:, lanes] - tn_ref[:, lanes] * mean_ref[:text_rows, :]) * tinv_ref[...]
            lane = lax.broadcasted_iota(jnp.int32, (text_rows, WIDE), 1)
            values = jnp.where(lane < HEAD, 0.0, tdv_ref[...])
            wide = jnp.concatenate([tdk_ref[...], values], axis=1).astype(bf16)
            d_text[...] = lax.dot_general(wide, text_mix_ref[...], turned, preferred_element_type=f32).astype(bf16)
            for copy in loads:
                copy.wait()
            grad_text[...] = lax.dot_general(own_caps[...], d_text[...], sunk, preferred_element_type=f32).astype(bf16)
            text_items[0].start()
            for copy in text_shares:
                copy.wait_send()
            for copy in b_times:
                copy.wait_recv()
            for i in range(GROUPS):
                total = grad_qkv[part(i, time, 1), :].astype(f32)
                for k in range(others):
                    total = total + b_time[k, i].astype(f32)
                b_sum[i] = total.astype(bf16)
            b_items[0].start()

        def back_product(which):
            return lax.dot_general(du_ref[rows_at(which, TOK), :], qkv_w[...], turned, preferred_element_type=f32)

        ring_sum(plan, link, me, buffers, back_product, meanwhile)

        d_in = buffers[4][...]
        rows = latent_ref[...]
        inverse = scale_of(rows)
        hat = rows * inverse
        gain = gain_ref[0:1, :]
        is_first = first_ref[...] > 0.5
        scale = jnp.where(is_first, mod_ref[0:1, :D], mod_ref[1:2, :D])
        sums_out[...] = jnp.zeros_like(sums_out)
        values = d_in * (hat * gain)
        total = jnp.sum(values, axis=0, keepdims=True)
        start = jnp.sum(jnp.where(is_first, values, 0.0), axis=0, keepdims=True)
        sums_out[1:2, :] = start
        sums_out[2:3, :] = total - start
        d_norm = d_in * (1.0 + scale)
        sums_out[0:1, :] = jnp.sum(d_norm * hat, axis=0, keepdims=True)
        latent_grad[...] = d_state_ref[...] + norm_back(d_norm * gain, hat, inverse)

        total = a_sum[time].astype(f32)
        for k, copy in enumerate(a_times):
            copy.wait_recv()
            total = total + a_time[k].astype(f32)
        qkv_out[:half, :] = total.astype(bf16)
        b_items[0].wait_recv()
        qkv_out[half:, :] = (b_sum[item].astype(f32) + b_item[...].astype(f32)).astype(bf16)
        text_items[0].wait_recv()
        text_out[...] = (grad_text[rows_at(item, span), :].astype(f32) + text_item[...].astype(f32)).astype(bf16)
        for copy in far_copies + text_copies + shares + a_items + b_times + a_times + b_items + text_items:
            copy.wait_send()
        moves.finish()

    qmask, _, bmask = lane_masks()
    links = 2 * others + 2 * (M - 1) + plan.times + GROUPS * others + others + 2 + 7
    result = pl.pallas_call(
        kernel,
        out_shape=[
            jax.ShapeDtypeStruct((TOK, D), f32),
            jax.ShapeDtypeStruct((8, D), f32),
            jax.ShapeDtypeStruct((8, WIDE), f32),
            jax.ShapeDtypeStruct((set_rows, local3), bf16),
            jax.ShapeDtypeStruct((span, 2 * LOCAL), bf16),
        ]
        + moves.out_shapes(),
        in_specs=[VMEM, ANY] + [VMEM] * 19 + [ANY] + [VMEM] * 9 + [ANY] * n_in,
        out_specs=[VMEM] * 5 + [ANY] * n_out,
        scratch_shapes=[
            pltpu.VMEM((ROWS, WIDE), bf16),
            pltpu.VMEM((ROWS, WIDE), bf16),
            pltpu.VMEM((ROWS, 2 * LOCAL), bf16),
            pltpu.VMEM((ROWS, WIDE), bf16),
            pltpu.VMEM((ROWS, WIDE), bf16),
            pltpu.VMEM((ROWS, WIDE), f32),
            pltpu.VMEM((ROWS, WIDE), f32),
            pltpu.VMEM((ROWS, WIDE), f32),
            pltpu.VMEM((text_rows, WIDE), f32),
            pltpu.VMEM((text_rows, WIDE), f32),
            pltpu.VMEM((room, ROWS, 2 * LOCAL), bf16),
            pltpu.VMEM((room, ROWS, 2 * LOCAL), bf16),
            pltpu.VMEM((text_rows, 2 * LOCAL), bf16),
            pltpu.VMEM((room, text_rows, 2 * LOCAL), bf16),
            pltpu.VMEM((ROWS, local3), bf16),
            pltpu.VMEM((text_rows, 2 * LOCAL), bf16),
            pltpu.VMEM((text_rows, text_deep), bf16),
            pltpu.VMEM((D, local3), bf16),
            pltpu.VMEM((text_deep, 2 * LOCAL), bf16),
            pltpu.VMEM((plan.times, half, local3), bf16),
            pltpu.VMEM((plan.times, half, local3), bf16),
            pltpu.VMEM((room, half, local3), bf16),
            pltpu.VMEM((room, GROUPS, half, local3), bf16),
            pltpu.VMEM((GROUPS, half, local3), bf16),
            pltpu.VMEM((half, local3), bf16),
            pltpu.VMEM((span, 2 * LOCAL), bf16),
            pltpu.VMEM((M, folded, 128), f32),
            pltpu.VMEM((M, text_folded, 128), f32),
            pltpu.VMEM((ROWS, 128), f32),
        ]
        + RING_BUFFERS
        + [
            pltpu.SemaphoreType.DMA((links,)),
            pltpu.SemaphoreType.DMA((links,)),
            pltpu.SemaphoreType.DMA((1 + GROUPS,)),
        ]
        + moves.scratch(),
        name="attention_backward",
        compiler_params=params(plan, 63),
    )(
        query,
        packed_all,
        features,
        text_packed,
        text_features,
        self_out,
        cross_out,
        d_mixed,
        gates_q,
        gates_v,
        jnp.asarray(qmask, bf16),
        jnp.asarray(bmask, bf16),
        *hats,
        *inverses,
        text_hat,
        text_inverse,
        cos,
        sin,
        gain_wide,
        captions,
        attn_all,
        qkv_full,
        mix,
        text_mix,
        latents,
        d_state,
        modulation,
        gains,
        first_rows,
        *moves.operands(),
    )
    return result[:5], result[5:]


def finish(plan, small, jobs):
    moves = Transfers(list(jobs))
    n_in, n_out = len(moves.sent), len(moves.jobs)
    peers = plan.all

    def kernel(*refs):
        small_ref = refs[0]
        ins = refs[1 : 1 + n_in]
        all_ref = refs[1 + n_in]
        outs = refs[2 + n_in : 2 + n_in + n_out]
        recv_ref, sum_ref, all_in, send_sem, recv_sem = refs[2 + n_in + n_out : 7 + n_in + n_out]
        me = here()
        greet(me, moves.peers() | set(peers))
        link = Links(me, send_sem, recv_sem)
        moves.bind(me, ins, outs, refs[7 + n_in + n_out :])
        copies = []
        for i, mask in enumerate(peers):
            dest = flip(me, mask)
            copies.append(link(small_ref.at[plan.set_of(dest), dest[2]], recv_ref.at[i], mask))
            copies[-1].start()
        moves.start()
        own = small_ref[plan.set_of(me), me[2]]
        group, everyone = own[:8], own[8:]
        for i, mask in enumerate(peers):
            copies[i].wait_recv()
            if mask[0] == 0:
                group = group + recv_ref[i, :8, :]
            everyone = everyone + recv_ref[i, 8:, :]
        sum_ref[:8, :] = group
        sum_ref[8:, :] = everyone
        place = plan.set_of(me) * M + me[2]
        shares = [link(sum_ref, all_in.at[place], mask) for mask in peers]
        for copy in shares:
            copy.start()
        all_in[place] = sum_ref[...]
        for copy in shares:
            copy.wait_recv()
        all_ref[...] = all_in[...]
        for copy in copies + shares:
            copy.wait_send()
        moves.finish()

    devices = plan.sets * M
    result = pl.pallas_call(
        kernel,
        out_shape=[jax.ShapeDtypeStruct((devices, 16, 128), f32)] + moves.out_shapes(),
        in_specs=[VMEM] + [ANY] * n_in,
        out_specs=[VMEM] + [ANY] * n_out,
        scratch_shapes=[
            pltpu.VMEM((len(peers), 16, 128), f32),
            pltpu.VMEM((16, 128), f32),
            pltpu.VMEM((devices, 16, 128), f32),
            pltpu.SemaphoreType.DMA((2 * len(peers),)),
            pltpu.SemaphoreType.DMA((2 * len(peers),)),
        ]
        + moves.scratch(),
        name="finish",
        compiler_params=params(plan, 40),
    )(small, *moves.operands())
    return result[0], result[1:]


def feed_forward(
    plan, mixed, out_full, latents, cotangent, modulation, gains, first_rows, gate_full, up_shard, down_weight
):
    d_rows = down_weight.shape[0]
    width = plan.sets * d_rows
    deep = out_full.shape[0]
    up_job = plan.stack_time(up_shard)
    down_job = plan.stack_time(down_weight)
    moves = Transfers(
        [up_job, plan.stack_item(up_shard, up_job), down_job, plan.stack_item(down_weight, down_job)]
    )
    n_in, n_out = len(moves.sent), len(moves.jobs)
    turned = (((1,), (1,)), ((), ()))
    sunk = (((0,), (0,)), ((), ()))
    plain = (((1,), (0,)), ((), ()))
    chip_rows = 2 * TOK
    part_rows = D // GROUPS
    others = len(plan.time)
    slab = plan.times * d_rows

    def kernel(*refs):
        (mixed_ref, out_w, latent_ref, cot_ref, mod_ref, gain_ref, first_ref, gate_w) = refs[:8]
        ins = refs[8 : 8 + n_in]
        refs = refs[8 + n_in :]
        (result_ref, d_state_ref, d_mixed_ref, grad_out_ref, gate_sum_ref, up_sum_ref, down_grad_ref, sums_ref) = refs[:8]
        outs = refs[8 : 8 + n_out]
        refs = refs[8 + n_out :]
        (up_w, down_w, ffn_all, down_all, proj_all, gate_ref, up_ref, act_ref, d_gate_ref, d_up_ref) = refs[:10]
        (grad_gate, grad_up, grad_down, from_gate, from_up, from_down, down_sum, from_time) = refs[10:18]
        (to_mate, from_mate, to_chip, from_chip, part, proj_ref, state_ref, own_ref, send_sem, recv_sem, local_sem) = refs[
            18:29
        ]
        me = here()
        item, time, ring = me
        core, chip = ring % 2, ring // 2
        greet(me, moves.peers() | {plan.mate, plan.item} | set(plan.chips) | set(plan.time))
        moves.bind(me, ins, outs, refs[29:])
        moves.start(late=(2,))
        link = Links(me, send_sem, recv_sem)
        buffers = (to_mate, from_mate, to_chip, from_chip, part)

        def scatter(product, meanwhile=lambda: None):
            ring_sum(plan, link, me, buffers, product, meanwhile)

        def gather(all_ref, each, meanwhile=lambda: None, ready=lambda: None):
            ring_gather(plan, link, me, all_ref, each, meanwhile, ready)

        is_first = first_ref[...] > 0.5

        def modulated(index):
            cols = pl.ds(index * D, D)
            return jnp.where(is_first, mod_ref[0:1, cols], mod_ref[1:2, cols])

        def column_sums(at, values):
            total = jnp.sum(values, axis=0, keepdims=True)
            start = jnp.sum(jnp.where(is_first, values, 0.0), axis=0, keepdims=True)
            sums_ref[at : at + 1, :] = start
            sums_ref[at + 1 : at + 2, :] = total - start

        def scale_of(values):
            return lax.rsqrt(jnp.mean(values * values, axis=1, keepdims=True) + epsilon)

        def norm_back(d_hat, hat, inverse):
            return inverse * (d_hat - hat * jnp.mean(d_hat * hat, axis=1, keepdims=True))

        def load(job, target):
            moves.take(job)
            copy = pltpu.make_async_copy(outs[job], target, local_sem.at[0])
            copy.start()
            copy.wait()

        def out_product(block):
            return jnp.dot(mixed_ref[rows_at(block, TOK), :], out_w[...], preferred_element_type=f32)

        def next_weights():
            moves.chain(late=(3,))
            moves.start_job(2)

        scatter(out_product, next_weights)
        proj_ref[...] = part[...]
        proj = proj_ref[...]
        gate_attn = jnp.tanh(modulated(1))
        state_ref[...] = latent_ref[...] + gate_attn * (proj * scale_of(proj) * gain_ref[1:2, :])
        state = state_ref[...]
        ffn_in = state * scale_of(state) * gain_ref[2:3, :] * (1.0 + modulated(2))
        ffn_all[rows_at(ring, TOK), :] = ffn_in.astype(bf16)

        def forward_chip(which):
            rows = rows_at(which, chip_rows)
            block = ffn_all[rows, :]
            gate = jnp.dot(block, gate_w[...], preferred_element_type=f32)
            up = jnp.dot(block, up_w[...], preferred_element_type=f32)
            gate_ref[rows, :] = gate
            up_ref[rows, :] = up
            act_ref[rows, :] = (gate * (1.0 / (1.0 + jnp.exp(-gate))) * up).astype(bf16)

        def weights_here():
            load(1, up_w)

        gather(ffn_all, forward_chip, moves.chain, weights_here)

        load(3, down_w)

        def down_product(block):
            return jnp.dot(act_ref[rows_at(block, TOK), :], down_w[...], preferred_element_type=f32)

        scatter(down_product)

        down = part[...]
        inverse = scale_of(down)
        hat = down * inverse
        gate_ffn = jnp.tanh(modulated(3))
        gain = gain_ref[3:4, :]
        cot = cot_ref[...]
        result_ref[...] = state_ref[...] + gate_ffn * (hat * gain)
        column_sums(7, cot * (hat * gain) * (1.0 - gate_ffn * gate_ffn))
        d_norm = cot * gate_ffn
        sums_ref[2:3, :] = jnp.sum(d_norm * hat, axis=0, keepdims=True)
        down_all[rows_at(ring, TOK), :] = norm_back(d_norm * gain, hat, inverse).astype(bf16)

        def backward_chip(which):
            rows = rows_at(which, chip_rows)
            d_act = lax.dot_general(down_all[rows, :], down_w[...], turned, preferred_element_type=f32)
            gate, up = gate_ref[rows, :], up_ref[rows, :]
            sigmoid = 1.0 / (1.0 + jnp.exp(-gate))
            d_up_ref[rows, :] = (d_act * (gate * sigmoid)).astype(bf16)
            d_gate_ref[rows, :] = (d_act * up * (sigmoid * (1.0 + gate * (1.0 - sigmoid)))).astype(bf16)

        gather(down_all, backward_chip)

        away = 1 - item
        down_link = link(grad_down.at[rows_at(away, slab)], from_down, plan.item)
        gate_link = link(grad_gate.at[rows_at(away, part_rows)], from_gate, plan.item)
        up_link = link(grad_up.at[rows_at(away, part_rows)], from_up, plan.item)
        time_links = [link(down_sum.at[rows_at(time ^ mask[1], d_rows)], from_time.at[i], mask) for i, mask in enumerate(plan.time)]

        def down_gradient():
            grad_down[...] = lax.dot_general(act_ref[...], down_all[...], sunk, preferred_element_type=f32).astype(bf16)
            down_link.start()

        down_gradient()

        def gate_gradients():
            grad_gate[...] = lax.dot_general(ffn_all[...], d_gate_ref[...], sunk, preferred_element_type=f32).astype(bf16)
            gate_link.start()
            grad_up[...] = lax.dot_general(ffn_all[...], d_up_ref[...], sunk, preferred_element_type=f32).astype(bf16)
            up_link.start()

        def back_product(block):
            rows = rows_at(block, TOK)
            return lax.dot_general(d_gate_ref[rows, :], gate_w[...], turned, preferred_element_type=f32) + lax.dot_general(
                d_up_ref[rows, :], up_w[...], turned, preferred_element_type=f32
            )

        scatter(back_product, gate_gradients)

        d_ffn = part[...]
        state = state_ref[...]
        inverse = scale_of(state)
        hat = state * inverse
        gain = gain_ref[2:3, :]
        column_sums(5, d_ffn * (hat * gain))
        d_norm = d_ffn * (1.0 + modulated(2))
        sums_ref[1:2, :] = jnp.sum(d_norm * hat, axis=0, keepdims=True)
        d_state_ref[...] = cot_ref[...] + norm_back(d_norm * gain, hat, inverse)
        d_state = d_state_ref[...]
        proj = proj_ref[...]
        inverse = scale_of(proj)
        hat = proj * inverse
        gate_attn = jnp.tanh(modulated(1))
        gain = gain_ref[1:2, :]
        column_sums(3, d_state * (hat * gain) * (1.0 - gate_attn * gate_attn))
        d_norm = d_state * gate_attn
        sums_ref[0:1, :] = jnp.sum(d_norm * hat, axis=0, keepdims=True)
        proj_all[rows_at(ring, TOK), :] = norm_back(d_norm * gain, hat, inverse).astype(bf16)

        def down_time():
            down_link.wait_recv()
            mine = grad_down[rows_at(item, slab), :].astype(f32) + from_down[...].astype(f32)
            down_sum[...] = mine.astype(bf16)
            for copy in time_links:
                copy.start()

        def mixed_chip(which):
            rows = rows_at(which, chip_rows)
            d_mixed_ref[rows, :] = lax.dot_general(
                proj_all[rows, :], out_w[...], turned, preferred_element_type=f32
            ).astype(bf16)

        gather(proj_all, mixed_chip, ready=down_time)
        grad_out_ref[...] = lax.dot_general(mixed_ref[...], proj_all[...], sunk, preferred_element_type=f32).astype(bf16)
        gate_link.wait_recv()
        gate_sum_ref[...] = (
            grad_gate[rows_at(item, part_rows), :].astype(f32) + from_gate[...].astype(f32)
        ).astype(bf16)
        own_ref[...] = down_sum[rows_at(time, d_rows), :].astype(f32)
        for i, copy in enumerate(time_links):
            copy.wait_recv()
            own_ref[...] += from_time[i].astype(f32)
        down_grad_ref[...] = own_ref[...]
        up_link.wait_recv()
        up_sum_ref[...] = (grad_up[rows_at(item, part_rows), :].astype(f32) + from_up[...].astype(f32)).astype(bf16)
        for copy in [down_link, gate_link, up_link] + time_links:
            copy.wait_send()
        moves.finish()

    links = 7 * 3 + 7 * 3 + 3 + others
    result = pl.pallas_call(
        kernel,
        out_shape=[
            jax.ShapeDtypeStruct((TOK, D), f32),
            jax.ShapeDtypeStruct((TOK, D), f32),
            jax.ShapeDtypeStruct((ROWS, deep), bf16),
            jax.ShapeDtypeStruct((deep, D), bf16),
            jax.ShapeDtypeStruct((part_rows, width), bf16),
            jax.ShapeDtypeStruct((part_rows, width), bf16),
            jax.ShapeDtypeStruct((d_rows, D), f32),
            jax.ShapeDtypeStruct((16, D), f32),
        ]
        + moves.out_shapes(),
        in_specs=[VMEM] * 8 + [ANY] * n_in,
        out_specs=[VMEM] * 8 + [ANY] * n_out,
        scratch_shapes=[
            pltpu.VMEM((D, width), bf16),
            pltpu.VMEM((width, D), bf16),
            pltpu.VMEM((ROWS, D), bf16),
            pltpu.VMEM((ROWS, D), bf16),
            pltpu.VMEM((ROWS, D), bf16),
            pltpu.VMEM((ROWS, width), f32),
            pltpu.VMEM((ROWS, width), f32),
            pltpu.VMEM((ROWS, width), bf16),
            pltpu.VMEM((ROWS, width), bf16),
            pltpu.VMEM((ROWS, width), bf16),
            pltpu.VMEM((D, width), bf16),
            pltpu.VMEM((D, width), bf16),
            pltpu.VMEM((width, D), bf16),
            pltpu.VMEM((part_rows, width), bf16),
            pltpu.VMEM((part_rows, width), bf16),
            pltpu.VMEM((slab, D), bf16),
            pltpu.VMEM((slab, D), bf16),
            pltpu.VMEM((max(others, 1), d_rows, D), bf16),
            pltpu.VMEM((4, TOK, D), bf16),
            pltpu.VMEM((4, TOK, D), bf16),
            pltpu.VMEM((3, TOK, D), bf16),
            pltpu.VMEM((3, TOK, D), bf16),
            pltpu.VMEM((TOK, D), f32),
            pltpu.VMEM((TOK, D), f32),
            pltpu.VMEM((TOK, D), f32),
            pltpu.VMEM((d_rows, D), f32),
            pltpu.SemaphoreType.DMA((links,)),
            pltpu.SemaphoreType.DMA((links,)),
            pltpu.SemaphoreType.DMA((1,)),
        ]
        + moves.scratch(),
        name="feed_forward",
        compiler_params=params(plan, 60),
    )(mixed, out_full, latents, cotangent, modulation, gains, first_rows, gate_full, *moves.operands())
    return result[:8]


def shards(
    latents,
    conditions,
    captions,
    row_counts,
    text_lengths,
    qkv_weight,
    text_weight,
    out_weight,
    gate_up_weight,
    down_weight,
    ada_weight,
    ada_bias,
    norm_gains,
    head_gates,
    cotangent,
):
    times = lax.axis_size("times")
    plan = Plan(times)
    sets, rows_axis = plan.sets, plan.rows
    devices = sets * M
    item, time, ring = here()
    place = (item * times + time) * M + ring
    group_place = time * M + ring
    heads = LOCAL // HEAD

    k_rows = qkv_weight.shape[0]
    t_rows = text_weight.shape[0]
    o_rows = out_weight.shape[0]
    d_rows = down_weight.shape[0]
    a_rows = ada_weight.shape[0]
    bias_n = ada_bias.shape[0]
    gain_n = norm_gains.shape[1]
    tiles = -(-(4 * D // 128) // rows_axis)

    package = jnp.concatenate(
        [norm_gains.astype(f32).reshape(-1), ada_bias.astype(f32), row_counts[0, 0].astype(f32)]
    )
    package_n = package.shape[0]
    lines = -(-package_n // 1024) * 8
    package = jnp.pad(package, (0, lines * 128 - package_n)).reshape(lines, 128)

    silu = jax.nn.silu(conditions[0].astype(f32)).astype(bf16).astype(f32)
    other_place = ((1 - item) * times + time) * M + ring
    cond = jnp.stack(
        [lax.dynamic_slice_in_dim(silu, p * a_rows, a_rows, 1) for p in (place, other_place)]
    )
    cond = jnp.pad(cond, ((0, 0), (0, 8 - FRAMES), (0, 128 - a_rows)))

    key_places, value_places = wide_order()
    mix = placing(np.concatenate([key_places, WIDE + key_places, 2 * WIDE + value_places]), 3 * WIDE)
    text_mix = placing(np.concatenate([key_places, WIDE + value_places]), 2 * WIDE)
    qkv_send = qkv_weight.reshape(k_rows, 3, M, LOCAL).transpose(2, 0, 1, 3).reshape(M, k_rows, 3 * LOCAL)
    text_send = text_weight.reshape(t_rows, 2, M, LOCAL).transpose(2, 0, 1, 3).reshape(M, t_rows, 2 * LOCAL)
    gate_up_send = gate_up_weight.reshape(k_rows, 2, sets, M, d_rows).transpose(1, 3, 0, 2, 4)
    gate_up_send = gate_up_send.reshape(2, M, k_rows, sets * d_rows)
    out_forth = [(o, (o % sets) * M + o // sets) for o in range(devices)]
    out_back = [(b, a) for a, b in out_forth]
    axes = ("items", "times", "ring")
    out_shard = lax.ppermute(out_weight, axes, out_forth)

    text_job = plan.scatter_ring(text_send)
    mod_tiles, cond_other, (packages, qkv_time, _, text_full) = prologue(
        plan,
        tiles,
        package,
        cond,
        ada_weight,
        [plan.scatter_group_ring(qkv_send), text_job, plan.swap_source(text_job)],
    )
    packages = packages.reshape(devices, lines * 128)
    gains = packages[:, : 7 * gain_n].reshape(devices, 7, gain_n).transpose(1, 0, 2).reshape(7, D)
    gains = jnp.pad(gains, ((0, 1), (0, 0)))
    bias = packages[:, 7 * gain_n : 7 * gain_n + bias_n].reshape(4 * D)
    counts_all = packages[:, 7 * gain_n + bias_n : package_n].astype(jnp.int32).reshape(GROUPS, rows_axis, FRAMES)
    counts = lax.dynamic_index_in_dim(counts_all, item, 0, keepdims=False)

    def from_tiles(array):
        lead = array.shape[:-3]
        array = array[..., : FRAMES * tiles, :].reshape(lead + (rows_axis, FRAMES, tiles, 128))
        array = jnp.moveaxis(array, -3, -4).reshape(lead + (FRAMES, rows_axis * tiles * 128))
        return array[..., : 4 * D]

    modulation = from_tiles(mod_tiles) + bias

    line = jnp.arange(TOK, dtype=jnp.int32)[None, :]
    clip = counts[:, :1]
    before = jnp.cumsum(counts, axis=0) - counts
    frame_all = (line >= clip).astype(jnp.int32)
    position_all = jnp.where(frame_all == 0, before[:, :1] + line, before[:, 1:] + line - clip)
    frame_k = frame_all.reshape(-1)
    frame_q = lax.dynamic_slice_in_dim(frame_k, time * ROWS, ROWS)
    position_q = lax.dynamic_slice_in_dim(position_all.reshape(-1), time * ROWS, ROWS).astype(f32)
    frame_own = lax.dynamic_index_in_dim(frame_all, group_place, 0, keepdims=False)
    first_rows = (frame_own == 0).astype(f32)[:, None]
    text_line = jnp.arange(FRAMES * TEXT, dtype=jnp.int32)
    text_frame = text_line // TEXT
    text_live = text_line % TEXT < jnp.repeat(text_lengths[0], TEXT)

    feature = jnp.arange(128, dtype=jnp.int32)[None, :]

    def key_features(apart_first, apart_second):
        ones = (feature >= SPARE + 2) & (feature < SPARE + 2 + 3 * heads)
        pick = jnp.where(feature == SPARE, apart_first[:, None], (feature == SPARE + 1) & apart_second[:, None])
        return jnp.where(pick | ones, 1.0, 0.0).astype(bf16)

    features = key_features(frame_k == 1, frame_k == 0)
    text_features = key_features(~((text_frame == 0) & text_live), ~((text_frame == 1) & text_live))
    query_features = jnp.where(feature == SPARE + frame_q[:, None], -APART, 0.0).astype(bf16)
    pair = jnp.arange(128, dtype=jnp.int32)
    frequency = theta_base ** (-2.0 * (pair % (HEAD // 2)).astype(f32) / HEAD)
    angle = position_q[:, None] * frequency[None, :]
    live_lane = (pair < SPARE)[None, :]
    cos, sin = jnp.where(live_lane, jnp.cos(angle), 0.0), jnp.where(live_lane, jnp.sin(angle), 0.0)
    own_gates = jnp.tanh(lax.dynamic_slice_in_dim(head_gates.astype(f32), ring * heads, heads))
    gates_v = jnp.concatenate([jnp.zeros((HEAD,), f32), jnp.repeat(own_gates, HEAD)]).reshape(1, WIDE)
    half_gates = jnp.pad(jnp.repeat(own_gates, HEAD // 2), (0, 128 - SPARE))
    gates_q = jnp.concatenate([half_gates, half_gates]).reshape(1, WIDE)
    gain_wide = lax.dynamic_slice(gains, (4, ring * LOCAL), (3, LOCAL))
    gain_wide = gain_wide.reshape(3, heads, HEAD // 2, 2).transpose(0, 3, 1, 2).reshape(3, 2, SPARE)
    gain_wide = jnp.pad(gain_wide, ((0, 5), (0, 0), (0, 128 - SPARE))).reshape(8, WIDE)

    inputs = latents[0]
    caption_rows = captions[0].reshape(FRAMES * TEXT, TEXT_DIM)
    forward, (qkv_full, _, out_full, _, up_shard, _, gate_full) = attention_forward(
        plan,
        inputs,
        modulation,
        gains,
        first_rows,
        caption_rows,
        text_full.reshape(GROUPS * M * t_rows, 2 * LOCAL),
        mix,
        text_mix,
        gain_wide,
        cos,
        sin,
        query_features,
        features,
        text_features,
        gates_v,
        qkv_time.reshape(times * M * k_rows, 3 * LOCAL),
        out_shard,
        gate_up_send[0],
        gate_up_send[1],
    )
    (mixed, self_out, cross_out, attn_all, query, packed_all, text_packed, qn, kn, q_inv, k_inv, tn, t_inv) = forward
    out_full = jnp.pad(out_full.reshape(LOCAL, D), ((HEAD, 0), (0, 0)))

    (result_rows, d_state, d_mixed, grad_out, gate_sum, up_sum, down_grad, ffn_sums) = feed_forward(
        plan,
        mixed,
        out_full,
        inputs,
        cotangent[0],
        modulation,
        gains,
        first_rows,
        gate_full.reshape(D, sets * d_rows),
        up_shard.reshape(M * k_rows, sets * d_rows),
        down_weight,
    )
    ring_shape = (times, M, k_rows, sets * d_rows)
    (grad_latent, attn_sums, wide_sums, qkv_sum, text_sum), (_, gate_parts, up_pieces, out_parts) = attention_backward(
        plan,
        query,
        packed_all,
        features,
        text_packed,
        text_features,
        self_out,
        cross_out,
        d_mixed,
        gates_q,
        gates_v,
        (qn, kn),
        (q_inv, k_inv),
        tn,
        t_inv,
        cos,
        sin,
        gain_wide,
        caption_rows,
        attn_all,
        qkv_full,
        mix,
        text_mix,
        inputs,
        d_state,
        modulation,
        gains,
        first_rows,
        gate_sum.reshape(ring_shape),
        up_sum.reshape(ring_shape),
        grad_out[HEAD:].reshape(sets, o_rows, D),
    )

    def add(parts, axis=0):
        return jnp.sum(parts.astype(f32), axis=axis)

    d_mod = jnp.concatenate([attn_sums[1:3], ffn_sums[3:5], ffn_sums[5:7], ffn_sums[7:9]], axis=1)
    d_mod = jnp.pad(d_mod, ((0, 0), (0, rows_axis * tiles * 128 - 4 * D)))
    d_mod = d_mod.reshape(FRAMES, rows_axis, tiles, 128).transpose(1, 0, 2, 3).reshape(rows_axis, FRAMES * tiles, 128)
    d_mod = jnp.pad(d_mod, ((0, 0), (0, 8 - FRAMES * tiles), (0, 0)))
    d_mod = jnp.tile(d_mod, (GROUPS, 1, 1))
    wide_gains = wide_sums[:3].reshape(3, 2, 128)[:, :, :SPARE].reshape(3, 2, heads, HEAD // 2)
    wide_gains = wide_gains.transpose(0, 2, 3, 1).reshape(3, LOCAL)
    wide_gains = wide_gains * jnp.stack([jnp.ones(()), jnp.ones(()), (time == 0).astype(f32)])[:, None]
    wide_gains = lax.dynamic_update_slice(jnp.zeros((3, D), f32), wide_gains, (0, ring * LOCAL))
    gate_sums = jnp.sum(wide_sums[3, HEAD:].reshape(heads, HEAD), axis=1) * (1.0 - own_gates * own_gates)
    gate_row = lax.dynamic_update_slice_in_dim(jnp.zeros((1, D), f32), gate_sums[None], ring * heads, 1)
    d_gains = jnp.concatenate([attn_sums[:1], ffn_sums[:3], wide_gains, gate_row], axis=0)
    gain_tiles = D // 128
    d_gains = d_gains.reshape(8, gain_tiles, 128).transpose(1, 0, 2)
    d_gains = jnp.pad(d_gains, ((0, devices - gain_tiles), (0, 0), (0, 0)))
    small = jnp.concatenate([d_mod, d_gains], axis=1).reshape(sets, M, 16, 128)
    small_all, (up_parts, qkv_pieces, text_pieces) = finish(
        plan,
        small,
        [
            plan.times_of_ring(up_pieces),
            plan.scatter_ring(qkv_sum.reshape(M, k_rows, 3 * LOCAL)),
            plan.scatter_ring(text_sum.reshape(M, t_rows, 2 * LOCAL)),
        ],
    )
    gains_all = small_all[:gain_tiles, 8:].transpose(1, 0, 2).reshape(8, D)
    gains_grad = lax.dynamic_slice_in_dim(gains_all[:7], place * gain_n, gain_n, 1)
    gates_grad = gains_all[7, :HEADS]
    d_mod_all = from_tiles(small_all[:, :8].reshape(GROUPS, rows_axis, 8, 128)).reshape(GROUPS * FRAMES, 4 * D)
    cond_own, cond_other = cond[0, :FRAMES], cond_other[:FRAMES]
    silu_both = jnp.where(
        item == 0, jnp.concatenate([cond_own, cond_other]), jnp.concatenate([cond_other, cond_own])
    )
    ada_grad = jnp.einsum("fc,fd->cd", silu_both[:, :a_rows], d_mod_all, precision=highest)
    bias_grad = lax.dynamic_slice_in_dim(jnp.sum(d_mod_all, axis=0), place * bias_n, bias_n)
    out_grad = lax.ppermute(add(out_parts), axes, out_back)
    qkv_grad = qkv_pieces.reshape(M, k_rows, 3, LOCAL).transpose(1, 2, 0, 3).reshape(k_rows, 3 * D).astype(f32)
    text_grad = text_pieces.reshape(M, t_rows, 2, LOCAL).transpose(1, 2, 0, 3).reshape(t_rows, 2 * D).astype(f32)
    gate_up_grad = jnp.stack([add(gate_parts, 1), add(up_parts, 0)]).reshape(2, M, k_rows, sets, d_rows)
    gate_up_grad = gate_up_grad.transpose(2, 0, 3, 1, 4).reshape(k_rows, 2 * FF)
    return (
        result_rows[None],
        grad_latent[None],
        qkv_grad,
        text_grad,
        out_grad,
        gate_up_grad,
        down_grad,
        ada_grad,
        bias_grad,
        gains_grad,
        gates_grad,
    )


def solution(mesh):
    items, rows = mesh.shape["items"], mesh.shape["rows"]
    fine = Mesh(mesh.devices.reshape(items, rows // M, M), ("items", "times", "ring"))
    whole = ("items", "times", "ring")
    rows_of = ("times", "ring")
    return jax.shard_map(
        shards,
        mesh=fine,
        in_specs=(
            P("items", rows_of, None),
            P("items", None, None),
            P("items", None, None, None),
            P("items", rows_of, None),
            P("items", None),
            P(whole, None),
            P(whole, None),
            P(whole, None),
            P(whole, None),
            P(whole, None),
            P(whole, None),
            P(whole),
            P(None, whole),
            P(),
            P("items", rows_of, None),
        ),
        out_specs=(
            P("items", rows_of, None),
            P("items", rows_of, None),
            P(whole, None),
            P(whole, None),
            P(whole, None),
            P(whole, None),
            P(whole, None),
            P(whole, None),
            P(whole),
            P(None, whole),
            P(),
        ),
        check_vma=False,
    )
```

```python
import jax
import jax.numpy as jnp
import numpy as np
from jax import lax
from jax.experimental import pallas as pl
from jax.experimental.pallas import tpu as pltpu
from jax.sharding import Mesh
from jax.sharding import PartitionSpec as P

D = 1536
HEADS = 24
HEAD = 64
FF = 4096
TEXT_DIM = 4096
COND = 1024
TEXT = 256
FRAMES = 2
TOK = 128
GROUPS = 2
M = 8
LOCAL = HEADS // M * HEAD
ROWS = M * TOK
WIDE = 256
SPARE = 96
APART = 8192.0

epsilon = 1e-05
theta_base = 10000.0
highest = lax.Precision.HIGHEST
MESH = pl.DeviceIdType.MESH
f32 = jnp.float32
bf16 = jnp.bfloat16
ANY = pl.BlockSpec(memory_space=pl.ANY)
VMEM = pl.BlockSpec(memory_space=pltpu.VMEM)


def flip(where, mask):
    return tuple(a if b == 0 else a ^ b for a, b in zip(where, mask))


class Job:
    def __init__(self, x, shape, masks, src, dst, pass_on=(), by=None, source=None, piece=None):
        self.x, self.shape, self.masks, self.src, self.dst = x, shape, masks, src, dst
        self.piece = piece
        self.pass_on, self.by, self.source = tuple(pass_on), by, source
        if source is not None:
            self.x = None
        self.dtype = x.dtype

    def count(self):
        return len(self.masks) + len(self.pass_on)

    def block(self):
        return self.piece or self.shape[len(self.dst((0, 0, 0))) :]

    def peers(self):
        return set(self.masks) | ({self.by} if self.pass_on else set())


class Transfers:
    def __init__(self, jobs):
        self.jobs = jobs
        self.sent = [j for j in jobs if j.source is None]
        self.total = sum(j.count() for j in jobs)

    def operands(self):
        return [j.x for j in self.sent]

    def out_shapes(self):
        return [jax.ShapeDtypeStruct(j.shape, j.dtype) for j in self.jobs]

    def scratch(self):
        if not self.jobs:
            return []
        return [
            pltpu.SemaphoreType.DMA((self.total,)),
            pltpu.SemaphoreType.DMA((self.total,)),
            pltpu.SemaphoreType.DMA((2, len(self.jobs))),
        ] + [pltpu.VMEM(j.block(), j.dtype) for j in self.jobs]

    def peers(self):
        found = set()
        for j in self.jobs:
            found |= j.peers()
        return found

    def bind(self, me, ins, outs, sems):
        self.me, self.outs, self.sems = me, outs, sems
        left = list(ins)
        self.ins = []
        for j in self.jobs:
            self.ins.append(left.pop(0) if j.source is None else outs[self.jobs.index(j.source)])
        self.base, at = [], 0
        for j in self.jobs:
            self.base.append(at)
            at += j.count()
        self.arrived, self.kept, self.settled, self.chained, self.forwarded = set(), set(), set(), set(), set()

    def remote(self, src, dst, slot, dest):
        return pltpu.make_async_remote_copy(
            src_ref=src,
            dst_ref=dst,
            send_sem=self.sems[0].at[slot],
            recv_sem=self.sems[1].at[slot],
            device_id=dest,
            device_id_type=MESH,
        )

    def send(self, k, i):
        j = self.jobs[k]
        if i < len(j.masks):
            dest = flip(self.me, j.masks[i])
            at = j.src(dest)
            src = self.ins[k] if at is None else self.ins[k].at[at]
            return self.remote(src, self.outs[k].at[j.dst(self.me)], self.base[k] + i, dest)
        mask = j.pass_on[i - len(j.masks)]
        block = self.outs[k].at[j.dst(flip(self.me, mask))]
        return self.remote(block, block, self.base[k] + i, flip(self.me, j.by))

    def own(self, k, leg):
        j = self.jobs[k]
        room = self.sems[3 + k]
        if leg == 0:
            at = j.src(self.me)
            src = self.ins[k] if at is None else self.ins[k].at[at]
            return pltpu.make_async_copy(src, room, self.sems[2].at[0, k])
        return pltpu.make_async_copy(room, self.outs[k].at[j.dst(self.me)], self.sems[2].at[1, k])

    def start_job(self, k):
        j = self.jobs[k]
        for i in range(len(j.masks)):
            self.send(k, i).start()
        self.own(k, 0).start()

    def start(self, late=()):
        for k, j in enumerate(self.jobs):
            if j.source is None and k not in late:
                self.start_job(k)

    def receive(self, k, i):
        if (k, i) not in self.arrived:
            self.arrived.add((k, i))
            self.send(k, i).wait_recv()

    def take(self, k):
        self.keep(k)
        for i in range(self.jobs[k].count()):
            self.receive(k, i)
        if k not in self.settled:
            self.settled.add(k)
            self.own(k, 1).wait()

    def keep(self, k):
        if k not in self.kept:
            self.kept.add(k)
            self.own(k, 0).wait()
            self.own(k, 1).start()

    def chain(self, late=()):
        for k, j in enumerate(self.jobs):
            if j.source is not None and k not in self.chained and k not in late:
                self.chained.add(k)
                self.take(self.jobs.index(j.source))
                self.start_job(k)

    def forward(self):
        self.chain()
        for k in range(len(self.jobs)):
            self.keep(k)
        for k, j in enumerate(self.jobs):
            if k not in self.forwarded:
                self.forwarded.add(k)
                for n, mask in enumerate(j.pass_on):
                    self.receive(k, j.masks.index(mask))
                    self.send(k, len(j.masks) + n).start()

    def finish(self):
        self.forward()
        for k, j in enumerate(self.jobs):
            self.take(k)
            for i in range(j.count()):
                self.send(k, i).wait_send()


class Plan:
    def __init__(self, times):
        self.times = times
        self.sets = GROUPS * times
        self.rows = times * M
        self.next_id = 0
        ones = [(i, t, m) for i in range(GROUPS) for t in range(times) for m in range(M)]
        self.all = ones[1:]
        self.ring = [(0, 0, m) for m in range(1, M)]
        self.chips = [(0, 0, m) for m in range(2, M, 2)]
        self.mate = (0, 0, 1)
        self.time = [(0, t, 0) for t in range(1, times)]
        self.item = (1, 0, 0)
        self.span = [(i, t, 0) for i in range(GROUPS) for t in range(times)][1:]
        self.group = [(0, t, m) for t in range(times) for m in range(M)][1:]

    def identity(self):
        self.next_id += 1
        return self.next_id

    def set_of(self, where):
        return where[0] * self.times + where[1]

    def gather_ring(self, x):
        return Job(
            x,
            (M,) + x.shape,
            [self.mate] + self.chips,
            lambda dest: None,
            lambda sender: (sender[2],),
            self.chips,
            self.mate,
        )

    def direct_ring(self, x):
        return Job(x, (M,) + x.shape, self.ring, lambda dest: None, lambda sender: (sender[2],))

    def scatter_ring(self, x):
        return Job(x, x.shape, self.ring, lambda dest: (dest[2],), lambda sender: (sender[2],))

    def gather_span(self, x, shape=None, source=None):
        return Job(
            x,
            (self.sets,) + (x.shape if shape is None else shape),
            [self.item] + self.time,
            lambda dest: None,
            lambda sender: (self.set_of(sender),),
            self.time,
            self.item,
            source,
        )

    def scatter_span(self, x):
        return Job(x, x.shape, self.span, lambda dest: (self.set_of(dest),), lambda sender: (self.set_of(sender),))

    def gather_time(self, x):
        return Job(x, (self.times,) + x.shape, self.time, lambda dest: None, lambda sender: (sender[1],))

    def stack_time(self, x):
        n = x.shape[0]
        return Job(
            x,
            (self.times * n,) + x.shape[1:],
            self.time,
            lambda dest: None,
            lambda sender: (pl.ds(pl.multiple_of(sender[1] * n, n), n),),
            piece=x.shape,
        )

    def stack_item(self, x, source=None):
        shape = x.shape if source is None else source.shape
        n = shape[0]
        return Job(
            x,
            (GROUPS * n,) + shape[1:],
            [self.item],
            lambda dest: None,
            lambda sender: (pl.ds(pl.multiple_of(sender[0] * n, n), n),),
            source=source,
            piece=shape,
        )

    def split_time(self, x):
        n = x.shape[0] // self.times
        return Job(
            x,
            (self.times, n) + x.shape[1:],
            self.time,
            lambda dest: (pl.ds(pl.multiple_of(dest[1] * n, n), n),),
            lambda sender: (sender[1],),
        )

    def scatter_group_ring(self, x):
        return Job(
            x,
            (self.times,) + x.shape,
            self.group,
            lambda dest: (dest[2],),
            lambda sender: (sender[1], sender[2]),
        )

    def swap_source(self, source):
        return Job(
            source.x if source.x is not None else source,
            (GROUPS,) + source.shape,
            [self.item],
            lambda dest: None,
            lambda sender: (sender[0],),
            source=source,
        )

    def gather_time_source(self, source):
        return Job(
            source,
            (self.times,) + source.shape,
            self.time,
            lambda dest: None,
            lambda sender: (sender[1],),
            source=source,
        )

    def ring_of_times(self, x, source=None):
        shape = x.shape if source is None else source.shape
        return Job(
            x if source is None else source,
            (M, shape[0]) + tuple(shape[2:]),
            self.ring,
            lambda dest: (slice(None), dest[2]),
            lambda sender: (sender[2],),
            source=source,
        )

    def times_of_ring(self, x):
        shape = x.shape
        return Job(
            x,
            (shape[1], shape[0]) + tuple(shape[2:]),
            self.time,
            lambda dest: (slice(None), dest[1]),
            lambda sender: (sender[1],),
        )

    def scatter_time(self, x):
        return Job(x, x.shape, self.time, lambda dest: (dest[1],), lambda sender: (sender[1],))

    def scatter_item(self, x):
        return Job(x, x.shape, [self.item], lambda dest: (dest[0],), lambda sender: (sender[0],))

    def gather_all(self, x):
        return Job(
            x,
            (self.sets, M) + x.shape,
            self.all,
            lambda dest: None,
            lambda sender: (self.set_of(sender), sender[2]),
        )

    def scatter_all(self, x):
        return Job(
            x,
            x.shape,
            self.all,
            lambda dest: (self.set_of(dest), dest[2]),
            lambda sender: (self.set_of(sender), sender[2]),
        )

    def swap_item(self, x):
        return Job(x, (GROUPS,) + x.shape, [self.item], lambda dest: None, lambda sender: (sender[0],))

    def gather_group(self, x):
        return Job(
            x,
            (self.times, M) + x.shape,
            self.group,
            lambda dest: None,
            lambda sender: (sender[1], sender[2]),
        )

    def scatter_group(self, x):
        return Job(
            x,
            x.shape,
            self.group,
            lambda dest: (dest[1], dest[2]),
            lambda sender: (sender[1], sender[2]),
        )


def here():
    return (lax.axis_index("items"), lax.axis_index("times"), lax.axis_index("ring"))


def greet(me, peers):
    barrier = pltpu.get_barrier_semaphore()
    for mask in sorted(peers):
        pl.semaphore_signal(barrier, inc=1, device_id=flip(me, mask), device_id_type=MESH)
    pl.semaphore_wait(barrier, len(peers))


def exchange(plan, name, jobs):
    moves = Transfers(jobs)
    n_in, n_out = len(moves.sent), len(jobs)

    def kernel(*refs):
        me = here()
        greet(me, moves.peers())
        moves.bind(me, refs[:n_in], refs[n_in : n_in + n_out], refs[n_in + n_out :])
        moves.start()
        moves.finish()

    return pl.pallas_call(
        kernel,
        out_shape=moves.out_shapes(),
        in_specs=[ANY] * n_in,
        out_specs=[ANY] * n_out,
        scratch_shapes=moves.scratch(),
        name=name,
        compiler_params=pltpu.CompilerParams(
            collective_id=plan.identity(), has_side_effects=True, vmem_limit_bytes=32 * 2**20
        ),
    )(*moves.operands())


def lane_masks():
    lane = np.arange(WIDE)
    query, value = np.zeros((8, WIDE), np.float32), np.zeros((8, WIDE), np.float32)
    back = np.zeros((8, WIDE), np.float32)
    inner = lane % 128
    for h in range(LOCAL // HEAD):
        query[h] = ((inner < SPARE) & (inner // (HEAD // 2) == h)) | (lane == 128 + SPARE) | (lane == 129 + SPARE)
        query[h] += (lane >= 130 + SPARE + 3 * h) & (lane < 133 + SPARE + 3 * h)
        value[h] = ((lane >= HEAD) & (lane // HEAD - 1 == h)) | (lane // 16 == h)
        back[h] = ((lane >= HEAD) & (lane // HEAD - 1 == h)) | (lane == 2 * h) | (lane == 2 * h + 1)
    return query, value, back


def wide_order():
    col = np.arange(LOCAL)
    head, pair, odd = col // HEAD, col % HEAD // 2, col % 2
    return odd * 128 + head * (HEAD // 2) + pair, HEAD + col


def placing(places, width):
    return (jnp.asarray(places, jnp.int32)[:, None] == jnp.arange(width, dtype=jnp.int32)[None, :]).astype(bf16)


def widen(packed_ref, feature, key_ref, value_ref, rows):
    lane = lax.broadcasted_iota(jnp.int32, (rows, 128), 1)
    first, second = packed_ref[:, :128].astype(f32), packed_ref[:, 128:256].astype(f32)
    key_ref[:rows, :128] = jnp.where(lane < SPARE, first, 0.0).astype(bf16)
    key_ref[:rows, 128:] = jnp.where(lane < SPARE, second, feature.astype(f32)).astype(bf16)
    moved = jnp.where(lane < SPARE, pltpu.roll(first, 96, 1), second)
    value_ref[:rows, :128] = jnp.where(lane < HEAD, 1.0, moved).astype(bf16)
    value_ref[:rows, 128:] = packed_ref[:, 256:]


def pack(key_first, key_second, value_first, value_second, packed_ref, rows):
    lane = lax.broadcasted_iota(jnp.int32, (rows, 128), 1)
    packed_ref[:, :128] = jnp.where(lane < SPARE, key_first, pltpu.roll(value_first, 32, 1)).astype(bf16)
    packed_ref[:, 128:256] = jnp.where(lane < SPARE, key_second, value_first).astype(bf16)
    if value_second is not None:
        packed_ref[:, 256:] = value_second.astype(bf16)


def unpack(packed, rows):
    lane = lax.broadcasted_iota(jnp.int32, (rows, 128), 1)
    first, second = packed[:, :128].astype(f32), packed[:, 128:256].astype(f32)
    moved = jnp.where(lane < SPARE, pltpu.roll(first, 96, 1), second)
    return (
        jnp.where(lane < SPARE, first, 0.0),
        jnp.where(lane < SPARE, second, 0.0),
        jnp.where(lane < HEAD, 0.0, moved),
        packed[:, 256:].astype(f32),
    )


def fold_rows(values):
    ones = jnp.ones((8, WIDE), f32)
    sums = lax.dot_general(ones, values, (((1,), (1,)), ((), ())), precision=highest, preferred_element_type=f32)
    return jnp.concatenate([sums[0:1, 128 * i : 128 * (i + 1)] for i in range(values.shape[0] // 128)], axis=0)


def spread_rows(folded, out_ref):
    n = folded.shape[0]
    row = lax.broadcasted_iota(jnp.int32, (n, 128), 0)
    ones = jnp.ones((n, 128), f32)
    for i in range(n):
        out_ref[128 * i : 128 * (i + 1), :] = lax.dot_general(
            jnp.where(row == i, folded, 0.0),
            ones,
            (((0,), (0,)), ((), ())),
            precision=highest,
            preferred_element_type=f32,
        )


class Links:
    def __init__(self, me, send_sem, recv_sem):
        self.me, self.send_sem, self.recv_sem, self.used = me, send_sem, recv_sem, 0

    def __call__(self, src, dst, mask):
        slot = self.used
        self.used += 1
        return pltpu.make_async_remote_copy(
            src_ref=src,
            dst_ref=dst,
            send_sem=self.send_sem.at[slot],
            recv_sem=self.recv_sem.at[slot],
            device_id=flip(self.me, mask),
            device_id_type=MESH,
        )


def rows_at(index, count):
    return pl.ds(pl.multiple_of(index * count, count), count)


ASIDE, ABOVE = (0, 0, 2), (0, 0, 4)


def ring_sum(plan, link, me, buffers, product, meanwhile=lambda: None):
    to_mate, from_mate, to_chip, from_chip, part = buffers
    core, chip = me[2] % 2, me[2] // 2
    mates = [link(to_mate.at[d], from_mate.at[d], plan.mate) for d in range(4)]
    across = link(to_chip.at[2], from_chip.at[2], ASIDE)
    aside = link(to_chip.at[0], from_chip.at[0], ASIDE)
    above = link(to_chip.at[1], from_chip.at[1], ABOVE)
    for d in (3, 1, 2, 0):
        to_mate[d] = product((chip ^ d) * 2 + 1 - core).astype(bf16)
        mates[d].start()

    def both_cores(d):
        total = product((chip ^ d) * 2 + core)
        mates[d].wait_recv()
        return total + from_mate[d].astype(f32)

    to_chip[2] = both_cores(3).astype(bf16)
    across.start()
    to_chip[0] = both_cores(1).astype(bf16)
    aside.start()
    part[...] = both_cores(2)
    across.wait_recv()
    to_chip[1] = (part[...] + from_chip[2].astype(f32)).astype(bf16)
    above.start()
    part[...] = both_cores(0)
    meanwhile()
    aside.wait_recv()
    above.wait_recv()
    part[...] = part[...] + (from_chip[0].astype(f32) + from_chip[1].astype(f32))
    for copy in mates + [across, aside, above]:
        copy.wait_send()


def ring_gather(plan, link, me, all_ref, each, meanwhile=lambda: None, ready=lambda: None):
    ring = me[2]
    chip = ring // 2

    def block(place):
        return all_ref.at[rows_at(place, TOK)]

    mate = link(block(ring), block(ring), plan.mate)
    aside = link(block(ring), block(ring), ASIDE)
    above = link(block(ring), block(ring), ABOVE)
    for copy in (above, aside, mate):
        copy.start()
    meanwhile()
    later = []

    def hand_over(place):
        later.append(link(block(place), block(place), plan.mate))
        later[-1].start()

    above.wait_recv()
    onward = link(block(ring ^ 4), block(ring ^ 4), ASIDE)
    onward.start()
    hand_over(ring ^ 4)
    aside.wait_recv()
    hand_over(ring ^ 2)
    ready()
    mate.wait_recv()
    each(chip)
    later[0].wait_recv()
    each(chip ^ 2)
    later[1].wait_recv()
    each(chip ^ 1)
    onward.wait_recv()
    hand_over(ring ^ 6)
    later[2].wait_recv()
    each(chip ^ 3)
    for copy in [mate, aside, above, onward] + later:
        copy.wait_send()


def ring_share(plan, link, all_ref):
    copies = [link(all_ref.at[0], all_ref.at[i + 1], mask) for i, mask in enumerate(plan.ring)]
    for copy in copies:
        copy.start()
    return copies


def scale_of(values):
    return lax.rsqrt(jnp.mean(values * values, axis=1, keepdims=True) + epsilon)


def norm_back(d_hat, hat, inverse):
    return inverse * (d_hat - hat * jnp.mean(d_hat * hat, axis=1, keepdims=True))


RING_BUFFERS = [
    pltpu.VMEM((4, TOK, D), bf16),
    pltpu.VMEM((4, TOK, D), bf16),
    pltpu.VMEM((3, TOK, D), bf16),
    pltpu.VMEM((3, TOK, D), bf16),
    pltpu.VMEM((TOK, D), f32),
]


def params(plan, megabytes):
    return pltpu.CompilerParams(
        collective_id=plan.identity(), has_side_effects=True, vmem_limit_bytes=megabytes * 2**20
    )


def prologue(plan, tiles, package, cond, ada_weight, jobs):
    moves = Transfers([plan.gather_all(package)] + list(jobs))
    n_in, n_out = len(moves.sent), len(moves.jobs)
    total_tiles = 4 * D // 128
    peers, group = plan.all, plan.group

    def kernel(*refs):
        cond_ref, ada_ref = refs[:2]
        ins = refs[2 : 2 + n_in]
        mod_ref, cond_out = refs[2 + n_in : 4 + n_in]
        outs = refs[4 + n_in : 4 + n_in + n_out]
        refs = refs[4 + n_in + n_out :]
        cond_in, part_ref, send_ref, recv_ref, sum_ref, mod_in, send_sem, recv_sem = refs[:8]
        me = here()
        greet(me, moves.peers() | set(peers))
        link = Links(me, send_sem, recv_sem)
        swap = link(cond_ref.at[1], cond_in, plan.item)
        swap.start()
        moves.bind(me, ins, outs, refs[8:])
        moves.start(late=range(1, n_out))
        deep = ada_ref.shape[0]
        part_ref[0] = jnp.dot(cond_ref[0][:, :deep].astype(bf16), ada_ref[...], preferred_element_type=f32)
        swap.wait_recv()
        cond_out[...] = cond_in[...]
        part_ref[1] = jnp.dot(cond_in[:, :deep].astype(bf16), ada_ref[...], preferred_element_type=f32)
        for g in range(GROUPS):
            for r in range(plan.rows):
                for f in range(FRAMES):
                    for j in range(tiles):
                        tile = r * tiles + j
                        at = f * tiles + j
                        if tile < total_tiles:
                            send_ref[g, r, at : at + 1, :] = part_ref[g, f : f + 1, 128 * tile : 128 * (tile + 1)]
        copies = []
        for i, mask in enumerate(peers):
            dest = flip(me, mask)
            copies.append(link(send_ref.at[mask[0], dest[1] * M + dest[2]], recv_ref.at[i], mask))
            copies[-1].start()
        for k, job in enumerate(moves.jobs):
            if k and job.source is None:
                moves.start_job(k)
        place = me[1] * M + me[2]
        total = send_ref[0, place]
        for i, copy in enumerate(copies):
            copy.wait_recv()
            total = total + recv_ref[i]
        sum_ref[...] = total
        mod_in[place] = total
        shares = [link(sum_ref, mod_in.at[place], mask) for mask in group]
        for copy in shares:
            copy.start()
        moves.chain()
        for copy in shares:
            copy.wait_recv()
        mod_ref[...] = mod_in[...]
        for copy in [swap] + copies + shares:
            copy.wait_send()
        moves.finish()

    links = 1 + len(peers) + len(group)
    result = pl.pallas_call(
        kernel,
        out_shape=[jax.ShapeDtypeStruct((plan.rows, 8, 128), f32), jax.ShapeDtypeStruct((8, 128), f32)]
        + moves.out_shapes(),
        in_specs=[VMEM] * 2 + [ANY] * n_in,
        out_specs=[VMEM] * 2 + [ANY] * n_out,
        scratch_shapes=[
            pltpu.VMEM((8, 128), f32),
            pltpu.VMEM((GROUPS, 8, 4 * D), f32),
            pltpu.VMEM((GROUPS, plan.rows, 8, 128), f32),
            pltpu.VMEM((len(peers), 8, 128), f32),
            pltpu.VMEM((8, 128), f32),
            pltpu.VMEM((plan.rows, 8, 128), f32),
            pltpu.SemaphoreType.DMA((links,)),
            pltpu.SemaphoreType.DMA((links,)),
        ]
        + moves.scratch(),
        name="prologue",
        compiler_params=params(plan, 40),
    )(cond, ada_weight, *moves.operands())
    return result[0], result[1], result[2:]


def attention_forward(
    plan,
    latents,
    modulation,
    gains,
    first_rows,
    captions,
    text_weight,
    mix,
    text_mix,
    gain_wide,
    cos,
    sin,
    query_features,
    features,
    text_features,
    gates,
    qkv_time,
    out_shard,
    gate_send,
    up_send,
):
    heads = LOCAL // HEAD
    text_rows = captions.shape[0]
    text_deep = text_weight.shape[0]
    others = len(plan.time)
    out_job = plan.gather_time(out_shard)
    gate_job = plan.scatter_ring(gate_send)
    gate_time = plan.gather_time_source(gate_job)
    jobs = [
        plan.stack_item(qkv_time),
        out_job,
        plan.swap_source(out_job),
        gate_job,
        plan.scatter_ring(up_send),
        gate_time,
        plan.swap_source(gate_time),
    ]
    moves = Transfers(jobs)
    n_in, n_out = len(moves.sent), len(moves.jobs)
    block = 256
    chip_rows = 2 * TOK
    span = text_deep // GROUPS
    folded = 2 * ROWS // 128 + text_rows // 128
    folded_rows = -(-folded // 8) * 8

    def kernel(*refs):
        (latent_ref, mod_ref, gain_ref, first_ref, caption_ref, text_w, mix_ref, text_mix_ref) = refs[:8]
        (wide_ref, cos_ref, sin_ref, qfeature_ref, feature_ref, text_feature_ref, gate_ref, qmask_ref, vmask_ref) = refs[8:17]
        ins = refs[17 : 17 + n_in]
        refs = refs[17 + n_in :]
        (mixed_ref, self_ref, cross_ref, attn_all, query_ref, packed_out, text_packed) = refs[:7]
        (qn_ref, kn_ref, qinv_ref, kinv_ref, tn_ref, tinv_ref) = refs[7:13]
        outs = refs[13 : 13 + n_out]
        refs = refs[13 + n_out :]
        (key_ref, value_ref, packed_ref, far_ref, max_ref, raw_w, weight_ref, raw_ref, own_caps, text_part, text_far) = refs[:11]
        (text_raw, sums_ref, send_sem, recv_sem, local_sem) = refs[11:16]
        me = here()
        item, time, ring = me
        greet(me, moves.peers() | {plan.mate} | set(plan.chips) | set(plan.ring) | set(plan.time))
        link = Links(me, send_sem, recv_sem)
        moves.bind(me, ins, outs, refs[16:])
        loads = []
        for i in range(GROUPS):
            where = pl.ds(pl.multiple_of((i * plan.times + time) * span, span), span)
            loads.append(
                pltpu.make_async_copy(caption_ref.at[:, where], own_caps.at[:, i * span : (i + 1) * span], local_sem.at[i])
            )
            loads[-1].start()

        is_first = first_ref[...] > 0.5
        scale = jnp.where(is_first, mod_ref[0:1, :D], mod_ref[1:2, :D])
        rows = latent_ref[...]
        attn_in = rows * scale_of(rows) * gain_ref[0:1, :] * (1.0 + scale)
        attn_all[rows_at(ring, TOK), :] = attn_in.astype(bf16)

        text_copies = [link(text_part, text_far.at[i], mask) for i, mask in enumerate(plan.time)]

        def text_projection():
            moves.start(late=(4,))
            for copy in loads:
                copy.wait()
            text_part[...] = jnp.dot(own_caps[...], text_w[...], preferred_element_type=f32).astype(bf16)
            for copy in text_copies:
                copy.start()

        def weights_here():
            moves.take(0)
            copy = pltpu.make_async_copy(outs[0], raw_w, local_sem.at[0])
            copy.start()
            copy.wait()
            weight_ref[...] = jnp.dot(raw_w[...], mix_ref[...], preferred_element_type=f32).astype(bf16)

        def project(which):
            where = rows_at(which, chip_rows)
            raw_ref[where, :] = jnp.dot(attn_all[where, :], weight_ref[...], preferred_element_type=f32)

        ring_gather(plan, link, me, attn_all, project, text_projection, weights_here)
        moves.start_job(4)
        moves.chain(late=(6,))

        packed_ref[:, 256:] = raw_ref[:, 2 * WIDE + 128 :].astype(bf16)
        value_copies = [
            link(packed_ref.at[:, 256:], far_ref.at[i, :, 256:], mask) for i, mask in enumerate(plan.time)
        ]
        for copy in value_copies:
            copy.start()

        total = text_part[...].astype(f32)
        for i, copy in enumerate(text_copies):
            copy.wait_recv()
            total = total + text_far[i].astype(f32)
        text_raw[...] = jnp.dot(total, text_mix_ref[...].astype(f32), precision=highest, preferred_element_type=f32)
        q_raw, k_raw, t_raw = raw_ref[:, :WIDE], raw_ref[:, WIDE : 2 * WIDE], text_raw[:, :WIDE]
        squares = [fold_rows(q_raw * q_raw), fold_rows(k_raw * k_raw), fold_rows(t_raw * t_raw)]
        if folded_rows > folded:
            squares.append(jnp.zeros((folded_rows - folded, 128), f32))
        sums_ref[0] = jnp.concatenate(squares, axis=0)
        shares = ring_share(plan, link, sums_ref)
        for copy in shares:
            copy.wait_recv()
        total = sums_ref[0]
        for i in range(1, M):
            total = total + sums_ref[i]
        inverse = lax.rsqrt(total / D + epsilon)
        n = ROWS // 128
        spread_rows(inverse[:n], qinv_ref)
        spread_rows(inverse[n : 2 * n], kinv_ref)
        spread_rows(inverse[2 * n : folded], tinv_ref)

        def turn(where, at, inv_ref, n_ref, gain_row):
            first = raw_ref[where, at : at + 128] * inv_ref[where, :]
            second = raw_ref[where, at + 128 : at + 256] * inv_ref[where, :]
            n_ref[where, :128], n_ref[where, 128:] = first, second
            first = first * wide_ref[gain_row : gain_row + 1, :128]
            second = second * wide_ref[gain_row : gain_row + 1, 128:]
            cosine, sine = cos_ref[where, :], sin_ref[where, :]
            return first * cosine - second * sine, second * cosine + first * sine

        def shape(at, carry):
            where = rows_at(at, block)
            first, second = turn(where, 0, qinv_ref, qn_ref, 0)
            query_ref[where, :128] = (first.astype(bf16).astype(f32) * 0.125).astype(bf16)
            lane = lax.broadcasted_iota(jnp.int32, (block, 128), 1)
            second = jnp.where(lane < SPARE, second.astype(bf16).astype(f32) * 0.125, qfeature_ref[where, :].astype(f32))
            query_ref[where, 128:] = second.astype(bf16)
            first, second = turn(where, WIDE, kinv_ref, kn_ref, 1)
            values = raw_ref[where, 2 * WIDE :]
            pack(first, second, values[:, :128], None, packed_ref.at[where, :], block)
            return carry

        lax.fori_loop(0, ROWS // block, shape, 0)
        key_copies = [
            link(packed_ref.at[:, :256], far_ref.at[i, :, :256], mask) for i, mask in enumerate(plan.time)
        ]
        for copy in key_copies:
            copy.start()
        moves.chain()
        first = text_raw[:, :128] * tinv_ref[...]
        second = text_raw[:, 128:256] * tinv_ref[...]
        tn_ref[:, :128], tn_ref[:, 128:] = first, second
        pack(
            first * wide_ref[2:3, :128],
            second * wide_ref[2:3, 128:],
            text_raw[:, 256:384],
            text_raw[:, 384:],
            text_packed,
            text_rows,
        )

        def segment(rows, first, out_ref):
            def body(at, carry):
                where = rows_at(at, block)
                query_rows = query_ref[where, :]
                total = jnp.zeros((block, WIDE), f32)
                tops = jnp.zeros((block, WIDE), f32)
                for h in range(heads):
                    own_query = query_rows * qmask_ref[h : h + 1, :]
                    scores = lax.dot_general(
                        own_query, key_ref[:rows, :], (((1,), (1,)), ((), ())), preferred_element_type=f32
                    )
                    top = jnp.max(scores, axis=1, keepdims=True)
                    weights = jnp.exp(scores - top).astype(bf16)
                    product = jnp.dot(weights, value_ref[:rows, :], preferred_element_type=f32)
                    total += product * vmask_ref[h : h + 1, :]
                    tops += top * vmask_ref[h : h + 1, :]
                if first:
                    out_ref[where, :] = total
                    max_ref[where, :] = tops
                else:
                    before = max_ref[where, :]
                    after = jnp.maximum(before, tops)
                    out_ref[where, :] = out_ref[where, :] * jnp.exp(before - after) + total * jnp.exp(tops - after)
                    max_ref[where, :] = after
                return carry

            lax.fori_loop(0, ROWS // block, body, 0)

        def close(out_ref):
            def body(at, carry):
                where = rows_at(at, block)
                lane = lax.broadcasted_iota(jnp.int32, (block, WIDE), 1)
                values = out_ref[where, :]
                share = jnp.ones((block, WIDE), f32)
                for h in range(heads):
                    share = jnp.where(
                        (lane >= HEAD * (h + 1)) & (lane < HEAD * (h + 2)), values[:, 16 * h : 16 * h + 1], share
                    )
                logs = max_ref[where, :] + jnp.log(jnp.maximum(values, 1e-30))
                out_ref[where, :] = jnp.where(
                    lane < HEAD, jnp.where(lane < 16 * heads, logs, 0.0), values / share
                )
                return carry

            lax.fori_loop(0, ROWS // block, body, 0)

        widen(text_packed, text_feature_ref[...], key_ref, value_ref, text_rows)
        segment(text_rows, True, cross_ref)
        close(cross_ref)
        widen(packed_ref, feature_ref[rows_at(time, ROWS), :], key_ref, value_ref, ROWS)
        packed_out[time] = packed_ref[...]
        segment(ROWS, True, self_ref)
        for i, mask in enumerate(plan.time):
            key_copies[i].wait_recv()
            value_copies[i].wait_recv()
            far = time ^ mask[1]
            packed_out[far] = far_ref[i]
            widen(far_ref.at[i], feature_ref[rows_at(far, ROWS), :], key_ref, value_ref, ROWS)
            segment(ROWS, False, self_ref)
        close(self_ref)
        lane = lax.broadcasted_iota(jnp.int32, (ROWS, WIDE), 1)
        both = self_ref[...] + gate_ref[...] * cross_ref[...]
        mixed_ref[...] = jnp.where(lane < HEAD, 0.0, both).astype(bf16)
        for copy in text_copies + shares + key_copies + value_copies:
            copy.wait_send()
        moves.finish()

    qmask, vmask, _ = lane_masks()
    links = 7 + (M - 1) + 3 * others
    result = pl.pallas_call(
        kernel,
        out_shape=[
            jax.ShapeDtypeStruct((ROWS, WIDE), bf16),
            jax.ShapeDtypeStruct((ROWS, WIDE), f32),
            jax.ShapeDtypeStruct((ROWS, WIDE), f32),
            jax.ShapeDtypeStruct((ROWS, D), bf16),
            jax.ShapeDtypeStruct((ROWS, WIDE), bf16),
            jax.ShapeDtypeStruct((plan.times, ROWS, 2 * LOCAL), bf16),
            jax.ShapeDtypeStruct((text_rows, 2 * LOCAL), bf16),
            jax.ShapeDtypeStruct((ROWS, WIDE), f32),
            jax.ShapeDtypeStruct((ROWS, WIDE), f32),
            jax.ShapeDtypeStruct((ROWS, 128), f32),
            jax.ShapeDtypeStruct((ROWS, 128), f32),
            jax.ShapeDtypeStruct((text_rows, WIDE), f32),
            jax.ShapeDtypeStruct((text_rows, 128), f32),
        ]
        + moves.out_shapes(),
        in_specs=[VMEM] * 4 + [ANY] + [VMEM] * 12 + [ANY] * n_in,
        out_specs=[VMEM] * 13 + [ANY] * n_out,
        scratch_shapes=[
            pltpu.VMEM((ROWS, WIDE), bf16),
            pltpu.VMEM((ROWS, WIDE), bf16),
            pltpu.VMEM((ROWS, 2 * LOCAL), bf16),
            pltpu.VMEM((max(others, 1), ROWS, 2 * LOCAL), bf16),
            pltpu.VMEM((ROWS, WIDE), f32),
            pltpu.VMEM((D, 3 * LOCAL), bf16),
            pltpu.VMEM((D, 3 * WIDE), bf16),
            pltpu.VMEM((ROWS, 3 * WIDE), f32),
            pltpu.VMEM((text_rows, text_deep), bf16),
            pltpu.VMEM((text_rows, 2 * LOCAL), bf16),
            pltpu.VMEM((max(others, 1), text_rows, 2 * LOCAL), bf16),
            pltpu.VMEM((text_rows, 2 * WIDE), f32),
            pltpu.VMEM((M, folded_rows, 128), f32),
            pltpu.SemaphoreType.DMA((links,)),
            pltpu.SemaphoreType.DMA((links,)),
            pltpu.SemaphoreType.DMA((GROUPS,)),
        ]
        + moves.scratch(),
        name="attention_forward",
        compiler_params=params(plan, 60),
    )(
        latents,
        modulation,
        gains,
        first_rows,
        captions,
        text_weight,
        mix,
        text_mix,
        gain_wide,
        cos,
        sin,
        query_features,
        features,
        text_features,
        gates,
        jnp.asarray(qmask, bf16),
        jnp.asarray(vmask, f32),
        *moves.operands(),
    )
    return result[:13], result[13:]


def attention_backward(
    plan,
    query,
    packed_all,
    features,
    text_packed,
    text_features,
    self_out,
    cross_out,
    d_mixed,
    gates_q,
    gates_v,
    hats,
    inverses,
    text_hat,
    text_inverse,
    cos,
    sin,
    gain_wide,
    captions,
    attn_all,
    qkv_full,
    mix,
    text_mix,
    latents,
    d_state,
    modulation,
    gains,
    first_rows,
    gate_sum,
    up_sum,
    grad_out,
):
    heads = LOCAL // HEAD
    text_rows = text_packed.shape[0]
    gate_job = plan.scatter_time(gate_sum)
    up_job = plan.ring_of_times(up_sum)
    jobs = [gate_job, plan.ring_of_times(None, gate_job), up_job, plan.scatter_span(grad_out)]
    moves = Transfers(jobs)
    n_in, n_out = len(moves.sent), len(moves.jobs)
    block = 256
    others = len(plan.time)
    room = max(others, 1)
    turned = (((1,), (1,)), ((), ()))
    sunk = (((0,), (0,)), ((), ()))
    local3 = qkv_full.shape[1]
    text_deep = captions.shape[1] // plan.times
    span = text_deep // GROUPS
    set_rows = D // plan.sets
    half = set_rows // 2
    folded = 2 * ROWS // 128
    text_folded = max(8, text_rows // 128)

    def kernel(*refs):
        (query_ref, packed_in, feature_ref, text_ref, text_feature_ref, self_ref, cross_ref, d_ref) = refs[:8]
        (gateq_ref, gatev_ref, qmask_ref, bmask_ref, qn_ref, kn_ref, qinv_ref, kinv_ref, tn_ref, tinv_ref) = refs[8:18]
        (cos_ref, sin_ref, wide_ref, caption_ref, attn_ref, qkv_w, mix_ref, text_mix_ref) = refs[18:26]
        (latent_ref, d_state_ref, mod_ref, gain_ref, first_ref) = refs[26:31]
        ins = refs[31 : 31 + n_in]
        refs = refs[31 + n_in :]
        latent_grad, sums_out, wide_out, qkv_out, text_out = refs[:5]
        outs = refs[5 : 5 + n_out]
        refs = refs[5 + n_out :]
        (key_ref, value_ref, near_ref, qs_ref, ds_ref, dq_ref, dk_ref, dv_ref, tdk_ref, tdv_ref) = refs[:10]
        (to_ref, from_ref, tto_ref, tfrom_ref, du_ref, d_text, own_caps, grad_qkv, grad_text) = refs[10:19]
        (a_item, a_sum, a_time, b_time, b_sum, b_item, text_item, share_ref, tshare_ref, mean_ref) = refs[19:29]
        buffers = refs[29:34]
        send_sem, recv_sem, local_sem = refs[34:37]
        me = here()
        item, time, ring = me
        greet(me, moves.peers() | set(plan.time) | set(plan.ring) | {plan.item})
        link = Links(me, send_sem, recv_sem)
        moves.bind(me, ins, outs, refs[37:])
        moves.start(late=(3,))
        loads = []
        for i in range(GROUPS):
            where = pl.ds(pl.multiple_of((i * plan.times + time) * span, span), span)
            loads.append(
                pltpu.make_async_copy(
                    caption_ref.at[:, where], own_caps.at[:, i * span : (i + 1) * span], local_sem.at[1 + i]
                )
            )
            loads[-1].start()

        def prepare(out_ref):
            def body(at, carry):
                where = rows_at(at, block)
                lane = lax.broadcasted_iota(jnp.int32, (block, 128), 1)
                tail = query_ref[where, 128:].astype(f32)
                out_rows = out_ref[where, :]
                d_rows = d_ref[where, :].astype(f32)
                product = d_rows * out_rows
                head_tile = jnp.where(lane < HEAD, 0.0, d_rows[:, :128])
                for h in range(heads):
                    log = -out_rows[:, 16 * h : 16 * h + 1]
                    for j in range(3):
                        piece = log.astype(bf16).astype(f32)
                        log = log - piece
                        tail = jnp.where(lane == SPARE + 2 + 3 * h + j, piece, tail)
                    delta = -jnp.sum(product * bmask_ref[h : h + 1, :].astype(f32), axis=1, keepdims=True)
                    for j in range(2):
                        piece = delta.astype(bf16).astype(f32)
                        delta = delta - piece
                        head_tile = jnp.where(lane == 2 * h + j, piece, head_tile)
                qs_ref[where, :128] = query_ref[where, :128]
                qs_ref[where, 128:] = tail.astype(bf16)
                ds_ref[where, :128] = head_tile.astype(bf16)
                ds_ref[where, 128:] = d_ref[where, 128:]
                return carry

            lax.fori_loop(0, ROWS // block, body, 0)

        def segment(rows, first, k_ref, v_ref, scale):
            k_ref[...] = jnp.zeros_like(k_ref)
            v_ref[...] = jnp.zeros_like(v_ref)

            def body(at, carry):
                where = rows_at(at, block)
                query_rows, d_rows = qs_ref[where, :], ds_ref[where, :]
                total = jnp.zeros((block, WIDE), f32)
                for h in range(heads):
                    own_query = query_rows * qmask_ref[h : h + 1, :]
                    own_d = d_rows * bmask_ref[h : h + 1, :]
                    keys = key_ref[:rows, :]
                    weights = jnp.exp(lax.dot_general(keys, own_query, turned, preferred_element_type=f32))
                    d_weights = lax.dot_general(value_ref[:rows, :], own_d, turned, preferred_element_type=f32)
                    d_scores = (weights * d_weights).astype(bf16)
                    v_ref[...] += jnp.dot(weights.astype(bf16), own_d, preferred_element_type=f32)
                    k_ref[...] += jnp.dot(d_scores, own_query, preferred_element_type=f32)
                    d_query = lax.dot_general(d_scores, keys, sunk, preferred_element_type=f32)
                    total += d_query * qmask_ref[h : h + 1, :].astype(f32)
                total = total * scale
                if first:
                    dq_ref[where, :] = total
                else:
                    dq_ref[where, :] += total
                return carry

            lax.fori_loop(0, ROWS // block, body, 0)

        def bring(which):
            copy = pltpu.make_async_copy(packed_in.at[which], near_ref, local_sem.at[0])
            copy.start()
            copy.wait()
            widen(near_ref, feature_ref[rows_at(which, ROWS), :], key_ref, value_ref, ROWS)

        far_copies = [link(to_ref.at[i], from_ref.at[i], mask) for i, mask in enumerate(plan.time)]
        text_copies = [link(tto_ref, tfrom_ref.at[i], mask) for i, mask in enumerate(plan.time)]

        prepare(self_ref)
        for i, mask in enumerate(plan.time):
            bring(time ^ mask[1])
            segment(ROWS, i == 0, dk_ref, dv_ref, 0.125)
            pack(dk_ref[:, :128], dk_ref[:, 128:], dv_ref[:, :128], dv_ref[:, 128:], to_ref.at[i], ROWS)
            far_copies[i].start()
        moves.chain()
        bring(time)
        segment(ROWS, others == 0, dk_ref, dv_ref, 0.125)
        prepare(cross_ref)
        widen(text_ref, text_feature_ref[...], key_ref, value_ref, text_rows)
        segment(text_rows, False, tdk_ref, tdv_ref, 0.125 * gateq_ref[...])
        tdk_ref[...] = tdk_ref[...] * gateq_ref[...]
        tdv_ref[...] = tdv_ref[...] * gatev_ref[...]
        pack(tdk_ref[:, :128], tdk_ref[:, 128:], tdv_ref[:, :128], tdv_ref[:, 128:], tto_ref, text_rows)
        for copy in text_copies:
            copy.start()
        wide_out[...] = jnp.zeros_like(wide_out)
        wide_out[3:4, :] = jnp.sum(d_ref[...].astype(f32) * cross_ref[...], axis=0, keepdims=True)
        for i in range(others):
            far_copies[i].wait_recv()
            k_first, k_second, v_first, v_second = unpack(from_ref.at[i], ROWS)
            dk_ref[:, :128] += k_first
            dk_ref[:, 128:] += k_second
            dv_ref[:, :128] += v_first
            dv_ref[:, 128:] += v_second

        moves.start_job(3)

        def unturn(d_all, hat_ref, gain_row):
            pieces = []
            for at in range(ROWS // block):
                where = slice(at * block, (at + 1) * block)
                first, second = d_all[where, :128], d_all[where, 128:]
                cosine, sine = cos_ref[where, :], sin_ref[where, :]
                lane = lax.broadcasted_iota(jnp.int32, (block, 128), 1)
                first, second = jnp.where(lane < SPARE, first, 0.0), jnp.where(lane < SPARE, second, 0.0)
                both = jnp.concatenate([first * cosine + second * sine, second * cosine - first * sine], axis=1)
                hat = hat_ref[where, :]
                wide_out[gain_row : gain_row + 1, :] += jnp.sum(both * hat, axis=0, keepdims=True)
                both = both * wide_ref[gain_row : gain_row + 1, :]
                d_all[where, :] = both
                pieces.append(fold_rows(both * hat))
            return pieces

        pieces = unturn(dq_ref, qn_ref, 0) + unturn(dk_ref, kn_ref, 1)
        share_ref[0] = jnp.concatenate(pieces, axis=0)
        shares = ring_share(plan, link, share_ref)
        for copy in shares:
            copy.wait_recv()
        total = share_ref[0]
        for i in range(1, M):
            total = total + share_ref[i]
        total = total / D
        n = ROWS // 128

        def settle(d_all, hat_ref, inv_ref, means):
            spread_rows(means, mean_ref)
            for c in (0, 128):
                lanes = slice(c, c + 128)
                d_all[:, lanes] = (d_all[:, lanes] - hat_ref[:, lanes] * mean_ref[...]) * inv_ref[...]

        settle(dq_ref, qn_ref, qinv_ref, total[:n])
        settle(dk_ref, kn_ref, kinv_ref, total[n:])
        for at in range(ROWS // block):
            where = slice(at * block, (at + 1) * block)
            lane = lax.broadcasted_iota(jnp.int32, (block, 128), 1)
            values = jnp.concatenate([jnp.where(lane < HEAD, 0.0, dv_ref[where, :128]), dv_ref[where, 128:]], axis=1)
            wide = jnp.concatenate([dq_ref[where, :], dk_ref[where, :], values], axis=1).astype(bf16)
            du_ref[where, :] = lax.dot_general(wide, mix_ref[...], turned, preferred_element_type=f32).astype(bf16)

        away = 1 - item

        def part(i, t, which):
            return pl.ds(pl.multiple_of((i * plan.times + t) * set_rows + which * half, half), half)

        a_items = [link(grad_qkv.at[part(away, t, 0)], a_item.at[t], plan.item) for t in range(plan.times)]
        b_times = [
            link(grad_qkv.at[part(i, time ^ mask[1], 1)], b_time.at[k, i], mask)
            for k, mask in enumerate(plan.time)
            for i in range(GROUPS)
        ]
        a_times = [link(a_sum.at[time ^ mask[1]], a_time.at[k], mask) for k, mask in enumerate(plan.time)]
        b_items = [link(b_sum.at[away], b_item, plan.item)]
        text_items = [link(grad_text.at[rows_at(away, span)], text_item, plan.item)]

        def meanwhile():
            grad_qkv[...] = lax.dot_general(attn_ref[...], du_ref[...], sunk, preferred_element_type=f32).astype(bf16)
            for copy in a_items + b_times:
                copy.start()
            for i, copy in enumerate(text_copies):
                copy.wait_recv()
                k_first, k_second, v_first, v_second = unpack(tfrom_ref.at[i], text_rows)
                tdk_ref[:, :128] += k_first
                tdk_ref[:, 128:] += k_second
                tdv_ref[:, :128] += v_first
                tdv_ref[:, 128:] += v_second
            lane = lax.broadcasted_iota(jnp.int32, (text_rows, WIDE), 1) % 128
            d_keys = jnp.where(lane < SPARE, tdk_ref[...], 0.0)
            hat = tn_ref[...]
            wide_out[2:3, :] = jnp.sum(d_keys * hat, axis=0, keepdims=True)
            d_keys = d_keys * wide_ref[2:3, :]
            tdk_ref[...] = d_keys
            sums = fold_rows(d_keys * hat)
            if text_folded > text_rows // 128:
                sums = jnp.concatenate([sums, jnp.zeros((text_folded - text_rows // 128, 128), f32)], axis=0)
            tshare_ref[0] = sums
            text_shares = ring_share(plan, link, tshare_ref)
            for t, copy in enumerate(a_items):
                copy.wait_recv()
                a_sum[t] = (grad_qkv[part(item, t, 0), :].astype(f32) + a_item[t].astype(f32)).astype(bf16)
            for copy in a_times:
                copy.start()
            for copy in text_shares:
                copy.wait_recv()
            total = tshare_ref[0]
            for i in range(1, M):
                total = total + tshare_ref[i]
            total = total / D
            spread_rows(total[: text_rows // 128], mean_ref.at[:text_rows])
            for c in (0, 128):
                lanes = slice(c, c + 128)
                tdk_ref[:, lanes] = (tdk_ref[:, lanes] - tn_ref[:, lanes] * mean_ref[:text_rows, :]) * tinv_ref[...]
            lane = lax.broadcasted_iota(jnp.int32, (text_rows, WIDE), 1)
            values = jnp.where(lane < HEAD, 0.0, tdv_ref[...])
            wide = jnp.concatenate([tdk_ref[...], values], axis=1).astype(bf16)
            d_text[...] = lax.dot_general(wide, text_mix_ref[...], turned, preferred_element_type=f32).astype(bf16)
            for copy in loads:
                copy.wait()
            grad_text[...] = lax.dot_general(own_caps[...], d_text[...], sunk, preferred_element_type=f32).astype(bf16)
            text_items[0].start()
            for copy in text_shares:
                copy.wait_send()
            for copy in b_times:
                copy.wait_recv()
            for i in range(GROUPS):
                total = grad_qkv[part(i, time, 1), :].astype(f32)
                for k in range(others):
                    total = total + b_time[k, i].astype(f32)
                b_sum[i] = total.astype(bf16)
            b_items[0].start()

        def back_product(which):
            return lax.dot_general(du_ref[rows_at(which, TOK), :], qkv_w[...], turned, preferred_element_type=f32)

        ring_sum(plan, link, me, buffers, back_product, meanwhile)

        d_in = buffers[4][...]
        rows = latent_ref[...]
        inverse = scale_of(rows)
        hat = rows * inverse
        gain = gain_ref[0:1, :]
        is_first = first_ref[...] > 0.5
        scale = jnp.where(is_first, mod_ref[0:1, :D], mod_ref[1:2, :D])
        sums_out[...] = jnp.zeros_like(sums_out)
        values = d_in * (hat * gain)
        total = jnp.sum(values, axis=0, keepdims=True)
        start = jnp.sum(jnp.where(is_first, values, 0.0), axis=0, keepdims=True)
        sums_out[1:2, :] = start
        sums_out[2:3, :] = total - start
        d_norm = d_in * (1.0 + scale)
        sums_out[0:1, :] = jnp.sum(d_norm * hat, axis=0, keepdims=True)
        latent_grad[...] = d_state_ref[...] + norm_back(d_norm * gain, hat, inverse)

        total = a_sum[time].astype(f32)
        for k, copy in enumerate(a_times):
            copy.wait_recv()
            total = total + a_time[k].astype(f32)
        qkv_out[:half, :] = total.astype(bf16)
        b_items[0].wait_recv()
        qkv_out[half:, :] = (b_sum[item].astype(f32) + b_item[...].astype(f32)).astype(bf16)
        text_items[0].wait_recv()
        text_out[...] = (grad_text[rows_at(item, span), :].astype(f32) + text_item[...].astype(f32)).astype(bf16)
        for copy in far_copies + text_copies + shares + a_items + b_times + a_times + b_items + text_items:
            copy.wait_send()
        moves.finish()

    qmask, _, bmask = lane_masks()
    links = 2 * others + 2 * (M - 1) + plan.times + GROUPS * others + others + 2 + 7
    result = pl.pallas_call(
        kernel,
        out_shape=[
            jax.ShapeDtypeStruct((TOK, D), f32),
            jax.ShapeDtypeStruct((8, D), f32),
            jax.ShapeDtypeStruct((8, WIDE), f32),
            jax.ShapeDtypeStruct((set_rows, local3), bf16),
            jax.ShapeDtypeStruct((span, 2 * LOCAL), bf16),
        ]
        + moves.out_shapes(),
        in_specs=[VMEM, ANY] + [VMEM] * 19 + [ANY] + [VMEM] * 9 + [ANY] * n_in,
        out_specs=[VMEM] * 5 + [ANY] * n_out,
        scratch_shapes=[
            pltpu.VMEM((ROWS, WIDE), bf16),
            pltpu.VMEM((ROWS, WIDE), bf16),
            pltpu.VMEM((ROWS, 2 * LOCAL), bf16),
            pltpu.VMEM((ROWS, WIDE), bf16),
            pltpu.VMEM((ROWS, WIDE), bf16),
            pltpu.VMEM((ROWS, WIDE), f32),
            pltpu.VMEM((ROWS, WIDE), f32),
            pltpu.VMEM((ROWS, WIDE), f32),
            pltpu.VMEM((text_rows, WIDE), f32),
            pltpu.VMEM((text_rows, WIDE), f32),
            pltpu.VMEM((room, ROWS, 2 * LOCAL), bf16),
            pltpu.VMEM((room, ROWS, 2 * LOCAL), bf16),
            pltpu.VMEM((text_rows, 2 * LOCAL), bf16),
            pltpu.VMEM((room, text_rows, 2 * LOCAL), bf16),
            pltpu.VMEM((ROWS, local3), bf16),
            pltpu.VMEM((text_rows, 2 * LOCAL), bf16),
            pltpu.VMEM((text_rows, text_deep), bf16),
            pltpu.VMEM((D, local3), bf16),
            pltpu.VMEM((text_deep, 2 * LOCAL), bf16),
            pltpu.VMEM((plan.times, half, local3), bf16),
            pltpu.VMEM((plan.times, half, local3), bf16),
            pltpu.VMEM((room, half, local3), bf16),
            pltpu.VMEM((room, GROUPS, half, local3), bf16),
            pltpu.VMEM((GROUPS, half, local3), bf16),
            pltpu.VMEM((half, local3), bf16),
            pltpu.VMEM((span, 2 * LOCAL), bf16),
            pltpu.VMEM((M, folded, 128), f32),
            pltpu.VMEM((M, text_folded, 128), f32),
            pltpu.VMEM((ROWS, 128), f32),
        ]
        + RING_BUFFERS
        + [
            pltpu.SemaphoreType.DMA((links,)),
            pltpu.SemaphoreType.DMA((links,)),
            pltpu.SemaphoreType.DMA((1 + GROUPS,)),
        ]
        + moves.scratch(),
        name="attention_backward",
        compiler_params=params(plan, 63),
    )(
        query,
        packed_all,
        features,
        text_packed,
        text_features,
        self_out,
        cross_out,
        d_mixed,
        gates_q,
        gates_v,
        jnp.asarray(qmask, bf16),
        jnp.asarray(bmask, bf16),
        *hats,
        *inverses,
        text_hat,
        text_inverse,
        cos,
        sin,
        gain_wide,
        captions,
        attn_all,
        qkv_full,
        mix,
        text_mix,
        latents,
        d_state,
        modulation,
        gains,
        first_rows,
        *moves.operands(),
    )
    return result[:5], result[5:]


def finish(plan, small, jobs):
    moves = Transfers(list(jobs))
    n_in, n_out = len(moves.sent), len(moves.jobs)
    peers = plan.all

    def kernel(*refs):
        small_ref = refs[0]
        ins = refs[1 : 1 + n_in]
        all_ref = refs[1 + n_in]
        outs = refs[2 + n_in : 2 + n_in + n_out]
        recv_ref, sum_ref, all_in, send_sem, recv_sem = refs[2 + n_in + n_out : 7 + n_in + n_out]
        me = here()
        greet(me, moves.peers() | set(peers))
        link = Links(me, send_sem, recv_sem)
        moves.bind(me, ins, outs, refs[7 + n_in + n_out :])
        copies = []
        for i, mask in enumerate(peers):
            dest = flip(me, mask)
            copies.append(link(small_ref.at[plan.set_of(dest), dest[2]], recv_ref.at[i], mask))
            copies[-1].start()
        moves.start()
        own = small_ref[plan.set_of(me), me[2]]
        group, everyone = own[:8], own[8:]
        for i, mask in enumerate(peers):
            copies[i].wait_recv()
            if mask[0] == 0:
                group = group + recv_ref[i, :8, :]
            everyone = everyone + recv_ref[i, 8:, :]
        sum_ref[:8, :] = group
        sum_ref[8:, :] = everyone
        place = plan.set_of(me) * M + me[2]
        shares = [link(sum_ref, all_in.at[place], mask) for mask in peers]
        for copy in shares:
            copy.start()
        all_in[place] = sum_ref[...]
        for copy in shares:
            copy.wait_recv()
        all_ref[...] = all_in[...]
        for copy in copies + shares:
            copy.wait_send()
        moves.finish()

    devices = plan.sets * M
    result = pl.pallas_call(
        kernel,
        out_shape=[jax.ShapeDtypeStruct((devices, 16, 128), f32)] + moves.out_shapes(),
        in_specs=[VMEM] + [ANY] * n_in,
        out_specs=[VMEM] + [ANY] * n_out,
        scratch_shapes=[
            pltpu.VMEM((len(peers), 16, 128), f32),
            pltpu.VMEM((16, 128), f32),
            pltpu.VMEM((devices, 16, 128), f32),
            pltpu.SemaphoreType.DMA((2 * len(peers),)),
            pltpu.SemaphoreType.DMA((2 * len(peers),)),
        ]
        + moves.scratch(),
        name="finish",
        compiler_params=params(plan, 40),
    )(small, *moves.operands())
    return result[0], result[1:]


def deliver(gate_parts, up_parts, qkv_pieces, text_pieces, whole, sets):
    times = gate_parts.shape[1]
    k_rows, wide = gate_parts.shape[2:]
    unit = wide // sets
    t_rows = text_pieces.shape[1]
    n = len(whole)

    def kernel(gate_ref, up_ref, qkv_ref, text_ref, *refs):
        ins, (gate_up_out, qkv_out, text_out), outs = refs[:n], refs[n : n + 3], refs[n + 3 :]
        for m in range(M):
            gate = sum(gate_ref[m, t].astype(f32) for t in range(times))
            up = sum(up_ref[t, m].astype(f32) for t in range(times))
            for j in range(sets):
                at = (j * M + m) * unit
                gate_up_out[:, at : at + unit] = gate[:, j * unit : (j + 1) * unit]
                gate_up_out[:, FF + at : FF + at + unit] = up[:, j * unit : (j + 1) * unit]
            piece = qkv_ref[m].astype(f32)
            for j in range(3):
                qkv_out[:, j * D + m * LOCAL : j * D + (m + 1) * LOCAL] = piece[:, j * LOCAL : (j + 1) * LOCAL]
            piece = text_ref[m].astype(f32)
            for j in range(2):
                text_out[:, j * D + m * LOCAL : j * D + (m + 1) * LOCAL] = piece[:, j * LOCAL : (j + 1) * LOCAL]
        for source, target in zip(ins, outs):
            target[...] = source[...]

    return pl.pallas_call(
        kernel,
        out_shape=[
            jax.ShapeDtypeStruct((k_rows, 2 * FF), f32),
            jax.ShapeDtypeStruct((k_rows, 3 * D), f32),
            jax.ShapeDtypeStruct((t_rows, 2 * D), f32),
        ]
        + [jax.ShapeDtypeStruct(x.shape, x.dtype) for x in whole],
        in_specs=[VMEM] * (4 + n),
        out_specs=[VMEM] * (3 + n),
        name="deliver",
        compiler_params=pltpu.CompilerParams(vmem_limit_bytes=48 * 2**20),
    )(gate_parts, up_parts, qkv_pieces, text_pieces, *whole)


def feed_forward(
    plan, mixed, out_full, latents, cotangent, modulation, gains, first_rows, gate_full, up_shard, down_weight
):
    d_rows = down_weight.shape[0]
    width = plan.sets * d_rows
    deep = out_full.shape[0]
    up_job = plan.stack_time(up_shard)
    down_job = plan.stack_time(down_weight)
    moves = Transfers(
        [up_job, plan.stack_item(up_shard, up_job), down_job, plan.stack_item(down_weight, down_job)]
    )
    n_in, n_out = len(moves.sent), len(moves.jobs)
    turned = (((1,), (1,)), ((), ()))
    sunk = (((0,), (0,)), ((), ()))
    plain = (((1,), (0,)), ((), ()))
    chip_rows = 2 * TOK
    part_rows = D // GROUPS
    others = len(plan.time)
    slab = plan.times * d_rows

    def kernel(*refs):
        (mixed_ref, out_w, latent_ref, cot_ref, mod_ref, gain_ref, first_ref, gate_w) = refs[:8]
        ins = refs[8 : 8 + n_in]
        refs = refs[8 + n_in :]
        (result_ref, d_state_ref, d_mixed_ref, grad_out_ref, gate_sum_ref, up_sum_ref, down_grad_ref, sums_ref) = refs[:8]
        outs = refs[8 : 8 + n_out]
        refs = refs[8 + n_out :]
        (up_w, down_w, ffn_all, down_all, proj_all, gate_ref, up_ref, act_ref, d_gate_ref, d_up_ref) = refs[:10]
        (grad_gate, grad_up, grad_down, from_gate, from_up, from_down, down_sum, from_time) = refs[10:18]
        (to_mate, from_mate, to_chip, from_chip, part, proj_ref, state_ref, own_ref, send_sem, recv_sem, local_sem) = refs[
            18:29
        ]
        me = here()
        item, time, ring = me
        core, chip = ring % 2, ring // 2
        greet(me, moves.peers() | {plan.mate, plan.item} | set(plan.chips) | set(plan.time))
        moves.bind(me, ins, outs, refs[29:])
        moves.start(late=(2,))
        link = Links(me, send_sem, recv_sem)
        buffers = (to_mate, from_mate, to_chip, from_chip, part)

        def scatter(product, meanwhile=lambda: None):
            ring_sum(plan, link, me, buffers, product, meanwhile)

        def gather(all_ref, each, meanwhile=lambda: None, ready=lambda: None):
            ring_gather(plan, link, me, all_ref, each, meanwhile, ready)

        is_first = first_ref[...] > 0.5

        def modulated(index):
            cols = pl.ds(index * D, D)
            return jnp.where(is_first, mod_ref[0:1, cols], mod_ref[1:2, cols])

        def column_sums(at, values):
            total = jnp.sum(values, axis=0, keepdims=True)
            start = jnp.sum(jnp.where(is_first, values, 0.0), axis=0, keepdims=True)
            sums_ref[at : at + 1, :] = start
            sums_ref[at + 1 : at + 2, :] = total - start

        def scale_of(values):
            return lax.rsqrt(jnp.mean(values * values, axis=1, keepdims=True) + epsilon)

        def norm_back(d_hat, hat, inverse):
            return inverse * (d_hat - hat * jnp.mean(d_hat * hat, axis=1, keepdims=True))

        def load(job, target):
            moves.take(job)
            copy = pltpu.make_async_copy(outs[job], target, local_sem.at[0])
            copy.start()
            copy.wait()

        def out_product(block):
            return jnp.dot(mixed_ref[rows_at(block, TOK), :], out_w[...], preferred_element_type=f32)

        def next_weights():
            moves.chain(late=(3,))
            moves.start_job(2)

        scatter(out_product, next_weights)
        proj_ref[...] = part[...]
        proj = proj_ref[...]
        gate_attn = jnp.tanh(modulated(1))
        state_ref[...] = latent_ref[...] + gate_attn * (proj * scale_of(proj) * gain_ref[1:2, :])
        state = state_ref[...]
        ffn_in = state * scale_of(state) * gain_ref[2:3, :] * (1.0 + modulated(2))
        ffn_all[rows_at(ring, TOK), :] = ffn_in.astype(bf16)

        def forward_chip(which):
            rows = rows_at(which, chip_rows)
            block = ffn_all[rows, :]
            gate = jnp.dot(block, gate_w[...], preferred_element_type=f32)
            up = jnp.dot(block, up_w[...], preferred_element_type=f32)
            gate_ref[rows, :] = gate
            up_ref[rows, :] = up
            act_ref[rows, :] = (gate * (1.0 / (1.0 + jnp.exp(-gate))) * up).astype(bf16)

        def weights_here():
            load(1, up_w)

        gather(ffn_all, forward_chip, moves.chain, weights_here)

        load(3, down_w)

        def down_product(block):
            return jnp.dot(act_ref[rows_at(block, TOK), :], down_w[...], preferred_element_type=f32)

        scatter(down_product)

        down = part[...]
        inverse = scale_of(down)
        hat = down * inverse
        gate_ffn = jnp.tanh(modulated(3))
        gain = gain_ref[3:4, :]
        cot = cot_ref[...]
        result_ref[...] = state_ref[...] + gate_ffn * (hat * gain)
        column_sums(7, cot * (hat * gain) * (1.0 - gate_ffn * gate_ffn))
        d_norm = cot * gate_ffn
        sums_ref[2:3, :] = jnp.sum(d_norm * hat, axis=0, keepdims=True)
        down_all[rows_at(ring, TOK), :] = norm_back(d_norm * gain, hat, inverse).astype(bf16)

        def backward_chip(which):
            rows = rows_at(which, chip_rows)
            d_act = lax.dot_general(down_all[rows, :], down_w[...], turned, preferred_element_type=f32)
            gate, up = gate_ref[rows, :], up_ref[rows, :]
            sigmoid = 1.0 / (1.0 + jnp.exp(-gate))
            d_up_ref[rows, :] = (d_act * (gate * sigmoid)).astype(bf16)
            d_gate_ref[rows, :] = (d_act * up * (sigmoid * (1.0 + gate * (1.0 - sigmoid)))).astype(bf16)

        gather(down_all, backward_chip)

        away = 1 - item
        down_link = link(grad_down.at[rows_at(away, slab)], from_down, plan.item)
        gate_link = link(grad_gate.at[rows_at(away, part_rows)], from_gate, plan.item)
        up_link = link(grad_up.at[rows_at(away, part_rows)], from_up, plan.item)
        time_links = [link(down_sum.at[rows_at(time ^ mask[1], d_rows)], from_time.at[i], mask) for i, mask in enumerate(plan.time)]

        def down_gradient():
            grad_down[...] = lax.dot_general(act_ref[...], down_all[...], sunk, preferred_element_type=f32).astype(bf16)
            down_link.start()

        down_gradient()

        def gate_gradients():
            grad_gate[...] = lax.dot_general(ffn_all[...], d_gate_ref[...], sunk, preferred_element_type=f32).astype(bf16)
            gate_link.start()
            grad_up[...] = lax.dot_general(ffn_all[...], d_up_ref[...], sunk, preferred_element_type=f32).astype(bf16)
            up_link.start()

        def back_product(block):
            rows = rows_at(block, TOK)
            return lax.dot_general(d_gate_ref[rows, :], gate_w[...], turned, preferred_element_type=f32) + lax.dot_general(
                d_up_ref[rows, :], up_w[...], turned, preferred_element_type=f32
            )

        scatter(back_product, gate_gradients)

        d_ffn = part[...]
        state = state_ref[...]
        inverse = scale_of(state)
        hat = state * inverse
        gain = gain_ref[2:3, :]
        column_sums(5, d_ffn * (hat * gain))
        d_norm = d_ffn * (1.0 + modulated(2))
        sums_ref[1:2, :] = jnp.sum(d_norm * hat, axis=0, keepdims=True)
        d_state_ref[...] = cot_ref[...] + norm_back(d_norm * gain, hat, inverse)
        d_state = d_state_ref[...]
        proj = proj_ref[...]
        inverse = scale_of(proj)
        hat = proj * inverse
        gate_attn = jnp.tanh(modulated(1))
        gain = gain_ref[1:2, :]
        column_sums(3, d_state * (hat * gain) * (1.0 - gate_attn * gate_attn))
        d_norm = d_state * gate_attn
        sums_ref[0:1, :] = jnp.sum(d_norm * hat, axis=0, keepdims=True)
        proj_all[rows_at(ring, TOK), :] = norm_back(d_norm * gain, hat, inverse).astype(bf16)

        def down_time():
            down_link.wait_recv()
            mine = grad_down[rows_at(item, slab), :].astype(f32) + from_down[...].astype(f32)
            down_sum[...] = mine.astype(bf16)
            for copy in time_links:
                copy.start()

        def mixed_chip(which):
            rows = rows_at(which, chip_rows)
            d_mixed_ref[rows, :] = lax.dot_general(
                proj_all[rows, :], out_w[...], turned, preferred_element_type=f32
            ).astype(bf16)

        gather(proj_all, mixed_chip, ready=down_time)
        grad_out_ref[...] = lax.dot_general(mixed_ref[...], proj_all[...], sunk, preferred_element_type=f32).astype(bf16)
        gate_link.wait_recv()
        gate_sum_ref[...] = (
            grad_gate[rows_at(item, part_rows), :].astype(f32) + from_gate[...].astype(f32)
        ).astype(bf16)
        own_ref[...] = down_sum[rows_at(time, d_rows), :].astype(f32)
        for i, copy in enumerate(time_links):
            copy.wait_recv()
            own_ref[...] += from_time[i].astype(f32)
        down_grad_ref[...] = own_ref[...]
        up_link.wait_recv()
        up_sum_ref[...] = (grad_up[rows_at(item, part_rows), :].astype(f32) + from_up[...].astype(f32)).astype(bf16)
        for copy in [down_link, gate_link, up_link] + time_links:
            copy.wait_send()
        moves.finish()

    links = 7 * 3 + 7 * 3 + 3 + others
    result = pl.pallas_call(
        kernel,
        out_shape=[
            jax.ShapeDtypeStruct((TOK, D), f32),
            jax.ShapeDtypeStruct((TOK, D), f32),
            jax.ShapeDtypeStruct((ROWS, deep), bf16),
            jax.ShapeDtypeStruct((deep, D), bf16),
            jax.ShapeDtypeStruct((part_rows, width), bf16),
            jax.ShapeDtypeStruct((part_rows, width), bf16),
            jax.ShapeDtypeStruct((d_rows, D), f32),
            jax.ShapeDtypeStruct((16, D), f32),
        ]
        + moves.out_shapes(),
        in_specs=[VMEM] * 8 + [ANY] * n_in,
        out_specs=[VMEM] * 8 + [ANY] * n_out,
        scratch_shapes=[
            pltpu.VMEM((D, width), bf16),
            pltpu.VMEM((width, D), bf16),
            pltpu.VMEM((ROWS, D), bf16),
            pltpu.VMEM((ROWS, D), bf16),
            pltpu.VMEM((ROWS, D), bf16),
            pltpu.VMEM((ROWS, width), f32),
            pltpu.VMEM((ROWS, width), f32),
            pltpu.VMEM((ROWS, width), bf16),
            pltpu.VMEM((ROWS, width), bf16),
            pltpu.VMEM((ROWS, width), bf16),
            pltpu.VMEM((D, width), bf16),
            pltpu.VMEM((D, width), bf16),
            pltpu.VMEM((width, D), bf16),
            pltpu.VMEM((part_rows, width), bf16),
            pltpu.VMEM((part_rows, width), bf16),
            pltpu.VMEM((slab, D), bf16),
            pltpu.VMEM((slab, D), bf16),
            pltpu.VMEM((max(others, 1), d_rows, D), bf16),
            pltpu.VMEM((4, TOK, D), bf16),
            pltpu.VMEM((4, TOK, D), bf16),
            pltpu.VMEM((3, TOK, D), bf16),
            pltpu.VMEM((3, TOK, D), bf16),
            pltpu.VMEM((TOK, D), f32),
            pltpu.VMEM((TOK, D), f32),
            pltpu.VMEM((TOK, D), f32),
            pltpu.VMEM((d_rows, D), f32),
            pltpu.SemaphoreType.DMA((links,)),
            pltpu.SemaphoreType.DMA((links,)),
            pltpu.SemaphoreType.DMA((1,)),
        ]
        + moves.scratch(),
        name="feed_forward",
        compiler_params=params(plan, 60),
    )(mixed, out_full, latents, cotangent, modulation, gains, first_rows, gate_full, *moves.operands())
    return result[:8]


def shards(
    latents,
    conditions,
    captions,
    row_counts,
    text_lengths,
    qkv_weight,
    text_weight,
    out_weight,
    gate_up_weight,
    down_weight,
    ada_weight,
    ada_bias,
    norm_gains,
    head_gates,
    cotangent,
):
    times = lax.axis_size("times")
    plan = Plan(times)
    sets, rows_axis = plan.sets, plan.rows
    devices = sets * M
    item, time, ring = here()
    place = (item * times + time) * M + ring
    group_place = time * M + ring
    heads = LOCAL // HEAD

    k_rows = qkv_weight.shape[0]
    t_rows = text_weight.shape[0]
    o_rows = out_weight.shape[0]
    d_rows = down_weight.shape[0]
    a_rows = ada_weight.shape[0]
    bias_n = ada_bias.shape[0]
    gain_n = norm_gains.shape[1]
    tiles = -(-(4 * D // 128) // rows_axis)

    package = jnp.concatenate(
        [norm_gains.astype(f32).reshape(-1), ada_bias.astype(f32), row_counts[0, 0].astype(f32)]
    )
    package_n = package.shape[0]
    lines = -(-package_n // 1024) * 8
    package = jnp.pad(package, (0, lines * 128 - package_n)).reshape(lines, 128)

    silu = jax.nn.silu(conditions[0].astype(f32)).astype(bf16).astype(f32)
    other_place = ((1 - item) * times + time) * M + ring
    cond = jnp.stack(
        [lax.dynamic_slice_in_dim(silu, p * a_rows, a_rows, 1) for p in (place, other_place)]
    )
    cond = jnp.pad(cond, ((0, 0), (0, 8 - FRAMES), (0, 128 - a_rows)))

    key_places, value_places = wide_order()
    mix = placing(np.concatenate([key_places, WIDE + key_places, 2 * WIDE + value_places]), 3 * WIDE)
    text_mix = placing(np.concatenate([key_places, WIDE + value_places]), 2 * WIDE)
    qkv_send = qkv_weight.reshape(k_rows, 3, M, LOCAL).transpose(2, 0, 1, 3).reshape(M, k_rows, 3 * LOCAL)
    text_send = text_weight.reshape(t_rows, 2, M, LOCAL).transpose(2, 0, 1, 3).reshape(M, t_rows, 2 * LOCAL)
    gate_up_send = gate_up_weight.reshape(k_rows, 2, sets, M, d_rows).transpose(1, 3, 0, 2, 4)
    gate_up_send = gate_up_send.reshape(2, M, k_rows, sets * d_rows)
    out_forth = [(o, (o % sets) * M + o // sets) for o in range(devices)]
    out_back = [(b, a) for a, b in out_forth]
    axes = ("items", "times", "ring")
    out_shard = lax.ppermute(out_weight, axes, out_forth)

    text_job = plan.scatter_ring(text_send)
    mod_tiles, cond_other, (packages, _, text_full, qkv_time) = prologue(
        plan,
        tiles,
        package,
        cond,
        ada_weight,
        [text_job, plan.swap_source(text_job), plan.scatter_group_ring(qkv_send)],
    )
    packages = packages.reshape(devices, lines * 128)
    gains = packages[:, : 7 * gain_n].reshape(devices, 7, gain_n).transpose(1, 0, 2).reshape(7, D)
    gains = jnp.pad(gains, ((0, 1), (0, 0)))
    bias = packages[:, 7 * gain_n : 7 * gain_n + bias_n].reshape(4 * D)
    counts_all = packages[:, 7 * gain_n + bias_n : package_n].astype(jnp.int32).reshape(GROUPS, rows_axis, FRAMES)
    counts = lax.dynamic_index_in_dim(counts_all, item, 0, keepdims=False)

    def from_tiles(array):
        lead = array.shape[:-3]
        array = array[..., : FRAMES * tiles, :].reshape(lead + (rows_axis, FRAMES, tiles, 128))
        array = jnp.moveaxis(array, -3, -4).reshape(lead + (FRAMES, rows_axis * tiles * 128))
        return array[..., : 4 * D]

    modulation = from_tiles(mod_tiles) + bias

    line = jnp.arange(TOK, dtype=jnp.int32)[None, :]
    clip = counts[:, :1]
    before = jnp.cumsum(counts, axis=0) - counts
    frame_all = (line >= clip).astype(jnp.int32)
    position_all = jnp.where(frame_all == 0, before[:, :1] + line, before[:, 1:] + line - clip)
    frame_k = frame_all.reshape(-1)
    frame_q = lax.dynamic_slice_in_dim(frame_k, time * ROWS, ROWS)
    position_q = lax.dynamic_slice_in_dim(position_all.reshape(-1), time * ROWS, ROWS).astype(f32)
    frame_own = lax.dynamic_index_in_dim(frame_all, group_place, 0, keepdims=False)
    first_rows = (frame_own == 0).astype(f32)[:, None]
    text_line = jnp.arange(FRAMES * TEXT, dtype=jnp.int32)
    text_frame = text_line // TEXT
    text_live = text_line % TEXT < jnp.repeat(text_lengths[0], TEXT)

    feature = jnp.arange(128, dtype=jnp.int32)[None, :]

    def key_features(apart_first, apart_second):
        ones = (feature >= SPARE + 2) & (feature < SPARE + 2 + 3 * heads)
        pick = jnp.where(feature == SPARE, apart_first[:, None], (feature == SPARE + 1) & apart_second[:, None])
        return jnp.where(pick | ones, 1.0, 0.0).astype(bf16)

    features = key_features(frame_k == 1, frame_k == 0)
    text_features = key_features(~((text_frame == 0) & text_live), ~((text_frame == 1) & text_live))
    query_features = jnp.where(feature == SPARE + frame_q[:, None], -APART, 0.0).astype(bf16)
    pair = jnp.arange(128, dtype=jnp.int32)
    frequency = theta_base ** (-2.0 * (pair % (HEAD // 2)).astype(f32) / HEAD)
    angle = position_q[:, None] * frequency[None, :]
    live_lane = (pair < SPARE)[None, :]
    cos, sin = jnp.where(live_lane, jnp.cos(angle), 0.0), jnp.where(live_lane, jnp.sin(angle), 0.0)
    own_gates = jnp.tanh(lax.dynamic_slice_in_dim(head_gates.astype(f32), ring * heads, heads))
    gates_v = jnp.concatenate([jnp.zeros((HEAD,), f32), jnp.repeat(own_gates, HEAD)]).reshape(1, WIDE)
    half_gates = jnp.pad(jnp.repeat(own_gates, HEAD // 2), (0, 128 - SPARE))
    gates_q = jnp.concatenate([half_gates, half_gates]).reshape(1, WIDE)
    gain_wide = lax.dynamic_slice(gains, (4, ring * LOCAL), (3, LOCAL))
    gain_wide = gain_wide.reshape(3, heads, HEAD // 2, 2).transpose(0, 3, 1, 2).reshape(3, 2, SPARE)
    gain_wide = jnp.pad(gain_wide, ((0, 5), (0, 0), (0, 128 - SPARE))).reshape(8, WIDE)

    inputs = latents[0]
    caption_rows = captions[0].reshape(FRAMES * TEXT, TEXT_DIM)
    forward, (qkv_full, _, out_full, _, up_shard, _, gate_full) = attention_forward(
        plan,
        inputs,
        modulation,
        gains,
        first_rows,
        caption_rows,
        text_full.reshape(GROUPS * M * t_rows, 2 * LOCAL),
        mix,
        text_mix,
        gain_wide,
        cos,
        sin,
        query_features,
        features,
        text_features,
        gates_v,
        qkv_time.reshape(times * M * k_rows, 3 * LOCAL),
        out_shard,
        gate_up_send[0],
        gate_up_send[1],
    )
    (mixed, self_out, cross_out, attn_all, query, packed_all, text_packed, qn, kn, q_inv, k_inv, tn, t_inv) = forward
    out_full = jnp.pad(out_full.reshape(LOCAL, D), ((HEAD, 0), (0, 0)))

    (result_rows, d_state, d_mixed, grad_out, gate_sum, up_sum, down_grad, ffn_sums) = feed_forward(
        plan,
        mixed,
        out_full,
        inputs,
        cotangent[0],
        modulation,
        gains,
        first_rows,
        gate_full.reshape(D, sets * d_rows),
        up_shard.reshape(M * k_rows, sets * d_rows),
        down_weight,
    )
    ring_shape = (times, M, k_rows, sets * d_rows)
    (grad_latent, attn_sums, wide_sums, qkv_sum, text_sum), (_, gate_parts, up_pieces, out_parts) = attention_backward(
        plan,
        query,
        packed_all,
        features,
        text_packed,
        text_features,
        self_out,
        cross_out,
        d_mixed,
        gates_q,
        gates_v,
        (qn, kn),
        (q_inv, k_inv),
        tn,
        t_inv,
        cos,
        sin,
        gain_wide,
        caption_rows,
        attn_all,
        qkv_full,
        mix,
        text_mix,
        inputs,
        d_state,
        modulation,
        gains,
        first_rows,
        gate_sum.reshape(ring_shape),
        up_sum.reshape(ring_shape),
        grad_out[HEAD:].reshape(sets, o_rows, D),
    )

    def add(parts, axis=0):
        return jnp.sum(parts.astype(f32), axis=axis)

    d_mod = jnp.concatenate([attn_sums[1:3], ffn_sums[3:5], ffn_sums[5:7], ffn_sums[7:9]], axis=1)
    d_mod = jnp.pad(d_mod, ((0, 0), (0, rows_axis * tiles * 128 - 4 * D)))
    d_mod = d_mod.reshape(FRAMES, rows_axis, tiles, 128).transpose(1, 0, 2, 3).reshape(rows_axis, FRAMES * tiles, 128)
    d_mod = jnp.pad(d_mod, ((0, 0), (0, 8 - FRAMES * tiles), (0, 0)))
    d_mod = jnp.tile(d_mod, (GROUPS, 1, 1))
    wide_gains = wide_sums[:3].reshape(3, 2, 128)[:, :, :SPARE].reshape(3, 2, heads, HEAD // 2)
    wide_gains = wide_gains.transpose(0, 2, 3, 1).reshape(3, LOCAL)
    wide_gains = wide_gains * jnp.stack([jnp.ones(()), jnp.ones(()), (time == 0).astype(f32)])[:, None]
    wide_gains = lax.dynamic_update_slice(jnp.zeros((3, D), f32), wide_gains, (0, ring * LOCAL))
    gate_sums = jnp.sum(wide_sums[3, HEAD:].reshape(heads, HEAD), axis=1) * (1.0 - own_gates * own_gates)
    gate_row = lax.dynamic_update_slice_in_dim(jnp.zeros((1, D), f32), gate_sums[None], ring * heads, 1)
    d_gains = jnp.concatenate([attn_sums[:1], ffn_sums[:3], wide_gains, gate_row], axis=0)
    gain_tiles = D // 128
    d_gains = d_gains.reshape(8, gain_tiles, 128).transpose(1, 0, 2)
    d_gains = jnp.pad(d_gains, ((0, devices - gain_tiles), (0, 0), (0, 0)))
    small = jnp.concatenate([d_mod, d_gains], axis=1).reshape(sets, M, 16, 128)
    small_all, (up_parts, qkv_pieces, text_pieces) = finish(
        plan,
        small,
        [
            plan.times_of_ring(up_pieces),
            plan.scatter_ring(qkv_sum.reshape(M, k_rows, 3 * LOCAL)),
            plan.scatter_ring(text_sum.reshape(M, t_rows, 2 * LOCAL)),
        ],
    )
    gains_all = small_all[:gain_tiles, 8:].transpose(1, 0, 2).reshape(8, D)
    gains_grad = lax.dynamic_slice_in_dim(gains_all[:7], place * gain_n, gain_n, 1)
    gates_grad = gains_all[7, :HEADS]
    d_mod_all = from_tiles(small_all[:, :8].reshape(GROUPS, rows_axis, 8, 128)).reshape(GROUPS * FRAMES, 4 * D)
    cond_own, cond_other = cond[0, :FRAMES], cond_other[:FRAMES]
    silu_both = jnp.where(
        item == 0, jnp.concatenate([cond_own, cond_other]), jnp.concatenate([cond_other, cond_own])
    )
    ada_grad = jnp.einsum("fc,fd->cd", silu_both[:, :a_rows], d_mod_all, precision=highest)
    bias_grad = lax.dynamic_slice_in_dim(jnp.sum(d_mod_all, axis=0), place * bias_n, bias_n)
    out_grad = lax.ppermute(add(out_parts), axes, out_back)
    gate_up_grad, qkv_grad, text_grad, result_rows, grad_latent, down_grad = deliver(
        gate_parts, up_parts, qkv_pieces, text_pieces, [result_rows, grad_latent, down_grad], sets
    )
    return (
        result_rows[None],
        grad_latent[None],
        qkv_grad,
        text_grad,
        out_grad,
        gate_up_grad,
        down_grad,
        ada_grad,
        bias_grad,
        gains_grad,
        gates_grad,
    )


def solution(mesh):
    items, rows = mesh.shape["items"], mesh.shape["rows"]
    fine = Mesh(mesh.devices.reshape(items, rows // M, M), ("items", "times", "ring"))
    whole = ("items", "times", "ring")
    rows_of = ("times", "ring")
    return jax.shard_map(
        shards,
        mesh=fine,
        in_specs=(
            P("items", rows_of, None),
            P("items", None, None),
            P("items", None, None, None),
            P("items", rows_of, None),
            P("items", None),
            P(whole, None),
            P(whole, None),
            P(whole, None),
            P(whole, None),
            P(whole, None),
            P(whole, None),
            P(whole),
            P(None, whole),
            P(),
            P("items", rows_of, None),
        ),
        out_specs=(
            P("items", rows_of, None),
            P("items", rows_of, None),
            P(whole, None),
            P(whole, None),
            P(whole, None),
            P(whole, None),
            P(whole, None),
            P(whole, None),
            P(whole),
            P(None, whole),
            P(),
        ),
        check_vma=False,
    )
```

```python
import jax
import jax.numpy as jnp
import numpy as np
from jax import lax
from jax.experimental import pallas as pl
from jax.experimental.pallas import tpu as pltpu
from jax.sharding import Mesh
from jax.sharding import PartitionSpec as P

D = 1536
HEADS = 24
HEAD = 64
FF = 4096
TEXT_DIM = 4096
COND = 1024
TEXT = 256
FRAMES = 2
TOK = 128
GROUPS = 2
M = 8
LOCAL = HEADS // M * HEAD
ROWS = M * TOK
WIDE = 256
SPARE = 96
APART = 8192.0

epsilon = 1e-05
theta_base = 10000.0
highest = lax.Precision.HIGHEST
MESH = pl.DeviceIdType.MESH
f32 = jnp.float32
bf16 = jnp.bfloat16
ANY = pl.BlockSpec(memory_space=pl.ANY)
VMEM = pl.BlockSpec(memory_space=pltpu.VMEM)


def flip(where, mask):
    return tuple(a if b == 0 else a ^ b for a, b in zip(where, mask))


class Job:
    def __init__(self, x, shape, masks, src, dst, pass_on=(), by=None, source=None, piece=None):
        self.x, self.shape, self.masks, self.src, self.dst = x, shape, masks, src, dst
        self.piece = piece
        self.pass_on, self.by, self.source = tuple(pass_on), by, source
        if source is not None:
            self.x = None
        self.dtype = x.dtype

    def count(self):
        return len(self.masks) + len(self.pass_on)

    def block(self):
        return self.piece or self.shape[len(self.dst((0, 0, 0))) :]

    def peers(self):
        return set(self.masks) | ({self.by} if self.pass_on else set())


class Transfers:
    def __init__(self, jobs):
        self.jobs = jobs
        self.sent = [j for j in jobs if j.source is None]
        self.total = sum(j.count() for j in jobs)

    def operands(self):
        return [j.x for j in self.sent]

    def out_shapes(self):
        return [jax.ShapeDtypeStruct(j.shape, j.dtype) for j in self.jobs]

    def scratch(self):
        if not self.jobs:
            return []
        return [
            pltpu.SemaphoreType.DMA((self.total,)),
            pltpu.SemaphoreType.DMA((self.total,)),
            pltpu.SemaphoreType.DMA((2, len(self.jobs))),
        ] + [pltpu.VMEM(j.block(), j.dtype) for j in self.jobs]

    def peers(self):
        found = set()
        for j in self.jobs:
            found |= j.peers()
        return found

    def bind(self, me, ins, outs, sems):
        self.me, self.outs, self.sems = me, outs, sems
        left = list(ins)
        self.ins = []
        for j in self.jobs:
            self.ins.append(left.pop(0) if j.source is None else outs[self.jobs.index(j.source)])
        self.base, at = [], 0
        for j in self.jobs:
            self.base.append(at)
            at += j.count()
        self.arrived, self.kept, self.settled, self.chained, self.forwarded = set(), set(), set(), set(), set()

    def remote(self, src, dst, slot, dest):
        return pltpu.make_async_remote_copy(
            src_ref=src,
            dst_ref=dst,
            send_sem=self.sems[0].at[slot],
            recv_sem=self.sems[1].at[slot],
            device_id=dest,
            device_id_type=MESH,
        )

    def send(self, k, i):
        j = self.jobs[k]
        if i < len(j.masks):
            dest = flip(self.me, j.masks[i])
            at = j.src(dest)
            src = self.ins[k] if at is None else self.ins[k].at[at]
            return self.remote(src, self.outs[k].at[j.dst(self.me)], self.base[k] + i, dest)
        mask = j.pass_on[i - len(j.masks)]
        block = self.outs[k].at[j.dst(flip(self.me, mask))]
        return self.remote(block, block, self.base[k] + i, flip(self.me, j.by))

    def own(self, k, leg):
        j = self.jobs[k]
        room = self.sems[3 + k]
        if leg == 0:
            at = j.src(self.me)
            src = self.ins[k] if at is None else self.ins[k].at[at]
            return pltpu.make_async_copy(src, room, self.sems[2].at[0, k])
        return pltpu.make_async_copy(room, self.outs[k].at[j.dst(self.me)], self.sems[2].at[1, k])

    def start_job(self, k):
        j = self.jobs[k]
        for i in range(len(j.masks)):
            self.send(k, i).start()
        self.own(k, 0).start()

    def start(self, late=()):
        for k, j in enumerate(self.jobs):
            if j.source is None and k not in late:
                self.start_job(k)

    def receive(self, k, i):
        if (k, i) not in self.arrived:
            self.arrived.add((k, i))
            self.send(k, i).wait_recv()

    def take(self, k):
        self.keep(k)
        for i in range(self.jobs[k].count()):
            self.receive(k, i)
        if k not in self.settled:
            self.settled.add(k)
            self.own(k, 1).wait()

    def keep(self, k):
        if k not in self.kept:
            self.kept.add(k)
            self.own(k, 0).wait()
            self.own(k, 1).start()

    def chain(self, late=()):
        for k, j in enumerate(self.jobs):
            if j.source is not None and k not in self.chained and k not in late:
                self.chained.add(k)
                self.take(self.jobs.index(j.source))
                self.start_job(k)

    def forward(self):
        self.chain()
        for k in range(len(self.jobs)):
            self.keep(k)
        for k, j in enumerate(self.jobs):
            if k not in self.forwarded:
                self.forwarded.add(k)
                for n, mask in enumerate(j.pass_on):
                    self.receive(k, j.masks.index(mask))
                    self.send(k, len(j.masks) + n).start()

    def finish(self):
        self.forward()
        for k, j in enumerate(self.jobs):
            self.take(k)
            for i in range(j.count()):
                self.send(k, i).wait_send()


class Plan:
    def __init__(self, times):
        self.times = times
        self.sets = GROUPS * times
        self.rows = times * M
        self.next_id = 0
        ones = [(i, t, m) for i in range(GROUPS) for t in range(times) for m in range(M)]
        self.all = ones[1:]
        self.ring = [(0, 0, m) for m in range(1, M)]
        self.chips = [(0, 0, m) for m in range(2, M, 2)]
        self.mate = (0, 0, 1)
        self.time = [(0, t, 0) for t in range(1, times)]
        self.item = (1, 0, 0)
        self.span = [(i, t, 0) for i in range(GROUPS) for t in range(times)][1:]
        self.group = [(0, t, m) for t in range(times) for m in range(M)][1:]

    def identity(self):
        self.next_id += 1
        return self.next_id

    def set_of(self, where):
        return where[0] * self.times + where[1]

    def gather_ring(self, x):
        return Job(
            x,
            (M,) + x.shape,
            [self.mate] + self.chips,
            lambda dest: None,
            lambda sender: (sender[2],),
            self.chips,
            self.mate,
        )

    def direct_ring(self, x):
        return Job(x, (M,) + x.shape, self.ring, lambda dest: None, lambda sender: (sender[2],))

    def scatter_ring(self, x):
        return Job(x, x.shape, self.ring, lambda dest: (dest[2],), lambda sender: (sender[2],))

    def gather_span(self, x, shape=None, source=None):
        return Job(
            x,
            (self.sets,) + (x.shape if shape is None else shape),
            [self.item] + self.time,
            lambda dest: None,
            lambda sender: (self.set_of(sender),),
            self.time,
            self.item,
            source,
        )

    def scatter_span(self, x):
        return Job(x, x.shape, self.span, lambda dest: (self.set_of(dest),), lambda sender: (self.set_of(sender),))

    def gather_time(self, x):
        return Job(x, (self.times,) + x.shape, self.time, lambda dest: None, lambda sender: (sender[1],))

    def stack_time(self, x):
        n = x.shape[0]
        return Job(
            x,
            (self.times * n,) + x.shape[1:],
            self.time,
            lambda dest: None,
            lambda sender: (pl.ds(pl.multiple_of(sender[1] * n, n), n),),
            piece=x.shape,
        )

    def stack_item(self, x, source=None):
        shape = x.shape if source is None else source.shape
        n = shape[0]
        return Job(
            x,
            (GROUPS * n,) + shape[1:],
            [self.item],
            lambda dest: None,
            lambda sender: (pl.ds(pl.multiple_of(sender[0] * n, n), n),),
            source=source,
            piece=shape,
        )

    def split_time(self, x):
        n = x.shape[0] // self.times
        return Job(
            x,
            (self.times, n) + x.shape[1:],
            self.time,
            lambda dest: (pl.ds(pl.multiple_of(dest[1] * n, n), n),),
            lambda sender: (sender[1],),
        )

    def scatter_group_ring(self, x):
        return Job(
            x,
            (self.times,) + x.shape,
            self.group,
            lambda dest: (dest[2],),
            lambda sender: (sender[1], sender[2]),
        )

    def swap_source(self, source):
        return Job(
            source.x if source.x is not None else source,
            (GROUPS,) + source.shape,
            [self.item],
            lambda dest: None,
            lambda sender: (sender[0],),
            source=source,
        )

    def gather_time_source(self, source):
        return Job(
            source,
            (self.times,) + source.shape,
            self.time,
            lambda dest: None,
            lambda sender: (sender[1],),
            source=source,
        )

    def ring_of_times(self, x, source=None):
        shape = x.shape if source is None else source.shape
        return Job(
            x if source is None else source,
            (M, shape[0]) + tuple(shape[2:]),
            self.ring,
            lambda dest: (slice(None), dest[2]),
            lambda sender: (sender[2],),
            source=source,
        )

    def times_of_ring(self, x):
        shape = x.shape
        return Job(
            x,
            (shape[1], shape[0]) + tuple(shape[2:]),
            self.time,
            lambda dest: (slice(None), dest[1]),
            lambda sender: (sender[1],),
        )

    def scatter_time(self, x):
        return Job(x, x.shape, self.time, lambda dest: (dest[1],), lambda sender: (sender[1],))

    def scatter_item(self, x):
        return Job(x, x.shape, [self.item], lambda dest: (dest[0],), lambda sender: (sender[0],))

    def gather_all(self, x):
        return Job(
            x,
            (self.sets, M) + x.shape,
            self.all,
            lambda dest: None,
            lambda sender: (self.set_of(sender), sender[2]),
        )

    def scatter_all(self, x):
        return Job(
            x,
            x.shape,
            self.all,
            lambda dest: (self.set_of(dest), dest[2]),
            lambda sender: (self.set_of(sender), sender[2]),
        )

    def swap_item(self, x):
        return Job(x, (GROUPS,) + x.shape, [self.item], lambda dest: None, lambda sender: (sender[0],))

    def gather_group(self, x):
        return Job(
            x,
            (self.times, M) + x.shape,
            self.group,
            lambda dest: None,
            lambda sender: (sender[1], sender[2]),
        )

    def scatter_group(self, x):
        return Job(
            x,
            x.shape,
            self.group,
            lambda dest: (dest[1], dest[2]),
            lambda sender: (sender[1], sender[2]),
        )


def here():
    return (lax.axis_index("items"), lax.axis_index("times"), lax.axis_index("ring"))


def greet(me, peers):
    barrier = pltpu.get_barrier_semaphore()
    for mask in sorted(peers):
        pl.semaphore_signal(barrier, inc=1, device_id=flip(me, mask), device_id_type=MESH)
    pl.semaphore_wait(barrier, len(peers))


def exchange(plan, name, jobs):
    moves = Transfers(jobs)
    n_in, n_out = len(moves.sent), len(jobs)

    def kernel(*refs):
        me = here()
        greet(me, moves.peers())
        moves.bind(me, refs[:n_in], refs[n_in : n_in + n_out], refs[n_in + n_out :])
        moves.start()
        moves.finish()

    return pl.pallas_call(
        kernel,
        out_shape=moves.out_shapes(),
        in_specs=[ANY] * n_in,
        out_specs=[ANY] * n_out,
        scratch_shapes=moves.scratch(),
        name=name,
        compiler_params=pltpu.CompilerParams(
            collective_id=plan.identity(), has_side_effects=True, vmem_limit_bytes=32 * 2**20
        ),
    )(*moves.operands())


def lane_masks():
    lane = np.arange(WIDE)
    query, value = np.zeros((8, WIDE), np.float32), np.zeros((8, WIDE), np.float32)
    back = np.zeros((8, WIDE), np.float32)
    inner = lane % 128
    for h in range(LOCAL // HEAD):
        query[h] = ((inner < SPARE) & (inner // (HEAD // 2) == h)) | (lane == 128 + SPARE) | (lane == 129 + SPARE)
        query[h] += (lane >= 130 + SPARE + 3 * h) & (lane < 133 + SPARE + 3 * h)
        value[h] = ((lane >= HEAD) & (lane // HEAD - 1 == h)) | (lane // 16 == h)
        back[h] = ((lane >= HEAD) & (lane // HEAD - 1 == h)) | (lane == 2 * h) | (lane == 2 * h + 1)
    return query, value, back


def wide_order():
    col = np.arange(LOCAL)
    head, pair, odd = col // HEAD, col % HEAD // 2, col % 2
    return odd * 128 + head * (HEAD // 2) + pair, HEAD + col


def placing(places, width):
    return (jnp.asarray(places, jnp.int32)[:, None] == jnp.arange(width, dtype=jnp.int32)[None, :]).astype(bf16)


def widen(packed_ref, feature, key_ref, value_ref, rows):
    lane = lax.broadcasted_iota(jnp.int32, (rows, 128), 1)
    first, second = packed_ref[:, :128].astype(f32), packed_ref[:, 128:256].astype(f32)
    key_ref[:rows, :128] = jnp.where(lane < SPARE, first, 0.0).astype(bf16)
    key_ref[:rows, 128:] = jnp.where(lane < SPARE, second, feature.astype(f32)).astype(bf16)
    moved = jnp.where(lane < SPARE, pltpu.roll(first, 96, 1), second)
    value_ref[:rows, :128] = jnp.where(lane < HEAD, 1.0, moved).astype(bf16)
    value_ref[:rows, 128:] = packed_ref[:, 256:]


def pack(key_first, key_second, value_first, value_second, packed_ref, rows):
    lane = lax.broadcasted_iota(jnp.int32, (rows, 128), 1)
    packed_ref[:, :128] = jnp.where(lane < SPARE, key_first, pltpu.roll(value_first, 32, 1)).astype(bf16)
    packed_ref[:, 128:256] = jnp.where(lane < SPARE, key_second, value_first).astype(bf16)
    if value_second is not None:
        packed_ref[:, 256:] = value_second.astype(bf16)


def unpack(packed, rows):
    lane = lax.broadcasted_iota(jnp.int32, (rows, 128), 1)
    first, second = packed[:, :128].astype(f32), packed[:, 128:256].astype(f32)
    moved = jnp.where(lane < SPARE, pltpu.roll(first, 96, 1), second)
    return (
        jnp.where(lane < SPARE, first, 0.0),
        jnp.where(lane < SPARE, second, 0.0),
        jnp.where(lane < HEAD, 0.0, moved),
        packed[:, 256:].astype(f32),
    )


def fold_rows(values):
    ones = jnp.ones((8, WIDE), f32)
    sums = lax.dot_general(ones, values, (((1,), (1,)), ((), ())), precision=highest, preferred_element_type=f32)
    return jnp.concatenate([sums[0:1, 128 * i : 128 * (i + 1)] for i in range(values.shape[0] // 128)], axis=0)


def spread_rows(folded, out_ref):
    n = folded.shape[0]
    row = lax.broadcasted_iota(jnp.int32, (n, 128), 0)
    ones = jnp.ones((n, 128), f32)
    for i in range(n):
        out_ref[128 * i : 128 * (i + 1), :] = lax.dot_general(
            jnp.where(row == i, folded, 0.0),
            ones,
            (((0,), (0,)), ((), ())),
            precision=highest,
            preferred_element_type=f32,
        )


class Links:
    def __init__(self, me, send_sem, recv_sem):
        self.me, self.send_sem, self.recv_sem, self.used = me, send_sem, recv_sem, 0

    def __call__(self, src, dst, mask):
        slot = self.used
        self.used += 1
        return pltpu.make_async_remote_copy(
            src_ref=src,
            dst_ref=dst,
            send_sem=self.send_sem.at[slot],
            recv_sem=self.recv_sem.at[slot],
            device_id=flip(self.me, mask),
            device_id_type=MESH,
        )


class HandOn:
    def __init__(self, plan, me, src, dst, to_index, send_sem, recv_sem):
        place = plan.set_of(me) * M + me[2]
        there = to_index(place)
        self.src, self.dst, self.away = src, dst, there != place
        self.copy = pltpu.make_async_remote_copy(
            src_ref=src,
            dst_ref=dst,
            send_sem=send_sem,
            recv_sem=recv_sem,
            device_id=(there // (plan.times * M), there // M % plan.times, there % M),
            device_id_type=MESH,
        )

    def start(self):
        @pl.when(self.away)
        def _():
            self.copy.start()

    def wait(self):
        @pl.when(self.away)
        def _():
            self.copy.wait_recv()
            self.copy.wait_send()

        @pl.when(jnp.logical_not(self.away))
        def _():
            self.dst[...] = self.src[...]


def rows_at(index, count):
    return pl.ds(pl.multiple_of(index * count, count), count)


ASIDE, ABOVE = (0, 0, 2), (0, 0, 4)


def ring_sum(plan, link, me, buffers, product, meanwhile=lambda: None):
    to_mate, from_mate, to_chip, from_chip, part = buffers
    core, chip = me[2] % 2, me[2] // 2
    mates = [link(to_mate.at[d], from_mate.at[d], plan.mate) for d in range(4)]
    across = link(to_chip.at[2], from_chip.at[2], ASIDE)
    aside = link(to_chip.at[0], from_chip.at[0], ASIDE)
    above = link(to_chip.at[1], from_chip.at[1], ABOVE)
    for d in (3, 1, 2, 0):
        to_mate[d] = product((chip ^ d) * 2 + 1 - core).astype(bf16)
        mates[d].start()

    def both_cores(d):
        total = product((chip ^ d) * 2 + core)
        mates[d].wait_recv()
        return total + from_mate[d].astype(f32)

    to_chip[2] = both_cores(3).astype(bf16)
    across.start()
    to_chip[0] = both_cores(1).astype(bf16)
    aside.start()
    part[...] = both_cores(2)
    across.wait_recv()
    to_chip[1] = (part[...] + from_chip[2].astype(f32)).astype(bf16)
    above.start()
    part[...] = both_cores(0)
    meanwhile()
    aside.wait_recv()
    above.wait_recv()
    part[...] = part[...] + (from_chip[0].astype(f32) + from_chip[1].astype(f32))
    for copy in mates + [across, aside, above]:
        copy.wait_send()


def ring_gather(plan, link, me, all_ref, each, meanwhile=lambda: None, ready=lambda: None):
    ring = me[2]
    chip = ring // 2

    def block(place):
        return all_ref.at[rows_at(place, TOK)]

    mate = link(block(ring), block(ring), plan.mate)
    aside = link(block(ring), block(ring), ASIDE)
    above = link(block(ring), block(ring), ABOVE)
    for copy in (above, aside, mate):
        copy.start()
    meanwhile()
    later = []

    def hand_over(place):
        later.append(link(block(place), block(place), plan.mate))
        later[-1].start()

    above.wait_recv()
    onward = link(block(ring ^ 4), block(ring ^ 4), ASIDE)
    onward.start()
    hand_over(ring ^ 4)
    aside.wait_recv()
    hand_over(ring ^ 2)
    ready()
    mate.wait_recv()
    each(chip)
    later[0].wait_recv()
    each(chip ^ 2)
    later[1].wait_recv()
    each(chip ^ 1)
    onward.wait_recv()
    hand_over(ring ^ 6)
    later[2].wait_recv()
    each(chip ^ 3)
    for copy in [mate, aside, above, onward] + later:
        copy.wait_send()


def ring_share(plan, link, all_ref):
    copies = [link(all_ref.at[0], all_ref.at[i + 1], mask) for i, mask in enumerate(plan.ring)]
    for copy in copies:
        copy.start()
    return copies


def scale_of(values):
    return lax.rsqrt(jnp.mean(values * values, axis=1, keepdims=True) + epsilon)


def norm_back(d_hat, hat, inverse):
    return inverse * (d_hat - hat * jnp.mean(d_hat * hat, axis=1, keepdims=True))


RING_BUFFERS = [
    pltpu.VMEM((4, TOK, D), bf16),
    pltpu.VMEM((4, TOK, D), bf16),
    pltpu.VMEM((3, TOK, D), bf16),
    pltpu.VMEM((3, TOK, D), bf16),
    pltpu.VMEM((TOK, D), f32),
]


def params(plan, megabytes):
    return pltpu.CompilerParams(
        collective_id=plan.identity(), has_side_effects=True, vmem_limit_bytes=megabytes * 2**20
    )


def prologue(plan, tiles, package, cond, ada_weight, jobs):
    moves = Transfers([plan.gather_all(package)] + list(jobs))
    n_in, n_out = len(moves.sent), len(moves.jobs)
    total_tiles = 4 * D // 128
    peers, group = plan.all, plan.group

    def kernel(*refs):
        cond_ref, ada_ref = refs[:2]
        ins = refs[2 : 2 + n_in]
        mod_ref, cond_out = refs[2 + n_in : 4 + n_in]
        outs = refs[4 + n_in : 4 + n_in + n_out]
        refs = refs[4 + n_in + n_out :]
        cond_in, part_ref, send_ref, recv_ref, sum_ref, mod_in, send_sem, recv_sem = refs[:8]
        me = here()
        greet(me, moves.peers() | set(peers))
        link = Links(me, send_sem, recv_sem)
        swap = link(cond_ref.at[1], cond_in, plan.item)
        swap.start()
        moves.bind(me, ins, outs, refs[8:])
        moves.start(late=range(1, n_out))
        deep = ada_ref.shape[0]
        part_ref[0] = jnp.dot(cond_ref[0][:, :deep].astype(bf16), ada_ref[...], preferred_element_type=f32)
        swap.wait_recv()
        cond_out[...] = cond_in[...]
        part_ref[1] = jnp.dot(cond_in[:, :deep].astype(bf16), ada_ref[...], preferred_element_type=f32)
        for g in range(GROUPS):
            for r in range(plan.rows):
                for f in range(FRAMES):
                    for j in range(tiles):
                        tile = r * tiles + j
                        at = f * tiles + j
                        if tile < total_tiles:
                            send_ref[g, r, at : at + 1, :] = part_ref[g, f : f + 1, 128 * tile : 128 * (tile + 1)]
        copies = []
        for i, mask in enumerate(peers):
            dest = flip(me, mask)
            copies.append(link(send_ref.at[mask[0], dest[1] * M + dest[2]], recv_ref.at[i], mask))
            copies[-1].start()
        for k, job in enumerate(moves.jobs):
            if k and job.source is None:
                moves.start_job(k)
        place = me[1] * M + me[2]
        total = send_ref[0, place]
        for i, copy in enumerate(copies):
            copy.wait_recv()
            total = total + recv_ref[i]
        sum_ref[...] = total
        mod_in[place] = total
        shares = [link(sum_ref, mod_in.at[place], mask) for mask in group]
        for copy in shares:
            copy.start()
        moves.chain()
        for copy in shares:
            copy.wait_recv()
        mod_ref[...] = mod_in[...]
        for copy in [swap] + copies + shares:
            copy.wait_send()
        moves.finish()

    links = 1 + len(peers) + len(group)
    result = pl.pallas_call(
        kernel,
        out_shape=[jax.ShapeDtypeStruct((plan.rows, 8, 128), f32), jax.ShapeDtypeStruct((8, 128), f32)]
        + moves.out_shapes(),
        in_specs=[VMEM] * 2 + [ANY] * n_in,
        out_specs=[VMEM] * 2 + [ANY] * n_out,
        scratch_shapes=[
            pltpu.VMEM((8, 128), f32),
            pltpu.VMEM((GROUPS, 8, 4 * D), f32),
            pltpu.VMEM((GROUPS, plan.rows, 8, 128), f32),
            pltpu.VMEM((len(peers), 8, 128), f32),
            pltpu.VMEM((8, 128), f32),
            pltpu.VMEM((plan.rows, 8, 128), f32),
            pltpu.SemaphoreType.DMA((links,)),
            pltpu.SemaphoreType.DMA((links,)),
        ]
        + moves.scratch(),
        name="prologue",
        compiler_params=params(plan, 40),
    )(cond, ada_weight, *moves.operands())
    return result[0], result[1], result[2:]


def attention_forward(
    plan,
    latents,
    modulation,
    gains,
    first_rows,
    captions,
    text_weight,
    mix,
    text_mix,
    gain_wide,
    cos,
    sin,
    query_features,
    features,
    text_features,
    gates,
    qkv_time,
    out_shard,
    gate_send,
    up_send,
):
    heads = LOCAL // HEAD
    text_rows = captions.shape[0]
    text_deep = text_weight.shape[0]
    others = len(plan.time)
    out_job = plan.gather_time(out_shard)
    gate_job = plan.scatter_ring(gate_send)
    gate_time = plan.gather_time_source(gate_job)
    jobs = [
        plan.stack_item(qkv_time),
        out_job,
        plan.swap_source(out_job),
        gate_job,
        plan.scatter_ring(up_send),
        gate_time,
        plan.swap_source(gate_time),
    ]
    moves = Transfers(jobs)
    n_in, n_out = len(moves.sent), len(moves.jobs)
    block = 256
    chip_rows = 2 * TOK
    span = text_deep // GROUPS
    folded = 2 * ROWS // 128 + text_rows // 128
    folded_rows = -(-folded // 8) * 8

    def kernel(*refs):
        (latent_ref, mod_ref, gain_ref, first_ref, caption_ref, text_w, mix_ref, text_mix_ref) = refs[:8]
        (wide_ref, cos_ref, sin_ref, qfeature_ref, feature_ref, text_feature_ref, gate_ref, qmask_ref, vmask_ref) = refs[8:17]
        ins = refs[17 : 17 + n_in]
        refs = refs[17 + n_in :]
        (mixed_ref, self_ref, cross_ref, attn_all, query_ref, packed_out, text_packed) = refs[:7]
        (qn_ref, kn_ref, qinv_ref, kinv_ref, tn_ref, tinv_ref) = refs[7:13]
        outs = refs[13 : 13 + n_out]
        refs = refs[13 + n_out :]
        (key_ref, value_ref, packed_ref, far_ref, max_ref, raw_w, weight_ref, raw_ref, own_caps, text_part, text_far) = refs[:11]
        (text_raw, sums_ref, send_sem, recv_sem, local_sem) = refs[11:16]
        me = here()
        item, time, ring = me
        greet(me, moves.peers() | {plan.mate} | set(plan.chips) | set(plan.ring) | set(plan.time))
        link = Links(me, send_sem, recv_sem)
        moves.bind(me, ins, outs, refs[16:])
        loads = []
        for i in range(GROUPS):
            where = pl.ds(pl.multiple_of((i * plan.times + time) * span, span), span)
            loads.append(
                pltpu.make_async_copy(caption_ref.at[:, where], own_caps.at[:, i * span : (i + 1) * span], local_sem.at[i])
            )
            loads[-1].start()

        is_first = first_ref[...] > 0.5
        scale = jnp.where(is_first, mod_ref[0:1, :D], mod_ref[1:2, :D])
        rows = latent_ref[...]
        attn_in = rows * scale_of(rows) * gain_ref[0:1, :] * (1.0 + scale)
        attn_all[rows_at(ring, TOK), :] = attn_in.astype(bf16)

        text_copies = [link(text_part, text_far.at[i], mask) for i, mask in enumerate(plan.time)]

        def text_projection():
            moves.start(late=(4,))
            for copy in loads:
                copy.wait()
            text_part[...] = jnp.dot(own_caps[...], text_w[...], preferred_element_type=f32).astype(bf16)
            for copy in text_copies:
                copy.start()

        def weights_here():
            moves.take(0)
            copy = pltpu.make_async_copy(outs[0], raw_w, local_sem.at[0])
            copy.start()
            copy.wait()
            weight_ref[...] = jnp.dot(raw_w[...], mix_ref[...], preferred_element_type=f32).astype(bf16)

        def project(which):
            where = rows_at(which, chip_rows)
            raw_ref[where, :] = jnp.dot(attn_all[where, :], weight_ref[...], preferred_element_type=f32)

        ring_gather(plan, link, me, attn_all, project, text_projection, weights_here)
        moves.start_job(4)
        moves.chain(late=(6,))

        packed_ref[:, 256:] = raw_ref[:, 2 * WIDE + 128 :].astype(bf16)
        value_copies = [
            link(packed_ref.at[:, 256:], far_ref.at[i, :, 256:], mask) for i, mask in enumerate(plan.time)
        ]
        for copy in value_copies:
            copy.start()

        total = text_part[...].astype(f32)
        for i, copy in enumerate(text_copies):
            copy.wait_recv()
            total = total + text_far[i].astype(f32)
        text_raw[...] = jnp.dot(total, text_mix_ref[...].astype(f32), precision=highest, preferred_element_type=f32)
        q_raw, k_raw, t_raw = raw_ref[:, :WIDE], raw_ref[:, WIDE : 2 * WIDE], text_raw[:, :WIDE]
        squares = [fold_rows(q_raw * q_raw), fold_rows(k_raw * k_raw), fold_rows(t_raw * t_raw)]
        if folded_rows > folded:
            squares.append(jnp.zeros((folded_rows - folded, 128), f32))
        sums_ref[0] = jnp.concatenate(squares, axis=0)
        shares = ring_share(plan, link, sums_ref)
        for copy in shares:
            copy.wait_recv()
        total = sums_ref[0]
        for i in range(1, M):
            total = total + sums_ref[i]
        inverse = lax.rsqrt(total / D + epsilon)
        n = ROWS // 128
        spread_rows(inverse[:n], qinv_ref)
        spread_rows(inverse[n : 2 * n], kinv_ref)
        spread_rows(inverse[2 * n : folded], tinv_ref)

        def turn(where, at, inv_ref, n_ref, gain_row):
            first = raw_ref[where, at : at + 128] * inv_ref[where, :]
            second = raw_ref[where, at + 128 : at + 256] * inv_ref[where, :]
            n_ref[where, :128], n_ref[where, 128:] = first, second
            first = first * wide_ref[gain_row : gain_row + 1, :128]
            second = second * wide_ref[gain_row : gain_row + 1, 128:]
            cosine, sine = cos_ref[where, :], sin_ref[where, :]
            return first * cosine - second * sine, second * cosine + first * sine

        def shape(at, carry):
            where = rows_at(at, block)
            first, second = turn(where, 0, qinv_ref, qn_ref, 0)
            query_ref[where, :128] = (first.astype(bf16).astype(f32) * 0.125).astype(bf16)
            lane = lax.broadcasted_iota(jnp.int32, (block, 128), 1)
            second = jnp.where(lane < SPARE, second.astype(bf16).astype(f32) * 0.125, qfeature_ref[where, :].astype(f32))
            query_ref[where, 128:] = second.astype(bf16)
            first, second = turn(where, WIDE, kinv_ref, kn_ref, 1)
            values = raw_ref[where, 2 * WIDE :]
            pack(first, second, values[:, :128], None, packed_ref.at[where, :], block)
            return carry

        lax.fori_loop(0, ROWS // block, shape, 0)
        key_copies = [
            link(packed_ref.at[:, :256], far_ref.at[i, :, :256], mask) for i, mask in enumerate(plan.time)
        ]
        for copy in key_copies:
            copy.start()
        moves.chain()
        first = text_raw[:, :128] * tinv_ref[...]
        second = text_raw[:, 128:256] * tinv_ref[...]
        tn_ref[:, :128], tn_ref[:, 128:] = first, second
        pack(
            first * wide_ref[2:3, :128],
            second * wide_ref[2:3, 128:],
            text_raw[:, 256:384],
            text_raw[:, 384:],
            text_packed,
            text_rows,
        )

        def segment(rows, first, out_ref):
            def body(at, carry):
                where = rows_at(at, block)
                query_rows = query_ref[where, :]
                total = jnp.zeros((block, WIDE), f32)
                tops = jnp.zeros((block, WIDE), f32)
                for h in range(heads):
                    own_query = query_rows * qmask_ref[h : h + 1, :]
                    scores = lax.dot_general(
                        own_query, key_ref[:rows, :], (((1,), (1,)), ((), ())), preferred_element_type=f32
                    )
                    top = jnp.max(scores, axis=1, keepdims=True)
                    weights = jnp.exp(scores - top).astype(bf16)
                    product = jnp.dot(weights, value_ref[:rows, :], preferred_element_type=f32)
                    total += product * vmask_ref[h : h + 1, :]
                    tops += top * vmask_ref[h : h + 1, :]
                if first:
                    out_ref[where, :] = total
                    max_ref[where, :] = tops
                else:
                    before = max_ref[where, :]
                    after = jnp.maximum(before, tops)
                    out_ref[where, :] = out_ref[where, :] * jnp.exp(before - after) + total * jnp.exp(tops - after)
                    max_ref[where, :] = after
                return carry

            lax.fori_loop(0, ROWS // block, body, 0)

        def close(out_ref):
            def body(at, carry):
                where = rows_at(at, block)
                lane = lax.broadcasted_iota(jnp.int32, (block, WIDE), 1)
                values = out_ref[where, :]
                share = jnp.ones((block, WIDE), f32)
                for h in range(heads):
                    share = jnp.where(
                        (lane >= HEAD * (h + 1)) & (lane < HEAD * (h + 2)), values[:, 16 * h : 16 * h + 1], share
                    )
                logs = max_ref[where, :] + jnp.log(jnp.maximum(values, 1e-30))
                out_ref[where, :] = jnp.where(
                    lane < HEAD, jnp.where(lane < 16 * heads, logs, 0.0), values / share
                )
                return carry

            lax.fori_loop(0, ROWS // block, body, 0)

        widen(text_packed, text_feature_ref[...], key_ref, value_ref, text_rows)
        segment(text_rows, True, cross_ref)
        close(cross_ref)
        widen(packed_ref, feature_ref[rows_at(time, ROWS), :], key_ref, value_ref, ROWS)
        packed_out[time] = packed_ref[...]
        segment(ROWS, True, self_ref)
        for i, mask in enumerate(plan.time):
            key_copies[i].wait_recv()
            value_copies[i].wait_recv()
            far = time ^ mask[1]
            packed_out[far] = far_ref[i]
            widen(far_ref.at[i], feature_ref[rows_at(far, ROWS), :], key_ref, value_ref, ROWS)
            segment(ROWS, False, self_ref)
        close(self_ref)
        lane = lax.broadcasted_iota(jnp.int32, (ROWS, WIDE), 1)
        both = self_ref[...] + gate_ref[...] * cross_ref[...]
        mixed_ref[...] = jnp.where(lane < HEAD, 0.0, both).astype(bf16)
        for copy in text_copies + shares + key_copies + value_copies:
            copy.wait_send()
        moves.finish()

    qmask, vmask, _ = lane_masks()
    links = 7 + (M - 1) + 3 * others
    result = pl.pallas_call(
        kernel,
        out_shape=[
            jax.ShapeDtypeStruct((ROWS, WIDE), bf16),
            jax.ShapeDtypeStruct((ROWS, WIDE), f32),
            jax.ShapeDtypeStruct((ROWS, WIDE), f32),
            jax.ShapeDtypeStruct((ROWS, D), bf16),
            jax.ShapeDtypeStruct((ROWS, WIDE), bf16),
            jax.ShapeDtypeStruct((plan.times, ROWS, 2 * LOCAL), bf16),
            jax.ShapeDtypeStruct((text_rows, 2 * LOCAL), bf16),
            jax.ShapeDtypeStruct((ROWS, WIDE), f32),
            jax.ShapeDtypeStruct((ROWS, WIDE), f32),
            jax.ShapeDtypeStruct((ROWS, 128), f32),
            jax.ShapeDtypeStruct((ROWS, 128), f32),
            jax.ShapeDtypeStruct((text_rows, WIDE), f32),
            jax.ShapeDtypeStruct((text_rows, 128), f32),
        ]
        + moves.out_shapes(),
        in_specs=[VMEM] * 4 + [ANY] + [VMEM] * 12 + [ANY] * n_in,
        out_specs=[VMEM] * 13 + [ANY] * n_out,
        scratch_shapes=[
            pltpu.VMEM((ROWS, WIDE), bf16),
            pltpu.VMEM((ROWS, WIDE), bf16),
            pltpu.VMEM((ROWS, 2 * LOCAL), bf16),
            pltpu.VMEM((max(others, 1), ROWS, 2 * LOCAL), bf16),
            pltpu.VMEM((ROWS, WIDE), f32),
            pltpu.VMEM((D, 3 * LOCAL), bf16),
            pltpu.VMEM((D, 3 * WIDE), bf16),
            pltpu.VMEM((ROWS, 3 * WIDE), f32),
            pltpu.VMEM((text_rows, text_deep), bf16),
            pltpu.VMEM((text_rows, 2 * LOCAL), bf16),
            pltpu.VMEM((max(others, 1), text_rows, 2 * LOCAL), bf16),
            pltpu.VMEM((text_rows, 2 * WIDE), f32),
            pltpu.VMEM((M, folded_rows, 128), f32),
            pltpu.SemaphoreType.DMA((links,)),
            pltpu.SemaphoreType.DMA((links,)),
            pltpu.SemaphoreType.DMA((GROUPS,)),
        ]
        + moves.scratch(),
        name="attention_forward",
        compiler_params=params(plan, 60),
    )(
        latents,
        modulation,
        gains,
        first_rows,
        captions,
        text_weight,
        mix,
        text_mix,
        gain_wide,
        cos,
        sin,
        query_features,
        features,
        text_features,
        gates,
        jnp.asarray(qmask, bf16),
        jnp.asarray(vmask, f32),
        *moves.operands(),
    )
    return result[:13], result[13:]


def attention_backward(
    plan,
    query,
    packed_all,
    features,
    text_packed,
    text_features,
    self_out,
    cross_out,
    d_mixed,
    gates_q,
    gates_v,
    hats,
    inverses,
    text_hat,
    text_inverse,
    cos,
    sin,
    gain_wide,
    captions,
    attn_all,
    qkv_full,
    mix,
    text_mix,
    latents,
    d_state,
    modulation,
    gains,
    first_rows,
    gate_sum,
    up_sum,
    grad_out,
):
    heads = LOCAL // HEAD
    text_rows = text_packed.shape[0]
    gate_job = plan.scatter_time(gate_sum)
    up_job = plan.ring_of_times(up_sum)
    jobs = [gate_job, plan.ring_of_times(None, gate_job), up_job, plan.scatter_span(grad_out)]
    moves = Transfers(jobs)
    n_in, n_out = len(moves.sent), len(moves.jobs)
    block = 256
    others = len(plan.time)
    room = max(others, 1)
    turned = (((1,), (1,)), ((), ()))
    sunk = (((0,), (0,)), ((), ()))
    local3 = qkv_full.shape[1]
    text_deep = captions.shape[1] // plan.times
    span = text_deep // GROUPS
    set_rows = D // plan.sets
    half = set_rows // 2
    folded = 2 * ROWS // 128
    text_folded = max(8, text_rows // 128)

    def kernel(*refs):
        (query_ref, packed_in, feature_ref, text_ref, text_feature_ref, self_ref, cross_ref, d_ref) = refs[:8]
        (gateq_ref, gatev_ref, qmask_ref, bmask_ref, qn_ref, kn_ref, qinv_ref, kinv_ref, tn_ref, tinv_ref) = refs[8:18]
        (cos_ref, sin_ref, wide_ref, caption_ref, attn_ref, qkv_w, mix_ref, text_mix_ref) = refs[18:26]
        (latent_ref, d_state_ref, mod_ref, gain_ref, first_ref) = refs[26:31]
        ins = refs[31 : 31 + n_in]
        refs = refs[31 + n_in :]
        latent_grad, sums_out, wide_out, qkv_out, text_out = refs[:5]
        outs = refs[5 : 5 + n_out]
        refs = refs[5 + n_out :]
        (key_ref, value_ref, near_ref, qs_ref, ds_ref, dq_ref, dk_ref, dv_ref, tdk_ref, tdv_ref) = refs[:10]
        (to_ref, from_ref, tto_ref, tfrom_ref, du_ref, d_text, own_caps, grad_qkv, grad_text) = refs[10:19]
        (a_item, a_sum, a_time, b_time, b_sum, b_item, text_item, share_ref, tshare_ref, mean_ref) = refs[19:29]
        buffers = refs[29:34]
        send_sem, recv_sem, local_sem = refs[34:37]
        me = here()
        item, time, ring = me
        greet(me, moves.peers() | set(plan.time) | set(plan.ring) | {plan.item})
        link = Links(me, send_sem, recv_sem)
        moves.bind(me, ins, outs, refs[37:])
        moves.start(late=(3,))
        loads = []
        for i in range(GROUPS):
            where = pl.ds(pl.multiple_of((i * plan.times + time) * span, span), span)
            loads.append(
                pltpu.make_async_copy(
                    caption_ref.at[:, where], own_caps.at[:, i * span : (i + 1) * span], local_sem.at[1 + i]
                )
            )
            loads[-1].start()

        def prepare(out_ref):
            def body(at, carry):
                where = rows_at(at, block)
                lane = lax.broadcasted_iota(jnp.int32, (block, 128), 1)
                tail = query_ref[where, 128:].astype(f32)
                out_rows = out_ref[where, :]
                d_rows = d_ref[where, :].astype(f32)
                product = d_rows * out_rows
                head_tile = jnp.where(lane < HEAD, 0.0, d_rows[:, :128])
                for h in range(heads):
                    log = -out_rows[:, 16 * h : 16 * h + 1]
                    for j in range(3):
                        piece = log.astype(bf16).astype(f32)
                        log = log - piece
                        tail = jnp.where(lane == SPARE + 2 + 3 * h + j, piece, tail)
                    delta = -jnp.sum(product * bmask_ref[h : h + 1, :].astype(f32), axis=1, keepdims=True)
                    for j in range(2):
                        piece = delta.astype(bf16).astype(f32)
                        delta = delta - piece
                        head_tile = jnp.where(lane == 2 * h + j, piece, head_tile)
                qs_ref[where, :128] = query_ref[where, :128]
                qs_ref[where, 128:] = tail.astype(bf16)
                ds_ref[where, :128] = head_tile.astype(bf16)
                ds_ref[where, 128:] = d_ref[where, 128:]
                return carry

            lax.fori_loop(0, ROWS // block, body, 0)

        def segment(rows, first, k_ref, v_ref, scale):
            k_ref[...] = jnp.zeros_like(k_ref)
            v_ref[...] = jnp.zeros_like(v_ref)

            def body(at, carry):
                where = rows_at(at, block)
                query_rows, d_rows = qs_ref[where, :], ds_ref[where, :]
                total = jnp.zeros((block, WIDE), f32)
                for h in range(heads):
                    own_query = query_rows * qmask_ref[h : h + 1, :]
                    own_d = d_rows * bmask_ref[h : h + 1, :]
                    keys = key_ref[:rows, :]
                    weights = jnp.exp(lax.dot_general(keys, own_query, turned, preferred_element_type=f32))
                    d_weights = lax.dot_general(value_ref[:rows, :], own_d, turned, preferred_element_type=f32)
                    d_scores = (weights * d_weights).astype(bf16)
                    v_ref[...] += jnp.dot(weights.astype(bf16), own_d, preferred_element_type=f32)
                    k_ref[...] += jnp.dot(d_scores, own_query, preferred_element_type=f32)
                    d_query = lax.dot_general(d_scores, keys, sunk, preferred_element_type=f32)
                    total += d_query * qmask_ref[h : h + 1, :].astype(f32)
                total = total * scale
                if first:
                    dq_ref[where, :] = total
                else:
                    dq_ref[where, :] += total
                return carry

            lax.fori_loop(0, ROWS // block, body, 0)

        def bring(which):
            copy = pltpu.make_async_copy(packed_in.at[which], near_ref, local_sem.at[0])
            copy.start()
            copy.wait()
            widen(near_ref, feature_ref[rows_at(which, ROWS), :], key_ref, value_ref, ROWS)

        far_copies = [link(to_ref.at[i], from_ref.at[i], mask) for i, mask in enumerate(plan.time)]
        text_copies = [link(tto_ref, tfrom_ref.at[i], mask) for i, mask in enumerate(plan.time)]

        prepare(self_ref)
        for i, mask in enumerate(plan.time):
            bring(time ^ mask[1])
            segment(ROWS, i == 0, dk_ref, dv_ref, 0.125)
            pack(dk_ref[:, :128], dk_ref[:, 128:], dv_ref[:, :128], dv_ref[:, 128:], to_ref.at[i], ROWS)
            far_copies[i].start()
        moves.chain()
        bring(time)
        segment(ROWS, others == 0, dk_ref, dv_ref, 0.125)
        prepare(cross_ref)
        widen(text_ref, text_feature_ref[...], key_ref, value_ref, text_rows)
        segment(text_rows, False, tdk_ref, tdv_ref, 0.125 * gateq_ref[...])
        tdk_ref[...] = tdk_ref[...] * gateq_ref[...]
        tdv_ref[...] = tdv_ref[...] * gatev_ref[...]
        pack(tdk_ref[:, :128], tdk_ref[:, 128:], tdv_ref[:, :128], tdv_ref[:, 128:], tto_ref, text_rows)
        for copy in text_copies:
            copy.start()
        wide_out[...] = jnp.zeros_like(wide_out)
        wide_out[3:4, :] = jnp.sum(d_ref[...].astype(f32) * cross_ref[...], axis=0, keepdims=True)
        for i in range(others):
            far_copies[i].wait_recv()
            k_first, k_second, v_first, v_second = unpack(from_ref.at[i], ROWS)
            dk_ref[:, :128] += k_first
            dk_ref[:, 128:] += k_second
            dv_ref[:, :128] += v_first
            dv_ref[:, 128:] += v_second

        moves.start_job(3)

        def unturn(d_all, hat_ref, gain_row):
            pieces = []
            for at in range(ROWS // block):
                where = slice(at * block, (at + 1) * block)
                first, second = d_all[where, :128], d_all[where, 128:]
                cosine, sine = cos_ref[where, :], sin_ref[where, :]
                lane = lax.broadcasted_iota(jnp.int32, (block, 128), 1)
                first, second = jnp.where(lane < SPARE, first, 0.0), jnp.where(lane < SPARE, second, 0.0)
                both = jnp.concatenate([first * cosine + second * sine, second * cosine - first * sine], axis=1)
                hat = hat_ref[where, :]
                wide_out[gain_row : gain_row + 1, :] += jnp.sum(both * hat, axis=0, keepdims=True)
                both = both * wide_ref[gain_row : gain_row + 1, :]
                d_all[where, :] = both
                pieces.append(fold_rows(both * hat))
            return pieces

        pieces = unturn(dq_ref, qn_ref, 0) + unturn(dk_ref, kn_ref, 1)
        share_ref[0] = jnp.concatenate(pieces, axis=0)
        shares = ring_share(plan, link, share_ref)
        for copy in shares:
            copy.wait_recv()
        total = share_ref[0]
        for i in range(1, M):
            total = total + share_ref[i]
        total = total / D
        n = ROWS // 128

        def settle(d_all, hat_ref, inv_ref, means):
            spread_rows(means, mean_ref)
            for c in (0, 128):
                lanes = slice(c, c + 128)
                d_all[:, lanes] = (d_all[:, lanes] - hat_ref[:, lanes] * mean_ref[...]) * inv_ref[...]

        settle(dq_ref, qn_ref, qinv_ref, total[:n])
        settle(dk_ref, kn_ref, kinv_ref, total[n:])
        for at in range(ROWS // block):
            where = slice(at * block, (at + 1) * block)
            lane = lax.broadcasted_iota(jnp.int32, (block, 128), 1)
            values = jnp.concatenate([jnp.where(lane < HEAD, 0.0, dv_ref[where, :128]), dv_ref[where, 128:]], axis=1)
            wide = jnp.concatenate([dq_ref[where, :], dk_ref[where, :], values], axis=1).astype(bf16)
            du_ref[where, :] = lax.dot_general(wide, mix_ref[...], turned, preferred_element_type=f32).astype(bf16)

        away = 1 - item

        def part(i, t, which):
            return pl.ds(pl.multiple_of((i * plan.times + t) * set_rows + which * half, half), half)

        a_items = [link(grad_qkv.at[part(away, t, 0)], a_item.at[t], plan.item) for t in range(plan.times)]
        b_times = [
            link(grad_qkv.at[part(i, time ^ mask[1], 1)], b_time.at[k, i], mask)
            for k, mask in enumerate(plan.time)
            for i in range(GROUPS)
        ]
        a_times = [link(a_sum.at[time ^ mask[1]], a_time.at[k], mask) for k, mask in enumerate(plan.time)]
        b_items = [link(b_sum.at[away], b_item, plan.item)]
        text_items = [link(grad_text.at[rows_at(away, span)], text_item, plan.item)]

        def meanwhile():
            grad_qkv[...] = lax.dot_general(attn_ref[...], du_ref[...], sunk, preferred_element_type=f32).astype(bf16)
            for copy in a_items + b_times:
                copy.start()
            for i, copy in enumerate(text_copies):
                copy.wait_recv()
                k_first, k_second, v_first, v_second = unpack(tfrom_ref.at[i], text_rows)
                tdk_ref[:, :128] += k_first
                tdk_ref[:, 128:] += k_second
                tdv_ref[:, :128] += v_first
                tdv_ref[:, 128:] += v_second
            lane = lax.broadcasted_iota(jnp.int32, (text_rows, WIDE), 1) % 128
            d_keys = jnp.where(lane < SPARE, tdk_ref[...], 0.0)
            hat = tn_ref[...]
            wide_out[2:3, :] = jnp.sum(d_keys * hat, axis=0, keepdims=True)
            d_keys = d_keys * wide_ref[2:3, :]
            tdk_ref[...] = d_keys
            sums = fold_rows(d_keys * hat)
            if text_folded > text_rows // 128:
                sums = jnp.concatenate([sums, jnp.zeros((text_folded - text_rows // 128, 128), f32)], axis=0)
            tshare_ref[0] = sums
            text_shares = ring_share(plan, link, tshare_ref)
            for t, copy in enumerate(a_items):
                copy.wait_recv()
                a_sum[t] = (grad_qkv[part(item, t, 0), :].astype(f32) + a_item[t].astype(f32)).astype(bf16)
            for copy in a_times:
                copy.start()
            for copy in text_shares:
                copy.wait_recv()
            total = tshare_ref[0]
            for i in range(1, M):
                total = total + tshare_ref[i]
            total = total / D
            spread_rows(total[: text_rows // 128], mean_ref.at[:text_rows])
            for c in (0, 128):
                lanes = slice(c, c + 128)
                tdk_ref[:, lanes] = (tdk_ref[:, lanes] - tn_ref[:, lanes] * mean_ref[:text_rows, :]) * tinv_ref[...]
            lane = lax.broadcasted_iota(jnp.int32, (text_rows, WIDE), 1)
            values = jnp.where(lane < HEAD, 0.0, tdv_ref[...])
            wide = jnp.concatenate([tdk_ref[...], values], axis=1).astype(bf16)
            d_text[...] = lax.dot_general(wide, text_mix_ref[...], turned, preferred_element_type=f32).astype(bf16)
            for copy in loads:
                copy.wait()
            grad_text[...] = lax.dot_general(own_caps[...], d_text[...], sunk, preferred_element_type=f32).astype(bf16)
            text_items[0].start()
            for copy in text_shares:
                copy.wait_send()
            for copy in b_times:
                copy.wait_recv()
            for i in range(GROUPS):
                total = grad_qkv[part(i, time, 1), :].astype(f32)
                for k in range(others):
                    total = total + b_time[k, i].astype(f32)
                b_sum[i] = total.astype(bf16)
            b_items[0].start()

        def back_product(which):
            return lax.dot_general(du_ref[rows_at(which, TOK), :], qkv_w[...], turned, preferred_element_type=f32)

        ring_sum(plan, link, me, buffers, back_product, meanwhile)

        d_in = buffers[4][...]
        rows = latent_ref[...]
        inverse = scale_of(rows)
        hat = rows * inverse
        gain = gain_ref[0:1, :]
        is_first = first_ref[...] > 0.5
        scale = jnp.where(is_first, mod_ref[0:1, :D], mod_ref[1:2, :D])
        sums_out[...] = jnp.zeros_like(sums_out)
        values = d_in * (hat * gain)
        total = jnp.sum(values, axis=0, keepdims=True)
        start = jnp.sum(jnp.where(is_first, values, 0.0), axis=0, keepdims=True)
        sums_out[1:2, :] = start
        sums_out[2:3, :] = total - start
        d_norm = d_in * (1.0 + scale)
        sums_out[0:1, :] = jnp.sum(d_norm * hat, axis=0, keepdims=True)
        latent_grad[...] = d_state_ref[...] + norm_back(d_norm * gain, hat, inverse)

        total = a_sum[time].astype(f32)
        for k, copy in enumerate(a_times):
            copy.wait_recv()
            total = total + a_time[k].astype(f32)
        qkv_out[:half, :] = total.astype(bf16)
        b_items[0].wait_recv()
        qkv_out[half:, :] = (b_sum[item].astype(f32) + b_item[...].astype(f32)).astype(bf16)
        text_items[0].wait_recv()
        text_out[...] = (grad_text[rows_at(item, span), :].astype(f32) + text_item[...].astype(f32)).astype(bf16)
        for copy in far_copies + text_copies + shares + a_items + b_times + a_times + b_items + text_items:
            copy.wait_send()
        moves.finish()

    qmask, _, bmask = lane_masks()
    links = 2 * others + 2 * (M - 1) + plan.times + GROUPS * others + others + 2 + 7
    result = pl.pallas_call(
        kernel,
        out_shape=[
            jax.ShapeDtypeStruct((TOK, D), f32),
            jax.ShapeDtypeStruct((8, D), f32),
            jax.ShapeDtypeStruct((8, WIDE), f32),
            jax.ShapeDtypeStruct((set_rows, local3), bf16),
            jax.ShapeDtypeStruct((span, 2 * LOCAL), bf16),
        ]
        + moves.out_shapes(),
        in_specs=[VMEM, ANY] + [VMEM] * 19 + [ANY] + [VMEM] * 9 + [ANY] * n_in,
        out_specs=[VMEM] * 5 + [ANY] * n_out,
        scratch_shapes=[
            pltpu.VMEM((ROWS, WIDE), bf16),
            pltpu.VMEM((ROWS, WIDE), bf16),
            pltpu.VMEM((ROWS, 2 * LOCAL), bf16),
            pltpu.VMEM((ROWS, WIDE), bf16),
            pltpu.VMEM((ROWS, WIDE), bf16),
            pltpu.VMEM((ROWS, WIDE), f32),
            pltpu.VMEM((ROWS, WIDE), f32),
            pltpu.VMEM((ROWS, WIDE), f32),
            pltpu.VMEM((text_rows, WIDE), f32),
            pltpu.VMEM((text_rows, WIDE), f32),
            pltpu.VMEM((room, ROWS, 2 * LOCAL), bf16),
            pltpu.VMEM((room, ROWS, 2 * LOCAL), bf16),
            pltpu.VMEM((text_rows, 2 * LOCAL), bf16),
            pltpu.VMEM((room, text_rows, 2 * LOCAL), bf16),
            pltpu.VMEM((ROWS, local3), bf16),
            pltpu.VMEM((text_rows, 2 * LOCAL), bf16),
            pltpu.VMEM((text_rows, text_deep), bf16),
            pltpu.VMEM((D, local3), bf16),
            pltpu.VMEM((text_deep, 2 * LOCAL), bf16),
            pltpu.VMEM((plan.times, half, local3), bf16),
            pltpu.VMEM((plan.times, half, local3), bf16),
            pltpu.VMEM((room, half, local3), bf16),
            pltpu.VMEM((room, GROUPS, half, local3), bf16),
            pltpu.VMEM((GROUPS, half, local3), bf16),
            pltpu.VMEM((half, local3), bf16),
            pltpu.VMEM((span, 2 * LOCAL), bf16),
            pltpu.VMEM((M, folded, 128), f32),
            pltpu.VMEM((M, text_folded, 128), f32),
            pltpu.VMEM((ROWS, 128), f32),
        ]
        + RING_BUFFERS
        + [
            pltpu.SemaphoreType.DMA((links,)),
            pltpu.SemaphoreType.DMA((links,)),
            pltpu.SemaphoreType.DMA((1 + GROUPS,)),
        ]
        + moves.scratch(),
        name="attention_backward",
        compiler_params=params(plan, 63),
    )(
        query,
        packed_all,
        features,
        text_packed,
        text_features,
        self_out,
        cross_out,
        d_mixed,
        gates_q,
        gates_v,
        jnp.asarray(qmask, bf16),
        jnp.asarray(bmask, bf16),
        *hats,
        *inverses,
        text_hat,
        text_inverse,
        cos,
        sin,
        gain_wide,
        captions,
        attn_all,
        qkv_full,
        mix,
        text_mix,
        latents,
        d_state,
        modulation,
        gains,
        first_rows,
        *moves.operands(),
    )
    return result[:5], result[5:]


def finish(plan, small, out_sum, jobs):
    moves = Transfers(list(jobs))
    n_in, n_out = len(moves.sent), len(moves.jobs)
    peers = plan.all

    def kernel(*refs):
        small_ref, out_ref = refs[:2]
        ins = refs[2 : 2 + n_in]
        all_ref, out_grad = refs[2 + n_in : 4 + n_in]
        outs = refs[4 + n_in : 4 + n_in + n_out]
        refs = refs[4 + n_in + n_out :]
        recv_ref, sum_ref, all_in, send_sem, recv_sem, out_in = refs[:6]
        me = here()
        greet(me, moves.peers() | set(peers))
        link = Links(me, send_sem, recv_sem)
        moves.bind(me, ins, outs, refs[6:])
        copies = []
        for i, mask in enumerate(peers):
            dest = flip(me, mask)
            copies.append(link(small_ref.at[plan.set_of(dest), dest[2]], recv_ref.at[i], mask))
            copies[-1].start()
        hand_on = HandOn(
            plan, me, out_ref, out_in, lambda p: p % M * plan.sets + p // M, send_sem.at[links], recv_sem.at[links]
        )
        hand_on.start()
        moves.start()
        own = small_ref[plan.set_of(me), me[2]]
        group, everyone = own[:8], own[8:]
        for i, mask in enumerate(peers):
            copies[i].wait_recv()
            if mask[0] == 0:
                group = group + recv_ref[i, :8, :]
            everyone = everyone + recv_ref[i, 8:, :]
        sum_ref[:8, :] = group
        sum_ref[8:, :] = everyone
        place = plan.set_of(me) * M + me[2]
        shares = [link(sum_ref, all_in.at[place], mask) for mask in peers]
        for copy in shares:
            copy.start()
        all_in[place] = sum_ref[...]
        for copy in shares:
            copy.wait_recv()
        all_ref[...] = all_in[...]
        hand_on.wait()
        out_grad[...] = out_in[...].astype(f32)
        for copy in copies + shares:
            copy.wait_send()
        moves.finish()

    devices = plan.sets * M
    links = 2 * len(peers)
    result = pl.pallas_call(
        kernel,
        out_shape=[jax.ShapeDtypeStruct((devices, 16, 128), f32), jax.ShapeDtypeStruct(out_sum.shape, f32)]
        + moves.out_shapes(),
        in_specs=[VMEM] * 2 + [ANY] * n_in,
        out_specs=[VMEM] * 2 + [ANY] * n_out,
        scratch_shapes=[
            pltpu.VMEM((len(peers), 16, 128), f32),
            pltpu.VMEM((16, 128), f32),
            pltpu.VMEM((devices, 16, 128), f32),
            pltpu.SemaphoreType.DMA((links + 1,)),
            pltpu.SemaphoreType.DMA((links + 1,)),
            pltpu.VMEM(out_sum.shape, out_sum.dtype),
        ]
        + moves.scratch(),
        name="finish",
        compiler_params=params(plan, 40),
    )(small, out_sum, *moves.operands())
    return result[0], result[1], result[2:]


def deliver(gate_parts, up_parts, qkv_pieces, text_pieces, whole, sets):
    times = gate_parts.shape[1]
    k_rows, wide = gate_parts.shape[2:]
    unit = wide // sets
    t_rows = text_pieces.shape[1]
    n = len(whole)

    def kernel(gate_ref, qkv_ref, text_ref, *refs):
        up_refs, refs = refs[:times], refs[times:]
        ins, (gate_up_out, qkv_out, text_out), outs = refs[:n], refs[n : n + 3], refs[n + 3 :]
        for m in range(M):
            gate = sum(gate_ref[m, t].astype(f32) for t in range(times))
            up = sum(up_ref[m].astype(f32) for up_ref in up_refs)
            for j in range(sets):
                at = (j * M + m) * unit
                gate_up_out[:, at : at + unit] = gate[:, j * unit : (j + 1) * unit]
                gate_up_out[:, FF + at : FF + at + unit] = up[:, j * unit : (j + 1) * unit]
            piece = qkv_ref[m].astype(f32)
            for j in range(3):
                qkv_out[:, j * D + m * LOCAL : j * D + (m + 1) * LOCAL] = piece[:, j * LOCAL : (j + 1) * LOCAL]
            piece = text_ref[m].astype(f32)
            for j in range(2):
                text_out[:, j * D + m * LOCAL : j * D + (m + 1) * LOCAL] = piece[:, j * LOCAL : (j + 1) * LOCAL]
        for source, target in zip(ins, outs):
            target[...] = source[...]

    return pl.pallas_call(
        kernel,
        out_shape=[
            jax.ShapeDtypeStruct((k_rows, 2 * FF), f32),
            jax.ShapeDtypeStruct((k_rows, 3 * D), f32),
            jax.ShapeDtypeStruct((t_rows, 2 * D), f32),
        ]
        + [jax.ShapeDtypeStruct(x.shape, x.dtype) for x in whole],
        in_specs=[VMEM] * (3 + times + n),
        out_specs=[VMEM] * (3 + n),
        name="deliver",
        compiler_params=pltpu.CompilerParams(vmem_limit_bytes=48 * 2**20),
    )(gate_parts, qkv_pieces, text_pieces, *up_parts, *whole)


def feed_forward(
    plan, mixed, out_full, latents, cotangent, modulation, gains, first_rows, gate_full, up_shard, down_weight
):
    d_rows = down_weight.shape[0]
    width = plan.sets * d_rows
    deep = out_full.shape[0]
    up_job = plan.stack_time(up_shard)
    down_job = plan.stack_time(down_weight)
    moves = Transfers(
        [up_job, plan.stack_item(up_shard, up_job), down_job, plan.stack_item(down_weight, down_job)]
    )
    n_in, n_out = len(moves.sent), len(moves.jobs)
    turned = (((1,), (1,)), ((), ()))
    sunk = (((0,), (0,)), ((), ()))
    plain = (((1,), (0,)), ((), ()))
    chip_rows = 2 * TOK
    part_rows = D // GROUPS
    others = len(plan.time)
    slab = plan.times * d_rows

    def kernel(*refs):
        (mixed_ref, out_w, latent_ref, cot_ref, mod_ref, gain_ref, first_ref, gate_w) = refs[:8]
        ins = refs[8 : 8 + n_in]
        refs = refs[8 + n_in :]
        (result_ref, d_state_ref, d_mixed_ref, grad_out_ref, gate_sum_ref, up_sum_ref, down_grad_ref, sums_ref) = refs[:8]
        outs = refs[8 : 8 + n_out]
        refs = refs[8 + n_out :]
        (up_w, down_w, ffn_all, down_all, proj_all, gate_ref, up_ref, act_ref, d_gate_ref, d_up_ref) = refs[:10]
        (grad_gate, grad_up, grad_down, from_gate, from_up, from_down, down_sum, from_time) = refs[10:18]
        (to_mate, from_mate, to_chip, from_chip, part, proj_ref, state_ref, own_ref, send_sem, recv_sem, local_sem) = refs[
            18:29
        ]
        me = here()
        item, time, ring = me
        core, chip = ring % 2, ring // 2
        greet(me, moves.peers() | {plan.mate, plan.item} | set(plan.chips) | set(plan.time))
        moves.bind(me, ins, outs, refs[29:])
        moves.start(late=(2,))
        link = Links(me, send_sem, recv_sem)
        buffers = (to_mate, from_mate, to_chip, from_chip, part)

        def scatter(product, meanwhile=lambda: None):
            ring_sum(plan, link, me, buffers, product, meanwhile)

        def gather(all_ref, each, meanwhile=lambda: None, ready=lambda: None):
            ring_gather(plan, link, me, all_ref, each, meanwhile, ready)

        is_first = first_ref[...] > 0.5

        def modulated(index):
            cols = pl.ds(index * D, D)
            return jnp.where(is_first, mod_ref[0:1, cols], mod_ref[1:2, cols])

        def column_sums(at, values):
            total = jnp.sum(values, axis=0, keepdims=True)
            start = jnp.sum(jnp.where(is_first, values, 0.0), axis=0, keepdims=True)
            sums_ref[at : at + 1, :] = start
            sums_ref[at + 1 : at + 2, :] = total - start

        def scale_of(values):
            return lax.rsqrt(jnp.mean(values * values, axis=1, keepdims=True) + epsilon)

        def norm_back(d_hat, hat, inverse):
            return inverse * (d_hat - hat * jnp.mean(d_hat * hat, axis=1, keepdims=True))

        def load(job, target):
            moves.take(job)
            copy = pltpu.make_async_copy(outs[job], target, local_sem.at[0])
            copy.start()
            copy.wait()

        def out_product(block):
            return jnp.dot(mixed_ref[rows_at(block, TOK), :], out_w[...], preferred_element_type=f32)

        def next_weights():
            moves.chain(late=(3,))
            moves.start_job(2)

        scatter(out_product, next_weights)
        proj_ref[...] = part[...]
        proj = proj_ref[...]
        gate_attn = jnp.tanh(modulated(1))
        state_ref[...] = latent_ref[...] + gate_attn * (proj * scale_of(proj) * gain_ref[1:2, :])
        state = state_ref[...]
        ffn_in = state * scale_of(state) * gain_ref[2:3, :] * (1.0 + modulated(2))
        ffn_all[rows_at(ring, TOK), :] = ffn_in.astype(bf16)

        def forward_chip(which):
            rows = rows_at(which, chip_rows)
            block = ffn_all[rows, :]
            gate = jnp.dot(block, gate_w[...], preferred_element_type=f32)
            up = jnp.dot(block, up_w[...], preferred_element_type=f32)
            gate_ref[rows, :] = gate
            up_ref[rows, :] = up
            act_ref[rows, :] = (gate * (1.0 / (1.0 + jnp.exp(-gate))) * up).astype(bf16)

        def weights_here():
            load(1, up_w)

        gather(ffn_all, forward_chip, moves.chain, weights_here)

        load(3, down_w)

        def down_product(block):
            return jnp.dot(act_ref[rows_at(block, TOK), :], down_w[...], preferred_element_type=f32)

        scatter(down_product)

        down = part[...]
        inverse = scale_of(down)
        hat = down * inverse
        gate_ffn = jnp.tanh(modulated(3))
        gain = gain_ref[3:4, :]
        cot = cot_ref[...]
        result_ref[...] = state_ref[...] + gate_ffn * (hat * gain)
        column_sums(7, cot * (hat * gain) * (1.0 - gate_ffn * gate_ffn))
        d_norm = cot * gate_ffn
        sums_ref[2:3, :] = jnp.sum(d_norm * hat, axis=0, keepdims=True)
        down_all[rows_at(ring, TOK), :] = norm_back(d_norm * gain, hat, inverse).astype(bf16)

        def backward_chip(which):
            rows = rows_at(which, chip_rows)
            d_act = lax.dot_general(down_all[rows, :], down_w[...], turned, preferred_element_type=f32)
            gate, up = gate_ref[rows, :], up_ref[rows, :]
            sigmoid = 1.0 / (1.0 + jnp.exp(-gate))
            d_up_ref[rows, :] = (d_act * (gate * sigmoid)).astype(bf16)
            d_gate_ref[rows, :] = (d_act * up * (sigmoid * (1.0 + gate * (1.0 - sigmoid)))).astype(bf16)

        gather(down_all, backward_chip)

        away = 1 - item
        down_link = link(grad_down.at[rows_at(away, slab)], from_down, plan.item)
        gate_link = link(grad_gate.at[rows_at(away, part_rows)], from_gate, plan.item)
        up_link = link(grad_up.at[rows_at(away, part_rows)], from_up, plan.item)
        time_links = [link(down_sum.at[rows_at(time ^ mask[1], d_rows)], from_time.at[i], mask) for i, mask in enumerate(plan.time)]

        def down_gradient():
            grad_down[...] = lax.dot_general(act_ref[...], down_all[...], sunk, preferred_element_type=f32).astype(bf16)
            down_link.start()

        down_gradient()

        def gate_gradients():
            grad_gate[...] = lax.dot_general(ffn_all[...], d_gate_ref[...], sunk, preferred_element_type=f32).astype(bf16)
            gate_link.start()
            grad_up[...] = lax.dot_general(ffn_all[...], d_up_ref[...], sunk, preferred_element_type=f32).astype(bf16)
            up_link.start()

        def back_product(block):
            rows = rows_at(block, TOK)
            return lax.dot_general(d_gate_ref[rows, :], gate_w[...], turned, preferred_element_type=f32) + lax.dot_general(
                d_up_ref[rows, :], up_w[...], turned, preferred_element_type=f32
            )

        scatter(back_product, gate_gradients)

        d_ffn = part[...]
        state = state_ref[...]
        inverse = scale_of(state)
        hat = state * inverse
        gain = gain_ref[2:3, :]
        column_sums(5, d_ffn * (hat * gain))
        d_norm = d_ffn * (1.0 + modulated(2))
        sums_ref[1:2, :] = jnp.sum(d_norm * hat, axis=0, keepdims=True)
        d_state_ref[...] = cot_ref[...] + norm_back(d_norm * gain, hat, inverse)
        d_state = d_state_ref[...]
        proj = proj_ref[...]
        inverse = scale_of(proj)
        hat = proj * inverse
        gate_attn = jnp.tanh(modulated(1))
        gain = gain_ref[1:2, :]
        column_sums(3, d_state * (hat * gain) * (1.0 - gate_attn * gate_attn))
        d_norm = d_state * gate_attn
        sums_ref[0:1, :] = jnp.sum(d_norm * hat, axis=0, keepdims=True)
        proj_all[rows_at(ring, TOK), :] = norm_back(d_norm * gain, hat, inverse).astype(bf16)

        def down_time():
            down_link.wait_recv()
            mine = grad_down[rows_at(item, slab), :].astype(f32) + from_down[...].astype(f32)
            down_sum[...] = mine.astype(bf16)
            for copy in time_links:
                copy.start()

        def mixed_chip(which):
            rows = rows_at(which, chip_rows)
            d_mixed_ref[rows, :] = lax.dot_general(
                proj_all[rows, :], out_w[...], turned, preferred_element_type=f32
            ).astype(bf16)

        gather(proj_all, mixed_chip, ready=down_time)
        grad_out_ref[...] = lax.dot_general(mixed_ref[...], proj_all[...], sunk, preferred_element_type=f32).astype(bf16)
        gate_link.wait_recv()
        gate_sum_ref[...] = (
            grad_gate[rows_at(item, part_rows), :].astype(f32) + from_gate[...].astype(f32)
        ).astype(bf16)
        own_ref[...] = down_sum[rows_at(time, d_rows), :].astype(f32)
        for i, copy in enumerate(time_links):
            copy.wait_recv()
            own_ref[...] += from_time[i].astype(f32)
        down_grad_ref[...] = own_ref[...]
        up_link.wait_recv()
        up_sum_ref[...] = (grad_up[rows_at(item, part_rows), :].astype(f32) + from_up[...].astype(f32)).astype(bf16)
        for copy in [down_link, gate_link, up_link] + time_links:
            copy.wait_send()
        moves.finish()

    links = 7 * 3 + 7 * 3 + 3 + others
    result = pl.pallas_call(
        kernel,
        out_shape=[
            jax.ShapeDtypeStruct((TOK, D), f32),
            jax.ShapeDtypeStruct((TOK, D), f32),
            jax.ShapeDtypeStruct((ROWS, deep), bf16),
            jax.ShapeDtypeStruct((deep, D), bf16),
            jax.ShapeDtypeStruct((part_rows, width), bf16),
            jax.ShapeDtypeStruct((part_rows, width), bf16),
            jax.ShapeDtypeStruct((d_rows, D), f32),
            jax.ShapeDtypeStruct((16, D), f32),
        ]
        + moves.out_shapes(),
        in_specs=[VMEM] * 8 + [ANY] * n_in,
        out_specs=[VMEM] * 8 + [ANY] * n_out,
        scratch_shapes=[
            pltpu.VMEM((D, width), bf16),
            pltpu.VMEM((width, D), bf16),
            pltpu.VMEM((ROWS, D), bf16),
            pltpu.VMEM((ROWS, D), bf16),
            pltpu.VMEM((ROWS, D), bf16),
            pltpu.VMEM((ROWS, width), f32),
            pltpu.VMEM((ROWS, width), f32),
            pltpu.VMEM((ROWS, width), bf16),
            pltpu.VMEM((ROWS, width), bf16),
            pltpu.VMEM((ROWS, width), bf16),
            pltpu.VMEM((D, width), bf16),
            pltpu.VMEM((D, width), bf16),
            pltpu.VMEM((width, D), bf16),
            pltpu.VMEM((part_rows, width), bf16),
            pltpu.VMEM((part_rows, width), bf16),
            pltpu.VMEM((slab, D), bf16),
            pltpu.VMEM((slab, D), bf16),
            pltpu.VMEM((max(others, 1), d_rows, D), bf16),
            pltpu.VMEM((4, TOK, D), bf16),
            pltpu.VMEM((4, TOK, D), bf16),
            pltpu.VMEM((3, TOK, D), bf16),
            pltpu.VMEM((3, TOK, D), bf16),
            pltpu.VMEM((TOK, D), f32),
            pltpu.VMEM((TOK, D), f32),
            pltpu.VMEM((TOK, D), f32),
            pltpu.VMEM((d_rows, D), f32),
            pltpu.SemaphoreType.DMA((links,)),
            pltpu.SemaphoreType.DMA((links,)),
            pltpu.SemaphoreType.DMA((1,)),
        ]
        + moves.scratch(),
        name="feed_forward",
        compiler_params=params(plan, 60),
    )(mixed, out_full, latents, cotangent, modulation, gains, first_rows, gate_full, *moves.operands())
    return result[:8]


def shards(
    latents,
    conditions,
    captions,
    row_counts,
    text_lengths,
    qkv_weight,
    text_weight,
    out_weight,
    gate_up_weight,
    down_weight,
    ada_weight,
    ada_bias,
    norm_gains,
    head_gates,
    cotangent,
):
    times = lax.axis_size("times")
    plan = Plan(times)
    sets, rows_axis = plan.sets, plan.rows
    devices = sets * M
    item, time, ring = here()
    place = (item * times + time) * M + ring
    group_place = time * M + ring
    heads = LOCAL // HEAD

    k_rows = qkv_weight.shape[0]
    t_rows = text_weight.shape[0]
    o_rows = out_weight.shape[0]
    d_rows = down_weight.shape[0]
    a_rows = ada_weight.shape[0]
    bias_n = ada_bias.shape[0]
    gain_n = norm_gains.shape[1]
    tiles = -(-(4 * D // 128) // rows_axis)

    package = jnp.concatenate(
        [norm_gains.astype(f32).reshape(-1), ada_bias.astype(f32), row_counts[0, 0].astype(f32)]
    )
    package_n = package.shape[0]
    lines = -(-package_n // 1024) * 8
    package = jnp.pad(package, (0, lines * 128 - package_n)).reshape(lines, 128)

    silu = jax.nn.silu(conditions[0].astype(f32)).astype(bf16).astype(f32)
    other_place = ((1 - item) * times + time) * M + ring
    cond = jnp.stack(
        [lax.dynamic_slice_in_dim(silu, p * a_rows, a_rows, 1) for p in (place, other_place)]
    )
    cond = jnp.pad(cond, ((0, 0), (0, 8 - FRAMES), (0, 128 - a_rows)))

    key_places, value_places = wide_order()
    mix = placing(np.concatenate([key_places, WIDE + key_places, 2 * WIDE + value_places]), 3 * WIDE)
    text_mix = placing(np.concatenate([key_places, WIDE + value_places]), 2 * WIDE)
    qkv_send = qkv_weight.reshape(k_rows, 3, M, LOCAL).transpose(2, 0, 1, 3).reshape(M, k_rows, 3 * LOCAL)
    text_send = text_weight.reshape(t_rows, 2, M, LOCAL).transpose(2, 0, 1, 3).reshape(M, t_rows, 2 * LOCAL)
    gate_up_send = gate_up_weight.reshape(k_rows, 2, sets, M, d_rows).transpose(1, 3, 0, 2, 4)
    gate_up_send = gate_up_send.reshape(2, M, k_rows, sets * d_rows)
    out_forth = [(o, (o % sets) * M + o // sets) for o in range(devices)]
    out_back = [(b, a) for a, b in out_forth]
    axes = ("items", "times", "ring")
    out_shard = lax.ppermute(out_weight, axes, out_forth)

    text_job = plan.scatter_ring(text_send)
    mod_tiles, cond_other, (packages, _, text_full, qkv_time) = prologue(
        plan,
        tiles,
        package,
        cond,
        ada_weight,
        [text_job, plan.swap_source(text_job), plan.scatter_group_ring(qkv_send)],
    )
    packages = packages.reshape(devices, lines * 128)
    gains = packages[:, : 7 * gain_n].reshape(devices, 7, gain_n).transpose(1, 0, 2).reshape(7, D)
    gains = jnp.pad(gains, ((0, 1), (0, 0)))
    bias = packages[:, 7 * gain_n : 7 * gain_n + bias_n].reshape(4 * D)
    counts_all = packages[:, 7 * gain_n + bias_n : package_n].astype(jnp.int32).reshape(GROUPS, rows_axis, FRAMES)
    counts = lax.dynamic_index_in_dim(counts_all, item, 0, keepdims=False)

    def from_tiles(array):
        lead = array.shape[:-3]
        array = array[..., : FRAMES * tiles, :].reshape(lead + (rows_axis, FRAMES, tiles, 128))
        array = jnp.moveaxis(array, -3, -4).reshape(lead + (FRAMES, rows_axis * tiles * 128))
        return array[..., : 4 * D]

    modulation = from_tiles(mod_tiles) + bias

    line = jnp.arange(TOK, dtype=jnp.int32)[None, :]
    clip = counts[:, :1]
    before = jnp.cumsum(counts, axis=0) - counts
    frame_all = (line >= clip).astype(jnp.int32)
    position_all = jnp.where(frame_all == 0, before[:, :1] + line, before[:, 1:] + line - clip)
    frame_k = frame_all.reshape(-1)
    frame_q = lax.dynamic_slice_in_dim(frame_k, time * ROWS, ROWS)
    position_q = lax.dynamic_slice_in_dim(position_all.reshape(-1), time * ROWS, ROWS).astype(f32)
    frame_own = lax.dynamic_index_in_dim(frame_all, group_place, 0, keepdims=False)
    first_rows = (frame_own == 0).astype(f32)[:, None]
    text_line = jnp.arange(FRAMES * TEXT, dtype=jnp.int32)
    text_frame = text_line // TEXT
    text_live = text_line % TEXT < jnp.repeat(text_lengths[0], TEXT)

    feature = jnp.arange(128, dtype=jnp.int32)[None, :]

    def key_features(apart_first, apart_second):
        ones = (feature >= SPARE + 2) & (feature < SPARE + 2 + 3 * heads)
        pick = jnp.where(feature == SPARE, apart_first[:, None], (feature == SPARE + 1) & apart_second[:, None])
        return jnp.where(pick | ones, 1.0, 0.0).astype(bf16)

    features = key_features(frame_k == 1, frame_k == 0)
    text_features = key_features(~((text_frame == 0) & text_live), ~((text_frame == 1) & text_live))
    query_features = jnp.where(feature == SPARE + frame_q[:, None], -APART, 0.0).astype(bf16)
    pair = jnp.arange(128, dtype=jnp.int32)
    frequency = theta_base ** (-2.0 * (pair % (HEAD // 2)).astype(f32) / HEAD)
    angle = position_q[:, None] * frequency[None, :]
    live_lane = (pair < SPARE)[None, :]
    cos, sin = jnp.where(live_lane, jnp.cos(angle), 0.0), jnp.where(live_lane, jnp.sin(angle), 0.0)
    own_gates = jnp.tanh(lax.dynamic_slice_in_dim(head_gates.astype(f32), ring * heads, heads))
    gates_v = jnp.concatenate([jnp.zeros((HEAD,), f32), jnp.repeat(own_gates, HEAD)]).reshape(1, WIDE)
    half_gates = jnp.pad(jnp.repeat(own_gates, HEAD // 2), (0, 128 - SPARE))
    gates_q = jnp.concatenate([half_gates, half_gates]).reshape(1, WIDE)
    gain_wide = lax.dynamic_slice(gains, (4, ring * LOCAL), (3, LOCAL))
    gain_wide = gain_wide.reshape(3, heads, HEAD // 2, 2).transpose(0, 3, 1, 2).reshape(3, 2, SPARE)
    gain_wide = jnp.pad(gain_wide, ((0, 5), (0, 0), (0, 128 - SPARE))).reshape(8, WIDE)

    inputs = latents[0]
    caption_rows = captions[0].reshape(FRAMES * TEXT, TEXT_DIM)
    forward, (qkv_full, _, out_full, _, up_shard, _, gate_full) = attention_forward(
        plan,
        inputs,
        modulation,
        gains,
        first_rows,
        caption_rows,
        text_full.reshape(GROUPS * M * t_rows, 2 * LOCAL),
        mix,
        text_mix,
        gain_wide,
        cos,
        sin,
        query_features,
        features,
        text_features,
        gates_v,
        qkv_time.reshape(times * M * k_rows, 3 * LOCAL),
        out_shard,
        gate_up_send[0],
        gate_up_send[1],
    )
    (mixed, self_out, cross_out, attn_all, query, packed_all, text_packed, qn, kn, q_inv, k_inv, tn, t_inv) = forward
    out_full = jnp.pad(out_full.reshape(LOCAL, D), ((HEAD, 0), (0, 0)))

    (result_rows, d_state, d_mixed, grad_out, gate_sum, up_sum, down_grad, ffn_sums) = feed_forward(
        plan,
        mixed,
        out_full,
        inputs,
        cotangent[0],
        modulation,
        gains,
        first_rows,
        gate_full.reshape(D, sets * d_rows),
        up_shard.reshape(M * k_rows, sets * d_rows),
        down_weight,
    )
    ring_shape = (times, M, k_rows, sets * d_rows)
    (grad_latent, attn_sums, wide_sums, qkv_sum, text_sum), (_, gate_parts, up_pieces, out_parts) = attention_backward(
        plan,
        query,
        packed_all,
        features,
        text_packed,
        text_features,
        self_out,
        cross_out,
        d_mixed,
        gates_q,
        gates_v,
        (qn, kn),
        (q_inv, k_inv),
        tn,
        t_inv,
        cos,
        sin,
        gain_wide,
        caption_rows,
        attn_all,
        qkv_full,
        mix,
        text_mix,
        inputs,
        d_state,
        modulation,
        gains,
        first_rows,
        gate_sum.reshape(ring_shape),
        up_sum.reshape(ring_shape),
        grad_out[HEAD:].reshape(sets, o_rows, D),
    )

    def add(parts, axis=0):
        return jnp.sum(parts.astype(f32), axis=axis)

    d_mod = jnp.concatenate([attn_sums[1:3], ffn_sums[3:5], ffn_sums[5:7], ffn_sums[7:9]], axis=1)
    d_mod = jnp.pad(d_mod, ((0, 0), (0, rows_axis * tiles * 128 - 4 * D)))
    d_mod = d_mod.reshape(FRAMES, rows_axis, tiles, 128).transpose(1, 0, 2, 3).reshape(rows_axis, FRAMES * tiles, 128)
    d_mod = jnp.pad(d_mod, ((0, 0), (0, 8 - FRAMES * tiles), (0, 0)))
    d_mod = jnp.tile(d_mod, (GROUPS, 1, 1))
    wide_gains = wide_sums[:3].reshape(3, 2, 128)[:, :, :SPARE].reshape(3, 2, heads, HEAD // 2)
    wide_gains = wide_gains.transpose(0, 2, 3, 1).reshape(3, LOCAL)
    wide_gains = wide_gains * jnp.stack([jnp.ones(()), jnp.ones(()), (time == 0).astype(f32)])[:, None]
    wide_gains = lax.dynamic_update_slice(jnp.zeros((3, D), f32), wide_gains, (0, ring * LOCAL))
    gate_sums = jnp.sum(wide_sums[3, HEAD:].reshape(heads, HEAD), axis=1) * (1.0 - own_gates * own_gates)
    gate_row = lax.dynamic_update_slice_in_dim(jnp.zeros((1, D), f32), gate_sums[None], ring * heads, 1)
    d_gains = jnp.concatenate([attn_sums[:1], ffn_sums[:3], wide_gains, gate_row], axis=0)
    gain_tiles = D // 128
    d_gains = d_gains.reshape(8, gain_tiles, 128).transpose(1, 0, 2)
    d_gains = jnp.pad(d_gains, ((0, devices - gain_tiles), (0, 0), (0, 0)))
    small = jnp.concatenate([d_mod, d_gains], axis=1).reshape(sets, M, 16, 128)
    out_sum = add(out_parts).astype(bf16)
    up_own = lax.dynamic_index_in_dim(up_pieces, time, 1, keepdims=False)
    up_sends = [lax.dynamic_index_in_dim(up_pieces, time ^ t, 1, keepdims=False) for t in range(1, times)]
    small, out_sum, up_sends = lax.optimization_barrier((small, out_sum, up_sends))
    up_parts = [up_own] + [
        lax.ppermute(x, "times", [(a, a ^ (t + 1)) for a in range(times)]) for t, x in enumerate(up_sends)
    ]
    small_all, out_grad, (qkv_pieces, text_pieces) = finish(
        plan,
        small,
        out_sum,
        [
            plan.scatter_ring(qkv_sum.reshape(M, k_rows, 3 * LOCAL)),
            plan.scatter_ring(text_sum.reshape(M, t_rows, 2 * LOCAL)),
        ],
    )
    gains_all = small_all[:gain_tiles, 8:].transpose(1, 0, 2).reshape(8, D)
    gains_grad = lax.dynamic_slice_in_dim(gains_all[:7], place * gain_n, gain_n, 1)
    gates_grad = gains_all[7, :HEADS]
    d_mod_all = from_tiles(small_all[:, :8].reshape(GROUPS, rows_axis, 8, 128)).reshape(GROUPS * FRAMES, 4 * D)
    cond_own, cond_other = cond[0, :FRAMES], cond_other[:FRAMES]
    silu_both = jnp.where(
        item == 0, jnp.concatenate([cond_own, cond_other]), jnp.concatenate([cond_other, cond_own])
    )
    ada_grad = jnp.einsum("fc,fd->cd", silu_both[:, :a_rows], d_mod_all, precision=highest)
    bias_grad = lax.dynamic_slice_in_dim(jnp.sum(d_mod_all, axis=0), place * bias_n, bias_n)
    gate_up_grad, qkv_grad, text_grad, result_rows, grad_latent, down_grad, out_grad = deliver(
        gate_parts, up_parts, qkv_pieces, text_pieces, [result_rows, grad_latent, down_grad, out_grad], sets
    )
    return (
        result_rows[None],
        grad_latent[None],
        qkv_grad,
        text_grad,
        out_grad,
        gate_up_grad,
        down_grad,
        ada_grad,
        bias_grad,
        gains_grad,
        gates_grad,
    )


def solution(mesh):
    items, rows = mesh.shape["items"], mesh.shape["rows"]
    fine = Mesh(mesh.devices.reshape(items, rows // M, M), ("items", "times", "ring"))
    whole = ("items", "times", "ring")
    rows_of = ("times", "ring")
    return jax.shard_map(
        shards,
        mesh=fine,
        in_specs=(
            P("items", rows_of, None),
            P("items", None, None),
            P("items", None, None, None),
            P("items", rows_of, None),
            P("items", None),
            P(whole, None),
            P(whole, None),
            P(whole, None),
            P(whole, None),
            P(whole, None),
            P(whole, None),
            P(whole),
            P(None, whole),
            P(),
            P("items", rows_of, None),
        ),
        out_specs=(
            P("items", rows_of, None),
            P("items", rows_of, None),
            P(whole, None),
            P(whole, None),
            P(whole, None),
            P(whole, None),
            P(whole, None),
            P(whole, None),
            P(whole),
            P(None, whole),
            P(),
        ),
        check_vma=False,
    )
```
